32 devices in a mesh: pipe: 2 (over y), expert: 16 (over z, x, core).
Axes of the slice: x: 2, y: 2, z: 4, core: 2. Of those that a mesh axis runs over, the one named last changes fastest.
Arguments:
- upstream: bfloat16 [2, 1024, 2048], P('pipe', 'expert'), may hold values from -6 to 6
- expert_ids: int32 [2, 1024, 8], P('pipe', 'expert'), may hold values from 0 to 15, all different within a row; in each aligned block of 64 rows (0 to 63, 64 to 127, ..., all dimensions but the last counted through in order) at most 64 rows name the same one
- gate_weights: bfloat16 [2, 1024, 8], P('pipe', 'expert'), may hold values from 0.099609375 to 2
- expert_weight: bfloat16 [2, 16, 768, 2048], P('pipe', 'expert'), may hold values from -0.125 to 0.125
Outputs:
- hidden_grad: bfloat16 [2, 1024, 8, 768], P('pipe', 'expert')
The draws below stay inside these ranges and needn't reach their ends.
Inputs may be any that keep to these rules, and one draw needn't show every extreme that they name: `expert_ids`: each token names 8 different experts. Among the 64 tokens of one device (aligned blocks of the section's tokens) no expert is named by more than 64 tokens, and in some blocks one expert is named by exactly 64.
All inputs are finite; a program needn't handle non-finite values.
Results may differ from the reference program's by a relative error of at most 0.001.
Values may be sent and summed in bfloat16 or wider, within the bound.
No kernel may reach another device: no remote copies, remote signals or barrier semaphores. Data moves between devices by JAX's collectives and lax.ppermute only.
A program may use at most 64 MiB of HBM per device.

```python
import math
import jax
import jax.numpy as jnp
import numpy as np
from jax import lax

D = 2048
HID = 768
TOPK = 8
TOK_DEV = 64
SECTIONS = 2
EXPERTS = 16
TOKENS = 1024
MOST = 64
N_EXPERT = 16


def block_scale(stream_key, dims, pieces, low, top_value):
    def one(dim, blocks):
        heights = jax.random.uniform(jax.random.fold_in(jax.random.fold_in(stream_key, 6), dim), (blocks,), jnp.float32, low / len(pieces), top_value / len(pieces))
        return jnp.repeat(jnp.exp(heights), dims[dim] // blocks).reshape((-1,) + (1,) * (len(dims) - dim - 1))

    factor_of = one(*pieces[0])
    for cut in pieces[1:]:
        factor_of = factor_of * one(*cut)
    return factor_of


def shared_out(rng, own, number, rows, amount, top, limit, skew):
    sequence = jax.random.permutation(rng, amount)
    packed, common = shares(amount, rows * top, limit, skew, True), shares(amount, rows * top, limit, skew, False)
    places = jnp.arange(amount)

    def named(lengths, rotation):
        used = int((lengths > 0).sum())
        fixed = max(1, used // 4)
        shifted = fixed + (places - fixed + rotation * (used - fixed)) % max(1, amount - fixed)
        return jnp.zeros((amount,), jnp.int32).at[sequence[jnp.where(places < fixed, places, shifted)]].set(jnp.asarray(lengths, jnp.int32))

    lengths = jnp.where(number % 4 == 0, named(packed, number // 4), named(common, number - number // 4 - 1))
    mixed = jax.random.permutation(jax.random.fold_in(own, 3), amount)
    giver, sink = mixed[0:amount // 2 * 2:2], mixed[1:amount // 2 * 2:2]
    slack = jnp.minimum(lengths[giver] - 1, limit - lengths[sink]) // 2
    slack = jnp.where((giver == sequence[0]) | (sink == sequence[0]) | (lengths[sink] == 0), 0, jnp.maximum(slack, 0))
    shifted = jax.random.randint(jax.random.fold_in(own, 4), (amount // 2,), 0, 1 << 20) % (slack + 1)
    lengths = lengths.at[giver].add(-shifted).at[sink].add(shifted)
    labels = jnp.searchsorted(jnp.cumsum(lengths), jnp.arange(rows * top), side="right").astype(jnp.int32)
    grid = labels.reshape(top, rows).T
    grid = grid[jax.random.permutation(jax.random.fold_in(own, 1), rows)]
    rotation = jax.random.randint(jax.random.fold_in(own, 2), (rows, 1), 0, top)
    return jnp.take_along_axis(grid, (jnp.arange(top)[None, :] + rotation) % top, axis=1)


def shares(amount, total, most, lean, full):
    weights = [(1 << 20) // math.isqrt(rank ** lean) + 1 for rank in range(1, amount + 1)]
    largest = most if full else min(most, max(-(-total // amount), total * weights[0] // sum(weights)))
    least = 1 if total - largest >= amount - 1 else 0
    counts, rest = [largest] + [least] * (amount - 1), total - largest - least * (amount - 1)
    while rest > 0:
        free = [i for i in range(1, amount) if counts[i] < largest] or [i for i in range(1, amount) if counts[i] < most]
        mass, budget = sum([weights[i] for i in free]), rest
        for i in free:
            more = min(most - counts[i], max(1, budget * weights[i] // mass), rest)
            counts[i] = counts[i] + more
            rest = rest - more
    return np.array(counts)


def centred(key, shape, spread, reach, shards=(), kind=jnp.bfloat16):
    result = spread * jax.random.normal(key, shape, jnp.float32)
    if shards:
        result = result * block_scale(key, shape, shards, -0.22, 0.18)
    return jnp.clip(result, -reach, reach).astype(kind)


def setup_inputs(seed: int = 0) -> dict:
    key_of = jax.random.split(jax.random.key(seed), 5)
    upstream = centred(key_of[0], (SECTIONS, TOKENS, D), 1.0, 6.0, ((0, 2), (1, 16)))
    expert_ids_keys = jax.random.split(jax.random.fold_in(key_of[1], 1), SECTIONS * TOKENS // TOK_DEV)
    expert_ids_turns = jax.random.permutation(jax.random.fold_in(key_of[1], 3), SECTIONS * TOKENS // TOK_DEV)
    expert_ids = jax.vmap(lambda own, number: shared_out(jax.random.fold_in(key_of[1], 2), own, number, TOK_DEV, EXPERTS, TOPK, MOST, 2))(expert_ids_keys, expert_ids_turns).reshape((SECTIONS, TOKENS, TOPK))
    gate_weights = jnp.clip(jnp.exp(math.log(2.0) - 2.9996462 * jax.random.uniform(key_of[2], (SECTIONS, TOKENS, TOPK), jnp.float32) ** block_scale(key_of[2], (SECTIONS, TOKENS, TOPK), ((0, 2), (1, 16)), -0.2, 0.2)), 0.099609375, 2.0).astype(jnp.bfloat16)
    expert_weight = centred(key_of[3], (SECTIONS, EXPERTS, HID, D), D ** -0.5, 0.125, ((0, 2), (1, 16)))
    return {"upstream": upstream, "expert_ids": expert_ids, "gate_weights": gate_weights, "expert_weight": expert_weight}


def route_ranks(flat_routes):
    owners = jnp.arange(EXPERTS, dtype=jnp.int32)
    matched = (flat_routes[:, None] == owners[None, :]).astype(jnp.int32)
    before = (jnp.cumsum(matched, axis=0) - matched).astype(jnp.int32)
    return jnp.sum(before * matched, axis=1).astype(jnp.int32)


def reference(upstream, expert_ids, gate_weights, expert_weight):
    section_grads = jnp.roll(upstream, -1, axis=0)
    capacity = N_EXPERT * MOST
    route_count = TOKENS * TOPK

    def one_section(inputs):
        token_grads, section_ids, section_gates, section_weights = inputs
        flat_routes = section_ids.reshape(route_count).astype(jnp.int32)
        slot_rank = route_ranks(flat_routes)
        route_index = jnp.arange(route_count, dtype=jnp.int32)
        slot_table = jnp.zeros((EXPERTS, capacity), jnp.int32).at[flat_routes, slot_rank].set(route_index)

        def one_expert(expert_pair):
            slot_routes, weight_mat = expert_pair
            token_index = (slot_routes // TOPK).astype(jnp.int32)
            slot_rows = jnp.take(token_grads, token_index, axis=0).astype(jnp.float32)
            return jnp.dot(slot_rows, weight_mat.astype(jnp.float32).T, precision=lax.Precision.HIGHEST)

        products = lax.map(one_expert, (slot_table, section_weights))
        route_prod = products[flat_routes, slot_rank]
        scaled = section_gates.reshape(route_count, 1).astype(jnp.float32) * route_prod
        return scaled.astype(jnp.bfloat16).reshape(TOKENS, TOPK, HID)

    return lax.map(one_section, (section_grads, expert_ids, gate_weights, expert_weight))
```

```python
import jax
import jax.numpy as jnp
from jax import lax
from jax.sharding import PartitionSpec as P


def shifted(block, axis, distance):
    devices = range(lax.axis_size(axis))
    route = [((i - distance) % len(devices), i) for i in devices]
    return lax.ppermute(block, axis, route)


def per_device(upstream, expert_ids, gate_weights, expert_weight):
    section_grad = shifted(upstream, "pipe", -1)[0]
    route_ids = expert_ids[0]
    route_gates = gate_weights[0]
    weight_mat = expert_weight[0, 0]
    tokens, top = route_ids.shape
    owners = lax.axis_size("expert")
    hidden = weight_mat.shape[0]

    matched = route_ids[:, :, None] == jnp.arange(owners, dtype=jnp.int32)
    dense_gates = jnp.sum(
        jnp.where(matched, route_gates[:, :, None].astype(jnp.float32), 0.0), axis=1
    ).T.astype(jnp.bfloat16)
    got_gates = lax.all_to_all(dense_gates, "expert", split_axis=0, concat_axis=0, tiled=True)

    got_rows = lax.all_gather(section_grad, "expert", axis=0, tiled=True)
    product = lax.dot_general(
        got_rows, weight_mat, (((1,), (1,)), ((), ())), preferred_element_type=jnp.float32
    )
    scaled = product.reshape(owners, tokens, hidden) * got_gates.astype(jnp.float32)[:, :, None]
    returned = lax.all_to_all(
        scaled.astype(jnp.bfloat16), "expert", split_axis=0, concat_axis=0, tiled=True
    )
    same = jnp.arange(tokens)[:, None] == jnp.arange(tokens)[None, :]
    pick = (matched[:, :, :, None] & same[:, None, None, :]).astype(jnp.bfloat16)
    out = lax.dot_general(
        pick.reshape(tokens * top, owners * tokens),
        returned.reshape(owners * tokens, hidden),
        (((1,), (0,)), ((), ())),
        preferred_element_type=jnp.float32,
    )
    return out.astype(jnp.bfloat16).reshape(1, tokens, top, hidden)


def solution(mesh):
    in_specs = (
        P("pipe", "expert", None),
        P("pipe", "expert", None),
        P("pipe", "expert", None),
        P("pipe", "expert", None, None),
    )
    out_specs = P("pipe", "expert", None, None)
    return jax.shard_map(
        per_device, mesh=mesh, in_specs=in_specs, out_specs=out_specs, check_vma=False
    )
```

```python
import functools

import jax
import jax.numpy as jnp
from jax import lax
from jax.experimental import pallas as pl
from jax.experimental.pallas import tpu as pltpu
from jax.sharding import PartitionSpec as P

COLUMNS = 2
CORES = 2


def shifted(block, axis, distance):
    devices = range(lax.axis_size(axis))
    route = [((i - distance) % len(devices), i) for i in devices]
    return lax.ppermute(block, axis, route)


def ring_order(owners):
    height = owners // (COLUMNS * CORES)
    up = [z * COLUMNS for z in range(height)]
    down = [z * COLUMNS + 1 for z in reversed(range(height))]
    return up + down


def ring_route(owners, distance, flip):
    order = ring_order(owners)
    route = []
    for place, chip in enumerate(order):
        target = order[(place + distance) % len(order)]
        for core in range(CORES):
            route.append((chip * CORES + core, target * CORES + (core ^ flip)))
    return route


def send(block, owners, distance, flip):
    return lax.ppermute(block, "expert", ring_route(owners, distance, flip))


def expert_kernel(count, *refs):
    rows, (weight, gates), outs = refs[:count], refs[count : count + 2], refs[count + 2 :]
    stacked = jnp.concatenate([r[...] for r in rows], axis=0)
    scale = jnp.concatenate([gates[:, j : j + 1] for j in range(gates.shape[1])], axis=0)
    product = lax.dot_general(
        stacked, weight[...], (((1,), (1,)), ((), ())), preferred_element_type=jnp.float32
    )
    scaled = (product * scale).astype(jnp.bfloat16)
    tokens = gates.shape[0]
    for j, out in enumerate(outs):
        out[...] = scaled[j * tokens : (j + 1) * tokens]


def expert_rows(rows, weight, gates):
    tokens, blocks = gates.shape
    hidden, depth = weight.shape
    return pl.pallas_call(
        functools.partial(expert_kernel, len(rows)),
        out_shape=[jax.ShapeDtypeStruct((tokens, hidden), jnp.bfloat16)] * blocks,
        compiler_params=pltpu.CompilerParams(vmem_limit_bytes=40 << 20),
        cost_estimate=pl.CostEstimate(
            flops=2 * blocks * tokens * hidden * depth,
            bytes_accessed=2 * (blocks * tokens * (hidden + depth) + hidden * depth),
            transcendentals=0,
        ),
    )(*rows, weight, gates)


def pick_kernel(labels_ref, *refs):
    blocks, out = refs[:-1], refs[-1]
    tokens, hidden = blocks[0].shape
    top = out.shape[0] // tokens
    span = 16
    routes = span * top
    column = lax.broadcasted_iota(jnp.int32, (routes, len(blocks) * span), 1)
    token = lax.broadcasted_iota(jnp.int32, (routes, len(blocks) * span), 0) // top
    for g in range(tokens // span):
        stacked = jnp.concatenate([b[g * span : (g + 1) * span, :] for b in blocks], axis=0)
        wanted = labels_ref[g * routes : (g + 1) * routes, :] * span + token
        pick = jnp.where(column == wanted, 1.0, 0.0).astype(jnp.bfloat16)
        rows = jnp.dot(pick, stacked, preferred_element_type=jnp.float32)
        out[g * routes : (g + 1) * routes, :] = rows.astype(jnp.bfloat16)


def pick_routes(labels, blocks):
    tokens, hidden = blocks[0].shape
    return pl.pallas_call(
        pick_kernel,
        out_shape=jax.ShapeDtypeStruct((labels.shape[0], hidden), jnp.bfloat16),
        compiler_params=pltpu.CompilerParams(vmem_limit_bytes=40 << 20),
    )(labels, *blocks)


def dense_device(section_grad, route_ids, route_gates, weight_mat):
    tokens, top = route_ids.shape
    owners = lax.axis_size("expert")
    hidden = weight_mat.shape[0]
    order = ring_order(owners)
    size = len(order)
    place_of_chip = jnp.array([order.index(c) for c in range(size)], jnp.int32)
    chip_of_place = jnp.array(order, jnp.int32)
    me = lax.axis_index("expert")
    my_place, my_core = place_of_chip[me // CORES], me % CORES

    matched = route_ids[:, :, None] == jnp.arange(owners, dtype=jnp.int32)
    dense_gates = jnp.sum(
        jnp.where(matched, route_gates[:, :, None].astype(jnp.float32), 0.0), axis=1
    ).T.astype(jnp.bfloat16)
    got_gates = lax.all_to_all(dense_gates, "expert", split_axis=0, concat_axis=0, tiled=True)
    labels = jnp.arange(owners, dtype=jnp.int32)
    label_owner = (
        chip_of_place[(my_place + labels // CORES) % size] * CORES + (my_core ^ (labels % CORES))
    )
    gates = jnp.take(got_gates, label_owner, axis=0).T.astype(jnp.float32)
    route_labels = (place_of_chip[route_ids // CORES] - my_place) % size * CORES + (
        (route_ids % CORES) ^ my_core
    )

    half = tokens // 2
    own = {0: section_grad}
    back = ahead = section_grad
    for step in range(1, size // 2):
        back, ahead = send(back, owners, 1, 0), send(ahead, owners, -1, 0)
        own[size - step], own[step] = back, ahead
    top_half = send(back[:half], owners, 1, 0)
    low_half = send(ahead[half:], owners, -1, 0)

    results = {}

    def products(distances, pieces):
        names = [d * CORES + c for d in distances for c in range(CORES)]
        picked = jnp.concatenate([gates[:, n : n + 1] for n in names], axis=1)
        results.update(zip(names, expert_rows(pieces, weight_mat, picked)))

    for step in range(size // 2):
        distances = [0] if step == 0 else [size - step, step]
        pieces = []
        for d in distances:
            pieces += [own[d], send(own[d], owners, 0, 1)]
        products(distances, pieces)
    products(
        [size // 2], [top_half, low_half, send(top_half, owners, 0, 1), send(low_half, owners, 0, 1)]
    )

    received = [None] * owners
    for d in range(size):
        for c in range(CORES):
            block = results[d * CORES + c]
            if d or c:
                block = send(block, owners, d, c)
            received[(-d) % size * CORES + c] = block
    out = pick_routes(route_labels.reshape(tokens * top, 1), received)
    return out.reshape(1, tokens, top, hidden)


def slotted_device(section_grad, route_ids, route_gates, weight_mat, capacity):
    tokens, top = route_ids.shape
    owners = lax.axis_size("expert")
    ids = jnp.arange(owners, dtype=jnp.int32)
    slots = jnp.arange(capacity, dtype=jnp.int32)
    matched = (route_ids[:, :, None] == ids[None, None, :]).astype(jnp.int32)
    hits = jnp.sum(matched, axis=1)
    rank = jnp.cumsum(hits, axis=0) - hits
    position = route_ids * capacity + jnp.sum(matched * rank[:, None, :], axis=2)
    gate_owner = jnp.einsum(
        "tk,tke->te", route_gates.astype(jnp.float32), matched.astype(jnp.float32)
    )
    slot_pick = (hits[:, :, None] == 1) & (rank[:, :, None] == slots[None, None, :])
    send_rows = jnp.einsum(
        "tem,td->emd",
        slot_pick.astype(jnp.bfloat16),
        section_grad,
        preferred_element_type=jnp.float32,
    ).astype(jnp.bfloat16)
    send_gates = jnp.einsum("tem,te->em", slot_pick.astype(jnp.float32), gate_owner).astype(
        jnp.bfloat16
    )
    got_rows = lax.all_to_all(send_rows, "expert", split_axis=0, concat_axis=0, tiled=True)
    got_gates = lax.all_to_all(send_gates, "expert", split_axis=0, concat_axis=0, tiled=True)
    product = lax.dot_general(
        got_rows.reshape(owners * capacity, got_rows.shape[2]),
        weight_mat,
        (((1,), (1,)), ((), ())),
        preferred_element_type=jnp.float32,
    ).reshape(owners, capacity, weight_mat.shape[0])
    returned = lax.all_to_all(
        (product * got_gates.astype(jnp.float32)[:, :, None]).astype(jnp.bfloat16),
        "expert",
        split_axis=0,
        concat_axis=0,
        tiled=True,
    )
    flat = returned.reshape(owners * capacity, returned.shape[2])
    out = jnp.take(flat, position.reshape(tokens * top), axis=0)
    return out.reshape(1, tokens, top, returned.shape[2])


def per_device(upstream, expert_ids, gate_weights, expert_weight):
    section_grad = shifted(upstream, "pipe", -1)[0]
    route_ids = expert_ids[0]
    route_gates = gate_weights[0]
    weight_mat = expert_weight[0, 0]
    tokens, top = route_ids.shape
    owners = lax.axis_size("expert")
    capacity = 2 * tokens * top // owners
    if capacity >= tokens:
        return dense_device(section_grad, route_ids, route_gates, weight_mat)
    return slotted_device(section_grad, route_ids, route_gates, weight_mat, capacity)


def solution(mesh):
    in_specs = (
        P("pipe", "expert", None),
        P("pipe", "expert", None),
        P("pipe", "expert", None),
        P("pipe", "expert", None, None),
    )
    out_specs = P("pipe", "expert", None, None)
    return jax.shard_map(
        per_device, mesh=mesh, in_specs=in_specs, out_specs=out_specs, check_vma=False
    )
```

```python
import functools

import jax
import jax.numpy as jnp
from jax import lax
from jax.experimental import pallas as pl
from jax.experimental.pallas import tpu as pltpu
from jax.sharding import PartitionSpec as P

COLUMNS = 2
CORES = 2


def shifted(block, axis, distance):
    devices = range(lax.axis_size(axis))
    route = [((i - distance) % len(devices), i) for i in devices]
    return lax.ppermute(block, axis, route)


def ring_chip(place, size):
    height = size // COLUMNS
    return jnp.where(place < height, place * COLUMNS, (size - 1 - place) * COLUMNS + 1)


def ring_place(chip, size):
    z, x = chip // COLUMNS, lax.rem(chip, COLUMNS)
    return jnp.where(x == 0, z, size - 1 - z)


def ring_order(owners):
    height = owners // (COLUMNS * CORES)
    up = [z * COLUMNS for z in range(height)]
    down = [z * COLUMNS + 1 for z in reversed(range(height))]
    return up + down


def ring_route(owners, distance, flip):
    order = ring_order(owners)
    route = []
    for place, chip in enumerate(order):
        target = order[(place + distance) % len(order)]
        for core in range(CORES):
            route.append((chip * CORES + core, target * CORES + (core ^ flip)))
    return route


def send(block, owners, distance, flip):
    return lax.ppermute(block, "expert", ring_route(owners, distance, flip))


def products_kernel(count, places, weight, other, gates, *refs):
    rows, (out, stage, sem) = refs[:count], refs[-3:]
    size = out.shape[0]
    tokens = gates.shape[2]
    me = lax.axis_index("expert")
    place, core = ring_place(me // CORES, size), lax.rem(me, CORES)
    stacked = jnp.concatenate([r[...] for r in rows], axis=0)
    copies = []
    for c, mat in enumerate((weight, other)):
        product = lax.dot_general(
            stacked, mat[...], (((1,), (1,)), ((), ())), preferred_element_type=jnp.float32
        )
        expert = core if c == 0 else 1 - core
        for j, distance in enumerate(places):
            chip = ring_chip(lax.rem(place + distance, size), size)
            scale = gates[chip, expert]
            stage[c, j] = (product[j * tokens : (j + 1) * tokens] * scale).astype(jnp.bfloat16)
            copies.append(
                pltpu.make_async_copy(stage.at[c, j], out.at[chip, expert], sem.at[c, j])
            )
            copies[-1].start()
    for copy in copies:
        copy.wait()


def add_products(buffer, places, pieces, weight, other, gates):
    size, experts, tokens, _ = gates.shape
    hidden, depth = weight.shape
    n = len(places)
    kept = [] if buffer is None else [buffer]
    whole = pl.BlockSpec(memory_space=pltpu.VMEM)
    return pl.pallas_call(
        functools.partial(products_kernel, len(pieces), places),
        in_specs=[whole] * (3 + len(pieces)) + [pl.BlockSpec(memory_space=pl.ANY)] * len(kept),
        out_specs=pl.BlockSpec(memory_space=pl.ANY),
        out_shape=jax.ShapeDtypeStruct((size, experts, tokens, hidden), jnp.bfloat16),
        input_output_aliases={3 + len(pieces): 0} if kept else {},
        scratch_shapes=[
            pltpu.VMEM((experts, n, tokens, hidden), jnp.bfloat16),
            pltpu.SemaphoreType.DMA((experts, n)),
        ],
        compiler_params=pltpu.CompilerParams(vmem_limit_bytes=40 << 20),
        cost_estimate=pl.CostEstimate(
            flops=2 * experts * n * tokens * hidden * depth,
            bytes_accessed=2 * (n * tokens * (2 * hidden + depth) + 2 * hidden * depth),
            transcendentals=0,
        ),
    )(weight, other, gates, *pieces, *kept)


def pick_kernel(ids, blocks, out):
    owners, tokens, hidden = blocks.shape
    top = out.shape[0] // tokens
    span = 16
    routes = span * top
    column = lax.broadcasted_iota(jnp.int32, (routes, owners * span), 1)
    token = lax.broadcasted_iota(jnp.int32, (routes, owners * span), 0) // top
    for g in range(tokens // span):
        stacked = jnp.concatenate([blocks[e, g * span : (g + 1) * span, :] for e in range(owners)], axis=0)
        wanted = ids[g * routes : (g + 1) * routes, :] * span + token
        pick = jnp.where(column == wanted, 1.0, 0.0).astype(jnp.bfloat16)
        rows = jnp.dot(pick, stacked, preferred_element_type=jnp.float32)
        out[g * routes : (g + 1) * routes, :] = rows.astype(jnp.bfloat16)


def pick_routes(ids, blocks):
    return pl.pallas_call(
        pick_kernel,
        out_shape=jax.ShapeDtypeStruct((ids.shape[0], blocks.shape[2]), jnp.bfloat16),
        compiler_params=pltpu.CompilerParams(vmem_limit_bytes=40 << 20),
    )(ids, blocks)


def dense_device(section_grad, route_ids, route_gates, weight_mat):
    tokens, top = route_ids.shape
    owners = lax.axis_size("expert")
    hidden = weight_mat.shape[0]
    size = owners // CORES
    same_core = [list(range(core, owners, CORES)) for core in range(CORES)]

    other_mat = send(weight_mat, owners, 0, 1)
    matched = route_ids[:, :, None] == jnp.arange(owners, dtype=jnp.int32)
    dense_gates = jnp.sum(
        jnp.where(matched, route_gates[:, :, None].astype(jnp.float32), 0.0), axis=1
    ).T.astype(jnp.bfloat16)
    dense_gates, section_grad = lax.optimization_barrier((dense_gates, section_grad))
    got_gates = lax.all_to_all(
        dense_gates.reshape(size, CORES * tokens),
        "expert",
        split_axis=0,
        concat_axis=0,
        tiled=True,
        axis_index_groups=same_core,
    )
    gates = got_gates.astype(jnp.float32).reshape(size, CORES, tokens, 1)

    half = tokens // 2
    own = {0: section_grad}
    back = ahead = section_grad
    for step in range(1, size // 2):
        back, ahead = send(back, owners, 1, 0), send(ahead, owners, -1, 0)
        own[size - step], own[step] = back, ahead
    top_half = send(back[:half], owners, 1, 0)
    low_half = send(ahead[half:], owners, -1, 0)

    buffer = None
    early = [0] + [d for s in range(1, size // 2 - 1) for d in (size - s, s)]
    late = [size // 2 + 1, size // 2 - 1]
    for places in (early, late):
        pieces = [own[d] for d in places]
        buffer = add_products(buffer, places, pieces, weight_mat, other_mat, gates)
    buffer = add_products(buffer, [size // 2], [top_half, low_half], weight_mat, other_mat, gates)

    returned = lax.all_to_all(
        buffer.reshape(size, CORES * tokens, hidden),
        "expert",
        split_axis=0,
        concat_axis=0,
        tiled=True,
        axis_index_groups=same_core,
    )
    out = pick_routes(
        route_ids.reshape(tokens * top, 1), returned.reshape(owners, tokens, hidden)
    )
    return out.reshape(1, tokens, top, hidden)


def slotted_device(section_grad, route_ids, route_gates, weight_mat, capacity):
    tokens, top = route_ids.shape
    owners = lax.axis_size("expert")
    ids = jnp.arange(owners, dtype=jnp.int32)
    slots = jnp.arange(capacity, dtype=jnp.int32)
    matched = (route_ids[:, :, None] == ids[None, None, :]).astype(jnp.int32)
    hits = jnp.sum(matched, axis=1)
    rank = jnp.cumsum(hits, axis=0) - hits
    position = route_ids * capacity + jnp.sum(matched * rank[:, None, :], axis=2)
    gate_owner = jnp.einsum(
        "tk,tke->te", route_gates.astype(jnp.float32), matched.astype(jnp.float32)
    )
    slot_pick = (hits[:, :, None] == 1) & (rank[:, :, None] == slots[None, None, :])
    send_rows = jnp.einsum(
        "tem,td->emd",
        slot_pick.astype(jnp.bfloat16),
        section_grad,
        preferred_element_type=jnp.float32,
    ).astype(jnp.bfloat16)
    send_gates = jnp.einsum("tem,te->em", slot_pick.astype(jnp.float32), gate_owner).astype(
        jnp.bfloat16
    )
    got_rows = lax.all_to_all(send_rows, "expert", split_axis=0, concat_axis=0, tiled=True)
    got_gates = lax.all_to_all(send_gates, "expert", split_axis=0, concat_axis=0, tiled=True)
    product = lax.dot_general(
        got_rows.reshape(owners * capacity, got_rows.shape[2]),
        weight_mat,
        (((1,), (1,)), ((), ())),
        preferred_element_type=jnp.float32,
    ).reshape(owners, capacity, weight_mat.shape[0])
    returned = lax.all_to_all(
        (product * got_gates.astype(jnp.float32)[:, :, None]).astype(jnp.bfloat16),
        "expert",
        split_axis=0,
        concat_axis=0,
        tiled=True,
    )
    flat = returned.reshape(owners * capacity, returned.shape[2])
    out = jnp.take(flat, position.reshape(tokens * top), axis=0)
    return out.reshape(1, tokens, top, returned.shape[2])


def per_device(upstream, expert_ids, gate_weights, expert_weight):
    section_grad = shifted(upstream, "pipe", -1)[0]
    route_ids = expert_ids[0]
    route_gates = gate_weights[0]
    weight_mat = expert_weight[0, 0]
    tokens, top = route_ids.shape
    owners = lax.axis_size("expert")
    capacity = 2 * tokens * top // owners
    if capacity >= tokens:
        return dense_device(section_grad, route_ids, route_gates, weight_mat)
    return slotted_device(section_grad, route_ids, route_gates, weight_mat, capacity)


def solution(mesh):
    in_specs = (
        P("pipe", "expert", None),
        P("pipe", "expert", None),
        P("pipe", "expert", None),
        P("pipe", "expert", None, None),
    )
    out_specs = P("pipe", "expert", None, None)
    return jax.shard_map(
        per_device, mesh=mesh, in_specs=in_specs, out_specs=out_specs, check_vma=False
    )
```

```python
import functools

import jax
import jax.numpy as jnp
from jax import lax
from jax.experimental import pallas as pl
from jax.experimental.pallas import tpu as pltpu
from jax.sharding import PartitionSpec as P

COLUMNS = 2
CORES = 2


def shifted(block, axis, distance):
    devices = range(lax.axis_size(axis))
    route = [((i - distance) % len(devices), i) for i in devices]
    return lax.ppermute(block, axis, route)


def ring_chip(place, size):
    height = size // COLUMNS
    return jnp.where(place < height, place * COLUMNS, (size - 1 - place) * COLUMNS + 1)


def ring_place(chip, size):
    z, x = chip // COLUMNS, lax.rem(chip, COLUMNS)
    return jnp.where(x == 0, z, size - 1 - z)


def ring_order(owners):
    height = owners // (COLUMNS * CORES)
    up = [z * COLUMNS for z in range(height)]
    down = [z * COLUMNS + 1 for z in reversed(range(height))]
    return up + down


def ring_route(owners, distance, flip):
    order = ring_order(owners)
    route = []
    for place, chip in enumerate(order):
        target = order[(place + distance) % len(order)]
        for core in range(CORES):
            route.append((chip * CORES + core, target * CORES + (core ^ flip)))
    return route


def send(block, owners, distance, flip):
    return lax.ppermute(block, "expert", ring_route(owners, distance, flip))


def products_kernel(count, places, weight, other, gates, *refs):
    rows, (out, stage, sem) = refs[:count], refs[-3:]
    size = out.shape[0]
    tokens = gates.shape[2]
    me = lax.axis_index("expert")
    place, core = ring_place(me // CORES, size), lax.rem(me, CORES)
    stacked = jnp.concatenate([r[...] for r in rows], axis=0)
    copies = []
    for c, mat in enumerate((weight, other)):
        product = lax.dot_general(
            stacked, mat[...], (((1,), (1,)), ((), ())), preferred_element_type=jnp.float32
        )
        expert = core if c == 0 else 1 - core
        for j, distance in enumerate(places):
            chip = ring_chip(lax.rem(place + distance, size), size)
            scale = gates[chip, expert]
            stage[c, j] = (product[j * tokens : (j + 1) * tokens] * scale).astype(jnp.bfloat16)
            copies.append(
                pltpu.make_async_copy(stage.at[c, j], out.at[chip, expert], sem.at[c, j])
            )
            copies[-1].start()
    for copy in copies:
        copy.wait()


def add_products(buffer, places, pieces, weight, other, gates):
    size, experts, tokens, _ = gates.shape
    hidden, depth = weight.shape
    n = len(places)
    kept = [] if buffer is None else [buffer]
    whole = pl.BlockSpec(memory_space=pltpu.VMEM)
    return pl.pallas_call(
        functools.partial(products_kernel, len(pieces), places),
        in_specs=[whole] * (3 + len(pieces)) + [pl.BlockSpec(memory_space=pltpu.HBM)] * len(kept),
        out_specs=pl.BlockSpec(memory_space=pltpu.HBM),
        out_shape=jax.ShapeDtypeStruct((size, experts, tokens, hidden), jnp.bfloat16),
        input_output_aliases={3 + len(pieces): 0} if kept else {},
        scratch_shapes=[
            pltpu.VMEM((experts, n, tokens, hidden), jnp.bfloat16),
            pltpu.SemaphoreType.DMA((experts, n)),
        ],
        compiler_params=pltpu.CompilerParams(vmem_limit_bytes=16 << 20),
        cost_estimate=pl.CostEstimate(
            flops=2 * experts * n * tokens * hidden * depth,
            bytes_accessed=2 * (n * tokens * (2 * hidden + depth) + 2 * hidden * depth),
            transcendentals=0,
        ),
    )(weight, other, gates, *pieces, *kept)


def pick_kernel(ids, blocks, out):
    owners, tokens, hidden = blocks.shape
    top = out.shape[0] // tokens
    span = 16
    routes = span * top
    column = lax.broadcasted_iota(jnp.int32, (routes, owners * span), 1)
    token = lax.broadcasted_iota(jnp.int32, (routes, owners * span), 0) // top
    for g in range(tokens // span):
        stacked = jnp.concatenate([blocks[e, g * span : (g + 1) * span, :] for e in range(owners)], axis=0)
        wanted = ids[g * routes : (g + 1) * routes, :] * span + token
        pick = jnp.where(column == wanted, 1.0, 0.0).astype(jnp.bfloat16)
        rows = jnp.dot(pick, stacked, preferred_element_type=jnp.float32)
        out[g * routes : (g + 1) * routes, :] = rows.astype(jnp.bfloat16)


def pick_routes(ids, blocks):
    return pl.pallas_call(
        pick_kernel,
        out_shape=jax.ShapeDtypeStruct((ids.shape[0], blocks.shape[2]), jnp.bfloat16),
        compiler_params=pltpu.CompilerParams(vmem_limit_bytes=16 << 20),
    )(ids, blocks)


def dense_device(section_grad, route_ids, route_gates, weight_mat):
    tokens, top = route_ids.shape
    owners = lax.axis_size("expert")
    hidden = weight_mat.shape[0]
    size = owners // CORES
    same_core = [list(range(core, owners, CORES)) for core in range(CORES)]

    other_mat = send(weight_mat, owners, 0, 1)
    matched = route_ids[:, :, None] == jnp.arange(owners, dtype=jnp.int32)
    dense_gates = jnp.sum(
        jnp.where(matched, route_gates[:, :, None].astype(jnp.float32), 0.0), axis=1
    ).T.astype(jnp.bfloat16)
    got_gates = lax.all_to_all(
        dense_gates.reshape(size, CORES * tokens),
        "expert",
        split_axis=0,
        concat_axis=0,
        tiled=True,
        axis_index_groups=same_core,
    )
    section_grad, got_gates = lax.optimization_barrier((section_grad, got_gates))
    gates = got_gates.astype(jnp.float32).reshape(size, CORES, tokens, 1)

    half = tokens // 2
    buffer = None
    back = ahead = section_grad
    waiting = {0: section_grad}
    for step in range(1, size // 2):
        next_back, next_ahead = send(back, owners, 1, 0), send(ahead, owners, -1, 0)
        if step > 1:
            buffer = add_products(
                buffer, list(waiting), list(waiting.values()), weight_mat, other_mat, gates
            )
            waiting = {}
            next_back, next_ahead, buffer = lax.optimization_barrier(
                (next_back, next_ahead, buffer)
            )
        back, ahead = next_back, next_ahead
        waiting.update({size - step: back, step: ahead})
    top_half = send(back[:half], owners, 1, 0)
    low_half = send(ahead[half:], owners, -1, 0)
    buffer = add_products(
        buffer, list(waiting), list(waiting.values()), weight_mat, other_mat, gates
    )
    buffer = add_products(buffer, [size // 2], [top_half, low_half], weight_mat, other_mat, gates)

    returned = lax.all_to_all(
        buffer.reshape(size, CORES * tokens, hidden),
        "expert",
        split_axis=0,
        concat_axis=0,
        tiled=True,
        axis_index_groups=same_core,
    )
    out = pick_routes(
        route_ids.reshape(tokens * top, 1), returned.reshape(owners, tokens, hidden)
    )
    return out.reshape(1, tokens, top, hidden)


def slotted_device(section_grad, route_ids, route_gates, weight_mat, capacity):
    tokens, top = route_ids.shape
    owners = lax.axis_size("expert")
    ids = jnp.arange(owners, dtype=jnp.int32)
    slots = jnp.arange(capacity, dtype=jnp.int32)
    matched = (route_ids[:, :, None] == ids[None, None, :]).astype(jnp.int32)
    hits = jnp.sum(matched, axis=1)
    rank = jnp.cumsum(hits, axis=0) - hits
    position = route_ids * capacity + jnp.sum(matched * rank[:, None, :], axis=2)
    gate_owner = jnp.einsum(
        "tk,tke->te", route_gates.astype(jnp.float32), matched.astype(jnp.float32)
    )
    slot_pick = (hits[:, :, None] == 1) & (rank[:, :, None] == slots[None, None, :])
    send_rows = jnp.einsum(
        "tem,td->emd",
        slot_pick.astype(jnp.bfloat16),
        section_grad,
        preferred_element_type=jnp.float32,
    ).astype(jnp.bfloat16)
    send_gates = jnp.einsum("tem,te->em", slot_pick.astype(jnp.float32), gate_owner).astype(
        jnp.bfloat16
    )
    got_rows = lax.all_to_all(send_rows, "expert", split_axis=0, concat_axis=0, tiled=True)
    got_gates = lax.all_to_all(send_gates, "expert", split_axis=0, concat_axis=0, tiled=True)
    product = lax.dot_general(
        got_rows.reshape(owners * capacity, got_rows.shape[2]),
        weight_mat,
        (((1,), (1,)), ((), ())),
        preferred_element_type=jnp.float32,
    ).reshape(owners, capacity, weight_mat.shape[0])
    returned = lax.all_to_all(
        (product * got_gates.astype(jnp.float32)[:, :, None]).astype(jnp.bfloat16),
        "expert",
        split_axis=0,
        concat_axis=0,
        tiled=True,
    )
    flat = returned.reshape(owners * capacity, returned.shape[2])
    out = jnp.take(flat, position.reshape(tokens * top), axis=0)
    return out.reshape(1, tokens, top, returned.shape[2])


def per_device(upstream, expert_ids, gate_weights, expert_weight):
    section_grad = shifted(upstream, "pipe", -1)[0]
    route_ids = expert_ids[0]
    route_gates = gate_weights[0]
    weight_mat = expert_weight[0, 0]
    tokens, top = route_ids.shape
    owners = lax.axis_size("expert")
    capacity = 2 * tokens * top // owners
    if capacity >= tokens:
        return dense_device(section_grad, route_ids, route_gates, weight_mat)
    return slotted_device(section_grad, route_ids, route_gates, weight_mat, capacity)


def solution(mesh):
    in_specs = (
        P("pipe", "expert", None),
        P("pipe", "expert", None),
        P("pipe", "expert", None),
        P("pipe", "expert", None, None),
    )
    out_specs = P("pipe", "expert", None, None)
    return jax.shard_map(
        per_device, mesh=mesh, in_specs=in_specs, out_specs=out_specs, check_vma=False
    )
```

```python
import functools

import jax
import jax.numpy as jnp
from jax import lax
from jax.experimental import pallas as pl
from jax.experimental.pallas import tpu as pltpu
from jax.sharding import PartitionSpec as P

COLUMNS = 2
CORES = 2


def shifted(block, axis, distance):
    devices = range(lax.axis_size(axis))
    route = [((i - distance) % len(devices), i) for i in devices]
    return lax.ppermute(block, axis, route)


def ring_chip(place, size):
    height = size // COLUMNS
    return jnp.where(place < height, place * COLUMNS, (size - 1 - place) * COLUMNS + 1)


def ring_place(chip, size):
    z, x = chip // COLUMNS, lax.rem(chip, COLUMNS)
    return jnp.where(x == 0, z, size - 1 - z)


def ring_order(owners):
    height = owners // (COLUMNS * CORES)
    up = [z * COLUMNS for z in range(height)]
    down = [z * COLUMNS + 1 for z in reversed(range(height))]
    return up + down


def ring_route(owners, distance, flip):
    order = ring_order(owners)
    route = []
    for place, chip in enumerate(order):
        target = order[(place + distance) % len(order)]
        for core in range(CORES):
            route.append((chip * CORES + core, target * CORES + (core ^ flip)))
    return route


def send(block, owners, distance, flip):
    return lax.ppermute(block, "expert", ring_route(owners, distance, flip))


def scaled_products(rows, weight, gates, expert, distances, size):
    tokens = rows.shape[0] // len(distances)
    product = lax.dot_general(
        rows, weight[...], (((1,), (1,)), ((), ())), preferred_element_type=jnp.float32
    )
    parts = []
    for j, distance in enumerate(distances):
        start = (-distance) % size * tokens
        block = gates[start : start + tokens, :].astype(jnp.float32)
        column = lax.broadcasted_iota(jnp.int32, block.shape, 1)
        scale = jnp.sum(jnp.where(column == expert, block, 0.0), axis=1, keepdims=True)
        parts.append((product[j * tokens : (j + 1) * tokens] * scale).astype(jnp.bfloat16))
    return parts


def products_kernel(count, size, distances, weight, other, gates, *refs):
    rows, out = refs[:count], refs[count]
    me = lax.axis_index("expert")
    core = lax.rem(me, CORES)
    stacked = jnp.concatenate([r[...] for r in rows], axis=0)
    for mat, to in ((weight, core), (other, 1 - core)):
        expert = me - core + to
        for j, part in enumerate(scaled_products(stacked, mat, gates, expert, distances, size)):
            out[j, to] = part


def products(distances, pieces, size, weight, other, gates):
    hidden, depth = weight.shape
    tokens = pieces[0].shape[0]
    n = len(distances)
    return pl.pallas_call(
        functools.partial(products_kernel, len(pieces), size, distances),
        out_shape=jax.ShapeDtypeStruct((n, CORES, tokens, hidden), jnp.bfloat16),
        compiler_params=pltpu.CompilerParams(vmem_limit_bytes=16 << 20),
        cost_estimate=pl.CostEstimate(
            flops=2 * CORES * n * tokens * hidden * depth,
            bytes_accessed=2 * (n * tokens * (2 * hidden + depth) + 2 * hidden * depth),
            transcendentals=0,
        ),
    )(weight, other, gates, *pieces)


def layout_kernel(groups, far, weight, other, gates, top, low, *refs):
    blocks, (out, stage, sem, far_sem) = refs[: len(groups)], refs[len(groups) :]
    size = out.shape[0]
    me = lax.axis_index("expert")
    core = lax.rem(me, CORES)
    place = ring_place(me // CORES, size)

    def slot(distance):
        return out.at[ring_chip(lax.rem(place + distance, size), size)]

    copies = []
    for block, distances in zip(blocks, groups):
        for j, distance in enumerate(distances):
            copies.append(pltpu.make_async_copy(block.at[j], slot(distance), sem.at[len(copies)]))
            copies[-1].start()
    stacked = jnp.concatenate([top[...], low[...]], axis=0)
    for mat, to in ((weight, core), (other, 1 - core)):
        expert = me - core + to
        stage[to] = scaled_products(stacked, mat, gates, expert, [far], size)[0]
    copies.append(pltpu.make_async_copy(stage, slot(far), far_sem))
    copies[-1].start()
    for copy in copies:
        copy.wait()


def laid_out(groups, blocks, far, top, low, size, weight, other, gates):
    hidden, depth = weight.shape
    tokens = blocks[0].shape[2]
    whole = pl.BlockSpec(memory_space=pltpu.VMEM)
    return pl.pallas_call(
        functools.partial(layout_kernel, groups, far),
        in_specs=[whole] * (5 + len(blocks)),
        out_specs=pl.BlockSpec(memory_space=pltpu.HBM),
        out_shape=pltpu.HBM((size, CORES, tokens, hidden), jnp.bfloat16),
        scratch_shapes=[
            pltpu.VMEM((CORES, tokens, hidden), jnp.bfloat16),
            pltpu.SemaphoreType.DMA((size - 1,)),
            pltpu.SemaphoreType.DMA,
        ],
        compiler_params=pltpu.CompilerParams(vmem_limit_bytes=16 << 20),
        cost_estimate=pl.CostEstimate(
            flops=2 * CORES * tokens * hidden * depth,
            bytes_accessed=2 * (size * tokens * 4 * hidden + 2 * hidden * depth),
            transcendentals=0,
        ),
    )(weight, other, gates, top, low, *blocks)


def pick_kernel(ids, blocks, out):
    owners, tokens, hidden = blocks.shape
    top = out.shape[0] // tokens
    span = 16
    routes = span * top
    column = lax.broadcasted_iota(jnp.int32, (routes, owners * span), 1)
    token = lax.broadcasted_iota(jnp.int32, (routes, owners * span), 0) // top
    for g in range(tokens // span):
        stacked = jnp.concatenate([blocks[e, g * span : (g + 1) * span, :] for e in range(owners)], axis=0)
        wanted = ids[g * routes : (g + 1) * routes, :] * span + token
        pick = jnp.where(column == wanted, 1.0, 0.0).astype(jnp.bfloat16)
        rows = jnp.dot(pick, stacked, preferred_element_type=jnp.float32)
        out[g * routes : (g + 1) * routes, :] = rows.astype(jnp.bfloat16)


def pick_routes(ids, blocks):
    return pl.pallas_call(
        pick_kernel,
        out_shape=jax.ShapeDtypeStruct((ids.shape[0], blocks.shape[2]), jnp.bfloat16),
        compiler_params=pltpu.CompilerParams(vmem_limit_bytes=16 << 20),
    )(ids, blocks)


def dense_device(section_grad, route_ids, route_gates, weight_mat):
    tokens, top = route_ids.shape
    owners = lax.axis_size("expert")
    hidden = weight_mat.shape[0]
    size = owners // CORES
    same_core = [list(range(core, owners, CORES)) for core in range(CORES)]

    other_mat = send(weight_mat, owners, 0, 1)
    matched = route_ids[:, :, None] == jnp.arange(owners, dtype=jnp.int32)
    gates = jnp.sum(
        jnp.where(matched, route_gates[:, :, None].astype(jnp.float32), 0.0), axis=1
    ).astype(jnp.bfloat16)
    own_gates, reach = gates, 1
    while reach < size:
        gates = jnp.concatenate([gates, send(gates, owners, reach, 0)], axis=0)
        reach *= 2

    half = tokens // 2
    back = ahead = section_grad
    waiting = {0: section_grad}
    groups, blocks = [], []
    for step in range(1, size // 2):
        next_back, next_ahead = send(back, owners, 1, 0), send(ahead, owners, -1, 0)
        groups.append(list(waiting))
        blocks.append(
            products(
                list(waiting),
                list(waiting.values()),
                size,
                weight_mat,
                other_mat,
                own_gates if step == 1 else gates,
            )
        )
        back, ahead, blocks[-1] = lax.optimization_barrier((next_back, next_ahead, blocks[-1]))
        waiting = {size - step: back, step: ahead}
    top_half = send(back[:half], owners, 1, 0)
    low_half = send(ahead[half:], owners, -1, 0)
    groups.append(list(waiting))
    blocks.append(
        products(list(waiting), list(waiting.values()), size, weight_mat, other_mat, gates)
    )
    buffer = laid_out(
        groups, blocks, size // 2, top_half, low_half, size, weight_mat, other_mat, gates
    )

    returned = lax.all_to_all(
        buffer.reshape(size, CORES * tokens, hidden),
        "expert",
        split_axis=0,
        concat_axis=0,
        tiled=True,
        axis_index_groups=same_core,
    )
    out = pick_routes(
        route_ids.reshape(tokens * top, 1), returned.reshape(owners, tokens, hidden)
    )
    return out.reshape(1, tokens, top, hidden)


def slotted_device(section_grad, route_ids, route_gates, weight_mat, capacity):
    tokens, top = route_ids.shape
    owners = lax.axis_size("expert")
    ids = jnp.arange(owners, dtype=jnp.int32)
    slots = jnp.arange(capacity, dtype=jnp.int32)
    matched = (route_ids[:, :, None] == ids[None, None, :]).astype(jnp.int32)
    hits = jnp.sum(matched, axis=1)
    rank = jnp.cumsum(hits, axis=0) - hits
    position = route_ids * capacity + jnp.sum(matched * rank[:, None, :], axis=2)
    gate_owner = jnp.einsum(
        "tk,tke->te", route_gates.astype(jnp.float32), matched.astype(jnp.float32)
    )
    slot_pick = (hits[:, :, None] == 1) & (rank[:, :, None] == slots[None, None, :])
    send_rows = jnp.einsum(
        "tem,td->emd",
        slot_pick.astype(jnp.bfloat16),
        section_grad,
        preferred_element_type=jnp.float32,
    ).astype(jnp.bfloat16)
    send_gates = jnp.einsum("tem,te->em", slot_pick.astype(jnp.float32), gate_owner).astype(
        jnp.bfloat16
    )
    got_rows = lax.all_to_all(send_rows, "expert", split_axis=0, concat_axis=0, tiled=True)
    got_gates = lax.all_to_all(send_gates, "expert", split_axis=0, concat_axis=0, tiled=True)
    product = lax.dot_general(
        got_rows.reshape(owners * capacity, got_rows.shape[2]),
        weight_mat,
        (((1,), (1,)), ((), ())),
        preferred_element_type=jnp.float32,
    ).reshape(owners, capacity, weight_mat.shape[0])
    returned = lax.all_to_all(
        (product * got_gates.astype(jnp.float32)[:, :, None]).astype(jnp.bfloat16),
        "expert",
        split_axis=0,
        concat_axis=0,
        tiled=True,
    )
    flat = returned.reshape(owners * capacity, returned.shape[2])
    out = jnp.take(flat, position.reshape(tokens * top), axis=0)
    return out.reshape(1, tokens, top, returned.shape[2])


def per_device(upstream, expert_ids, gate_weights, expert_weight):
    section_grad = shifted(upstream, "pipe", -1)[0]
    route_ids = expert_ids[0]
    route_gates = gate_weights[0]
    weight_mat = expert_weight[0, 0]
    tokens, top = route_ids.shape
    owners = lax.axis_size("expert")
    capacity = 2 * tokens * top // owners
    if capacity >= tokens:
        return dense_device(section_grad, route_ids, route_gates, weight_mat)
    return slotted_device(section_grad, route_ids, route_gates, weight_mat, capacity)


def solution(mesh):
    in_specs = (
        P("pipe", "expert", None),
        P("pipe", "expert", None),
        P("pipe", "expert", None),
        P("pipe", "expert", None, None),
    )
    out_specs = P("pipe", "expert", None, None)
    return jax.shard_map(
        per_device, mesh=mesh, in_specs=in_specs, out_specs=out_specs, check_vma=False
    )
```

```python
import functools

import jax
import jax.numpy as jnp
from jax import lax
from jax.experimental import pallas as pl
from jax.experimental.pallas import tpu as pltpu
from jax.sharding import PartitionSpec as P

COLUMNS = 2
CORES = 2
LANES = 128


def shifted(block, axis, distance):
    devices = range(lax.axis_size(axis))
    route = [((i - distance) % len(devices), i) for i in devices]
    return lax.ppermute(block, axis, route)


def ring_place(chip, size):
    z, x = lax.div(chip, COLUMNS), lax.rem(chip, COLUMNS)
    return jnp.where(x == 0, z, size - 1 - z)


def ring_order(owners):
    height = owners // (COLUMNS * CORES)
    up = [z * COLUMNS for z in range(height)]
    down = [z * COLUMNS + 1 for z in reversed(range(height))]
    return up + down


def ring_route(owners, distance, flip):
    order = ring_order(owners)
    route = []
    for place, chip in enumerate(order):
        target = order[(place + distance) % len(order)]
        for core in range(CORES):
            route.append((chip * CORES + core, target * CORES + (core ^ flip)))
    return route


def send(block, owners, distance, flip):
    return lax.ppermute(block, "expert", ring_route(owners, distance, flip))


def widen_kernel(ids, gates, rows, out):
    depth = rows.shape[1]
    out[:, :depth] = rows[...]
    expert = lax.broadcasted_iota(jnp.int32, (rows.shape[0], LANES), 1)
    total = jnp.zeros(expert.shape, jnp.float32)
    for k in range(ids.shape[1]):
        gate = gates[:, k : k + 1].astype(jnp.float32)
        total += jnp.where(expert == ids[:, k : k + 1], gate, 0.0)
    out[:, depth:] = total.astype(jnp.bfloat16)


def widened(ids, gates, rows):
    return pl.pallas_call(
        widen_kernel,
        out_shape=jax.ShapeDtypeStruct((rows.shape[0], rows.shape[1] + LANES), jnp.bfloat16),
        compiler_params=pltpu.CompilerParams(vmem_limit_bytes=16 << 20),
    )(ids, gates, rows)


def products_kernel(count, weight, other, *refs):
    rows, outs = refs[:count], refs[count:]
    hidden, depth = weight.shape
    tokens = outs[0].shape[1]
    me = lax.axis_index("expert")
    core = lax.rem(me, CORES)
    stacked = jnp.concatenate([r[...] for r in rows], axis=0)
    gates = stacked[:, depth:].astype(jnp.float32)
    column = lax.broadcasted_iota(jnp.int32, gates.shape, 1)
    for mat, to in ((weight, core), (other, 1 - core)):
        scale = jnp.sum(jnp.where(column == me - core + to, gates, 0.0), axis=1, keepdims=True)
        product = lax.dot_general(
            stacked[:, :depth],
            mat[...],
            (((1,), (1,)), ((), ())),
            preferred_element_type=jnp.float32,
        )
        scaled = (product * scale).astype(jnp.bfloat16)
        for j, out in enumerate(outs):
            out[to] = scaled[j * tokens : (j + 1) * tokens]


def products(pieces, tokens, weight, other):
    hidden, depth = weight.shape
    total = sum(p.shape[0] for p in pieces)
    return pl.pallas_call(
        functools.partial(products_kernel, len(pieces)),
        out_shape=[jax.ShapeDtypeStruct((CORES, tokens, hidden), jnp.bfloat16)] * (total // tokens),
        compiler_params=pltpu.CompilerParams(vmem_limit_bytes=16 << 20),
        cost_estimate=pl.CostEstimate(
            flops=2 * CORES * total * hidden * depth,
            bytes_accessed=2 * (total * (2 * hidden + depth) + 2 * hidden * depth),
            transcendentals=0,
        ),
    )(weight, other, *pieces)


def pick_kernel(labels, *refs):
    blocks, out = refs[:-1], refs[-1]
    experts, tokens, _ = blocks[0].shape
    top = out.shape[0] // tokens
    span = 16
    routes = span * top
    owners = len(blocks) * experts
    column = lax.broadcasted_iota(jnp.int32, (routes, owners * span), 1)
    token = lax.broadcasted_iota(jnp.int32, (routes, owners * span), 0) // top
    for g in range(tokens // span):
        stacked = jnp.concatenate(
            [b[c, g * span : (g + 1) * span, :] for b in blocks for c in range(experts)], axis=0
        )
        wanted = labels[g * routes : (g + 1) * routes, :] * span + token
        pick = jnp.where(column == wanted, 1.0, 0.0).astype(jnp.bfloat16)
        rows = jnp.dot(pick, stacked, preferred_element_type=jnp.float32)
        out[g * routes : (g + 1) * routes, :] = rows.astype(jnp.bfloat16)


def pick_routes(labels, blocks):
    return pl.pallas_call(
        pick_kernel,
        out_shape=jax.ShapeDtypeStruct((labels.shape[0], blocks[0].shape[2]), jnp.bfloat16),
        compiler_params=pltpu.CompilerParams(vmem_limit_bytes=16 << 20),
    )(labels, *blocks)


def dense_device(section_grad, route_ids, route_gates, weight_mat):
    tokens, top = route_ids.shape
    owners = lax.axis_size("expert")
    hidden = weight_mat.shape[0]
    size = owners // CORES
    place = ring_place(lax.axis_index("expert") // CORES, size)
    labels = lax.rem(ring_place(route_ids // CORES, size) - place + size, size) * CORES + lax.rem(
        route_ids, CORES
    )

    other_mat = send(weight_mat, owners, 0, 1)
    rows = widened(route_ids, route_gates, section_grad)

    half, far = tokens // 2, size // 2
    back = ahead = rows
    waiting = {0: rows}
    received = [None] * size
    for step in range(1, far + 1):
        if step < far:
            next_back, next_ahead = send(back, owners, 1, 0), send(ahead, owners, -1, 0)
        else:
            next_back, next_ahead = (
                send(back[:half], owners, 1, 0),
                send(ahead[half:], owners, -1, 0),
            )
        results = products(list(waiting.values()), tokens, weight_mat, other_mat)
        back, ahead, results = lax.optimization_barrier((next_back, next_ahead, results))
        for distance, result in zip(waiting, results):
            received[(-distance) % size] = send(result, owners, distance, 0) if distance else result
        waiting = {size - step: back, step: ahead}
    (result,) = products([back, ahead], tokens, weight_mat, other_mat)
    received[far] = send(result, owners, far, 0)
    out = pick_routes(labels.reshape(tokens * top, 1), received)
    return out.reshape(1, tokens, top, hidden)


def slotted_device(section_grad, route_ids, route_gates, weight_mat, capacity):
    tokens, top = route_ids.shape
    owners = lax.axis_size("expert")
    ids = jnp.arange(owners, dtype=jnp.int32)
    slots = jnp.arange(capacity, dtype=jnp.int32)
    matched = (route_ids[:, :, None] == ids[None, None, :]).astype(jnp.int32)
    hits = jnp.sum(matched, axis=1)
    rank = jnp.cumsum(hits, axis=0) - hits
    position = route_ids * capacity + jnp.sum(matched * rank[:, None, :], axis=2)
    gate_owner = jnp.einsum(
        "tk,tke->te", route_gates.astype(jnp.float32), matched.astype(jnp.float32)
    )
    slot_pick = (hits[:, :, None] == 1) & (rank[:, :, None] == slots[None, None, :])
    send_rows = jnp.einsum(
        "tem,td->emd",
        slot_pick.astype(jnp.bfloat16),
        section_grad,
        preferred_element_type=jnp.float32,
    ).astype(jnp.bfloat16)
    send_gates = jnp.einsum("tem,te->em", slot_pick.astype(jnp.float32), gate_owner).astype(
        jnp.bfloat16
    )
    got_rows = lax.all_to_all(send_rows, "expert", split_axis=0, concat_axis=0, tiled=True)
    got_gates = lax.all_to_all(send_gates, "expert", split_axis=0, concat_axis=0, tiled=True)
    product = lax.dot_general(
        got_rows.reshape(owners * capacity, got_rows.shape[2]),
        weight_mat,
        (((1,), (1,)), ((), ())),
        preferred_element_type=jnp.float32,
    ).reshape(owners, capacity, weight_mat.shape[0])
    returned = lax.all_to_all(
        (product * got_gates.astype(jnp.float32)[:, :, None]).astype(jnp.bfloat16),
        "expert",
        split_axis=0,
        concat_axis=0,
        tiled=True,
    )
    flat = returned.reshape(owners * capacity, returned.shape[2])
    out = jnp.take(flat, position.reshape(tokens * top), axis=0)
    return out.reshape(1, tokens, top, returned.shape[2])


def per_device(upstream, expert_ids, gate_weights, expert_weight):
    section_grad = shifted(upstream, "pipe", -1)[0]
    route_ids = expert_ids[0]
    route_gates = gate_weights[0]
    weight_mat = expert_weight[0, 0]
    tokens, top = route_ids.shape
    owners = lax.axis_size("expert")
    capacity = 2 * tokens * top // owners
    if capacity >= tokens:
        return dense_device(section_grad, route_ids, route_gates, weight_mat)
    return slotted_device(section_grad, route_ids, route_gates, weight_mat, capacity)


def solution(mesh):
    in_specs = (
        P("pipe", "expert", None),
        P("pipe", "expert", None),
        P("pipe", "expert", None),
        P("pipe", "expert", None, None),
    )
    out_specs = P("pipe", "expert", None, None)
    return jax.shard_map(
        per_device, mesh=mesh, in_specs=in_specs, out_specs=out_specs, check_vma=False
    )
```

```python
import functools

import jax
import jax.numpy as jnp
from jax import lax
from jax.experimental import pallas as pl
from jax.experimental.pallas import tpu as pltpu
from jax.sharding import PartitionSpec as P

COLUMNS = 2
CORES = 2
LANES = 128


def shifted(block, axis, distance):
    devices = range(lax.axis_size(axis))
    route = [((i - distance) % len(devices), i) for i in devices]
    return lax.ppermute(block, axis, route)


def ring_place(chip, size):
    z, x = lax.div(chip, COLUMNS), lax.rem(chip, COLUMNS)
    return jnp.where(x == 0, z, size - 1 - z)


def ring_order(owners):
    height = owners // (COLUMNS * CORES)
    up = [z * COLUMNS for z in range(height)]
    down = [z * COLUMNS + 1 for z in reversed(range(height))]
    return up + down


def ring_route(owners, distance, flip):
    order = ring_order(owners)
    route = []
    for place, chip in enumerate(order):
        target = order[(place + distance) % len(order)]
        for core in range(CORES):
            route.append((chip * CORES + core, target * CORES + (core ^ flip)))
    return route


def send(block, owners, distance, flip):
    return lax.ppermute(block, "expert", ring_route(owners, distance, flip))


def gates_kernel(ids, gates, out):
    top, tokens = ids.shape
    expert = lax.broadcasted_iota(jnp.int32, (LANES, tokens), 0)
    total = jnp.zeros((LANES, tokens), jnp.float32)
    for k in range(top):
        gate = gates[k : k + 1, :].astype(jnp.float32)
        total += jnp.where(expert == ids[k : k + 1, :], gate, 0.0)
    out[...] = total.T.astype(jnp.bfloat16)


def gate_columns(ids, gates):
    return pl.pallas_call(
        gates_kernel,
        out_shape=jax.ShapeDtypeStruct((ids.shape[1], LANES), jnp.bfloat16),
        compiler_params=pltpu.CompilerParams(vmem_limit_bytes=16 << 20),
    )(ids, gates)


def widen_kernel(rows, columns, out):
    depth = rows.shape[1]
    out[:, :depth] = rows[...]
    out[:, depth:] = columns[...]


def widened(rows, columns):
    width = rows.shape[1] + columns.shape[1]
    return pl.pallas_call(
        widen_kernel,
        out_shape=jax.ShapeDtypeStruct((rows.shape[0], width), jnp.bfloat16),
        compiler_params=pltpu.CompilerParams(vmem_limit_bytes=16 << 20),
    )(rows, columns)


def products_kernel(count, weight, other, *refs):
    rows, outs = refs[:count], refs[count:]
    hidden, depth = weight.shape
    tokens = outs[0].shape[1]
    me = lax.axis_index("expert")
    core = lax.rem(me, CORES)
    stacked = jnp.concatenate([r[...] for r in rows], axis=0)
    gates = stacked[:, depth:].astype(jnp.float32)
    column = lax.broadcasted_iota(jnp.int32, gates.shape, 1)
    for mat, to in ((weight, core), (other, 1 - core)):
        scale = jnp.sum(jnp.where(column == me - core + to, gates, 0.0), axis=1, keepdims=True)
        product = lax.dot_general(
            stacked[:, :depth],
            mat[...],
            (((1,), (1,)), ((), ())),
            preferred_element_type=jnp.float32,
        )
        scaled = (product * scale).astype(jnp.bfloat16)
        for j, out in enumerate(outs):
            out[to] = scaled[j * tokens : (j + 1) * tokens]


def products(pieces, tokens, weight, other):
    hidden, depth = weight.shape
    total = sum(p.shape[0] for p in pieces)
    return pl.pallas_call(
        functools.partial(products_kernel, len(pieces)),
        out_shape=[jax.ShapeDtypeStruct((CORES, tokens, hidden), jnp.bfloat16)] * (total // tokens),
        compiler_params=pltpu.CompilerParams(vmem_limit_bytes=16 << 20),
        cost_estimate=pl.CostEstimate(
            flops=2 * CORES * total * hidden * depth,
            bytes_accessed=2 * (total * (2 * hidden + depth) + 2 * hidden * depth),
            transcendentals=0,
        ),
    )(weight, other, *pieces)


def pick_kernel(ids, *refs):
    blocks, out = refs[:-1], refs[-1]
    experts, tokens, _ = blocks[0].shape
    size = len(blocks)
    top = ids.shape[0]
    span = 16
    place = ring_place(lax.div(lax.axis_index("expert"), CORES), size)
    chip = lax.div(ids[...], CORES)
    label = lax.rem(ring_place(chip, size) - place + size, size) * CORES + lax.rem(ids[...], CORES)
    column = lax.broadcasted_iota(jnp.int32, (top, size * experts * span), 1)
    for g in range(tokens // span):
        stacked = jnp.concatenate(
            [b[c, g * span : (g + 1) * span, :] for b in blocks for c in range(experts)], axis=0
        )
        picks = [
            jnp.where(column == label[:, g * span + t : g * span + t + 1] * span + t, 1.0, 0.0)
            for t in range(span)
        ]
        pick = jnp.concatenate(picks, axis=0).astype(jnp.bfloat16)
        rows = jnp.dot(pick, stacked, preferred_element_type=jnp.float32)
        out[g * span * top : (g + 1) * span * top, :] = rows.astype(jnp.bfloat16)


def pick_routes(ids, blocks):
    top, tokens = ids.shape
    return pl.pallas_call(
        pick_kernel,
        out_shape=jax.ShapeDtypeStruct((top * tokens, blocks[0].shape[2]), jnp.bfloat16),
        compiler_params=pltpu.CompilerParams(vmem_limit_bytes=16 << 20),
    )(ids, *blocks)


def dense_device(section_grad, route_ids, route_gates, weight_mat):
    tokens, top = route_ids.shape
    owners = lax.axis_size("expert")
    size = owners // CORES
    other_mat = send(weight_mat, owners, 0, 1)
    section_grad, columns = lax.optimization_barrier(
        (section_grad, gate_columns(route_ids.T, route_gates.T))
    )
    rows = widened(section_grad, columns)

    half, far = tokens // 2, size // 2
    back = ahead = rows
    waiting = {0: rows}
    received = [None] * size
    for step in range(1, far + 1):
        if step < far:
            next_back, next_ahead = send(back, owners, 1, 0), send(ahead, owners, -1, 0)
        else:
            next_back, next_ahead = (
                send(back[:half], owners, 1, 0),
                send(ahead[half:], owners, -1, 0),
            )
        results = products(list(waiting.values()), tokens, weight_mat, other_mat)
        for distance, result in zip(waiting, results):
            received[(-distance) % size] = send(result, owners, distance, 0) if distance else result
        back, ahead, _ = lax.optimization_barrier((next_back, next_ahead, results))
        waiting = {size - step: back, step: ahead}
    (result,) = products([back, ahead], tokens, weight_mat, other_mat)
    received[far] = send(result, owners, far, 0)
    out = pick_routes(route_ids.T, received)
    return out.reshape(1, tokens, top, weight_mat.shape[0])


def slotted_device(section_grad, route_ids, route_gates, weight_mat, capacity):
    tokens, top = route_ids.shape
    owners = lax.axis_size("expert")
    ids = jnp.arange(owners, dtype=jnp.int32)
    slots = jnp.arange(capacity, dtype=jnp.int32)
    matched = (route_ids[:, :, None] == ids[None, None, :]).astype(jnp.int32)
    hits = jnp.sum(matched, axis=1)
    rank = jnp.cumsum(hits, axis=0) - hits
    position = route_ids * capacity + jnp.sum(matched * rank[:, None, :], axis=2)
    gate_owner = jnp.einsum(
        "tk,tke->te", route_gates.astype(jnp.float32), matched.astype(jnp.float32)
    )
    slot_pick = (hits[:, :, None] == 1) & (rank[:, :, None] == slots[None, None, :])
    send_rows = jnp.einsum(
        "tem,td->emd",
        slot_pick.astype(jnp.bfloat16),
        section_grad,
        preferred_element_type=jnp.float32,
    ).astype(jnp.bfloat16)
    send_gates = jnp.einsum("tem,te->em", slot_pick.astype(jnp.float32), gate_owner).astype(
        jnp.bfloat16
    )
    got_rows = lax.all_to_all(send_rows, "expert", split_axis=0, concat_axis=0, tiled=True)
    got_gates = lax.all_to_all(send_gates, "expert", split_axis=0, concat_axis=0, tiled=True)
    product = lax.dot_general(
        got_rows.reshape(owners * capacity, got_rows.shape[2]),
        weight_mat,
        (((1,), (1,)), ((), ())),
        preferred_element_type=jnp.float32,
    ).reshape(owners, capacity, weight_mat.shape[0])
    returned = lax.all_to_all(
        (product * got_gates.astype(jnp.float32)[:, :, None]).astype(jnp.bfloat16),
        "expert",
        split_axis=0,
        concat_axis=0,
        tiled=True,
    )
    flat = returned.reshape(owners * capacity, returned.shape[2])
    out = jnp.take(flat, position.reshape(tokens * top), axis=0)
    return out.reshape(1, tokens, top, returned.shape[2])


def per_device(upstream, expert_ids, gate_weights, expert_weight):
    section_grad = shifted(upstream, "pipe", -1)[0]
    route_ids = expert_ids[0]
    route_gates = gate_weights[0]
    weight_mat = expert_weight[0, 0]
    tokens, top = route_ids.shape
    owners = lax.axis_size("expert")
    capacity = 2 * tokens * top // owners
    if capacity >= tokens:
        return dense_device(section_grad, route_ids, route_gates, weight_mat)
    return slotted_device(section_grad, route_ids, route_gates, weight_mat, capacity)


def solution(mesh):
    in_specs = (
        P("pipe", "expert", None),
        P("pipe", "expert", None),
        P("pipe", "expert", None),
        P("pipe", "expert", None, None),
    )
    out_specs = P("pipe", "expert", None, None)
    return jax.shard_map(
        per_device, mesh=mesh, in_specs=in_specs, out_specs=out_specs, check_vma=False
    )
```

```python
import functools

import jax
import jax.numpy as jnp
from jax import lax
from jax.experimental import pallas as pl
from jax.experimental.pallas import tpu as pltpu
from jax.sharding import PartitionSpec as P

CORES = 2
X, Z_NEAR, Z_FAR = 1, 2, 4
LANES = 128


def shifted(block, axis, distance):
    devices = range(lax.axis_size(axis))
    route = [((i - distance) % len(devices), i) for i in devices]
    return lax.ppermute(block, axis, route)


def send(block, owners, flip, core=0):
    route = [(i, ((i // CORES) ^ flip) * CORES + ((i % CORES) ^ core)) for i in range(owners)]
    return lax.ppermute(block, "expert", route)


def gates_kernel(ids, gates, out):
    top, tokens = ids.shape
    expert = lax.broadcasted_iota(jnp.int32, (LANES, tokens), 0)
    total = jnp.zeros((LANES, tokens), jnp.float32)
    for k in range(top):
        gate = gates[k : k + 1, :].astype(jnp.float32)
        total += jnp.where(expert == ids[k : k + 1, :], gate, 0.0)
    out[...] = total.T.astype(jnp.bfloat16)


def gate_columns(ids, gates):
    return pl.pallas_call(
        gates_kernel,
        out_shape=jax.ShapeDtypeStruct((ids.shape[1], LANES), jnp.bfloat16),
        compiler_params=pltpu.CompilerParams(vmem_limit_bytes=16 << 20),
    )(ids, gates)


def widen_kernel(rows, columns, out):
    depth = rows.shape[1]
    out[:, :depth] = rows[...]
    out[:, depth:] = columns[...]


def widened(rows, columns):
    width = rows.shape[1] + columns.shape[1]
    return pl.pallas_call(
        widen_kernel,
        out_shape=jax.ShapeDtypeStruct((rows.shape[0], width), jnp.bfloat16),
        compiler_params=pltpu.CompilerParams(vmem_limit_bytes=16 << 20),
    )(rows, columns)


def products_kernel(count, weight, other, *refs):
    rows, outs = refs[:count], refs[count:]
    hidden, depth = weight.shape
    tokens = outs[0].shape[1]
    me = lax.axis_index("expert")
    core = lax.rem(me, CORES)
    stacked = jnp.concatenate([r[...] for r in rows], axis=0)
    gates = stacked[:, depth:].astype(jnp.float32)
    column = lax.broadcasted_iota(jnp.int32, gates.shape, 1)
    for mat, to in ((weight, core), (other, 1 - core)):
        scale = jnp.sum(jnp.where(column == me - core + to, gates, 0.0), axis=1, keepdims=True)
        product = lax.dot_general(
            stacked[:, :depth],
            mat[...],
            (((1,), (1,)), ((), ())),
            preferred_element_type=jnp.float32,
        )
        scaled = (product * scale).astype(jnp.bfloat16)
        for j, out in enumerate(outs):
            out[to] = scaled[j * tokens : (j + 1) * tokens]


def products(pieces, tokens, weight, other):
    hidden, depth = weight.shape
    total = sum(p.shape[0] for p in pieces)
    return pl.pallas_call(
        functools.partial(products_kernel, len(pieces)),
        out_shape=[jax.ShapeDtypeStruct((CORES, tokens, hidden), jnp.bfloat16)] * (total // tokens),
        compiler_params=pltpu.CompilerParams(vmem_limit_bytes=16 << 20),
        cost_estimate=pl.CostEstimate(
            flops=2 * CORES * total * hidden * depth,
            bytes_accessed=2 * (total * (2 * hidden + depth) + 2 * hidden * depth),
            transcendentals=0,
        ),
    )(weight, other, *pieces)


def pick_kernel(ids, *refs):
    blocks, out = refs[:-1], refs[-1]
    experts, tokens, _ = blocks[0].shape
    top = ids.shape[0]
    span = 16
    chip = lax.div(lax.axis_index("expert"), CORES)
    label = (lax.div(ids[...], CORES) ^ chip) * CORES + lax.rem(ids[...], CORES)
    column = lax.broadcasted_iota(jnp.int32, (top, len(blocks) * experts * span), 1)
    for g in range(tokens // span):
        stacked = jnp.concatenate(
            [b[c, g * span : (g + 1) * span, :] for b in blocks for c in range(experts)], axis=0
        )
        picks = [
            jnp.where(column == label[:, g * span + t : g * span + t + 1] * span + t, 1.0, 0.0)
            for t in range(span)
        ]
        pick = jnp.concatenate(picks, axis=0).astype(jnp.bfloat16)
        rows = jnp.dot(pick, stacked, preferred_element_type=jnp.float32)
        out[g * span * top : (g + 1) * span * top, :] = rows.astype(jnp.bfloat16)


def pick_routes(ids, blocks):
    top, tokens = ids.shape
    return pl.pallas_call(
        pick_kernel,
        out_shape=jax.ShapeDtypeStruct((top * tokens, blocks[0].shape[2]), jnp.bfloat16),
        compiler_params=pltpu.CompilerParams(vmem_limit_bytes=16 << 20),
    )(ids, *blocks)


def dense_device(section_grad, route_ids, route_gates, weight_mat):
    tokens, top = route_ids.shape
    owners = lax.axis_size("expert")
    other_mat = send(weight_mat, owners, 0, 1)
    section_grad, columns = lax.optimization_barrier(
        (section_grad, gate_columns(route_ids.T, route_gates.T))
    )
    rows = widened(section_grad, columns)

    def work(*pieces):
        return products(list(pieces), tokens, weight_mat, other_mat)

    tie = lax.optimization_barrier
    far = send(rows, owners, Z_FAR)
    near = send(rows, owners, Z_NEAR)
    side = send(rows, owners, X)
    near, side, (out_own,) = tie((near, side, work(rows)))
    near_side = send(near, owners, X)
    far, (out_side, out_near) = tie((far, work(side, near)))
    cross = send(far, owners, Z_NEAR)
    far_side = send(far, owners, X)
    (out_far,) = work(far)
    back_far = send(out_far, owners, Z_FAR)
    cross, _ = tie((cross, out_far))
    cross_side = send(cross, owners, X)
    (out_cross,) = work(cross)
    back_cross = send(out_cross, owners, Z_NEAR ^ Z_FAR)
    far_side, near_side, back_far, out_side, out_near, _ = tie(
        (far_side, near_side, back_far, out_side, out_near, out_cross)
    )
    out_far_side, out_near_side = work(far_side, near_side)
    back_far_side = send(out_far_side, owners, X ^ Z_FAR)
    back_near_side = send(out_near_side, owners, X ^ Z_NEAR)
    back_side = send(out_side, owners, X)
    back_near = send(out_near, owners, Z_NEAR)
    cross_side, _ = tie((cross_side, out_far_side))
    (out_cross_side,) = work(cross_side)
    received = {
        0: out_own,
        X: back_side,
        Z_NEAR: back_near,
        X ^ Z_NEAR: back_near_side,
        Z_FAR: back_far,
        X ^ Z_FAR: back_far_side,
        Z_NEAR ^ Z_FAR: back_cross,
        X ^ Z_NEAR ^ Z_FAR: send(out_cross_side, owners, X ^ Z_NEAR ^ Z_FAR),
    }
    out = pick_routes(route_ids.T, [received[flip] for flip in sorted(received)])
    return out.reshape(1, tokens, top, weight_mat.shape[0])


def slotted_device(section_grad, route_ids, route_gates, weight_mat, capacity):
    tokens, top = route_ids.shape
    owners = lax.axis_size("expert")
    ids = jnp.arange(owners, dtype=jnp.int32)
    slots = jnp.arange(capacity, dtype=jnp.int32)
    matched = (route_ids[:, :, None] == ids[None, None, :]).astype(jnp.int32)
    hits = jnp.sum(matched, axis=1)
    rank = jnp.cumsum(hits, axis=0) - hits
    position = route_ids * capacity + jnp.sum(matched * rank[:, None, :], axis=2)
    gate_owner = jnp.einsum(
        "tk,tke->te", route_gates.astype(jnp.float32), matched.astype(jnp.float32)
    )
    slot_pick = (hits[:, :, None] == 1) & (rank[:, :, None] == slots[None, None, :])
    send_rows = jnp.einsum(
        "tem,td->emd",
        slot_pick.astype(jnp.bfloat16),
        section_grad,
        preferred_element_type=jnp.float32,
    ).astype(jnp.bfloat16)
    send_gates = jnp.einsum("tem,te->em", slot_pick.astype(jnp.float32), gate_owner).astype(
        jnp.bfloat16
    )
    got_rows = lax.all_to_all(send_rows, "expert", split_axis=0, concat_axis=0, tiled=True)
    got_gates = lax.all_to_all(send_gates, "expert", split_axis=0, concat_axis=0, tiled=True)
    product = lax.dot_general(
        got_rows.reshape(owners * capacity, got_rows.shape[2]),
        weight_mat,
        (((1,), (1,)), ((), ())),
        preferred_element_type=jnp.float32,
    ).reshape(owners, capacity, weight_mat.shape[0])
    returned = lax.all_to_all(
        (product * got_gates.astype(jnp.float32)[:, :, None]).astype(jnp.bfloat16),
        "expert",
        split_axis=0,
        concat_axis=0,
        tiled=True,
    )
    flat = returned.reshape(owners * capacity, returned.shape[2])
    out = jnp.take(flat, position.reshape(tokens * top), axis=0)
    return out.reshape(1, tokens, top, returned.shape[2])


def per_device(upstream, expert_ids, gate_weights, expert_weight):
    section_grad = shifted(upstream, "pipe", -1)[0]
    route_ids = expert_ids[0]
    route_gates = gate_weights[0]
    weight_mat = expert_weight[0, 0]
    tokens, top = route_ids.shape
    owners = lax.axis_size("expert")
    capacity = 2 * tokens * top // owners
    if capacity >= tokens and owners == CORES * 2 * Z_FAR:
        return dense_device(section_grad, route_ids, route_gates, weight_mat)
    return slotted_device(section_grad, route_ids, route_gates, weight_mat, capacity)


def solution(mesh):
    in_specs = (
        P("pipe", "expert", None),
        P("pipe", "expert", None),
        P("pipe", "expert", None),
        P("pipe", "expert", None, None),
    )
    out_specs = P("pipe", "expert", None, None)
    return jax.shard_map(
        per_device, mesh=mesh, in_specs=in_specs, out_specs=out_specs, check_vma=False
    )
```

```python
import functools

import jax
import jax.numpy as jnp
from jax import lax
from jax.experimental import pallas as pl
from jax.experimental.pallas import tpu as pltpu
from jax.sharding import PartitionSpec as P

CORES = 2
X, Z_NEAR, Z_FAR = 1, 2, 4
LANES = 128


def shifted(block, axis, distance):
    devices = range(lax.axis_size(axis))
    route = [((i - distance) % len(devices), i) for i in devices]
    return lax.ppermute(block, axis, route)


def send(block, owners, flip, core=0):
    route = [(i, ((i // CORES) ^ flip) * CORES + ((i % CORES) ^ core)) for i in range(owners)]
    return lax.ppermute(block, "expert", route)


def gates_kernel(ids, gates, out):
    top, tokens = ids.shape
    expert = lax.broadcasted_iota(jnp.int32, (LANES, tokens), 0)
    total = jnp.zeros((LANES, tokens), jnp.float32)
    for k in range(top):
        gate = gates[k : k + 1, :].astype(jnp.float32)
        total += jnp.where(expert == ids[k : k + 1, :], gate, 0.0)
    out[...] = total.T.astype(jnp.bfloat16)


def gate_columns(ids, gates):
    return pl.pallas_call(
        gates_kernel,
        out_shape=jax.ShapeDtypeStruct((ids.shape[1], LANES), jnp.bfloat16),
        compiler_params=pltpu.CompilerParams(vmem_limit_bytes=16 << 20),
    )(ids, gates)


def widen_kernel(rows, columns, out):
    depth = rows.shape[1]
    out[:, :depth] = rows[...]
    out[:, depth:] = columns[...]


def widened(rows, columns):
    width = rows.shape[1] + columns.shape[1]
    return pl.pallas_call(
        widen_kernel,
        out_shape=jax.ShapeDtypeStruct((rows.shape[0], width), jnp.bfloat16),
        compiler_params=pltpu.CompilerParams(vmem_limit_bytes=16 << 20),
    )(rows, columns)


def products_kernel(count, weight, other, *refs):
    rows, outs = refs[:count], refs[count:]
    hidden, depth = weight.shape
    tokens = outs[0].shape[1]
    me = lax.axis_index("expert")
    core = lax.rem(me, CORES)
    stacked = jnp.concatenate([r[...] for r in rows], axis=0)
    gates = stacked[:, depth:].astype(jnp.float32)
    column = lax.broadcasted_iota(jnp.int32, gates.shape, 1)
    for mat, to in ((weight, core), (other, 1 - core)):
        scale = jnp.sum(jnp.where(column == me - core + to, gates, 0.0), axis=1, keepdims=True)
        product = lax.dot_general(
            stacked[:, :depth],
            mat[...],
            (((1,), (1,)), ((), ())),
            preferred_element_type=jnp.float32,
        )
        scaled = (product * scale).astype(jnp.bfloat16)
        for j, out in enumerate(outs):
            out[to] = scaled[j * tokens : (j + 1) * tokens]


def products(pieces, tokens, weight, other):
    hidden, depth = weight.shape
    total = sum(p.shape[0] for p in pieces)
    return pl.pallas_call(
        functools.partial(products_kernel, len(pieces)),
        out_shape=[jax.ShapeDtypeStruct((CORES, tokens, hidden), jnp.bfloat16)] * (total // tokens),
        compiler_params=pltpu.CompilerParams(vmem_limit_bytes=16 << 20),
        cost_estimate=pl.CostEstimate(
            flops=2 * CORES * total * hidden * depth,
            bytes_accessed=2 * (total * (2 * hidden + depth) + 2 * hidden * depth),
            transcendentals=0,
        ),
    )(weight, other, *pieces)


def pick_kernel(ids, *refs):
    blocks, out = refs[:-1], refs[-1]
    experts, tokens, _ = blocks[0].shape
    top = ids.shape[0]
    span = 16
    chip = lax.div(lax.axis_index("expert"), CORES)
    label = (lax.div(ids[...], CORES) ^ chip) * CORES + lax.rem(ids[...], CORES)
    column = lax.broadcasted_iota(jnp.int32, (top, len(blocks) * experts * span), 1)
    for g in range(tokens // span):
        stacked = jnp.concatenate(
            [b[c, g * span : (g + 1) * span, :] for b in blocks for c in range(experts)], axis=0
        )
        picks = [
            jnp.where(column == label[:, g * span + t : g * span + t + 1] * span + t, 1.0, 0.0)
            for t in range(span)
        ]
        pick = jnp.concatenate(picks, axis=0).astype(jnp.bfloat16)
        rows = jnp.dot(pick, stacked, preferred_element_type=jnp.float32)
        out[g * span * top : (g + 1) * span * top, :] = rows.astype(jnp.bfloat16)


def pick_routes(ids, blocks):
    top, tokens = ids.shape
    return pl.pallas_call(
        pick_kernel,
        out_shape=jax.ShapeDtypeStruct((top * tokens, blocks[0].shape[2]), jnp.bfloat16),
        compiler_params=pltpu.CompilerParams(vmem_limit_bytes=16 << 20),
    )(ids, *blocks)


def dense_device(section_grad, route_ids, route_gates, weight_mat):
    tokens, top = route_ids.shape
    owners = lax.axis_size("expert")
    other_mat = send(weight_mat, owners, 0, 1)
    section_grad, columns = lax.optimization_barrier(
        (section_grad, gate_columns(route_ids.T, route_gates.T))
    )
    rows = widened(section_grad, columns)

    def work(*pieces):
        return products(list(pieces), tokens, weight_mat, other_mat)

    tie = lax.optimization_barrier
    far = send(rows, owners, Z_FAR)
    near = send(rows, owners, Z_NEAR)
    side = send(rows, owners, X)
    (out_own,) = work(rows)
    far, _ = tie((far, out_own))
    cross = send(far, owners, Z_NEAR)
    (out_far,) = work(far)
    back_far = send(out_far, owners, Z_FAR)
    near, side, _ = tie((near, side, out_far))
    far_side = send(tie((far, near))[0], owners, X)
    out_side, out_near = work(side, near)
    cross, near, _ = tie((cross, near, out_side))
    cross_side = send(cross, owners, X)
    near_side = send(near, owners, X)
    (out_cross,) = work(cross)
    back_cross = send(out_cross, owners, Z_NEAR ^ Z_FAR)
    far_side, back_far, out_side, out_near, _ = tie(
        (far_side, back_far, out_side, out_near, out_cross)
    )
    (out_far_side,) = work(far_side)
    back_far_side = send(out_far_side, owners, X ^ Z_FAR)
    cross_side, near_side, _ = tie((cross_side, near_side, out_far_side))
    (out_cross_side, out_near_side) = work(cross_side, near_side)
    back_near_side = send(out_near_side, owners, X ^ Z_NEAR)
    back_side = send(out_side, owners, X)
    back_near = send(out_near, owners, Z_NEAR)
    received = {
        0: out_own,
        X: back_side,
        Z_NEAR: back_near,
        X ^ Z_NEAR: back_near_side,
        Z_FAR: back_far,
        X ^ Z_FAR: back_far_side,
        Z_NEAR ^ Z_FAR: back_cross,
        X ^ Z_NEAR ^ Z_FAR: send(out_cross_side, owners, X ^ Z_NEAR ^ Z_FAR),
    }
    out = pick_routes(route_ids.T, [received[flip] for flip in sorted(received)])
    return out.reshape(1, tokens, top, weight_mat.shape[0])


def slotted_device(section_grad, route_ids, route_gates, weight_mat, capacity):
    tokens, top = route_ids.shape
    owners = lax.axis_size("expert")
    ids = jnp.arange(owners, dtype=jnp.int32)
    slots = jnp.arange(capacity, dtype=jnp.int32)
    matched = (route_ids[:, :, None] == ids[None, None, :]).astype(jnp.int32)
    hits = jnp.sum(matched, axis=1)
    rank = jnp.cumsum(hits, axis=0) - hits
    position = route_ids * capacity + jnp.sum(matched * rank[:, None, :], axis=2)
    gate_owner = jnp.einsum(
        "tk,tke->te", route_gates.astype(jnp.float32), matched.astype(jnp.float32)
    )
    slot_pick = (hits[:, :, None] == 1) & (rank[:, :, None] == slots[None, None, :])
    send_rows = jnp.einsum(
        "tem,td->emd",
        slot_pick.astype(jnp.bfloat16),
        section_grad,
        preferred_element_type=jnp.float32,
    ).astype(jnp.bfloat16)
    send_gates = jnp.einsum("tem,te->em", slot_pick.astype(jnp.float32), gate_owner).astype(
        jnp.bfloat16
    )
    got_rows = lax.all_to_all(send_rows, "expert", split_axis=0, concat_axis=0, tiled=True)
    got_gates = lax.all_to_all(send_gates, "expert", split_axis=0, concat_axis=0, tiled=True)
    product = lax.dot_general(
        got_rows.reshape(owners * capacity, got_rows.shape[2]),
        weight_mat,
        (((1,), (1,)), ((), ())),
        preferred_element_type=jnp.float32,
    ).reshape(owners, capacity, weight_mat.shape[0])
    returned = lax.all_to_all(
        (product * got_gates.astype(jnp.float32)[:, :, None]).astype(jnp.bfloat16),
        "expert",
        split_axis=0,
        concat_axis=0,
        tiled=True,
    )
    flat = returned.reshape(owners * capacity, returned.shape[2])
    out = jnp.take(flat, position.reshape(tokens * top), axis=0)
    return out.reshape(1, tokens, top, returned.shape[2])


def per_device(upstream, expert_ids, gate_weights, expert_weight):
    section_grad = shifted(upstream, "pipe", -1)[0]
    route_ids = expert_ids[0]
    route_gates = gate_weights[0]
    weight_mat = expert_weight[0, 0]
    tokens, top = route_ids.shape
    owners = lax.axis_size("expert")
    capacity = 2 * tokens * top // owners
    if capacity >= tokens and owners == CORES * 2 * Z_FAR:
        return dense_device(section_grad, route_ids, route_gates, weight_mat)
    return slotted_device(section_grad, route_ids, route_gates, weight_mat, capacity)


def solution(mesh):
    in_specs = (
        P("pipe", "expert", None),
        P("pipe", "expert", None),
        P("pipe", "expert", None),
        P("pipe", "expert", None, None),
    )
    out_specs = P("pipe", "expert", None, None)
    return jax.shard_map(
        per_device, mesh=mesh, in_specs=in_specs, out_specs=out_specs, check_vma=False
    )
```

```python
import functools

import jax
import jax.numpy as jnp
from jax import lax
from jax.experimental import pallas as pl
from jax.experimental.pallas import tpu as pltpu
from jax.sharding import PartitionSpec as P

CORES = 2
X, Z_NEAR, Z_FAR = 1, 2, 4
LANES = 128


def shifted(block, axis, distance):
    devices = range(lax.axis_size(axis))
    route = [((i - distance) % len(devices), i) for i in devices]
    return lax.ppermute(block, axis, route)


def send(block, owners, flip, core=0):
    route = [(i, ((i // CORES) ^ flip) * CORES + ((i % CORES) ^ core)) for i in range(owners)]
    return lax.ppermute(block, "expert", route)


def gates_kernel(ids, gates, out):
    top, tokens = ids.shape
    expert = lax.broadcasted_iota(jnp.int32, (LANES, tokens), 0)
    total = jnp.zeros((LANES, tokens), jnp.float32)
    for k in range(top):
        gate = gates[k : k + 1, :].astype(jnp.float32)
        total += jnp.where(expert == ids[k : k + 1, :], gate, 0.0)
    out[...] = total.T.astype(jnp.bfloat16)


def gate_columns(ids, gates):
    return pl.pallas_call(
        gates_kernel,
        out_shape=jax.ShapeDtypeStruct((ids.shape[1], LANES), jnp.bfloat16),
        compiler_params=pltpu.CompilerParams(vmem_limit_bytes=16 << 20),
    )(ids, gates)


def widen_kernel(rows, columns, out):
    depth = rows.shape[1]
    out[:, :depth] = rows[...]
    out[:, depth:] = columns[...]


def widened(rows, columns):
    width = rows.shape[1] + columns.shape[1]
    return pl.pallas_call(
        widen_kernel,
        out_shape=jax.ShapeDtypeStruct((rows.shape[0], width), jnp.bfloat16),
        compiler_params=pltpu.CompilerParams(vmem_limit_bytes=16 << 20),
    )(rows, columns)


def products_kernel(count, weight, other, *refs):
    rows, outs = refs[:count], refs[count:]
    hidden, depth = weight.shape
    tokens = outs[0].shape[1]
    me = lax.axis_index("expert")
    core = lax.rem(me, CORES)
    stacked = jnp.concatenate([r[...] for r in rows], axis=0)
    gates = stacked[:, depth:].astype(jnp.float32)
    column = lax.broadcasted_iota(jnp.int32, gates.shape, 1)
    for mat, to in ((weight, core), (other, 1 - core)):
        scale = jnp.sum(jnp.where(column == me - core + to, gates, 0.0), axis=1, keepdims=True)
        product = lax.dot_general(
            stacked[:, :depth],
            mat[...],
            (((1,), (1,)), ((), ())),
            preferred_element_type=jnp.float32,
        )
        scaled = (product * scale).astype(jnp.bfloat16)
        for j, out in enumerate(outs):
            out[to] = scaled[j * tokens : (j + 1) * tokens]


def products(pieces, tokens, weight, other):
    hidden, depth = weight.shape
    total = sum(p.shape[0] for p in pieces)
    return pl.pallas_call(
        functools.partial(products_kernel, len(pieces)),
        out_shape=[jax.ShapeDtypeStruct((CORES, tokens, hidden), jnp.bfloat16)] * (total // tokens),
        compiler_params=pltpu.CompilerParams(vmem_limit_bytes=16 << 20),
        cost_estimate=pl.CostEstimate(
            flops=20 * CORES * total * hidden * depth,
            bytes_accessed=2 * (total * (2 * hidden + depth) + 2 * hidden * depth),
            transcendentals=0,
        ),
    )(weight, other, *pieces)


def pick_kernel(ids, *refs):
    blocks, out = refs[:-1], refs[-1]
    experts, tokens, _ = blocks[0].shape
    top = ids.shape[0]
    span = 16
    chip = lax.div(lax.axis_index("expert"), CORES)
    label = (lax.div(ids[...], CORES) ^ chip) * CORES + lax.rem(ids[...], CORES)
    column = lax.broadcasted_iota(jnp.int32, (top, len(blocks) * experts * span), 1)
    for g in range(tokens // span):
        stacked = jnp.concatenate(
            [b[c, g * span : (g + 1) * span, :] for b in blocks for c in range(experts)], axis=0
        )
        picks = [
            jnp.where(column == label[:, g * span + t : g * span + t + 1] * span + t, 1.0, 0.0)
            for t in range(span)
        ]
        pick = jnp.concatenate(picks, axis=0).astype(jnp.bfloat16)
        rows = jnp.dot(pick, stacked, preferred_element_type=jnp.float32)
        out[g * span * top : (g + 1) * span * top, :] = rows.astype(jnp.bfloat16)


def pick_routes(ids, blocks):
    top, tokens = ids.shape
    return pl.pallas_call(
        pick_kernel,
        out_shape=jax.ShapeDtypeStruct((top * tokens, blocks[0].shape[2]), jnp.bfloat16),
        compiler_params=pltpu.CompilerParams(vmem_limit_bytes=16 << 20),
    )(ids, *blocks)


def dense_device(section_grad, route_ids, route_gates, weight_mat):
    tokens, top = route_ids.shape
    owners = lax.axis_size("expert")
    other_mat = send(weight_mat, owners, 0, 1)
    section_grad, columns = lax.optimization_barrier(
        (section_grad, gate_columns(route_ids.T, route_gates.T))
    )
    rows = widened(section_grad, columns)

    def work(*pieces):
        return products(list(pieces), tokens, weight_mat, other_mat)

    tie = lax.optimization_barrier
    far = send(rows, owners, Z_FAR)
    near = send(rows, owners, Z_NEAR)
    side = send(rows, owners, X)
    (out_own,) = work(rows)
    far, _ = tie((far, out_own))
    cross = send(far, owners, Z_NEAR)
    (out_far,) = work(far)
    back_far = send(out_far, owners, Z_FAR)
    near, side, _ = tie((near, side, out_far))
    far_side = send(tie((far, near))[0], owners, X)
    out_side, out_near = work(side, near)
    cross, near, _ = tie((cross, near, out_side))
    cross_side = send(cross, owners, X)
    near_side = send(near, owners, X)
    (out_cross,) = work(cross)
    back_cross = send(out_cross, owners, Z_NEAR ^ Z_FAR)
    far_side, back_far, out_side, out_near, _ = tie(
        (far_side, back_far, out_side, out_near, out_cross)
    )
    (out_far_side,) = work(far_side)
    back_far_side = send(out_far_side, owners, X ^ Z_FAR)
    cross_side, near_side, back_cross, _ = tie((cross_side, near_side, back_cross, out_far_side))
    (out_cross_side, out_near_side) = work(cross_side, near_side)
    back_near_side = send(out_near_side, owners, X ^ Z_NEAR)
    back_side = send(out_side, owners, X)
    back_near = send(out_near, owners, Z_NEAR)
    received = {
        0: out_own,
        X: back_side,
        Z_NEAR: back_near,
        X ^ Z_NEAR: back_near_side,
        Z_FAR: back_far,
        X ^ Z_FAR: back_far_side,
        Z_NEAR ^ Z_FAR: back_cross,
        X ^ Z_NEAR ^ Z_FAR: send(out_cross_side, owners, X ^ Z_NEAR ^ Z_FAR),
    }
    out = pick_routes(route_ids.T, [received[flip] for flip in sorted(received)])
    return out.reshape(1, tokens, top, weight_mat.shape[0])


def slotted_device(section_grad, route_ids, route_gates, weight_mat, capacity):
    tokens, top = route_ids.shape
    owners = lax.axis_size("expert")
    ids = jnp.arange(owners, dtype=jnp.int32)
    slots = jnp.arange(capacity, dtype=jnp.int32)
    matched = (route_ids[:, :, None] == ids[None, None, :]).astype(jnp.int32)
    hits = jnp.sum(matched, axis=1)
    rank = jnp.cumsum(hits, axis=0) - hits
    position = route_ids * capacity + jnp.sum(matched * rank[:, None, :], axis=2)
    gate_owner = jnp.einsum(
        "tk,tke->te", route_gates.astype(jnp.float32), matched.astype(jnp.float32)
    )
    slot_pick = (hits[:, :, None] == 1) & (rank[:, :, None] == slots[None, None, :])
    send_rows = jnp.einsum(
        "tem,td->emd",
        slot_pick.astype(jnp.bfloat16),
        section_grad,
        preferred_element_type=jnp.float32,
    ).astype(jnp.bfloat16)
    send_gates = jnp.einsum("tem,te->em", slot_pick.astype(jnp.float32), gate_owner).astype(
        jnp.bfloat16
    )
    got_rows = lax.all_to_all(send_rows, "expert", split_axis=0, concat_axis=0, tiled=True)
    got_gates = lax.all_to_all(send_gates, "expert", split_axis=0, concat_axis=0, tiled=True)
    product = lax.dot_general(
        got_rows.reshape(owners * capacity, got_rows.shape[2]),
        weight_mat,
        (((1,), (1,)), ((), ())),
        preferred_element_type=jnp.float32,
    ).reshape(owners, capacity, weight_mat.shape[0])
    returned = lax.all_to_all(
        (product * got_gates.astype(jnp.float32)[:, :, None]).astype(jnp.bfloat16),
        "expert",
        split_axis=0,
        concat_axis=0,
        tiled=True,
    )
    flat = returned.reshape(owners * capacity, returned.shape[2])
    out = jnp.take(flat, position.reshape(tokens * top), axis=0)
    return out.reshape(1, tokens, top, returned.shape[2])


def per_device(upstream, expert_ids, gate_weights, expert_weight):
    section_grad = shifted(upstream, "pipe", -1)[0]
    route_ids = expert_ids[0]
    route_gates = gate_weights[0]
    weight_mat = expert_weight[0, 0]
    tokens, top = route_ids.shape
    owners = lax.axis_size("expert")
    capacity = 2 * tokens * top // owners
    if capacity >= tokens and owners == CORES * 2 * Z_FAR:
        return dense_device(section_grad, route_ids, route_gates, weight_mat)
    return slotted_device(section_grad, route_ids, route_gates, weight_mat, capacity)


def solution(mesh):
    in_specs = (
        P("pipe", "expert", None),
        P("pipe", "expert", None),
        P("pipe", "expert", None),
        P("pipe", "expert", None, None),
    )
    out_specs = P("pipe", "expert", None, None)
    return jax.shard_map(
        per_device, mesh=mesh, in_specs=in_specs, out_specs=out_specs, check_vma=False
    )
```

```python
import functools

import jax
import jax.numpy as jnp
from jax import lax
from jax.experimental import pallas as pl
from jax.experimental.pallas import tpu as pltpu
from jax.sharding import PartitionSpec as P

CORES = 2
X, Z_NEAR, Z_FAR = 1, 2, 4
LANES = 128


def shifted(block, axis, distance):
    devices = range(lax.axis_size(axis))
    route = [((i - distance) % len(devices), i) for i in devices]
    return lax.ppermute(block, axis, route)


def send(block, owners, flip, core=0):
    route = [(i, ((i // CORES) ^ flip) * CORES + ((i % CORES) ^ core)) for i in range(owners)]
    return lax.ppermute(block, "expert", route)


def send_across(block, owners, flip):
    sections = lax.axis_size("pipe")
    route = []
    for s in range(sections):
        for i in range(owners):
            target = ((i // CORES) ^ flip) * CORES + i % CORES
            route.append((s * owners + i, (s - 1) % sections * owners + target))
    return lax.ppermute(block, ("pipe", "expert"), route)


def gates_kernel(ids, gates, weight, out):
    top, tokens = ids.shape
    expert = lax.broadcasted_iota(jnp.int32, (LANES, tokens), 0)
    total = jnp.zeros((LANES, tokens), jnp.float32)
    for k in range(top):
        gate = gates[k : k + 1, :].astype(jnp.float32)
        total += jnp.where(expert == ids[k : k + 1, :], gate, 0.0)
    out[...] = total.T.astype(jnp.bfloat16)


def gate_columns(ids, gates, weight):
    return pl.pallas_call(
        gates_kernel,
        out_shape=jax.ShapeDtypeStruct((ids.shape[1], LANES), jnp.bfloat16),
        compiler_params=pltpu.CompilerParams(vmem_limit_bytes=16 << 20),
    )(ids, gates, weight)


def widen_kernel(rows, columns, out):
    depth = rows.shape[1]
    out[:, :depth] = rows[...]
    out[:, depth:] = columns[...]


def widened(rows, columns):
    width = rows.shape[1] + columns.shape[1]
    return pl.pallas_call(
        widen_kernel,
        out_shape=jax.ShapeDtypeStruct((rows.shape[0], width), jnp.bfloat16),
        compiler_params=pltpu.CompilerParams(vmem_limit_bytes=16 << 20),
    )(rows, columns)


def products_kernel(paired, weight, other, *refs):
    hidden, depth = weight.shape
    rows, gates, at = [], [], 0
    for pair in paired:
        rows.append(refs[at][:, :depth])
        gates.append(refs[at + 1][...] if pair else refs[at][:, depth:])
        at += 1 + pair
    outs = refs[at:]
    tokens = outs[0].shape[1]
    me = lax.axis_index("expert")
    core = lax.rem(me, CORES)
    stacked = jnp.concatenate(rows, axis=0)
    gates = jnp.concatenate(gates, axis=0).astype(jnp.float32)
    column = lax.broadcasted_iota(jnp.int32, gates.shape, 1)
    for mat, to in ((weight, core), (other, 1 - core)):
        scale = jnp.sum(jnp.where(column == me - core + to, gates, 0.0), axis=1, keepdims=True)
        product = lax.dot_general(
            stacked, mat[...], (((1,), (1,)), ((), ())), preferred_element_type=jnp.float32
        )
        scaled = (product * scale).astype(jnp.bfloat16)
        for j, out in enumerate(outs):
            out[to] = scaled[j * tokens : (j + 1) * tokens]


def products(pieces, weight, other):
    hidden, depth = weight.shape
    paired = [isinstance(p, tuple) for p in pieces]
    operands = [x for p in pieces for x in (p if isinstance(p, tuple) else (p,))]
    tokens = operands[0].shape[0]
    total = len(pieces) * tokens
    return pl.pallas_call(
        functools.partial(products_kernel, paired),
        out_shape=[jax.ShapeDtypeStruct((CORES, tokens, hidden), jnp.bfloat16)] * len(pieces),
        compiler_params=pltpu.CompilerParams(vmem_limit_bytes=16 << 20),
        cost_estimate=pl.CostEstimate(
            flops=20 * CORES * total * hidden * depth,
            bytes_accessed=2 * (total * (2 * hidden + depth) + 2 * hidden * depth),
            transcendentals=0,
        ),
    )(weight, other, *operands)


def pick_kernel(ids, *refs):
    blocks, out = refs[:-1], refs[-1]
    experts, tokens, _ = blocks[0].shape
    top = ids.shape[0]
    span = 16
    chip = lax.div(lax.axis_index("expert"), CORES)
    label = (lax.div(ids[...], CORES) ^ chip) * CORES + lax.rem(ids[...], CORES)
    column = lax.broadcasted_iota(jnp.int32, (top, len(blocks) * experts * span), 1)
    for g in range(tokens // span):
        stacked = jnp.concatenate(
            [b[c, g * span : (g + 1) * span, :] for b in blocks for c in range(experts)], axis=0
        )
        picks = [
            jnp.where(column == label[:, g * span + t : g * span + t + 1] * span + t, 1.0, 0.0)
            for t in range(span)
        ]
        pick = jnp.concatenate(picks, axis=0).astype(jnp.bfloat16)
        rows = jnp.dot(pick, stacked, preferred_element_type=jnp.float32)
        out[g * span * top : (g + 1) * span * top, :] = rows.astype(jnp.bfloat16)


def pick_routes(ids, blocks):
    top, tokens = ids.shape
    return pl.pallas_call(
        pick_kernel,
        out_shape=jax.ShapeDtypeStruct((top * tokens, blocks[0].shape[2]), jnp.bfloat16),
        compiler_params=pltpu.CompilerParams(vmem_limit_bytes=16 << 20),
    )(ids, *blocks)


def dense_device(upstream, route_ids, route_gates, weight_mat):
    tokens, top = route_ids.shape
    owners = lax.axis_size("expert")
    tie = lax.optimization_barrier

    def work(*pieces):
        return products(list(pieces), weight_mat, other_mat)

    rows = send_across(upstream, owners, 0)
    far = send_across(upstream, owners, Z_FAR)
    near_side = send_across(upstream, owners, X ^ Z_NEAR)
    other_mat = send(weight_mat, owners, 0, 1)
    columns = gate_columns(route_ids.T, route_gates.T, weight_mat)
    far_columns = send(columns, owners, Z_FAR)
    near_side_columns = send(columns, owners, X ^ Z_NEAR)
    rows, columns, other_mat = tie((rows, columns, other_mat))
    rows = widened(rows, columns)
    near = send(rows, owners, Z_NEAR)
    side = send(rows, owners, X)
    far, far_columns, rows = tie((far, far_columns, rows))
    far = widened(far, far_columns)
    cross = send(far, owners, Z_NEAR)
    (out_far,) = work(far)
    back_far = send(out_far, owners, Z_FAR)
    near, side, near_side, near_side_columns, _ = tie(
        (near, side, near_side, near_side_columns, out_far)
    )
    far_side = send(tie((far, out_far))[0], owners, X)
    out_side, out_near, out_near_side = work(side, near, (near_side, near_side_columns))
    cross, _ = tie((cross, out_side))
    cross_side = send(cross, owners, X)
    (out_cross,) = work(cross)
    back_cross = send(out_cross, owners, Z_NEAR ^ Z_FAR)
    far_side, back_far, out_side, out_near, out_near_side, _ = tie(
        (far_side, back_far, out_side, out_near, out_near_side, out_cross)
    )
    back_side = send(out_side, owners, X)
    back_near = send(out_near, owners, Z_NEAR)
    (out_far_side,) = work(far_side)
    back_far_side = send(out_far_side, owners, X ^ Z_FAR)
    cross_side, back_side, _ = tie((cross_side, back_side, out_far_side))
    (out_cross_side,) = work(cross_side)
    back_cross_side = send(out_cross_side, owners, X ^ Z_NEAR ^ Z_FAR)
    back_near_side = send(out_near_side, owners, X ^ Z_NEAR)
    rows, _ = tie((rows, out_cross_side))
    (out_own,) = work(rows)
    received = {
        0: out_own,
        X: back_side,
        Z_NEAR: back_near,
        X ^ Z_NEAR: back_near_side,
        Z_FAR: back_far,
        X ^ Z_FAR: back_far_side,
        Z_NEAR ^ Z_FAR: back_cross,
        X ^ Z_NEAR ^ Z_FAR: back_cross_side,
    }
    out = pick_routes(route_ids.T, [received[flip] for flip in sorted(received)])
    return out.reshape(1, tokens, top, weight_mat.shape[0])


def slotted_device(section_grad, route_ids, route_gates, weight_mat, capacity):
    tokens, top = route_ids.shape
    owners = lax.axis_size("expert")
    ids = jnp.arange(owners, dtype=jnp.int32)
    slots = jnp.arange(capacity, dtype=jnp.int32)
    matched = (route_ids[:, :, None] == ids[None, None, :]).astype(jnp.int32)
    hits = jnp.sum(matched, axis=1)
    rank = jnp.cumsum(hits, axis=0) - hits
    position = route_ids * capacity + jnp.sum(matched * rank[:, None, :], axis=2)
    gate_owner = jnp.einsum(
        "tk,tke->te", route_gates.astype(jnp.float32), matched.astype(jnp.float32)
    )
    slot_pick = (hits[:, :, None] == 1) & (rank[:, :, None] == slots[None, None, :])
    send_rows = jnp.einsum(
        "tem,td->emd",
        slot_pick.astype(jnp.bfloat16),
        section_grad,
        preferred_element_type=jnp.float32,
    ).astype(jnp.bfloat16)
    send_gates = jnp.einsum("tem,te->em", slot_pick.astype(jnp.float32), gate_owner).astype(
        jnp.bfloat16
    )
    got_rows = lax.all_to_all(send_rows, "expert", split_axis=0, concat_axis=0, tiled=True)
    got_gates = lax.all_to_all(send_gates, "expert", split_axis=0, concat_axis=0, tiled=True)
    product = lax.dot_general(
        got_rows.reshape(owners * capacity, got_rows.shape[2]),
        weight_mat,
        (((1,), (1,)), ((), ())),
        preferred_element_type=jnp.float32,
    ).reshape(owners, capacity, weight_mat.shape[0])
    returned = lax.all_to_all(
        (product * got_gates.astype(jnp.float32)[:, :, None]).astype(jnp.bfloat16),
        "expert",
        split_axis=0,
        concat_axis=0,
        tiled=True,
    )
    flat = returned.reshape(owners * capacity, returned.shape[2])
    out = jnp.take(flat, position.reshape(tokens * top), axis=0)
    return out.reshape(1, tokens, top, returned.shape[2])


def per_device(upstream, expert_ids, gate_weights, expert_weight):
    route_ids = expert_ids[0]
    route_gates = gate_weights[0]
    weight_mat = expert_weight[0, 0]
    tokens, top = route_ids.shape
    owners = lax.axis_size("expert")
    capacity = 2 * tokens * top // owners
    if capacity >= tokens and owners == CORES * 2 * Z_FAR:
        return dense_device(upstream[0], route_ids, route_gates, weight_mat)
    section_grad = shifted(upstream, "pipe", -1)[0]
    return slotted_device(section_grad, route_ids, route_gates, weight_mat, capacity)


def solution(mesh):
    in_specs = (
        P("pipe", "expert", None),
        P("pipe", "expert", None),
        P("pipe", "expert", None),
        P("pipe", "expert", None, None),
    )
    out_specs = P("pipe", "expert", None, None)
    return jax.shard_map(
        per_device, mesh=mesh, in_specs=in_specs, out_specs=out_specs, check_vma=False
    )
```

```python
import functools

import jax
import jax.numpy as jnp
from jax import lax
from jax.experimental import pallas as pl
from jax.experimental.pallas import tpu as pltpu
from jax.sharding import PartitionSpec as P

CORES = 2
X, Z_NEAR, Z_FAR = 1, 2, 4
LANES = 128


def shifted(block, axis, distance):
    devices = range(lax.axis_size(axis))
    route = [((i - distance) % len(devices), i) for i in devices]
    return lax.ppermute(block, axis, route)


def send(block, owners, flip, core=0):
    route = [(i, ((i // CORES) ^ flip) * CORES + ((i % CORES) ^ core)) for i in range(owners)]
    return lax.ppermute(block, "expert", route)


def send_across(block, owners, flip):
    sections = lax.axis_size("pipe")
    route = []
    for s in range(sections):
        for i in range(owners):
            target = ((i // CORES) ^ flip) * CORES + i % CORES
            route.append((s * owners + i, (s - 1) % sections * owners + target))
    return lax.ppermute(block, ("pipe", "expert"), route)


def gates_kernel(ids, gates, weight, out):
    top, tokens = ids.shape
    expert = lax.broadcasted_iota(jnp.int32, (LANES, tokens), 0)
    total = jnp.zeros((LANES, tokens), jnp.float32)
    for k in range(top):
        gate = gates[k : k + 1, :].astype(jnp.float32)
        total += jnp.where(expert == ids[k : k + 1, :], gate, 0.0)
    out[...] = total.T.astype(jnp.bfloat16)


def gate_columns(ids, gates, weight):
    return pl.pallas_call(
        gates_kernel,
        out_shape=jax.ShapeDtypeStruct((ids.shape[1], LANES), jnp.bfloat16),
        compiler_params=pltpu.CompilerParams(vmem_limit_bytes=16 << 20),
    )(ids, gates, weight)


def widen_kernel(rows, columns, out):
    depth = rows.shape[1]
    out[:, :depth] = rows[...]
    out[:, depth:] = columns[...]


def widened(rows, columns):
    width = rows.shape[1] + columns.shape[1]
    return pl.pallas_call(
        widen_kernel,
        out_shape=jax.ShapeDtypeStruct((rows.shape[0], width), jnp.bfloat16),
        compiler_params=pltpu.CompilerParams(vmem_limit_bytes=16 << 20),
    )(rows, columns)


def products_kernel(paired, weight, other, *refs):
    hidden, depth = weight.shape
    rows, gates, at = [], [], 0
    for pair in paired:
        rows.append(refs[at][:, :depth])
        gates.append(refs[at + 1][...] if pair else refs[at][:, depth:])
        at += 1 + pair
    outs = refs[at:]
    tokens = outs[0].shape[1]
    me = lax.axis_index("expert")
    core = lax.rem(me, CORES)
    stacked = jnp.concatenate(rows, axis=0)
    gates = jnp.concatenate(gates, axis=0).astype(jnp.float32)
    column = lax.broadcasted_iota(jnp.int32, gates.shape, 1)
    for mat, to in ((weight, core), (other, 1 - core)):
        scale = jnp.sum(jnp.where(column == me - core + to, gates, 0.0), axis=1, keepdims=True)
        product = lax.dot_general(
            stacked, mat[...], (((1,), (1,)), ((), ())), preferred_element_type=jnp.float32
        )
        scaled = (product * scale).astype(jnp.bfloat16)
        for j, out in enumerate(outs):
            out[to] = scaled[j * tokens : (j + 1) * tokens]


def products(pieces, weight, other):
    hidden, depth = weight.shape
    paired = [isinstance(p, tuple) for p in pieces]
    operands = [x for p in pieces for x in (p if isinstance(p, tuple) else (p,))]
    tokens = operands[0].shape[0]
    total = len(pieces) * tokens
    return pl.pallas_call(
        functools.partial(products_kernel, paired),
        out_shape=[jax.ShapeDtypeStruct((CORES, tokens, hidden), jnp.bfloat16)] * len(pieces),
        compiler_params=pltpu.CompilerParams(vmem_limit_bytes=16 << 20),
        cost_estimate=pl.CostEstimate(
            flops=20 * CORES * total * hidden * depth,
            bytes_accessed=2 * (total * (2 * hidden + depth) + 2 * hidden * depth),
            transcendentals=0,
        ),
    )(weight, other, *operands)


def pick_kernel(ids, *refs):
    blocks, out = refs[:-1], refs[-1]
    experts, tokens, _ = blocks[0].shape
    top = ids.shape[0]
    span = 16
    chip = lax.div(lax.axis_index("expert"), CORES)
    label = (lax.div(ids[...], CORES) ^ chip) * CORES + lax.rem(ids[...], CORES)
    column = lax.broadcasted_iota(jnp.int32, (top, len(blocks) * experts * span), 1)
    for g in range(tokens // span):
        stacked = jnp.concatenate(
            [b[c, g * span : (g + 1) * span, :] for b in blocks for c in range(experts)], axis=0
        )
        picks = [
            jnp.where(column == label[:, g * span + t : g * span + t + 1] * span + t, 1.0, 0.0)
            for t in range(span)
        ]
        pick = jnp.concatenate(picks, axis=0).astype(jnp.bfloat16)
        rows = jnp.dot(pick, stacked, preferred_element_type=jnp.float32)
        out[g * span * top : (g + 1) * span * top, :] = rows.astype(jnp.bfloat16)


def pick_routes(ids, blocks):
    top, tokens = ids.shape
    return pl.pallas_call(
        pick_kernel,
        out_shape=jax.ShapeDtypeStruct((top * tokens, blocks[0].shape[2]), jnp.bfloat16),
        compiler_params=pltpu.CompilerParams(vmem_limit_bytes=16 << 20),
    )(ids, *blocks)


def dense_device(upstream, route_ids, route_gates, weight_mat):
    tokens, top = route_ids.shape
    owners = lax.axis_size("expert")
    tie = lax.optimization_barrier

    def work(*pieces):
        return products(list(pieces), weight_mat, other_mat)

    rows = send_across(upstream, owners, 0)
    far = send_across(upstream, owners, Z_FAR)
    other_mat = send(weight_mat, owners, 0, 1)
    columns = gate_columns(route_ids.T, route_gates.T, weight_mat)
    far_columns = send(columns, owners, Z_FAR)
    rows, columns, other_mat = tie((rows, columns, other_mat))
    rows = widened(rows, columns)
    near = send(rows, owners, Z_NEAR)
    side = send(rows, owners, X)
    far, far_columns, rows = tie((far, far_columns, rows))
    far = widened(far, far_columns)
    cross = send(far, owners, Z_NEAR)
    (out_far,) = work(far)
    back_far = send(out_far, owners, Z_FAR)
    far_side = send(tie((far, out_far))[0], owners, X)
    near, side, _ = tie((near, side, out_far))
    out_side, out_near = work(side, near)
    cross, near, _ = tie((cross, near, out_side))
    cross_side = send(cross, owners, X)
    near_side = send(near, owners, X)
    (out_cross,) = work(cross)
    back_cross = send(out_cross, owners, Z_NEAR ^ Z_FAR)
    far_side, back_far, out_side, out_near, _ = tie(
        (far_side, back_far, out_side, out_near, out_cross)
    )
    back_side = send(out_side, owners, X)
    back_near = send(out_near, owners, Z_NEAR)
    (out_far_side,) = work(far_side)
    back_far_side = send(out_far_side, owners, X ^ Z_FAR)
    cross_side, _ = tie((cross_side, out_far_side))
    (out_cross_side,) = work(cross_side)
    near_side, back_side, _ = tie((near_side, back_side, out_cross_side))
    (out_near_side,) = work(near_side)
    back_cross_side = send(out_cross_side, owners, X ^ Z_NEAR ^ Z_FAR)
    back_near_side = send(out_near_side, owners, X ^ Z_NEAR)
    rows, _ = tie((rows, out_near_side))
    (out_own,) = work(rows)
    received = {
        0: out_own,
        X: back_side,
        Z_NEAR: back_near,
        X ^ Z_NEAR: back_near_side,
        Z_FAR: back_far,
        X ^ Z_FAR: back_far_side,
        Z_NEAR ^ Z_FAR: back_cross,
        X ^ Z_NEAR ^ Z_FAR: back_cross_side,
    }
    out = pick_routes(route_ids.T, [received[flip] for flip in sorted(received)])
    return out.reshape(1, tokens, top, weight_mat.shape[0])


def slotted_device(section_grad, route_ids, route_gates, weight_mat, capacity):
    tokens, top = route_ids.shape
    owners = lax.axis_size("expert")
    ids = jnp.arange(owners, dtype=jnp.int32)
    slots = jnp.arange(capacity, dtype=jnp.int32)
    matched = (route_ids[:, :, None] == ids[None, None, :]).astype(jnp.int32)
    hits = jnp.sum(matched, axis=1)
    rank = jnp.cumsum(hits, axis=0) - hits
    position = route_ids * capacity + jnp.sum(matched * rank[:, None, :], axis=2)
    gate_owner = jnp.einsum(
        "tk,tke->te", route_gates.astype(jnp.float32), matched.astype(jnp.float32)
    )
    slot_pick = (hits[:, :, None] == 1) & (rank[:, :, None] == slots[None, None, :])
    send_rows = jnp.einsum(
        "tem,td->emd",
        slot_pick.astype(jnp.bfloat16),
        section_grad,
        preferred_element_type=jnp.float32,
    ).astype(jnp.bfloat16)
    send_gates = jnp.einsum("tem,te->em", slot_pick.astype(jnp.float32), gate_owner).astype(
        jnp.bfloat16
    )
    got_rows = lax.all_to_all(send_rows, "expert", split_axis=0, concat_axis=0, tiled=True)
    got_gates = lax.all_to_all(send_gates, "expert", split_axis=0, concat_axis=0, tiled=True)
    product = lax.dot_general(
        got_rows.reshape(owners * capacity, got_rows.shape[2]),
        weight_mat,
        (((1,), (1,)), ((), ())),
        preferred_element_type=jnp.float32,
    ).reshape(owners, capacity, weight_mat.shape[0])
    returned = lax.all_to_all(
        (product * got_gates.astype(jnp.float32)[:, :, None]).astype(jnp.bfloat16),
        "expert",
        split_axis=0,
        concat_axis=0,
        tiled=True,
    )
    flat = returned.reshape(owners * capacity, returned.shape[2])
    out = jnp.take(flat, position.reshape(tokens * top), axis=0)
    return out.reshape(1, tokens, top, returned.shape[2])


def per_device(upstream, expert_ids, gate_weights, expert_weight):
    route_ids = expert_ids[0]
    route_gates = gate_weights[0]
    weight_mat = expert_weight[0, 0]
    tokens, top = route_ids.shape
    owners = lax.axis_size("expert")
    capacity = 2 * tokens * top // owners
    if capacity >= tokens and owners == CORES * 2 * Z_FAR:
        return dense_device(upstream[0], route_ids, route_gates, weight_mat)
    section_grad = shifted(upstream, "pipe", -1)[0]
    return slotted_device(section_grad, route_ids, route_gates, weight_mat, capacity)


def solution(mesh):
    in_specs = (
        P("pipe", "expert", None),
        P("pipe", "expert", None),
        P("pipe", "expert", None),
        P("pipe", "expert", None, None),
    )
    out_specs = P("pipe", "expert", None, None)
    return jax.shard_map(
        per_device, mesh=mesh, in_specs=in_specs, out_specs=out_specs, check_vma=False
    )
```

```python
import functools

import jax
import jax.numpy as jnp
from jax import lax
from jax.experimental import pallas as pl
from jax.experimental.pallas import tpu as pltpu
from jax.sharding import PartitionSpec as P

CORES = 2
X, Z_NEAR, Z_FAR = 1, 2, 4
LANES = 128


def shifted(block, axis, distance):
    devices = range(lax.axis_size(axis))
    route = [((i - distance) % len(devices), i) for i in devices]
    return lax.ppermute(block, axis, route)


def send(block, owners, flip, core=0):
    route = [(i, ((i // CORES) ^ flip) * CORES + ((i % CORES) ^ core)) for i in range(owners)]
    return lax.ppermute(block, "expert", route)


def send_across(block, owners, flip):
    sections = lax.axis_size("pipe")
    route = []
    for s in range(sections):
        for i in range(owners):
            target = ((i // CORES) ^ flip) * CORES + i % CORES
            route.append((s * owners + i, (s - 1) % sections * owners + target))
    return lax.ppermute(block, ("pipe", "expert"), route)


def gates_kernel(ids, gates, weight, out):
    top, tokens = ids.shape
    expert = lax.broadcasted_iota(jnp.int32, (LANES, tokens), 0)
    total = jnp.zeros((LANES, tokens), jnp.float32)
    for k in range(top):
        gate = gates[k : k + 1, :].astype(jnp.float32)
        total += jnp.where(expert == ids[k : k + 1, :], gate, 0.0)
    out[...] = total.T.astype(jnp.bfloat16)


def gate_columns(ids, gates, weight):
    return pl.pallas_call(
        gates_kernel,
        out_shape=jax.ShapeDtypeStruct((ids.shape[1], LANES), jnp.bfloat16),
        compiler_params=pltpu.CompilerParams(vmem_limit_bytes=16 << 20),
    )(ids, gates, weight)


def widen_kernel(rows, columns, out):
    depth = rows.shape[1]
    out[:, :depth] = rows[...]
    out[:, depth:] = columns[...]


def widened(rows, columns):
    width = rows.shape[1] + columns.shape[1]
    return pl.pallas_call(
        widen_kernel,
        out_shape=jax.ShapeDtypeStruct((rows.shape[0], width), jnp.bfloat16),
        compiler_params=pltpu.CompilerParams(vmem_limit_bytes=16 << 20),
    )(rows, columns)


def products_kernel(paired, weight, other, *refs):
    hidden, depth = weight.shape
    rows, gates, at = [], [], 0
    for pair in paired:
        rows.append(refs[at][:, :depth])
        gates.append(refs[at + 1][...] if pair else refs[at][:, depth:])
        at += 1 + pair
    outs = refs[at:]
    tokens = outs[0].shape[1]
    me = lax.axis_index("expert")
    core = lax.rem(me, CORES)
    stacked = jnp.concatenate(rows, axis=0)
    gates = jnp.concatenate(gates, axis=0).astype(jnp.float32)
    column = lax.broadcasted_iota(jnp.int32, gates.shape, 1)
    for mat, to in ((weight, core), (other, 1 - core)):
        scale = jnp.sum(jnp.where(column == me - core + to, gates, 0.0), axis=1, keepdims=True)
        product = lax.dot_general(
            stacked, mat[...], (((1,), (1,)), ((), ())), preferred_element_type=jnp.float32
        )
        scaled = (product * scale).astype(jnp.bfloat16)
        for j, out in enumerate(outs):
            out[to] = scaled[j * tokens : (j + 1) * tokens]


def products(pieces, weight, other):
    hidden, depth = weight.shape
    paired = [isinstance(p, tuple) for p in pieces]
    operands = [x for p in pieces for x in (p if isinstance(p, tuple) else (p,))]
    tokens = operands[0].shape[0]
    total = len(pieces) * tokens
    return pl.pallas_call(
        functools.partial(products_kernel, paired),
        out_shape=[jax.ShapeDtypeStruct((CORES, tokens, hidden), jnp.bfloat16)] * len(pieces),
        compiler_params=pltpu.CompilerParams(vmem_limit_bytes=16 << 20),
        cost_estimate=pl.CostEstimate(
            flops=20 * CORES * total * hidden * depth,
            bytes_accessed=2 * (total * (2 * hidden + depth) + 2 * hidden * depth),
            transcendentals=0,
        ),
    )(weight, other, *operands)


def pick_kernel(ids, *refs):
    blocks, out = refs[:-1], refs[-1]
    experts, tokens, _ = blocks[0].shape
    top = ids.shape[0]
    span = 16
    chip = lax.div(lax.axis_index("expert"), CORES)
    label = (lax.div(ids[...], CORES) ^ chip) * CORES + lax.rem(ids[...], CORES)
    column = lax.broadcasted_iota(jnp.int32, (top, len(blocks) * experts * span), 1)
    for g in range(tokens // span):
        stacked = jnp.concatenate(
            [b[c, g * span : (g + 1) * span, :] for b in blocks for c in range(experts)], axis=0
        )
        picks = [
            jnp.where(column == label[:, g * span + t : g * span + t + 1] * span + t, 1.0, 0.0)
            for t in range(span)
        ]
        pick = jnp.concatenate(picks, axis=0).astype(jnp.bfloat16)
        rows = jnp.dot(pick, stacked, preferred_element_type=jnp.float32)
        out[g * span * top : (g + 1) * span * top, :] = rows.astype(jnp.bfloat16)


def pick_routes(ids, blocks):
    top, tokens = ids.shape
    return pl.pallas_call(
        pick_kernel,
        out_shape=jax.ShapeDtypeStruct((top * tokens, blocks[0].shape[2]), jnp.bfloat16),
        compiler_params=pltpu.CompilerParams(vmem_limit_bytes=16 << 20),
    )(ids, *blocks)


def dense_device(upstream, route_ids, route_gates, weight_mat):
    tokens, top = route_ids.shape
    owners = lax.axis_size("expert")
    tie = lax.optimization_barrier

    def work(*pieces):
        return products(list(pieces), weight_mat, other_mat)

    far = send_across(upstream, owners, Z_FAR)
    rows = send_across(upstream, owners, 0)
    other_mat = send(weight_mat, owners, 0, 1)
    columns = gate_columns(route_ids.T, route_gates.T, weight_mat)
    far_columns = send(columns, owners, Z_FAR)
    far, far_columns, other_mat = tie((far, far_columns, other_mat))
    far = widened(far, far_columns)
    cross = send(far, owners, Z_NEAR)
    far_side = send(far, owners, X)
    (out_far,) = work(far)
    back_far = send(out_far, owners, Z_FAR)
    rows, columns, _ = tie((rows, columns, out_far))
    rows = widened(rows, columns)
    near = send(rows, owners, Z_NEAR)
    side = send(rows, owners, X)
    cross, rows = tie((cross, rows))
    cross_side = send(cross, owners, X)
    (out_cross,) = work(cross)
    back_cross = send(out_cross, owners, Z_NEAR ^ Z_FAR)
    far_side, back_far, _ = tie((far_side, back_far, out_cross))
    (out_far_side,) = work(far_side)
    back_far_side = send(out_far_side, owners, X ^ Z_FAR)
    near, cross_side, _ = tie((near, cross_side, out_far_side))
    near_side = send(near, owners, X)
    (out_cross_side,) = work(cross_side)
    back_cross_side = send(out_cross_side, owners, X ^ Z_NEAR ^ Z_FAR)
    side, near, _ = tie((side, near, out_cross_side))
    out_side, out_near = work(side, near)
    back_side = send(out_side, owners, X)
    back_near = send(out_near, owners, Z_NEAR)
    near_side, _ = tie((near_side, out_near))
    (out_near_side,) = work(near_side)
    back_near_side = send(out_near_side, owners, X ^ Z_NEAR)
    rows, _ = tie((rows, out_near_side))
    (out_own,) = work(rows)
    received = {
        0: out_own,
        X: back_side,
        Z_NEAR: back_near,
        X ^ Z_NEAR: back_near_side,
        Z_FAR: back_far,
        X ^ Z_FAR: back_far_side,
        Z_NEAR ^ Z_FAR: back_cross,
        X ^ Z_NEAR ^ Z_FAR: back_cross_side,
    }
    out = pick_routes(route_ids.T, [received[flip] for flip in sorted(received)])
    return out.reshape(1, tokens, top, weight_mat.shape[0])


def slotted_device(section_grad, route_ids, route_gates, weight_mat, capacity):
    tokens, top = route_ids.shape
    owners = lax.axis_size("expert")
    ids = jnp.arange(owners, dtype=jnp.int32)
    slots = jnp.arange(capacity, dtype=jnp.int32)
    matched = (route_ids[:, :, None] == ids[None, None, :]).astype(jnp.int32)
    hits = jnp.sum(matched, axis=1)
    rank = jnp.cumsum(hits, axis=0) - hits
    position = route_ids * capacity + jnp.sum(matched * rank[:, None, :], axis=2)
    gate_owner = jnp.einsum(
        "tk,tke->te", route_gates.astype(jnp.float32), matched.astype(jnp.float32)
    )
    slot_pick = (hits[:, :, None] == 1) & (rank[:, :, None] == slots[None, None, :])
    send_rows = jnp.einsum(
        "tem,td->emd",
        slot_pick.astype(jnp.bfloat16),
        section_grad,
        preferred_element_type=jnp.float32,
    ).astype(jnp.bfloat16)
    send_gates = jnp.einsum("tem,te->em", slot_pick.astype(jnp.float32), gate_owner).astype(
        jnp.bfloat16
    )
    got_rows = lax.all_to_all(send_rows, "expert", split_axis=0, concat_axis=0, tiled=True)
    got_gates = lax.all_to_all(send_gates, "expert", split_axis=0, concat_axis=0, tiled=True)
    product = lax.dot_general(
        got_rows.reshape(owners * capacity, got_rows.shape[2]),
        weight_mat,
        (((1,), (1,)), ((), ())),
        preferred_element_type=jnp.float32,
    ).reshape(owners, capacity, weight_mat.shape[0])
    returned = lax.all_to_all(
        (product * got_gates.astype(jnp.float32)[:, :, None]).astype(jnp.bfloat16),
        "expert",
        split_axis=0,
        concat_axis=0,
        tiled=True,
    )
    flat = returned.reshape(owners * capacity, returned.shape[2])
    out = jnp.take(flat, position.reshape(tokens * top), axis=0)
    return out.reshape(1, tokens, top, returned.shape[2])


def per_device(upstream, expert_ids, gate_weights, expert_weight):
    route_ids = expert_ids[0]
    route_gates = gate_weights[0]
    weight_mat = expert_weight[0, 0]
    tokens, top = route_ids.shape
    owners = lax.axis_size("expert")
    capacity = 2 * tokens * top // owners
    if capacity >= tokens and owners == CORES * 2 * Z_FAR:
        return dense_device(upstream[0], route_ids, route_gates, weight_mat)
    section_grad = shifted(upstream, "pipe", -1)[0]
    return slotted_device(section_grad, route_ids, route_gates, weight_mat, capacity)


def solution(mesh):
    in_specs = (
        P("pipe", "expert", None),
        P("pipe", "expert", None),
        P("pipe", "expert", None),
        P("pipe", "expert", None, None),
    )
    out_specs = P("pipe", "expert", None, None)
    return jax.shard_map(
        per_device, mesh=mesh, in_specs=in_specs, out_specs=out_specs, check_vma=False
    )
```

```python
import functools

import jax
import jax.numpy as jnp
from jax import lax
from jax.experimental import pallas as pl
from jax.experimental.pallas import tpu as pltpu
from jax.sharding import PartitionSpec as P

CORES = 2
X, Z_NEAR, Z_FAR = 1, 2, 4
LANES = 128


def shifted(block, axis, distance):
    devices = range(lax.axis_size(axis))
    route = [((i - distance) % len(devices), i) for i in devices]
    return lax.ppermute(block, axis, route)


def send(block, owners, flip, core=0):
    route = [(i, ((i // CORES) ^ flip) * CORES + ((i % CORES) ^ core)) for i in range(owners)]
    return lax.ppermute(block, "expert", route)


def send_across(block, owners, flip):
    sections = lax.axis_size("pipe")
    route = []
    for s in range(sections):
        for i in range(owners):
            target = ((i // CORES) ^ flip) * CORES + i % CORES
            route.append((s * owners + i, (s - 1) % sections * owners + target))
    return lax.ppermute(block, ("pipe", "expert"), route)


def gates_kernel(ids, gates, weight, out):
    top, tokens = ids.shape
    expert = lax.broadcasted_iota(jnp.int32, (LANES, tokens), 0)
    total = jnp.zeros((LANES, tokens), jnp.float32)
    for k in range(top):
        gate = gates[k : k + 1, :].astype(jnp.float32)
        total += jnp.where(expert == ids[k : k + 1, :], gate, 0.0)
    out[...] = total.T.astype(jnp.bfloat16)


def gate_columns(ids, gates, weight):
    return pl.pallas_call(
        gates_kernel,
        out_shape=jax.ShapeDtypeStruct((ids.shape[1], LANES), jnp.bfloat16),
        compiler_params=pltpu.CompilerParams(vmem_limit_bytes=16 << 20),
    )(ids, gates, weight)


def widen_kernel(rows, columns, out):
    depth = rows.shape[1]
    out[:, :depth] = rows[...]
    out[:, depth:] = columns[...]


def widened(rows, columns):
    width = rows.shape[1] + columns.shape[1]
    return pl.pallas_call(
        widen_kernel,
        out_shape=jax.ShapeDtypeStruct((rows.shape[0], width), jnp.bfloat16),
        compiler_params=pltpu.CompilerParams(vmem_limit_bytes=16 << 20),
    )(rows, columns)


def products_kernel(paired, weight, other, *refs):
    hidden, depth = weight.shape
    rows, gates, at = [], [], 0
    for pair in paired:
        rows.append(refs[at][:, :depth])
        gates.append(refs[at + 1][...] if pair else refs[at][:, depth:])
        at += 1 + pair
    outs = refs[at:]
    tokens = outs[0].shape[1]
    me = lax.axis_index("expert")
    core = lax.rem(me, CORES)
    stacked = jnp.concatenate(rows, axis=0)
    gates = jnp.concatenate(gates, axis=0).astype(jnp.float32)
    column = lax.broadcasted_iota(jnp.int32, gates.shape, 1)
    for mat, to in ((weight, core), (other, 1 - core)):
        scale = jnp.sum(jnp.where(column == me - core + to, gates, 0.0), axis=1, keepdims=True)
        product = lax.dot_general(
            stacked, mat[...], (((1,), (1,)), ((), ())), preferred_element_type=jnp.float32
        )
        scaled = (product * scale).astype(jnp.bfloat16)
        for j, out in enumerate(outs):
            out[to] = scaled[j * tokens : (j + 1) * tokens]


def products(pieces, weight, other):
    hidden, depth = weight.shape
    paired = [isinstance(p, tuple) for p in pieces]
    operands = [x for p in pieces for x in (p if isinstance(p, tuple) else (p,))]
    tokens = operands[0].shape[0]
    total = len(pieces) * tokens
    return pl.pallas_call(
        functools.partial(products_kernel, paired),
        out_shape=[jax.ShapeDtypeStruct((CORES, tokens, hidden), jnp.bfloat16)] * len(pieces),
        compiler_params=pltpu.CompilerParams(vmem_limit_bytes=16 << 20),
        cost_estimate=pl.CostEstimate(
            flops=20 * CORES * total * hidden * depth,
            bytes_accessed=2 * (total * (2 * hidden + depth) + 2 * hidden * depth),
            transcendentals=0,
        ),
    )(weight, other, *operands)


def pick_kernel(flips, ids, *refs):
    blocks, kept, out = refs[: len(flips)], refs[len(flips) : -1], refs[-1]
    experts, tokens, _ = blocks[0].shape
    top = ids.shape[0]
    span = 16
    chip = lax.div(lax.axis_index("expert"), CORES)
    flip = lax.div(ids[...], CORES) ^ chip
    place = jnp.full(flip.shape, -1, jnp.int32)
    for j, known in enumerate(flips):
        place = jnp.where(flip == known, j * CORES + lax.rem(ids[...], CORES), place)
    column = lax.broadcasted_iota(jnp.int32, (top, len(blocks) * experts * span), 1)
    for g in range(tokens // span):
        stacked = jnp.concatenate(
            [b[c, g * span : (g + 1) * span, :] for b in blocks for c in range(experts)], axis=0
        )
        picks = [
            jnp.where(column == place[:, g * span + t : g * span + t + 1] * span + t, 1.0, 0.0)
            for t in range(span)
        ]
        pick = jnp.concatenate(picks, axis=0).astype(jnp.bfloat16)
        rows = jnp.dot(pick, stacked, preferred_element_type=jnp.float32).astype(jnp.bfloat16)
        part = slice(g * span * top, (g + 1) * span * top)
        out[part, :] = rows + kept[0][part, :] if kept else rows


def pick_routes(ids, received, *kept):
    top, tokens = ids.shape
    flips = sorted(received)
    blocks = [received[flip] for flip in flips]
    return pl.pallas_call(
        functools.partial(pick_kernel, flips),
        out_shape=jax.ShapeDtypeStruct((top * tokens, blocks[0].shape[2]), jnp.bfloat16),
        compiler_params=pltpu.CompilerParams(vmem_limit_bytes=16 << 20),
    )(ids, *blocks, *kept)


def dense_device(upstream, route_ids, route_gates, weight_mat):
    tokens, top = route_ids.shape
    owners = lax.axis_size("expert")
    tie = lax.optimization_barrier

    def work(*pieces):
        return products(list(pieces), weight_mat, other_mat)

    far = send_across(upstream, owners, Z_FAR)
    rows = send_across(upstream, owners, 0)
    other_mat = send(weight_mat, owners, 0, 1)
    columns = gate_columns(route_ids.T, route_gates.T, weight_mat)
    far_columns = send(columns, owners, Z_FAR)
    far, far_columns, other_mat = tie((far, far_columns, other_mat))
    far = widened(far, far_columns)
    cross = send(far, owners, Z_NEAR)
    far_side = send(far, owners, X)
    (out_far,) = work(far)
    back_far = send(out_far, owners, Z_FAR)
    rows, columns, _ = tie((rows, columns, out_far))
    rows = widened(rows, columns)
    near = send(rows, owners, Z_NEAR)
    cross, rows = tie((cross, rows))
    cross_side = send(cross, owners, X)
    far_side, _ = tie((far_side, cross))
    out_cross, out_far_side = work(cross, far_side)
    back_cross = send(out_cross, owners, Z_NEAR ^ Z_FAR)
    back_far_side = send(out_far_side, owners, X ^ Z_FAR)
    near, _ = tie((near, out_cross))
    near_side = send(near, owners, X)
    side = send(tie((rows, near))[0], owners, X)
    cross_side, back_far, _ = tie((cross_side, back_far, near))
    (out_cross_side,) = work(cross_side)
    back_cross_side = send(out_cross_side, owners, X ^ Z_NEAR ^ Z_FAR)
    rows, _ = tie((rows, out_cross_side))
    (out_own,) = work(rows)
    side, near, near_side, _ = tie((side, near, near_side, out_own))
    out_side, out_near, out_near_side = work(side, near, near_side)
    back_side = send(out_side, owners, X)
    back_near = send(out_near, owners, Z_NEAR)
    back_near_side = send(out_near_side, owners, X ^ Z_NEAR)
    far_parts = {
        0: out_own,
        Z_FAR: back_far,
        X ^ Z_FAR: back_far_side,
        Z_NEAR ^ Z_FAR: back_cross,
        X ^ Z_NEAR ^ Z_FAR: back_cross_side,
    }
    near_parts = {X: back_side, Z_NEAR: back_near, X ^ Z_NEAR: back_near_side}
    out = pick_routes(route_ids.T, near_parts, pick_routes(route_ids.T, far_parts))
    return out.reshape(1, tokens, top, weight_mat.shape[0])


def slotted_device(section_grad, route_ids, route_gates, weight_mat, capacity):
    tokens, top = route_ids.shape
    owners = lax.axis_size("expert")
    ids = jnp.arange(owners, dtype=jnp.int32)
    slots = jnp.arange(capacity, dtype=jnp.int32)
    matched = (route_ids[:, :, None] == ids[None, None, :]).astype(jnp.int32)
    hits = jnp.sum(matched, axis=1)
    rank = jnp.cumsum(hits, axis=0) - hits
    position = route_ids * capacity + jnp.sum(matched * rank[:, None, :], axis=2)
    gate_owner = jnp.einsum(
        "tk,tke->te", route_gates.astype(jnp.float32), matched.astype(jnp.float32)
    )
    slot_pick = (hits[:, :, None] == 1) & (rank[:, :, None] == slots[None, None, :])
    send_rows = jnp.einsum(
        "tem,td->emd",
        slot_pick.astype(jnp.bfloat16),
        section_grad,
        preferred_element_type=jnp.float32,
    ).astype(jnp.bfloat16)
    send_gates = jnp.einsum("tem,te->em", slot_pick.astype(jnp.float32), gate_owner).astype(
        jnp.bfloat16
    )
    got_rows = lax.all_to_all(send_rows, "expert", split_axis=0, concat_axis=0, tiled=True)
    got_gates = lax.all_to_all(send_gates, "expert", split_axis=0, concat_axis=0, tiled=True)
    product = lax.dot_general(
        got_rows.reshape(owners * capacity, got_rows.shape[2]),
        weight_mat,
        (((1,), (1,)), ((), ())),
        preferred_element_type=jnp.float32,
    ).reshape(owners, capacity, weight_mat.shape[0])
    returned = lax.all_to_all(
        (product * got_gates.astype(jnp.float32)[:, :, None]).astype(jnp.bfloat16),
        "expert",
        split_axis=0,
        concat_axis=0,
        tiled=True,
    )
    flat = returned.reshape(owners * capacity, returned.shape[2])
    out = jnp.take(flat, position.reshape(tokens * top), axis=0)
    return out.reshape(1, tokens, top, returned.shape[2])


def per_device(upstream, expert_ids, gate_weights, expert_weight):
    route_ids = expert_ids[0]
    route_gates = gate_weights[0]
    weight_mat = expert_weight[0, 0]
    tokens, top = route_ids.shape
    owners = lax.axis_size("expert")
    capacity = 2 * tokens * top // owners
    if capacity >= tokens and owners == CORES * 2 * Z_FAR:
        return dense_device(upstream[0], route_ids, route_gates, weight_mat)
    section_grad = shifted(upstream, "pipe", -1)[0]
    return slotted_device(section_grad, route_ids, route_gates, weight_mat, capacity)


def solution(mesh):
    in_specs = (
        P("pipe", "expert", None),
        P("pipe", "expert", None),
        P("pipe", "expert", None),
        P("pipe", "expert", None, None),
    )
    out_specs = P("pipe", "expert", None, None)
    return jax.shard_map(
        per_device, mesh=mesh, in_specs=in_specs, out_specs=out_specs, check_vma=False
    )
```

```python
import functools

import jax
import jax.numpy as jnp
from jax import lax
from jax.experimental import pallas as pl
from jax.experimental.pallas import tpu as pltpu
from jax.sharding import PartitionSpec as P

CORES = 2
X, Z_NEAR, Z_FAR = 1, 2, 4
LANES = 128


def shifted(block, axis, distance):
    devices = range(lax.axis_size(axis))
    route = [((i - distance) % len(devices), i) for i in devices]
    return lax.ppermute(block, axis, route)


def send(block, owners, flip, core=0):
    route = [(i, ((i // CORES) ^ flip) * CORES + ((i % CORES) ^ core)) for i in range(owners)]
    return lax.ppermute(block, "expert", route)


def send_across(block, owners, flip):
    sections = lax.axis_size("pipe")
    route = []
    for s in range(sections):
        for i in range(owners):
            target = ((i // CORES) ^ flip) * CORES + i % CORES
            route.append((s * owners + i, (s - 1) % sections * owners + target))
    return lax.ppermute(block, ("pipe", "expert"), route)


def gates_kernel(ids, gates, weight, out):
    top, tokens = ids.shape
    expert = lax.broadcasted_iota(jnp.int32, (LANES, tokens), 0)
    total = jnp.zeros((LANES, tokens), jnp.float32)
    for k in range(top):
        gate = gates[k : k + 1, :].astype(jnp.float32)
        total += jnp.where(expert == ids[k : k + 1, :], gate, 0.0)
    out[...] = total.T.astype(jnp.bfloat16)


def gate_columns(ids, gates, weight):
    return pl.pallas_call(
        gates_kernel,
        out_shape=jax.ShapeDtypeStruct((ids.shape[1], LANES), jnp.bfloat16),
        compiler_params=pltpu.CompilerParams(vmem_limit_bytes=16 << 20),
    )(ids, gates, weight)


def widen_kernel(rows, columns, out):
    depth = rows.shape[1]
    out[:, :depth] = rows[...]
    out[:, depth:] = columns[...]


def widened(rows, columns):
    width = rows.shape[1] + columns.shape[1]
    return pl.pallas_call(
        widen_kernel,
        out_shape=jax.ShapeDtypeStruct((rows.shape[0], width), jnp.bfloat16),
        compiler_params=pltpu.CompilerParams(vmem_limit_bytes=16 << 20),
    )(rows, columns)


def products_kernel(count, stack, weight, other, *refs):
    hidden, depth = weight.shape
    pieces, outs = refs[:count], refs[count + stack :]
    tokens = outs[0].shape[1]
    me = lax.axis_index("expert")
    core = lax.rem(me, CORES)
    stacked = jnp.concatenate([p[...] for p in pieces], axis=0)
    if stack:
        refs[count][...] = stacked
    gates = stacked[:, depth:].astype(jnp.float32)
    column = lax.broadcasted_iota(jnp.int32, gates.shape, 1)
    for mat, to in ((weight, core), (other, 1 - core)):
        scale = jnp.sum(jnp.where(column == me - core + to, gates, 0.0), axis=1, keepdims=True)
        product = lax.dot_general(
            stacked[:, :depth],
            mat[...],
            (((1,), (1,)), ((), ())),
            preferred_element_type=jnp.float32,
        )
        scaled = (product * scale).astype(jnp.bfloat16)
        for j, out in enumerate(outs):
            out[to] = scaled[j * tokens : (j + 1) * tokens]


def products(pieces, tokens, weight, other, stack=False):
    hidden, depth = weight.shape
    total = sum(p.shape[0] for p in pieces)
    one = jax.ShapeDtypeStruct((CORES, tokens, hidden), jnp.bfloat16)
    both = jax.ShapeDtypeStruct((total, pieces[0].shape[1]), jnp.bfloat16)
    return pl.pallas_call(
        functools.partial(products_kernel, len(pieces), int(stack)),
        out_shape=[both] * int(stack) + [one] * (total // tokens),
        compiler_params=pltpu.CompilerParams(vmem_limit_bytes=16 << 20),
        cost_estimate=pl.CostEstimate(
            flops=20 * CORES * total * hidden * depth,
            bytes_accessed=2 * (total * (2 * hidden + depth) + 2 * hidden * depth),
            transcendentals=0,
        ),
    )(weight, other, *pieces)


def pick_kernel(flips, ids, *refs):
    blocks, kept, out = refs[: len(flips)], refs[len(flips) : -1], refs[-1]
    experts, tokens, _ = blocks[0].shape
    top = ids.shape[0]
    span = 16
    chip = lax.div(lax.axis_index("expert"), CORES)
    flip = lax.div(ids[...], CORES) ^ chip
    place = jnp.full(flip.shape, -1, jnp.int32)
    for j, known in enumerate(flips):
        place = jnp.where(flip == known, j * CORES + lax.rem(ids[...], CORES), place)
    column = lax.broadcasted_iota(jnp.int32, (top, len(blocks) * experts * span), 1)
    for g in range(tokens // span):
        stacked = jnp.concatenate(
            [b[c, g * span : (g + 1) * span, :] for b in blocks for c in range(experts)], axis=0
        )
        picks = [
            jnp.where(column == place[:, g * span + t : g * span + t + 1] * span + t, 1.0, 0.0)
            for t in range(span)
        ]
        pick = jnp.concatenate(picks, axis=0).astype(jnp.bfloat16)
        rows = jnp.dot(pick, stacked, preferred_element_type=jnp.float32).astype(jnp.bfloat16)
        part = slice(g * span * top, (g + 1) * span * top)
        out[part, :] = rows + kept[0][part, :] if kept else rows


def pick_routes(ids, received, *kept):
    top, tokens = ids.shape
    flips = sorted(received)
    blocks = [received[flip] for flip in flips]
    return pl.pallas_call(
        functools.partial(pick_kernel, flips),
        out_shape=jax.ShapeDtypeStruct((top * tokens, blocks[0].shape[2]), jnp.bfloat16),
        compiler_params=pltpu.CompilerParams(vmem_limit_bytes=16 << 20),
    )(ids, *blocks, *kept)


def dense_device(upstream, route_ids, route_gates, weight_mat):
    tokens, top = route_ids.shape
    owners = lax.axis_size("expert")
    tie = lax.optimization_barrier

    def work(*pieces, stack=False):
        return products(list(pieces), tokens, weight_mat, other_mat, stack)

    rows = send_across(upstream, owners, 0)
    far = send_across(upstream, owners, Z_FAR)
    other_mat = send(weight_mat, owners, 0, 1)
    columns = gate_columns(route_ids.T, route_gates.T, weight_mat)
    far_columns = send(columns, owners, Z_FAR)
    rows, columns = tie((rows, columns))
    rows = widened(rows, columns)
    side = send(rows, owners, X)
    far, far_columns, rows, other_mat = tie((far, far_columns, rows, other_mat))
    far = widened(far, far_columns)
    cross = send(far, owners, Z_NEAR)
    far_side = send(far, owners, X)
    (out_far,) = work(far)
    back_far = send(out_far, owners, Z_FAR)
    side, rows, _ = tie((side, rows, out_far))
    pair, out_own, out_side = work(rows, side, stack=True)
    pair = send(pair, owners, Z_NEAR)
    cross, out_side, _ = tie((cross, out_side, out_own))
    back_side = send(out_side, owners, X)
    cross_side = send(cross, owners, X)
    far_side, _ = tie((far_side, cross))
    out_cross, out_far_side = work(cross, far_side)
    back_cross = send(out_cross, owners, Z_NEAR ^ Z_FAR)
    back_far_side = send(out_far_side, owners, X ^ Z_FAR)
    cross_side, back_far, back_side, _ = tie((cross_side, back_far, back_side, out_cross))
    (out_cross_side,) = work(cross_side)
    back_cross_side = send(out_cross_side, owners, X ^ Z_NEAR ^ Z_FAR)
    pair, _ = tie((pair, out_cross_side))
    out_near, out_near_side = work(pair)
    back_near = send(out_near, owners, Z_NEAR)
    back_near_side = send(out_near_side, owners, X ^ Z_NEAR)
    far_parts = {
        0: out_own,
        Z_FAR: back_far,
        X ^ Z_FAR: back_far_side,
        Z_NEAR ^ Z_FAR: back_cross,
        X ^ Z_NEAR ^ Z_FAR: back_cross_side,
    }
    near_parts = {X: back_side, Z_NEAR: back_near, X ^ Z_NEAR: back_near_side}
    out = pick_routes(route_ids.T, near_parts, pick_routes(route_ids.T, far_parts))
    return out.reshape(1, tokens, top, weight_mat.shape[0])


def slotted_device(section_grad, route_ids, route_gates, weight_mat, capacity):
    tokens, top = route_ids.shape
    owners = lax.axis_size("expert")
    ids = jnp.arange(owners, dtype=jnp.int32)
    slots = jnp.arange(capacity, dtype=jnp.int32)
    matched = (route_ids[:, :, None] == ids[None, None, :]).astype(jnp.int32)
    hits = jnp.sum(matched, axis=1)
    rank = jnp.cumsum(hits, axis=0) - hits
    position = route_ids * capacity + jnp.sum(matched * rank[:, None, :], axis=2)
    gate_owner = jnp.einsum(
        "tk,tke->te", route_gates.astype(jnp.float32), matched.astype(jnp.float32)
    )
    slot_pick = (hits[:, :, None] == 1) & (rank[:, :, None] == slots[None, None, :])
    send_rows = jnp.einsum(
        "tem,td->emd",
        slot_pick.astype(jnp.bfloat16),
        section_grad,
        preferred_element_type=jnp.float32,
    ).astype(jnp.bfloat16)
    send_gates = jnp.einsum("tem,te->em", slot_pick.astype(jnp.float32), gate_owner).astype(
        jnp.bfloat16
    )
    got_rows = lax.all_to_all(send_rows, "expert", split_axis=0, concat_axis=0, tiled=True)
    got_gates = lax.all_to_all(send_gates, "expert", split_axis=0, concat_axis=0, tiled=True)
    product = lax.dot_general(
        got_rows.reshape(owners * capacity, got_rows.shape[2]),
        weight_mat,
        (((1,), (1,)), ((), ())),
        preferred_element_type=jnp.float32,
    ).reshape(owners, capacity, weight_mat.shape[0])
    returned = lax.all_to_all(
        (product * got_gates.astype(jnp.float32)[:, :, None]).astype(jnp.bfloat16),
        "expert",
        split_axis=0,
        concat_axis=0,
        tiled=True,
    )
    flat = returned.reshape(owners * capacity, returned.shape[2])
    out = jnp.take(flat, position.reshape(tokens * top), axis=0)
    return out.reshape(1, tokens, top, returned.shape[2])


def per_device(upstream, expert_ids, gate_weights, expert_weight):
    route_ids = expert_ids[0]
    route_gates = gate_weights[0]
    weight_mat = expert_weight[0, 0]
    tokens, top = route_ids.shape
    owners = lax.axis_size("expert")
    capacity = 2 * tokens * top // owners
    if capacity >= tokens and owners == CORES * 2 * Z_FAR:
        return dense_device(upstream[0], route_ids, route_gates, weight_mat)
    section_grad = shifted(upstream, "pipe", -1)[0]
    return slotted_device(section_grad, route_ids, route_gates, weight_mat, capacity)


def solution(mesh):
    in_specs = (
        P("pipe", "expert", None),
        P("pipe", "expert", None),
        P("pipe", "expert", None),
        P("pipe", "expert", None, None),
    )
    out_specs = P("pipe", "expert", None, None)
    return jax.shard_map(
        per_device, mesh=mesh, in_specs=in_specs, out_specs=out_specs, check_vma=False
    )
```

```python
import functools

import jax
import jax.numpy as jnp
from jax import lax
from jax.experimental import pallas as pl
from jax.experimental.pallas import tpu as pltpu
from jax.sharding import PartitionSpec as P

CORES = 2
X, Z_NEAR, Z_FAR = 1, 2, 4
LANES = 128


def shifted(block, axis, distance):
    devices = range(lax.axis_size(axis))
    route = [((i - distance) % len(devices), i) for i in devices]
    return lax.ppermute(block, axis, route)


def send(block, owners, flip, core=0):
    route = [(i, ((i // CORES) ^ flip) * CORES + ((i % CORES) ^ core)) for i in range(owners)]
    return lax.ppermute(block, "expert", route)


def send_across(block, owners, flip):
    sections = lax.axis_size("pipe")
    route = []
    for s in range(sections):
        for i in range(owners):
            target = ((i // CORES) ^ flip) * CORES + i % CORES
            route.append((s * owners + i, (s - 1) % sections * owners + target))
    return lax.ppermute(block, ("pipe", "expert"), route)


def gates_kernel(ids, gates, weight, out):
    top, tokens = ids.shape
    expert = lax.broadcasted_iota(jnp.int32, (LANES, tokens), 0)
    total = jnp.zeros((LANES, tokens), jnp.float32)
    for k in range(top):
        gate = gates[k : k + 1, :].astype(jnp.float32)
        total += jnp.where(expert == ids[k : k + 1, :], gate, 0.0)
    out[...] = total.T.astype(jnp.bfloat16)


def gate_columns(ids, gates, weight):
    return pl.pallas_call(
        gates_kernel,
        out_shape=jax.ShapeDtypeStruct((ids.shape[1], LANES), jnp.bfloat16),
        compiler_params=pltpu.CompilerParams(vmem_limit_bytes=16 << 20),
    )(ids, gates, weight)


def widen_kernel(rows, columns, out):
    depth = rows.shape[1]
    out[:, :depth] = rows[...]
    out[:, depth:] = columns[...]


def widened(rows, columns):
    width = rows.shape[1] + columns.shape[1]
    return pl.pallas_call(
        widen_kernel,
        out_shape=jax.ShapeDtypeStruct((rows.shape[0], width), jnp.bfloat16),
        compiler_params=pltpu.CompilerParams(vmem_limit_bytes=16 << 20),
    )(rows, columns)


def products_kernel(count, stack, weight, other, *refs):
    hidden, depth = weight.shape
    pieces, outs = refs[:count], refs[count + stack :]
    tokens = outs[0].shape[1]
    me = lax.axis_index("expert")
    core = lax.rem(me, CORES)
    stacked = jnp.concatenate([p[...] for p in pieces], axis=0)
    if stack:
        refs[count][...] = stacked
    gates = stacked[:, depth:].astype(jnp.float32)
    column = lax.broadcasted_iota(jnp.int32, gates.shape, 1)
    for mat, to in ((weight, core), (other, 1 - core)):
        scale = jnp.sum(jnp.where(column == me - core + to, gates, 0.0), axis=1, keepdims=True)
        product = lax.dot_general(
            stacked[:, :depth],
            mat[...],
            (((1,), (1,)), ((), ())),
            preferred_element_type=jnp.float32,
        )
        scaled = (product * scale).astype(jnp.bfloat16)
        for j, out in enumerate(outs):
            out[to] = scaled[j * tokens : (j + 1) * tokens]


def products(pieces, tokens, weight, other, stack=False):
    hidden, depth = weight.shape
    total = sum(p.shape[0] for p in pieces)
    one = jax.ShapeDtypeStruct((CORES, tokens, hidden), jnp.bfloat16)
    both = jax.ShapeDtypeStruct((total, pieces[0].shape[1]), jnp.bfloat16)
    return pl.pallas_call(
        functools.partial(products_kernel, len(pieces), int(stack)),
        out_shape=[both] * int(stack) + [one] * (total // tokens),
        compiler_params=pltpu.CompilerParams(vmem_limit_bytes=16 << 20),
        cost_estimate=pl.CostEstimate(
            flops=20 * CORES * total * hidden * depth,
            bytes_accessed=2 * (total * (2 * hidden + depth) + 2 * hidden * depth),
            transcendentals=0,
        ),
    )(weight, other, *pieces)


def pick_kernel(flips, ids, *refs):
    blocks, kept, out = refs[: len(flips)], refs[len(flips) : -1], refs[-1]
    experts, tokens, _ = blocks[0].shape
    top = ids.shape[0]
    span = 16
    chip = lax.div(lax.axis_index("expert"), CORES)
    flip = lax.div(ids[...], CORES) ^ chip
    place = jnp.full(flip.shape, -1, jnp.int32)
    for j, known in enumerate(flips):
        place = jnp.where(flip == known, j * CORES + lax.rem(ids[...], CORES), place)
    column = lax.broadcasted_iota(jnp.int32, (top, len(blocks) * experts * span), 1)
    for g in range(tokens // span):
        stacked = jnp.concatenate(
            [b[c, g * span : (g + 1) * span, :] for b in blocks for c in range(experts)], axis=0
        )
        picks = [
            jnp.where(column == place[:, g * span + t : g * span + t + 1] * span + t, 1.0, 0.0)
            for t in range(span)
        ]
        pick = jnp.concatenate(picks, axis=0).astype(jnp.bfloat16)
        rows = jnp.dot(pick, stacked, preferred_element_type=jnp.float32).astype(jnp.bfloat16)
        part = slice(g * span * top, (g + 1) * span * top)
        out[part, :] = rows + kept[0][part, :] if kept else rows


def pick_routes(ids, received, *kept):
    top, tokens = ids.shape
    flips = sorted(received)
    blocks = [received[flip] for flip in flips]
    return pl.pallas_call(
        functools.partial(pick_kernel, flips),
        out_shape=jax.ShapeDtypeStruct((top * tokens, blocks[0].shape[2]), jnp.bfloat16),
        compiler_params=pltpu.CompilerParams(vmem_limit_bytes=16 << 20),
    )(ids, *blocks, *kept)


def dense_device(upstream, route_ids, route_gates, weight_mat):
    tokens, top = route_ids.shape
    owners = lax.axis_size("expert")
    tie = lax.optimization_barrier

    def work(*pieces, stack=False):
        return products(list(pieces), tokens, weight_mat, other_mat, stack)

    rows = send_across(upstream, owners, 0)
    far = send_across(upstream, owners, Z_FAR)
    other_mat = send(weight_mat, owners, 0, 1)
    columns = gate_columns(route_ids.T, route_gates.T, weight_mat)
    far_columns = send(columns, owners, Z_FAR)
    rows, columns = tie((rows, columns))
    rows = widened(rows, columns)
    side = send(rows, owners, X)
    (out_own,) = work(rows)
    far, far_columns, _ = tie((far, far_columns, out_own))
    far = widened(far, far_columns)
    cross = send(far, owners, Z_NEAR)
    far_side = send(far, owners, X)
    (out_far,) = work(far)
    back_far = send(out_far, owners, Z_FAR)
    rows, side, _ = tie((rows, side, out_far))
    near = send(rows, owners, Z_NEAR)
    cross_side = send(cross, owners, X)
    far_side, _ = tie((far_side, cross))
    out_cross, out_far_side = work(cross, far_side)
    back_cross = send(out_cross, owners, Z_NEAR ^ Z_FAR)
    near, out_far_side, _ = tie((near, out_far_side, out_cross))
    near_side = send(near, owners, X)
    back_far_side = send(out_far_side, owners, X ^ Z_FAR)
    cross_side, back_far, _ = tie((cross_side, back_far, near))
    (out_cross_side,) = work(cross_side)
    back_cross_side = send(out_cross_side, owners, X ^ Z_NEAR ^ Z_FAR)
    near_side, _ = tie((near_side, out_cross_side))
    out_side, out_near, out_near_side = work(side, near, near_side)
    back_near_side = send(out_near_side, owners, X ^ Z_NEAR)
    back_side = send(out_side, owners, X)
    back_near = send(out_near, owners, Z_NEAR)
    far_parts = {
        0: out_own,
        Z_FAR: back_far,
        X ^ Z_FAR: back_far_side,
        Z_NEAR ^ Z_FAR: back_cross,
        X ^ Z_NEAR ^ Z_FAR: back_cross_side,
    }
    near_parts = {X: back_side, Z_NEAR: back_near, X ^ Z_NEAR: back_near_side}
    out = pick_routes(route_ids.T, near_parts, pick_routes(route_ids.T, far_parts))
    return out.reshape(1, tokens, top, weight_mat.shape[0])


def slotted_device(section_grad, route_ids, route_gates, weight_mat, capacity):
    tokens, top = route_ids.shape
    owners = lax.axis_size("expert")
    ids = jnp.arange(owners, dtype=jnp.int32)
    slots = jnp.arange(capacity, dtype=jnp.int32)
    matched = (route_ids[:, :, None] == ids[None, None, :]).astype(jnp.int32)
    hits = jnp.sum(matched, axis=1)
    rank = jnp.cumsum(hits, axis=0) - hits
    position = route_ids * capacity + jnp.sum(matched * rank[:, None, :], axis=2)
    gate_owner = jnp.einsum(
        "tk,tke->te", route_gates.astype(jnp.float32), matched.astype(jnp.float32)
    )
    slot_pick = (hits[:, :, None] == 1) & (rank[:, :, None] == slots[None, None, :])
    send_rows = jnp.einsum(
        "tem,td->emd",
        slot_pick.astype(jnp.bfloat16),
        section_grad,
        preferred_element_type=jnp.float32,
    ).astype(jnp.bfloat16)
    send_gates = jnp.einsum("tem,te->em", slot_pick.astype(jnp.float32), gate_owner).astype(
        jnp.bfloat16
    )
    got_rows = lax.all_to_all(send_rows, "expert", split_axis=0, concat_axis=0, tiled=True)
    got_gates = lax.all_to_all(send_gates, "expert", split_axis=0, concat_axis=0, tiled=True)
    product = lax.dot_general(
        got_rows.reshape(owners * capacity, got_rows.shape[2]),
        weight_mat,
        (((1,), (1,)), ((), ())),
        preferred_element_type=jnp.float32,
    ).reshape(owners, capacity, weight_mat.shape[0])
    returned = lax.all_to_all(
        (product * got_gates.astype(jnp.float32)[:, :, None]).astype(jnp.bfloat16),
        "expert",
        split_axis=0,
        concat_axis=0,
        tiled=True,
    )
    flat = returned.reshape(owners * capacity, returned.shape[2])
    out = jnp.take(flat, position.reshape(tokens * top), axis=0)
    return out.reshape(1, tokens, top, returned.shape[2])


def per_device(upstream, expert_ids, gate_weights, expert_weight):
    route_ids = expert_ids[0]
    route_gates = gate_weights[0]
    weight_mat = expert_weight[0, 0]
    tokens, top = route_ids.shape
    owners = lax.axis_size("expert")
    capacity = 2 * tokens * top // owners
    if capacity >= tokens and owners == CORES * 2 * Z_FAR:
        return dense_device(upstream[0], route_ids, route_gates, weight_mat)
    section_grad = shifted(upstream, "pipe", -1)[0]
    return slotted_device(section_grad, route_ids, route_gates, weight_mat, capacity)


def solution(mesh):
    in_specs = (
        P("pipe", "expert", None),
        P("pipe", "expert", None),
        P("pipe", "expert", None),
        P("pipe", "expert", None, None),
    )
    out_specs = P("pipe", "expert", None, None)
    return jax.shard_map(
        per_device, mesh=mesh, in_specs=in_specs, out_specs=out_specs, check_vma=False
    )
```

```python
import functools

import jax
import jax.numpy as jnp
from jax import lax
from jax.experimental import pallas as pl
from jax.experimental.pallas import tpu as pltpu
from jax.sharding import PartitionSpec as P

CORES = 2
X, Z_NEAR, Z_FAR = 1, 2, 4
LANES = 128


def shifted(block, axis, distance):
    devices = range(lax.axis_size(axis))
    route = [((i - distance) % len(devices), i) for i in devices]
    return lax.ppermute(block, axis, route)


def send(block, owners, flip, core=0):
    route = [(i, ((i // CORES) ^ flip) * CORES + ((i % CORES) ^ core)) for i in range(owners)]
    return lax.ppermute(block, "expert", route)


def send_across(block, owners, flip):
    sections = lax.axis_size("pipe")
    route = []
    for s in range(sections):
        for i in range(owners):
            target = ((i // CORES) ^ flip) * CORES + i % CORES
            route.append((s * owners + i, (s - 1) % sections * owners + target))
    return lax.ppermute(block, ("pipe", "expert"), route)


def gates_kernel(ids, gates, out):
    top, tokens = ids.shape
    expert = lax.broadcasted_iota(jnp.int32, (LANES, tokens), 0)
    total = jnp.zeros((LANES, tokens), jnp.float32)
    for k in range(top):
        gate = gates[k : k + 1, :].astype(jnp.float32)
        total += jnp.where(expert == ids[k : k + 1, :], gate, 0.0)
    out[...] = total.T.astype(jnp.bfloat16)


def gate_columns(ids, gates):
    return pl.pallas_call(
        gates_kernel,
        out_shape=jax.ShapeDtypeStruct((ids.shape[1], LANES), jnp.bfloat16),
        compiler_params=pltpu.CompilerParams(vmem_limit_bytes=16 << 20),
    )(ids, gates)


def widen_kernel(rows, columns, out):
    depth = rows.shape[1]
    out[:, :depth] = rows[...]
    out[:, depth:] = columns[...]


def widened(rows, columns):
    width = rows.shape[1] + columns.shape[1]
    return pl.pallas_call(
        widen_kernel,
        out_shape=jax.ShapeDtypeStruct((rows.shape[0], width), jnp.bfloat16),
        compiler_params=pltpu.CompilerParams(vmem_limit_bytes=16 << 20),
    )(rows, columns)


def turn_kernel(weight, other, out):
    hidden = weight.shape[0]
    out[:, :hidden] = weight[...].T
    out[:, hidden:] = other[...].T


def turned(weight, other):
    hidden, depth = weight.shape
    return pl.pallas_call(
        turn_kernel,
        out_shape=jax.ShapeDtypeStruct((depth, CORES * hidden), weight.dtype),
        compiler_params=pltpu.CompilerParams(vmem_limit_bytes=24 << 20),
        cost_estimate=pl.CostEstimate(
            flops=4 * CORES * 1024 * hidden * depth, bytes_accessed=0, transcendentals=0
        ),
    )(weight, other)


def products_kernel(count, weights, *refs):
    pieces, outs = refs[:count], refs[count:]
    depth, width = weights.shape
    hidden = width // CORES
    tokens = outs[0].shape[1]
    me = lax.axis_index("expert")
    core = lax.rem(me, CORES)
    stacked = jnp.concatenate([p[...] for p in pieces], axis=0)
    gates = stacked[:, depth:].astype(jnp.float32)
    column = lax.broadcasted_iota(jnp.int32, gates.shape, 1)
    product = jnp.dot(stacked[:, :depth], weights[...], preferred_element_type=jnp.float32)
    for half, to in enumerate((core, 1 - core)):
        scale = jnp.sum(jnp.where(column == me - core + to, gates, 0.0), axis=1, keepdims=True)
        scaled = (product[:, half * hidden : (half + 1) * hidden] * scale).astype(jnp.bfloat16)
        for j, out in enumerate(outs):
            out[to] = scaled[j * tokens : (j + 1) * tokens]


def products(pieces, tokens, weights):
    depth, width = weights.shape
    total = sum(p.shape[0] for p in pieces)
    one = jax.ShapeDtypeStruct((CORES, tokens, width // CORES), jnp.bfloat16)
    return pl.pallas_call(
        functools.partial(products_kernel, len(pieces)),
        out_shape=[one] * (total // tokens),
        compiler_params=pltpu.CompilerParams(vmem_limit_bytes=16 << 20),
        cost_estimate=pl.CostEstimate(
            flops=20 * total * width * depth,
            bytes_accessed=2 * (total * (width + depth) + width * depth),
            transcendentals=0,
        ),
    )(weights, *pieces)


def pick_kernel(ids, *refs):
    blocks, out = refs[:-1], refs[-1]
    experts, tokens, _ = blocks[0].shape
    top = ids.shape[0]
    span = 16
    chip = lax.div(lax.axis_index("expert"), CORES)
    label = (lax.div(ids[...], CORES) ^ chip) * CORES + lax.rem(ids[...], CORES)
    column = lax.broadcasted_iota(jnp.int32, (top, len(blocks) * experts * span), 1)
    for g in range(tokens // span):
        stacked = jnp.concatenate(
            [b[c, g * span : (g + 1) * span, :] for b in blocks for c in range(experts)], axis=0
        )
        picks = [
            jnp.where(column == label[:, g * span + t : g * span + t + 1] * span + t, 1.0, 0.0)
            for t in range(span)
        ]
        pick = jnp.concatenate(picks, axis=0).astype(jnp.bfloat16)
        rows = jnp.dot(pick, stacked, preferred_element_type=jnp.float32)
        out[g * span * top : (g + 1) * span * top, :] = rows.astype(jnp.bfloat16)


def pick_routes(ids, blocks):
    top, tokens = ids.shape
    return pl.pallas_call(
        pick_kernel,
        out_shape=jax.ShapeDtypeStruct((top * tokens, blocks[0].shape[2]), jnp.bfloat16),
        compiler_params=pltpu.CompilerParams(vmem_limit_bytes=16 << 20),
    )(ids, *blocks)


def dense_device(upstream, route_ids, route_gates, weight_mat):
    tokens, top = route_ids.shape
    owners = lax.axis_size("expert")
    tie = lax.optimization_barrier

    def work(*pieces):
        return products(list(pieces), tokens, weights)

    far = send_across(upstream, owners, Z_FAR)
    rows = send_across(upstream, owners, 0)
    other_mat = send(weight_mat, owners, 0, 1)
    columns = gate_columns(route_ids.T, route_gates.T)
    far_columns = send(columns, owners, Z_FAR)
    weights = turned(weight_mat, other_mat)
    far, far_columns, weights = tie((far, far_columns, weights))
    far = widened(far, far_columns)
    cross = send(far, owners, Z_NEAR)
    far_side = send(far, owners, X)
    (out_far,) = work(far)
    back_far = send(out_far, owners, Z_FAR)
    rows, columns, _ = tie((rows, columns, out_far))
    rows = widened(rows, columns)
    near = send(rows, owners, Z_NEAR)
    side = send(rows, owners, X)
    cross, rows = tie((cross, rows))
    cross_side = send(cross, owners, X)
    (out_cross,) = work(cross)
    back_cross = send(out_cross, owners, Z_NEAR ^ Z_FAR)
    far_side, back_far, near, _ = tie((far_side, back_far, near, out_cross))
    near_side = send(near, owners, X)
    (out_far_side,) = work(far_side)
    back_far_side = send(out_far_side, owners, X ^ Z_FAR)
    cross_side, _ = tie((cross_side, out_far_side))
    (out_cross_side,) = work(cross_side)
    back_cross_side = send(out_cross_side, owners, X ^ Z_NEAR ^ Z_FAR)
    side, near_side, _ = tie((side, near_side, out_cross_side))
    out_side, out_near, out_near_side = work(side, near, near_side)
    back_near_side = send(out_near_side, owners, X ^ Z_NEAR)
    back_side = send(out_side, owners, X)
    back_near = send(out_near, owners, Z_NEAR)
    rows, _ = tie((rows, out_near_side))
    (out_own,) = work(rows)
    received = {
        0: out_own,
        X: back_side,
        Z_NEAR: back_near,
        X ^ Z_NEAR: back_near_side,
        Z_FAR: back_far,
        X ^ Z_FAR: back_far_side,
        Z_NEAR ^ Z_FAR: back_cross,
        X ^ Z_NEAR ^ Z_FAR: back_cross_side,
    }
    out = pick_routes(route_ids.T, [received[flip] for flip in sorted(received)])
    return out.reshape(1, tokens, top, weight_mat.shape[0])


def slotted_device(section_grad, route_ids, route_gates, weight_mat, capacity):
    tokens, top = route_ids.shape
    owners = lax.axis_size("expert")
    ids = jnp.arange(owners, dtype=jnp.int32)
    slots = jnp.arange(capacity, dtype=jnp.int32)
    matched = (route_ids[:, :, None] == ids[None, None, :]).astype(jnp.int32)
    hits = jnp.sum(matched, axis=1)
    rank = jnp.cumsum(hits, axis=0) - hits
    position = route_ids * capacity + jnp.sum(matched * rank[:, None, :], axis=2)
    gate_owner = jnp.einsum(
        "tk,tke->te", route_gates.astype(jnp.float32), matched.astype(jnp.float32)
    )
    slot_pick = (hits[:, :, None] == 1) & (rank[:, :, None] == slots[None, None, :])
    send_rows = jnp.einsum(
        "tem,td->emd",
        slot_pick.astype(jnp.bfloat16),
        section_grad,
        preferred_element_type=jnp.float32,
    ).astype(jnp.bfloat16)
    send_gates = jnp.einsum("tem,te->em", slot_pick.astype(jnp.float32), gate_owner).astype(
        jnp.bfloat16
    )
    got_rows = lax.all_to_all(send_rows, "expert", split_axis=0, concat_axis=0, tiled=True)
    got_gates = lax.all_to_all(send_gates, "expert", split_axis=0, concat_axis=0, tiled=True)
    product = lax.dot_general(
        got_rows.reshape(owners * capacity, got_rows.shape[2]),
        weight_mat,
        (((1,), (1,)), ((), ())),
        preferred_element_type=jnp.float32,
    ).reshape(owners, capacity, weight_mat.shape[0])
    returned = lax.all_to_all(
        (product * got_gates.astype(jnp.float32)[:, :, None]).astype(jnp.bfloat16),
        "expert",
        split_axis=0,
        concat_axis=0,
        tiled=True,
    )
    flat = returned.reshape(owners * capacity, returned.shape[2])
    out = jnp.take(flat, position.reshape(tokens * top), axis=0)
    return out.reshape(1, tokens, top, returned.shape[2])


def per_device(upstream, expert_ids, gate_weights, expert_weight):
    route_ids = expert_ids[0]
    route_gates = gate_weights[0]
    weight_mat = expert_weight[0, 0]
    tokens, top = route_ids.shape
    owners = lax.axis_size("expert")
    capacity = 2 * tokens * top // owners
    if capacity >= tokens and owners == CORES * 2 * Z_FAR:
        return dense_device(upstream[0], route_ids, route_gates, weight_mat)
    section_grad = shifted(upstream, "pipe", -1)[0]
    return slotted_device(section_grad, route_ids, route_gates, weight_mat, capacity)


def solution(mesh):
    in_specs = (
        P("pipe", "expert", None),
        P("pipe", "expert", None),
        P("pipe", "expert", None),
        P("pipe", "expert", None, None),
    )
    out_specs = P("pipe", "expert", None, None)
    return jax.shard_map(
        per_device, mesh=mesh, in_specs=in_specs, out_specs=out_specs, check_vma=False
    )
```

```python
import functools

import jax
import jax.numpy as jnp
from jax import lax
from jax.experimental import pallas as pl
from jax.experimental.pallas import tpu as pltpu
from jax.sharding import PartitionSpec as P

CORES = 2
X, Z_NEAR, Z_FAR = 1, 2, 4
LANES = 128


def shifted(block, axis, distance):
    devices = range(lax.axis_size(axis))
    route = [((i - distance) % len(devices), i) for i in devices]
    return lax.ppermute(block, axis, route)


def send(block, owners, flip, core=0):
    route = [(i, ((i // CORES) ^ flip) * CORES + ((i % CORES) ^ core)) for i in range(owners)]
    return lax.ppermute(block, "expert", route)


def send_across(block, owners, flip):
    sections = lax.axis_size("pipe")
    route = []
    for s in range(sections):
        for i in range(owners):
            target = ((i // CORES) ^ flip) * CORES + i % CORES
            route.append((s * owners + i, (s - 1) % sections * owners + target))
    return lax.ppermute(block, ("pipe", "expert"), route)


def gates_kernel(ids, gates, out):
    top, tokens = ids.shape
    expert = lax.broadcasted_iota(jnp.int32, (LANES, tokens), 0)
    total = jnp.zeros((LANES, tokens), jnp.float32)
    for k in range(top):
        gate = gates[k : k + 1, :].astype(jnp.float32)
        total += jnp.where(expert == ids[k : k + 1, :], gate, 0.0)
    out[...] = total.T.astype(jnp.bfloat16)


def gate_columns(ids, gates):
    return pl.pallas_call(
        gates_kernel,
        out_shape=jax.ShapeDtypeStruct((ids.shape[1], LANES), jnp.bfloat16),
        compiler_params=pltpu.CompilerParams(vmem_limit_bytes=16 << 20),
    )(ids, gates)


def widen_kernel(rows, columns, out):
    depth = rows.shape[1]
    out[:, :depth] = rows[...]
    out[:, depth:] = columns[...]


def widened(rows, columns):
    width = rows.shape[1] + columns.shape[1]
    return pl.pallas_call(
        widen_kernel,
        out_shape=jax.ShapeDtypeStruct((rows.shape[0], width), jnp.bfloat16),
        compiler_params=pltpu.CompilerParams(vmem_limit_bytes=16 << 20),
    )(rows, columns)


def turn_kernel(weight, other, out):
    hidden = weight.shape[0]
    out[:, :hidden] = weight[...].T
    out[:, hidden:] = other[...].T


def turned(weight, other):
    hidden, depth = weight.shape
    return pl.pallas_call(
        turn_kernel,
        out_shape=jax.ShapeDtypeStruct((depth, CORES * hidden), weight.dtype),
        compiler_params=pltpu.CompilerParams(vmem_limit_bytes=24 << 20),
        cost_estimate=pl.CostEstimate(
            flops=4 * CORES * 1024 * hidden * depth, bytes_accessed=0, transcendentals=0
        ),
    )(weight, other)


def products_kernel(count, weights, *refs):
    pieces, outs = refs[:count], refs[count:]
    depth, width = weights.shape
    hidden = width // CORES
    tokens = outs[0].shape[1]
    me = lax.axis_index("expert")
    core = lax.rem(me, CORES)
    stacked = jnp.concatenate([p[...] for p in pieces], axis=0)
    gates = stacked[:, depth:].astype(jnp.float32)
    column = lax.broadcasted_iota(jnp.int32, gates.shape, 1)
    product = jnp.dot(stacked[:, :depth], weights[...], preferred_element_type=jnp.float32)
    for half, to in enumerate((core, 1 - core)):
        scale = jnp.sum(jnp.where(column == me - core + to, gates, 0.0), axis=1, keepdims=True)
        scaled = (product[:, half * hidden : (half + 1) * hidden] * scale).astype(jnp.bfloat16)
        for j, out in enumerate(outs):
            out[to] = scaled[j * tokens : (j + 1) * tokens]


def products(pieces, tokens, weights):
    depth, width = weights.shape
    total = sum(p.shape[0] for p in pieces)
    one = jax.ShapeDtypeStruct((CORES, tokens, width // CORES), jnp.bfloat16)
    return pl.pallas_call(
        functools.partial(products_kernel, len(pieces)),
        out_shape=[one] * (total // tokens),
        compiler_params=pltpu.CompilerParams(vmem_limit_bytes=16 << 20),
        cost_estimate=pl.CostEstimate(
            flops=20 * total * width * depth,
            bytes_accessed=2 * (total * (width + depth) + width * depth),
            transcendentals=0,
        ),
    )(weights, *pieces)


def pick_kernel(ids, *refs):
    blocks, out = refs[:-1], refs[-1]
    experts, tokens, _ = blocks[0].shape
    top = ids.shape[0]
    span = 16
    chip = lax.div(lax.axis_index("expert"), CORES)
    label = (lax.div(ids[...], CORES) ^ chip) * CORES + lax.rem(ids[...], CORES)
    column = lax.broadcasted_iota(jnp.int32, (top, len(blocks) * experts * span), 1)
    for g in range(tokens // span):
        stacked = jnp.concatenate(
            [b[c, g * span : (g + 1) * span, :] for b in blocks for c in range(experts)], axis=0
        )
        picks = [
            jnp.where(column == label[:, g * span + t : g * span + t + 1] * span + t, 1.0, 0.0)
            for t in range(span)
        ]
        pick = jnp.concatenate(picks, axis=0).astype(jnp.bfloat16)
        rows = jnp.dot(pick, stacked, preferred_element_type=jnp.float32)
        out[g * span * top : (g + 1) * span * top, :] = rows.astype(jnp.bfloat16)


def pick_routes(ids, blocks):
    top, tokens = ids.shape
    return pl.pallas_call(
        pick_kernel,
        out_shape=jax.ShapeDtypeStruct((top * tokens, blocks[0].shape[2]), jnp.bfloat16),
        compiler_params=pltpu.CompilerParams(vmem_limit_bytes=16 << 20),
    )(ids, *blocks)


def dense_device(upstream, route_ids, route_gates, weight_mat):
    tokens, top = route_ids.shape
    owners = lax.axis_size("expert")
    tie = lax.optimization_barrier

    def work(*pieces):
        return products(list(pieces), tokens, weights)

    far = send_across(upstream, owners, Z_FAR)
    rows = send_across(upstream, owners, 0)
    other_mat = send(weight_mat, owners, 0, 1)
    columns = gate_columns(route_ids.T, route_gates.T)
    far_columns = send(columns, owners, Z_FAR)
    weights = turned(weight_mat, other_mat)
    rows, columns, weights = tie((rows, columns, weights))
    rows = widened(rows, columns)
    side = send(rows, owners, X)
    near = send(rows, owners, Z_NEAR)
    far, far_columns, rows = tie((far, far_columns, rows))
    far = widened(far, far_columns)
    cross = send(far, owners, Z_NEAR)
    far_side = send(far, owners, X)
    (out_far,) = work(far)
    back_far = send(out_far, owners, Z_FAR)
    side, _ = tie((side, out_far))
    near, side = tie((near, side))
    near_side = send(near, owners, X)
    cross, _ = tie((cross, near))
    cross_side = send(cross, owners, X)
    (out_cross,) = work(cross)
    back_cross = send(out_cross, owners, Z_NEAR ^ Z_FAR)
    far_side, back_far, _ = tie((far_side, back_far, out_cross))
    (out_far_side,) = work(far_side)
    back_far_side = send(out_far_side, owners, X ^ Z_FAR)
    cross_side, _ = tie((cross_side, out_far_side))
    (out_cross_side,) = work(cross_side)
    back_cross_side = send(out_cross_side, owners, X ^ Z_NEAR ^ Z_FAR)
    near_side, _ = tie((near_side, out_cross_side))
    out_side, out_near, out_near_side = work(side, near, near_side)
    back_near_side = send(out_near_side, owners, X ^ Z_NEAR)
    back_side = send(out_side, owners, X)
    back_near = send(out_near, owners, Z_NEAR)
    rows, _ = tie((rows, out_near_side))
    (out_own,) = work(rows)
    received = {
        0: out_own,
        X: back_side,
        Z_NEAR: back_near,
        X ^ Z_NEAR: back_near_side,
        Z_FAR: back_far,
        X ^ Z_FAR: back_far_side,
        Z_NEAR ^ Z_FAR: back_cross,
        X ^ Z_NEAR ^ Z_FAR: back_cross_side,
    }
    out = pick_routes(route_ids.T, [received[flip] for flip in sorted(received)])
    return out.reshape(1, tokens, top, weight_mat.shape[0])


def slotted_device(section_grad, route_ids, route_gates, weight_mat, capacity):
    tokens, top = route_ids.shape
    owners = lax.axis_size("expert")
    ids = jnp.arange(owners, dtype=jnp.int32)
    slots = jnp.arange(capacity, dtype=jnp.int32)
    matched = (route_ids[:, :, None] == ids[None, None, :]).astype(jnp.int32)
    hits = jnp.sum(matched, axis=1)
    rank = jnp.cumsum(hits, axis=0) - hits
    position = route_ids * capacity + jnp.sum(matched * rank[:, None, :], axis=2)
    gate_owner = jnp.einsum(
        "tk,tke->te", route_gates.astype(jnp.float32), matched.astype(jnp.float32)
    )
    slot_pick = (hits[:, :, None] == 1) & (rank[:, :, None] == slots[None, None, :])
    send_rows = jnp.einsum(
        "tem,td->emd",
        slot_pick.astype(jnp.bfloat16),
        section_grad,
        preferred_element_type=jnp.float32,
    ).astype(jnp.bfloat16)
    send_gates = jnp.einsum("tem,te->em", slot_pick.astype(jnp.float32), gate_owner).astype(
        jnp.bfloat16
    )
    got_rows = lax.all_to_all(send_rows, "expert", split_axis=0, concat_axis=0, tiled=True)
    got_gates = lax.all_to_all(send_gates, "expert", split_axis=0, concat_axis=0, tiled=True)
    product = lax.dot_general(
        got_rows.reshape(owners * capacity, got_rows.shape[2]),
        weight_mat,
        (((1,), (1,)), ((), ())),
        preferred_element_type=jnp.float32,
    ).reshape(owners, capacity, weight_mat.shape[0])
    returned = lax.all_to_all(
        (product * got_gates.astype(jnp.float32)[:, :, None]).astype(jnp.bfloat16),
        "expert",
        split_axis=0,
        concat_axis=0,
        tiled=True,
    )
    flat = returned.reshape(owners * capacity, returned.shape[2])
    out = jnp.take(flat, position.reshape(tokens * top), axis=0)
    return out.reshape(1, tokens, top, returned.shape[2])


def per_device(upstream, expert_ids, gate_weights, expert_weight):
    route_ids = expert_ids[0]
    route_gates = gate_weights[0]
    weight_mat = expert_weight[0, 0]
    tokens, top = route_ids.shape
    owners = lax.axis_size("expert")
    capacity = 2 * tokens * top // owners
    if capacity >= tokens and owners == CORES * 2 * Z_FAR:
        return dense_device(upstream[0], route_ids, route_gates, weight_mat)
    section_grad = shifted(upstream, "pipe", -1)[0]
    return slotted_device(section_grad, route_ids, route_gates, weight_mat, capacity)


def solution(mesh):
    in_specs = (
        P("pipe", "expert", None),
        P("pipe", "expert", None),
        P("pipe", "expert", None),
        P("pipe", "expert", None, None),
    )
    out_specs = P("pipe", "expert", None, None)
    return jax.shard_map(
        per_device, mesh=mesh, in_specs=in_specs, out_specs=out_specs, check_vma=False
    )
```

```python
import functools

import jax
import jax.numpy as jnp
from jax import lax
from jax.experimental import pallas as pl
from jax.experimental.pallas import tpu as pltpu
from jax.sharding import PartitionSpec as P

CORES = 2
X, Z_NEAR, Z_FAR = 1, 2, 4
LANES = 128


def shifted(block, axis, distance):
    devices = range(lax.axis_size(axis))
    route = [((i - distance) % len(devices), i) for i in devices]
    return lax.ppermute(block, axis, route)


def send(block, owners, flip, core=0):
    route = [(i, ((i // CORES) ^ flip) * CORES + ((i % CORES) ^ core)) for i in range(owners)]
    return lax.ppermute(block, "expert", route)


def send_across(block, owners, flip):
    sections = lax.axis_size("pipe")
    route = []
    for s in range(sections):
        for i in range(owners):
            target = ((i // CORES) ^ flip) * CORES + i % CORES
            route.append((s * owners + i, (s - 1) % sections * owners + target))
    return lax.ppermute(block, ("pipe", "expert"), route)


def gates_kernel(ids, gates, out):
    top, tokens = ids.shape
    expert = lax.broadcasted_iota(jnp.int32, (LANES, tokens), 0)
    total = jnp.zeros((LANES, tokens), jnp.float32)
    for k in range(top):
        gate = gates[k : k + 1, :].astype(jnp.float32)
        total += jnp.where(expert == ids[k : k + 1, :], gate, 0.0)
    out[...] = total.T.astype(jnp.bfloat16)


def gate_columns(ids, gates):
    return pl.pallas_call(
        gates_kernel,
        out_shape=jax.ShapeDtypeStruct((ids.shape[1], LANES), jnp.bfloat16),
        compiler_params=pltpu.CompilerParams(vmem_limit_bytes=16 << 20),
    )(ids, gates)


def widen_kernel(rows, columns, out):
    depth = rows.shape[1]
    out[:, :depth] = rows[...]
    out[:, depth:] = columns[...]


def widened(rows, columns):
    width = rows.shape[1] + columns.shape[1]
    return pl.pallas_call(
        widen_kernel,
        out_shape=jax.ShapeDtypeStruct((rows.shape[0], width), jnp.bfloat16),
        compiler_params=pltpu.CompilerParams(vmem_limit_bytes=16 << 20),
    )(rows, columns)


def turn_kernel(weight, other, out):
    hidden = weight.shape[0]
    out[:, :hidden] = weight[...].T
    out[:, hidden:] = other[...].T


def turned(weight, other):
    hidden, depth = weight.shape
    return pl.pallas_call(
        turn_kernel,
        out_shape=jax.ShapeDtypeStruct((depth, CORES * hidden), weight.dtype),
        compiler_params=pltpu.CompilerParams(vmem_limit_bytes=24 << 20),
        cost_estimate=pl.CostEstimate(
            flops=4 * CORES * 1024 * hidden * depth, bytes_accessed=0, transcendentals=0
        ),
    )(weight, other)


def products_kernel(count, weights, *refs):
    pieces, outs = refs[:count], refs[count:]
    depth, width = weights.shape
    hidden = width // CORES
    tokens = outs[0].shape[1]
    me = lax.axis_index("expert")
    core = lax.rem(me, CORES)
    stacked = jnp.concatenate([p[...] for p in pieces], axis=0)
    gates = stacked[:, depth:].astype(jnp.float32)
    column = lax.broadcasted_iota(jnp.int32, gates.shape, 1)
    product = jnp.dot(stacked[:, :depth], weights[...], preferred_element_type=jnp.float32)
    for half, to in enumerate((core, 1 - core)):
        scale = jnp.sum(jnp.where(column == me - core + to, gates, 0.0), axis=1, keepdims=True)
        scaled = (product[:, half * hidden : (half + 1) * hidden] * scale).astype(jnp.bfloat16)
        for j, out in enumerate(outs):
            out[to] = scaled[j * tokens : (j + 1) * tokens]


def products(pieces, tokens, weights):
    depth, width = weights.shape
    total = sum(p.shape[0] for p in pieces)
    one = jax.ShapeDtypeStruct((CORES, tokens, width // CORES), jnp.bfloat16)
    return pl.pallas_call(
        functools.partial(products_kernel, len(pieces)),
        out_shape=[one] * (total // tokens),
        compiler_params=pltpu.CompilerParams(vmem_limit_bytes=16 << 20),
        cost_estimate=pl.CostEstimate(
            flops=20 * total * width * depth,
            bytes_accessed=2 * (total * (width + depth) + width * depth),
            transcendentals=0,
        ),
    )(weights, *pieces)


def pick_kernel(flips, ids, *refs):
    blocks, kept, out = refs[: len(flips)], refs[len(flips) : -1], refs[-1]
    experts, tokens, _ = blocks[0].shape
    top = ids.shape[0]
    span = 16
    chip = lax.div(lax.axis_index("expert"), CORES)
    flip = lax.div(ids[...], CORES) ^ chip
    place = jnp.full(flip.shape, -1, jnp.int32)
    for j, known in enumerate(flips):
        place = jnp.where(flip == known, j * CORES + lax.rem(ids[...], CORES), place)
    column = lax.broadcasted_iota(jnp.int32, (top, len(blocks) * experts * span), 1)
    for g in range(tokens // span):
        stacked = jnp.concatenate(
            [b[c, g * span : (g + 1) * span, :] for b in blocks for c in range(experts)], axis=0
        )
        picks = [
            jnp.where(column == place[:, g * span + t : g * span + t + 1] * span + t, 1.0, 0.0)
            for t in range(span)
        ]
        pick = jnp.concatenate(picks, axis=0).astype(jnp.bfloat16)
        rows = jnp.dot(pick, stacked, preferred_element_type=jnp.float32).astype(jnp.bfloat16)
        part = slice(g * span * top, (g + 1) * span * top)
        out[part, :] = rows + kept[0][part, :] if kept else rows


def pick_routes(ids, received, *kept):
    top, tokens = ids.shape
    flips = sorted(received)
    blocks = [received[flip] for flip in flips]
    return pl.pallas_call(
        functools.partial(pick_kernel, flips),
        out_shape=jax.ShapeDtypeStruct((top * tokens, blocks[0].shape[2]), jnp.bfloat16),
        compiler_params=pltpu.CompilerParams(vmem_limit_bytes=16 << 20),
    )(ids, *blocks, *kept)


def dense_device(upstream, route_ids, route_gates, weight_mat):
    tokens, top = route_ids.shape
    owners = lax.axis_size("expert")
    tie = lax.optimization_barrier

    def work(*pieces):
        return products(list(pieces), tokens, weights)

    far = send_across(upstream, owners, Z_FAR)
    rows = send_across(upstream, owners, 0)
    other_mat = send(weight_mat, owners, 0, 1)
    columns = gate_columns(route_ids.T, route_gates.T)
    far_columns = send(columns, owners, Z_FAR)
    weights = turned(weight_mat, other_mat)
    rows, columns, weights = tie((rows, columns, weights))
    rows = widened(rows, columns)
    side = send(rows, owners, X)
    far, far_columns, rows = tie((far, far_columns, rows))
    far = widened(far, far_columns)
    cross = send(far, owners, Z_NEAR)
    far_side = send(far, owners, X)
    (out_far,) = work(far)
    back_far = send(out_far, owners, Z_FAR)
    side, rows, _ = tie((side, rows, out_far))
    near = send(rows, owners, Z_NEAR)
    out_side, out_own = work(side, rows)
    back_side = send(out_side, owners, X)
    cross, _ = tie((cross, out_own))
    cross_side = send(cross, owners, X)
    (out_cross,) = work(cross)
    back_cross = send(out_cross, owners, Z_NEAR ^ Z_FAR)
    far_side, back_far, near, _ = tie((far_side, back_far, near, out_cross))
    near_side = send(near, owners, X)
    (out_far_side,) = work(far_side)
    back_far_side = send(out_far_side, owners, X ^ Z_FAR)
    cross_side, near_side, back_side, _ = tie((cross_side, near_side, back_side, out_far_side))
    out_cross_side, out_near, out_near_side = work(cross_side, near, near_side)
    back_cross_side = send(out_cross_side, owners, X ^ Z_NEAR ^ Z_FAR)
    back_near_side = send(out_near_side, owners, X ^ Z_NEAR)
    back_near = send(out_near, owners, Z_NEAR)
    far_parts = {
        0: out_own,
        Z_FAR: back_far,
        X ^ Z_FAR: back_far_side,
        Z_NEAR ^ Z_FAR: back_cross,
        X ^ Z_NEAR ^ Z_FAR: back_cross_side,
    }
    near_parts = {X: back_side, Z_NEAR: back_near, X ^ Z_NEAR: back_near_side}
    out = pick_routes(route_ids.T, near_parts, pick_routes(route_ids.T, far_parts))
    return out.reshape(1, tokens, top, weight_mat.shape[0])


def slotted_device(section_grad, route_ids, route_gates, weight_mat, capacity):
    tokens, top = route_ids.shape
    owners = lax.axis_size("expert")
    ids = jnp.arange(owners, dtype=jnp.int32)
    slots = jnp.arange(capacity, dtype=jnp.int32)
    matched = (route_ids[:, :, None] == ids[None, None, :]).astype(jnp.int32)
    hits = jnp.sum(matched, axis=1)
    rank = jnp.cumsum(hits, axis=0) - hits
    position = route_ids * capacity + jnp.sum(matched * rank[:, None, :], axis=2)
    gate_owner = jnp.einsum(
        "tk,tke->te", route_gates.astype(jnp.float32), matched.astype(jnp.float32)
    )
    slot_pick = (hits[:, :, None] == 1) & (rank[:, :, None] == slots[None, None, :])
    send_rows = jnp.einsum(
        "tem,td->emd",
        slot_pick.astype(jnp.bfloat16),
        section_grad,
        preferred_element_type=jnp.float32,
    ).astype(jnp.bfloat16)
    send_gates = jnp.einsum("tem,te->em", slot_pick.astype(jnp.float32), gate_owner).astype(
        jnp.bfloat16
    )
    got_rows = lax.all_to_all(send_rows, "expert", split_axis=0, concat_axis=0, tiled=True)
    got_gates = lax.all_to_all(send_gates, "expert", split_axis=0, concat_axis=0, tiled=True)
    product = lax.dot_general(
        got_rows.reshape(owners * capacity, got_rows.shape[2]),
        weight_mat,
        (((1,), (1,)), ((), ())),
        preferred_element_type=jnp.float32,
    ).reshape(owners, capacity, weight_mat.shape[0])
    returned = lax.all_to_all(
        (product * got_gates.astype(jnp.float32)[:, :, None]).astype(jnp.bfloat16),
        "expert",
        split_axis=0,
        concat_axis=0,
        tiled=True,
    )
    flat = returned.reshape(owners * capacity, returned.shape[2])
    out = jnp.take(flat, position.reshape(tokens * top), axis=0)
    return out.reshape(1, tokens, top, returned.shape[2])


def per_device(upstream, expert_ids, gate_weights, expert_weight):
    route_ids = expert_ids[0]
    route_gates = gate_weights[0]
    weight_mat = expert_weight[0, 0]
    tokens, top = route_ids.shape
    owners = lax.axis_size("expert")
    capacity = 2 * tokens * top // owners
    if capacity >= tokens and owners == CORES * 2 * Z_FAR:
        return dense_device(upstream[0], route_ids, route_gates, weight_mat)
    section_grad = shifted(upstream, "pipe", -1)[0]
    return slotted_device(section_grad, route_ids, route_gates, weight_mat, capacity)


def solution(mesh):
    in_specs = (
        P("pipe", "expert", None),
        P("pipe", "expert", None),
        P("pipe", "expert", None),
        P("pipe", "expert", None, None),
    )
    out_specs = P("pipe", "expert", None, None)
    return jax.shard_map(
        per_device, mesh=mesh, in_specs=in_specs, out_specs=out_specs, check_vma=False
    )
```

```python
import functools

import jax
import jax.numpy as jnp
from jax import lax
from jax.experimental import pallas as pl
from jax.experimental.pallas import tpu as pltpu
from jax.sharding import PartitionSpec as P

CORES = 2
X, Z_NEAR, Z_FAR = 1, 2, 4
LANES = 128


def shifted(block, axis, distance):
    devices = range(lax.axis_size(axis))
    route = [((i - distance) % len(devices), i) for i in devices]
    return lax.ppermute(block, axis, route)


def send(block, owners, flip, core=0):
    route = [(i, ((i // CORES) ^ flip) * CORES + ((i % CORES) ^ core)) for i in range(owners)]
    return lax.ppermute(block, "expert", route)


def send_across(block, owners, flip):
    sections = lax.axis_size("pipe")
    route = []
    for s in range(sections):
        for i in range(owners):
            target = ((i // CORES) ^ flip) * CORES + i % CORES
            route.append((s * owners + i, (s - 1) % sections * owners + target))
    return lax.ppermute(block, ("pipe", "expert"), route)


def gates_kernel(ids, gates, out):
    top, tokens = ids.shape
    expert = lax.broadcasted_iota(jnp.int32, (LANES, tokens), 0)
    total = jnp.zeros((LANES, tokens), jnp.float32)
    for k in range(top):
        gate = gates[k : k + 1, :].astype(jnp.float32)
        total += jnp.where(expert == ids[k : k + 1, :], gate, 0.0)
    out[...] = total.T.astype(jnp.bfloat16)


def gate_columns(ids, gates):
    return pl.pallas_call(
        gates_kernel,
        out_shape=jax.ShapeDtypeStruct((ids.shape[1], LANES), jnp.bfloat16),
        compiler_params=pltpu.CompilerParams(vmem_limit_bytes=16 << 20),
    )(ids, gates)


def widen_kernel(rows, columns, out):
    depth = rows.shape[1]
    out[:, :depth] = rows[...]
    out[:, depth:] = columns[...]


def widened(rows, columns):
    width = rows.shape[1] + columns.shape[1]
    return pl.pallas_call(
        widen_kernel,
        out_shape=jax.ShapeDtypeStruct((rows.shape[0], width), jnp.bfloat16),
        compiler_params=pltpu.CompilerParams(vmem_limit_bytes=16 << 20),
    )(rows, columns)


def turn_kernel(weight, other, out):
    hidden = weight.shape[0]
    out[:, :hidden] = weight[...].T
    out[:, hidden:] = other[...].T


def turned(weight, other):
    hidden, depth = weight.shape
    return pl.pallas_call(
        turn_kernel,
        out_shape=jax.ShapeDtypeStruct((depth, CORES * hidden), weight.dtype),
        compiler_params=pltpu.CompilerParams(vmem_limit_bytes=24 << 20),
        cost_estimate=pl.CostEstimate(
            flops=4 * CORES * 1024 * hidden * depth, bytes_accessed=0, transcendentals=0
        ),
    )(weight, other)


def products_kernel(count, weights, *refs):
    pieces, outs = refs[:count], refs[count:]
    depth, width = weights.shape
    hidden = width // CORES
    tokens = outs[0].shape[1]
    me = lax.axis_index("expert")
    core = lax.rem(me, CORES)
    stacked = jnp.concatenate([p[...] for p in pieces], axis=0)
    gates = stacked[:, depth:].astype(jnp.float32)
    column = lax.broadcasted_iota(jnp.int32, gates.shape, 1)
    product = jnp.dot(stacked[:, :depth], weights[...], preferred_element_type=jnp.float32)
    for half, to in enumerate((core, 1 - core)):
        scale = jnp.sum(jnp.where(column == me - core + to, gates, 0.0), axis=1, keepdims=True)
        scaled = (product[:, half * hidden : (half + 1) * hidden] * scale).astype(jnp.bfloat16)
        for j, out in enumerate(outs):
            out[to] = scaled[j * tokens : (j + 1) * tokens]


def products(pieces, tokens, weights):
    depth, width = weights.shape
    total = sum(p.shape[0] for p in pieces)
    one = jax.ShapeDtypeStruct((CORES, tokens, width // CORES), jnp.bfloat16)
    return pl.pallas_call(
        functools.partial(products_kernel, len(pieces)),
        out_shape=[one] * (total // tokens),
        compiler_params=pltpu.CompilerParams(vmem_limit_bytes=16 << 20),
        cost_estimate=pl.CostEstimate(
            flops=20 * total * width * depth,
            bytes_accessed=2 * (total * (width + depth) + width * depth),
            transcendentals=0,
        ),
    )(weights, *pieces)


def pick_kernel(ids, *refs):
    blocks, out = refs[:-1], refs[-1]
    experts, tokens, _ = blocks[0].shape
    top = ids.shape[0]
    span = 16
    chip = lax.div(lax.axis_index("expert"), CORES)
    label = (lax.div(ids[...], CORES) ^ chip) * CORES + lax.rem(ids[...], CORES)
    column = lax.broadcasted_iota(jnp.int32, (top, len(blocks) * experts * span), 1)
    for g in range(tokens // span):
        stacked = jnp.concatenate(
            [b[c, g * span : (g + 1) * span, :] for b in blocks for c in range(experts)], axis=0
        )
        picks = [
            jnp.where(column == label[:, g * span + t : g * span + t + 1] * span + t, 1.0, 0.0)
            for t in range(span)
        ]
        pick = jnp.concatenate(picks, axis=0).astype(jnp.bfloat16)
        rows = jnp.dot(pick, stacked, preferred_element_type=jnp.float32)
        out[g * span * top : (g + 1) * span * top, :] = rows.astype(jnp.bfloat16)


def pick_routes(ids, blocks):
    top, tokens = ids.shape
    return pl.pallas_call(
        pick_kernel,
        out_shape=jax.ShapeDtypeStruct((top * tokens, blocks[0].shape[2]), jnp.bfloat16),
        compiler_params=pltpu.CompilerParams(vmem_limit_bytes=16 << 20),
    )(ids, *blocks)


def dense_device(upstream, route_ids, route_gates, weight_mat):
    tokens, top = route_ids.shape
    owners = lax.axis_size("expert")
    tie = lax.optimization_barrier

    def work(*pieces):
        return products(list(pieces), tokens, weights)

    far = send_across(upstream, owners, Z_FAR)
    rows = send_across(upstream, owners, 0)
    other_mat = send(weight_mat, owners, 0, 1)
    columns = gate_columns(route_ids.T, route_gates.T)
    far_columns = send(columns, owners, Z_FAR)
    weights = turned(weight_mat, other_mat)
    far, far_columns, weights = tie((far, far_columns, weights))
    far = widened(far, far_columns)
    cross = send(far, owners, Z_NEAR)
    far_side = send(far, owners, X)
    (out_far,) = work(far)
    back_far = send(out_far, owners, Z_FAR)
    rows, columns, _ = tie((rows, columns, out_far))
    rows = widened(rows, columns)
    near = send(rows, owners, Z_NEAR)
    side = send(rows, owners, X)
    cross, rows = tie((cross, rows))
    cross_side = send(cross, owners, X)
    (out_cross,) = work(cross)
    back_cross = send(out_cross, owners, Z_NEAR ^ Z_FAR)
    far_side, back_far, _ = tie((far_side, back_far, out_cross))
    (out_far_side,) = work(far_side)
    back_far_side = send(out_far_side, owners, X ^ Z_FAR)
    near, cross_side, _ = tie((near, cross_side, out_far_side))
    near_side = send(near, owners, X)
    (out_cross_side,) = work(cross_side)
    back_cross_side = send(out_cross_side, owners, X ^ Z_NEAR ^ Z_FAR)
    side, near, _ = tie((side, near, out_cross_side))
    out_side, out_near = work(side, near)
    back_side = send(out_side, owners, X)
    back_near = send(out_near, owners, Z_NEAR)
    near_side, _ = tie((near_side, out_near))
    (out_near_side,) = work(near_side)
    back_near_side = send(out_near_side, owners, X ^ Z_NEAR)
    rows, _ = tie((rows, out_near_side))
    (out_own,) = work(rows)
    received = {
        0: out_own,
        X: back_side,
        Z_NEAR: back_near,
        X ^ Z_NEAR: back_near_side,
        Z_FAR: back_far,
        X ^ Z_FAR: back_far_side,
        Z_NEAR ^ Z_FAR: back_cross,
        X ^ Z_NEAR ^ Z_FAR: back_cross_side,
    }
    out = pick_routes(route_ids.T, [received[flip] for flip in sorted(received)])
    return out.reshape(1, tokens, top, weight_mat.shape[0])


def slotted_device(section_grad, route_ids, route_gates, weight_mat, capacity):
    tokens, top = route_ids.shape
    owners = lax.axis_size("expert")
    ids = jnp.arange(owners, dtype=jnp.int32)
    slots = jnp.arange(capacity, dtype=jnp.int32)
    matched = (route_ids[:, :, None] == ids[None, None, :]).astype(jnp.int32)
    hits = jnp.sum(matched, axis=1)
    rank = jnp.cumsum(hits, axis=0) - hits
    position = route_ids * capacity + jnp.sum(matched * rank[:, None, :], axis=2)
    gate_owner = jnp.einsum(
        "tk,tke->te", route_gates.astype(jnp.float32), matched.astype(jnp.float32)
    )
    slot_pick = (hits[:, :, None] == 1) & (rank[:, :, None] == slots[None, None, :])
    send_rows = jnp.einsum(
        "tem,td->emd",
        slot_pick.astype(jnp.bfloat16),
        section_grad,
        preferred_element_type=jnp.float32,
    ).astype(jnp.bfloat16)
    send_gates = jnp.einsum("tem,te->em", slot_pick.astype(jnp.float32), gate_owner).astype(
        jnp.bfloat16
    )
    got_rows = lax.all_to_all(send_rows, "expert", split_axis=0, concat_axis=0, tiled=True)
    got_gates = lax.all_to_all(send_gates, "expert", split_axis=0, concat_axis=0, tiled=True)
    product = lax.dot_general(
        got_rows.reshape(owners * capacity, got_rows.shape[2]),
        weight_mat,
        (((1,), (1,)), ((), ())),
        preferred_element_type=jnp.float32,
    ).reshape(owners, capacity, weight_mat.shape[0])
    returned = lax.all_to_all(
        (product * got_gates.astype(jnp.float32)[:, :, None]).astype(jnp.bfloat16),
        "expert",
        split_axis=0,
        concat_axis=0,
        tiled=True,
    )
    flat = returned.reshape(owners * capacity, returned.shape[2])
    out = jnp.take(flat, position.reshape(tokens * top), axis=0)
    return out.reshape(1, tokens, top, returned.shape[2])


def per_device(upstream, expert_ids, gate_weights, expert_weight):
    route_ids = expert_ids[0]
    route_gates = gate_weights[0]
    weight_mat = expert_weight[0, 0]
    tokens, top = route_ids.shape
    owners = lax.axis_size("expert")
    capacity = 2 * tokens * top // owners
    if capacity >= tokens and owners == CORES * 2 * Z_FAR:
        return dense_device(upstream[0], route_ids, route_gates, weight_mat)
    section_grad = shifted(upstream, "pipe", -1)[0]
    return slotted_device(section_grad, route_ids, route_gates, weight_mat, capacity)


def solution(mesh):
    in_specs = (
        P("pipe", "expert", None),
        P("pipe", "expert", None),
        P("pipe", "expert", None),
        P("pipe", "expert", None, None),
    )
    out_specs = P("pipe", "expert", None, None)
    return jax.shard_map(
        per_device, mesh=mesh, in_specs=in_specs, out_specs=out_specs, check_vma=False
    )
```

```python
import functools

import jax
import jax.numpy as jnp
from jax import lax
from jax.experimental import pallas as pl
from jax.experimental.pallas import tpu as pltpu
from jax.sharding import PartitionSpec as P

CORES = 2
X, Z_NEAR, Z_FAR = 1, 2, 4
LANES = 128


def shifted(block, axis, distance):
    devices = range(lax.axis_size(axis))
    route = [((i - distance) % len(devices), i) for i in devices]
    return lax.ppermute(block, axis, route)


def send(block, owners, flip, core=0):
    route = [(i, ((i // CORES) ^ flip) * CORES + ((i % CORES) ^ core)) for i in range(owners)]
    return lax.ppermute(block, "expert", route)


def send_across(block, owners, flip):
    sections = lax.axis_size("pipe")
    route = []
    for s in range(sections):
        for i in range(owners):
            target = ((i // CORES) ^ flip) * CORES + i % CORES
            route.append((s * owners + i, (s - 1) % sections * owners + target))
    return lax.ppermute(block, ("pipe", "expert"), route)


def gates_kernel(ids, gates, out):
    top, tokens = ids.shape
    expert = lax.broadcasted_iota(jnp.int32, (LANES, tokens), 0)
    total = jnp.zeros((LANES, tokens), jnp.float32)
    for k in range(top):
        gate = gates[k : k + 1, :].astype(jnp.float32)
        total += jnp.where(expert == ids[k : k + 1, :], gate, 0.0)
    out[...] = total.T.astype(jnp.bfloat16)


def gate_columns(ids, gates):
    return pl.pallas_call(
        gates_kernel,
        out_shape=jax.ShapeDtypeStruct((ids.shape[1], LANES), jnp.bfloat16),
        compiler_params=pltpu.CompilerParams(vmem_limit_bytes=16 << 20),
    )(ids, gates)


def widen_kernel(rows, columns, out):
    depth = rows.shape[1]
    out[:, :depth] = rows[...]
    out[:, depth:] = columns[...]


def widened(rows, columns):
    width = rows.shape[1] + columns.shape[1]
    return pl.pallas_call(
        widen_kernel,
        out_shape=jax.ShapeDtypeStruct((rows.shape[0], width), jnp.bfloat16),
        compiler_params=pltpu.CompilerParams(vmem_limit_bytes=16 << 20),
    )(rows, columns)


def turn_kernel(weight, other, out):
    hidden = weight.shape[0]
    out[:, :hidden] = weight[...].T
    out[:, hidden:] = other[...].T


def turned(weight, other):
    hidden, depth = weight.shape
    return pl.pallas_call(
        turn_kernel,
        out_shape=jax.ShapeDtypeStruct((depth, CORES * hidden), weight.dtype),
        compiler_params=pltpu.CompilerParams(vmem_limit_bytes=24 << 20),
        cost_estimate=pl.CostEstimate(
            flops=4 * CORES * 1024 * hidden * depth, bytes_accessed=0, transcendentals=0
        ),
    )(weight, other)


def products_kernel(count, weights, *refs):
    pieces, outs = refs[:count], refs[count:]
    depth, width = weights.shape
    hidden = width // CORES
    tokens = outs[0].shape[1]
    me = lax.axis_index("expert")
    core = lax.rem(me, CORES)
    stacked = jnp.concatenate([p[...] for p in pieces], axis=0)
    gates = stacked[:, depth:].astype(jnp.float32)
    column = lax.broadcasted_iota(jnp.int32, gates.shape, 1)
    product = jnp.dot(stacked[:, :depth], weights[...], preferred_element_type=jnp.float32)
    for half, to in enumerate((core, 1 - core)):
        scale = jnp.sum(jnp.where(column == me - core + to, gates, 0.0), axis=1, keepdims=True)
        scaled = (product[:, half * hidden : (half + 1) * hidden] * scale).astype(jnp.bfloat16)
        for j, out in enumerate(outs):
            out[to] = scaled[j * tokens : (j + 1) * tokens]


def products(pieces, tokens, weights):
    depth, width = weights.shape
    total = sum(p.shape[0] for p in pieces)
    one = jax.ShapeDtypeStruct((CORES, tokens, width // CORES), jnp.bfloat16)
    return pl.pallas_call(
        functools.partial(products_kernel, len(pieces)),
        out_shape=[one] * (total // tokens),
        compiler_params=pltpu.CompilerParams(vmem_limit_bytes=16 << 20),
        cost_estimate=pl.CostEstimate(
            flops=20 * total * width * depth,
            bytes_accessed=2 * (total * (width + depth) + width * depth),
            transcendentals=0,
        ),
    )(weights, *pieces)


def pick_kernel(flips, ids, *refs):
    blocks, kept, out = refs[: len(flips)], refs[len(flips) : -1], refs[-1]
    experts, tokens, _ = blocks[0].shape
    top = ids.shape[0]
    span = 16
    chip = lax.div(lax.axis_index("expert"), CORES)
    flip = lax.div(ids[...], CORES) ^ chip
    place = jnp.full(flip.shape, -1, jnp.int32)
    for j, known in enumerate(flips):
        place = jnp.where(flip == known, j * CORES + lax.rem(ids[...], CORES), place)
    column = lax.broadcasted_iota(jnp.int32, (top, len(blocks) * experts * span), 1)
    for g in range(tokens // span):
        stacked = jnp.concatenate(
            [b[c, g * span : (g + 1) * span, :] for b in blocks for c in range(experts)], axis=0
        )
        picks = [
            jnp.where(column == place[:, g * span + t : g * span + t + 1] * span + t, 1.0, 0.0)
            for t in range(span)
        ]
        pick = jnp.concatenate(picks, axis=0).astype(jnp.bfloat16)
        rows = jnp.dot(pick, stacked, preferred_element_type=jnp.float32).astype(jnp.bfloat16)
        part = slice(g * span * top, (g + 1) * span * top)
        out[part, :] = rows + kept[0][part, :] if kept else rows


def pick_routes(ids, received, *kept):
    top, tokens = ids.shape
    flips = sorted(received)
    blocks = [received[flip] for flip in flips]
    return pl.pallas_call(
        functools.partial(pick_kernel, flips),
        out_shape=jax.ShapeDtypeStruct((top * tokens, blocks[0].shape[2]), jnp.bfloat16),
        compiler_params=pltpu.CompilerParams(vmem_limit_bytes=16 << 20),
    )(ids, *blocks, *kept)


def dense_device(upstream, route_ids, route_gates, weight_mat):
    tokens, top = route_ids.shape
    owners = lax.axis_size("expert")
    tie = lax.optimization_barrier

    def work(*pieces):
        return products(list(pieces), tokens, weights)

    far = send_across(upstream, owners, Z_FAR)
    rows = send_across(upstream, owners, 0)
    other_mat = send(weight_mat, owners, 0, 1)
    columns = gate_columns(route_ids.T, route_gates.T)
    far_columns = send(columns, owners, Z_FAR)
    weights = turned(weight_mat, other_mat)
    rows, columns, weights = tie((rows, columns, weights))
    rows = widened(rows, columns)
    side = send(rows, owners, X)
    near = send(rows, owners, Z_NEAR)
    far, far_columns, rows = tie((far, far_columns, rows))
    far = widened(far, far_columns)
    cross = send(far, owners, Z_NEAR)
    far_side = send(far, owners, X)
    (out_far,) = work(far)
    back_far = send(out_far, owners, Z_FAR)
    side, _ = tie((side, out_far))
    out_side, out_own = work(side, rows)
    back_side = send(out_side, owners, X)
    near, _ = tie((near, out_side))
    near_side = send(near, owners, X)
    cross, _ = tie((cross, near))
    cross_side = send(cross, owners, X)
    (out_cross,) = work(cross)
    back_cross = send(out_cross, owners, Z_NEAR ^ Z_FAR)
    far_side, back_far, back_side, _ = tie((far_side, back_far, back_side, out_cross))
    (out_far_side,) = work(far_side)
    back_far_side = send(out_far_side, owners, X ^ Z_FAR)
    cross_side, _ = tie((cross_side, out_far_side))
    (out_cross_side,) = work(cross_side)
    back_cross_side = send(out_cross_side, owners, X ^ Z_NEAR ^ Z_FAR)
    near_side, _ = tie((near_side, out_cross_side))
    out_near, out_near_side = work(near, near_side)
    back_near_side = send(out_near_side, owners, X ^ Z_NEAR)
    back_near = send(out_near, owners, Z_NEAR)
    far_parts = {
        0: out_own,
        Z_FAR: back_far,
        X ^ Z_FAR: back_far_side,
        Z_NEAR ^ Z_FAR: back_cross,
        X ^ Z_NEAR ^ Z_FAR: back_cross_side,
    }
    near_parts = {X: back_side, Z_NEAR: back_near, X ^ Z_NEAR: back_near_side}
    out = pick_routes(route_ids.T, near_parts, pick_routes(route_ids.T, far_parts))
    return out.reshape(1, tokens, top, weight_mat.shape[0])


def slotted_device(section_grad, route_ids, route_gates, weight_mat, capacity):
    tokens, top = route_ids.shape
    owners = lax.axis_size("expert")
    ids = jnp.arange(owners, dtype=jnp.int32)
    slots = jnp.arange(capacity, dtype=jnp.int32)
    matched = (route_ids[:, :, None] == ids[None, None, :]).astype(jnp.int32)
    hits = jnp.sum(matched, axis=1)
    rank = jnp.cumsum(hits, axis=0) - hits
    position = route_ids * capacity + jnp.sum(matched * rank[:, None, :], axis=2)
    gate_owner = jnp.einsum(
        "tk,tke->te", route_gates.astype(jnp.float32), matched.astype(jnp.float32)
    )
    slot_pick = (hits[:, :, None] == 1) & (rank[:, :, None] == slots[None, None, :])
    send_rows = jnp.einsum(
        "tem,td->emd",
        slot_pick.astype(jnp.bfloat16),
        section_grad,
        preferred_element_type=jnp.float32,
    ).astype(jnp.bfloat16)
    send_gates = jnp.einsum("tem,te->em", slot_pick.astype(jnp.float32), gate_owner).astype(
        jnp.bfloat16
    )
    got_rows = lax.all_to_all(send_rows, "expert", split_axis=0, concat_axis=0, tiled=True)
    got_gates = lax.all_to_all(send_gates, "expert", split_axis=0, concat_axis=0, tiled=True)
    product = lax.dot_general(
        got_rows.reshape(owners * capacity, got_rows.shape[2]),
        weight_mat,
        (((1,), (1,)), ((), ())),
        preferred_element_type=jnp.float32,
    ).reshape(owners, capacity, weight_mat.shape[0])
    returned = lax.all_to_all(
        (product * got_gates.astype(jnp.float32)[:, :, None]).astype(jnp.bfloat16),
        "expert",
        split_axis=0,
        concat_axis=0,
        tiled=True,
    )
    flat = returned.reshape(owners * capacity, returned.shape[2])
    out = jnp.take(flat, position.reshape(tokens * top), axis=0)
    return out.reshape(1, tokens, top, returned.shape[2])


def per_device(upstream, expert_ids, gate_weights, expert_weight):
    route_ids = expert_ids[0]
    route_gates = gate_weights[0]
    weight_mat = expert_weight[0, 0]
    tokens, top = route_ids.shape
    owners = lax.axis_size("expert")
    capacity = 2 * tokens * top // owners
    if capacity >= tokens and owners == CORES * 2 * Z_FAR:
        return dense_device(upstream[0], route_ids, route_gates, weight_mat)
    section_grad = shifted(upstream, "pipe", -1)[0]
    return slotted_device(section_grad, route_ids, route_gates, weight_mat, capacity)


def solution(mesh):
    in_specs = (
        P("pipe", "expert", None),
        P("pipe", "expert", None),
        P("pipe", "expert", None),
        P("pipe", "expert", None, None),
    )
    out_specs = P("pipe", "expert", None, None)
    return jax.shard_map(
        per_device, mesh=mesh, in_specs=in_specs, out_specs=out_specs, check_vma=False
    )
```

```python
import functools

import jax
import jax.numpy as jnp
from jax import lax
from jax.experimental import pallas as pl
from jax.experimental.pallas import tpu as pltpu
from jax.sharding import PartitionSpec as P

CORES = 2
X, Z_NEAR, Z_FAR = 1, 2, 4
LANES = 128


def shifted(block, axis, distance):
    devices = range(lax.axis_size(axis))
    route = [((i - distance) % len(devices), i) for i in devices]
    return lax.ppermute(block, axis, route)


def send(block, owners, flip, core=0):
    route = [(i, ((i // CORES) ^ flip) * CORES + ((i % CORES) ^ core)) for i in range(owners)]
    return lax.ppermute(block, "expert", route)


def send_across(block, owners, flip):
    sections = lax.axis_size("pipe")
    route = []
    for s in range(sections):
        for i in range(owners):
            target = ((i // CORES) ^ flip) * CORES + i % CORES
            route.append((s * owners + i, (s - 1) % sections * owners + target))
    return lax.ppermute(block, ("pipe", "expert"), route)


def gates_kernel(ids, gates, out):
    top, tokens = ids.shape
    expert = lax.broadcasted_iota(jnp.int32, (LANES, tokens), 0)
    total = jnp.zeros((LANES, tokens), jnp.float32)
    for k in range(top):
        gate = gates[k : k + 1, :].astype(jnp.float32)
        total += jnp.where(expert == ids[k : k + 1, :], gate, 0.0)
    out[...] = total.T.astype(jnp.bfloat16)


def gate_columns(ids, gates):
    return pl.pallas_call(
        gates_kernel,
        out_shape=jax.ShapeDtypeStruct((ids.shape[1], LANES), jnp.bfloat16),
        compiler_params=pltpu.CompilerParams(vmem_limit_bytes=16 << 20),
    )(ids, gates)


def widen_kernel(rows, columns, out):
    depth = rows.shape[1]
    out[:, :depth] = rows[...]
    out[:, depth:] = columns[...]


def widened(rows, columns):
    width = rows.shape[1] + columns.shape[1]
    return pl.pallas_call(
        widen_kernel,
        out_shape=jax.ShapeDtypeStruct((rows.shape[0], width), jnp.bfloat16),
        compiler_params=pltpu.CompilerParams(vmem_limit_bytes=16 << 20),
    )(rows, columns)


def turn_kernel(weight, other, out):
    hidden = weight.shape[0]
    out[:, :hidden] = weight[...].T
    out[:, hidden:] = other[...].T


def turned(weight, other):
    hidden, depth = weight.shape
    return pl.pallas_call(
        turn_kernel,
        out_shape=jax.ShapeDtypeStruct((depth, CORES * hidden), weight.dtype),
        compiler_params=pltpu.CompilerParams(vmem_limit_bytes=24 << 20),
        cost_estimate=pl.CostEstimate(
            flops=4 * CORES * 1024 * hidden * depth, bytes_accessed=0, transcendentals=0
        ),
    )(weight, other)


def products_kernel(count, weights, *refs):
    pieces, outs = refs[:count], refs[count:]
    depth, width = weights.shape
    hidden = width // CORES
    tokens = outs[0].shape[1]
    me = lax.axis_index("expert")
    core = lax.rem(me, CORES)
    stacked = jnp.concatenate([p[...] for p in pieces], axis=0)
    gates = stacked[:, depth:].astype(jnp.float32)
    column = lax.broadcasted_iota(jnp.int32, gates.shape, 1)
    product = jnp.dot(stacked[:, :depth], weights[...], preferred_element_type=jnp.float32)
    for half, to in enumerate((core, 1 - core)):
        scale = jnp.sum(jnp.where(column == me - core + to, gates, 0.0), axis=1, keepdims=True)
        scaled = (product[:, half * hidden : (half + 1) * hidden] * scale).astype(jnp.bfloat16)
        for j, out in enumerate(outs):
            out[to] = scaled[j * tokens : (j + 1) * tokens]


def products(pieces, tokens, weights):
    depth, width = weights.shape
    total = sum(p.shape[0] for p in pieces)
    one = jax.ShapeDtypeStruct((CORES, tokens, width // CORES), jnp.bfloat16)
    return pl.pallas_call(
        functools.partial(products_kernel, len(pieces)),
        out_shape=[one] * (total // tokens),
        compiler_params=pltpu.CompilerParams(vmem_limit_bytes=16 << 20),
        cost_estimate=pl.CostEstimate(
            flops=20 * total * width * depth,
            bytes_accessed=2 * (total * (width + depth) + width * depth),
            transcendentals=0,
        ),
    )(weights, *pieces)


def pick_kernel(flips, ids, *refs):
    blocks, kept, out = refs[: len(flips)], refs[len(flips) : -1], refs[-1]
    experts, tokens, _ = blocks[0].shape
    top = ids.shape[0]
    span = 16
    chip = lax.div(lax.axis_index("expert"), CORES)
    flip = lax.div(ids[...], CORES) ^ chip
    place = jnp.full(flip.shape, -1, jnp.int32)
    for j, known in enumerate(flips):
        place = jnp.where(flip == known, j * CORES + lax.rem(ids[...], CORES), place)
    column = lax.broadcasted_iota(jnp.int32, (top, len(blocks) * experts * span), 1)
    for g in range(tokens // span):
        stacked = jnp.concatenate(
            [b[c, g * span : (g + 1) * span, :] for b in blocks for c in range(experts)], axis=0
        )
        picks = [
            jnp.where(column == place[:, g * span + t : g * span + t + 1] * span + t, 1.0, 0.0)
            for t in range(span)
        ]
        pick = jnp.concatenate(picks, axis=0).astype(jnp.bfloat16)
        rows = jnp.dot(pick, stacked, preferred_element_type=jnp.float32).astype(jnp.bfloat16)
        part = slice(g * span * top, (g + 1) * span * top)
        out[part, :] = rows + kept[0][part, :] if kept else rows


def pick_routes(ids, received, *kept):
    top, tokens = ids.shape
    flips = sorted(received)
    blocks = [received[flip] for flip in flips]
    return pl.pallas_call(
        functools.partial(pick_kernel, flips),
        out_shape=jax.ShapeDtypeStruct((top * tokens, blocks[0].shape[2]), jnp.bfloat16),
        compiler_params=pltpu.CompilerParams(vmem_limit_bytes=16 << 20),
    )(ids, *blocks, *kept)


def dense_device(upstream, route_ids, route_gates, weight_mat):
    tokens, top = route_ids.shape
    owners = lax.axis_size("expert")
    tie = lax.optimization_barrier

    def work(*pieces):
        return products(list(pieces), tokens, weights)

    far = send_across(upstream, owners, Z_FAR)
    rows = send_across(upstream, owners, 0)
    far = send_across(upstream, owners, Z_FAR)
    other_mat = send(weight_mat, owners, 0, 1)
    columns = gate_columns(route_ids.T, route_gates.T)
    far_columns = send(columns, owners, Z_FAR)
    weights = turned(weight_mat, other_mat)
    rows, columns, weights = tie((rows, columns, weights))
    rows = widened(rows, columns)
    side = send(rows, owners, X)
    near = send(rows, owners, Z_NEAR)
    far, far_columns, rows = tie((far, far_columns, rows))
    far = widened(far, far_columns)
    cross = send(far, owners, Z_NEAR)
    far_side = send(far, owners, X)
    (out_far,) = work(far)
    back_far = send(out_far, owners, Z_FAR)
    side, _ = tie((side, out_far))
    near, far_side, side = tie((near, far_side, side))
    near_side = send(near, owners, X)
    out_far_side, out_side = work(far_side, side)
    back_far_side = send(out_far_side, owners, X ^ Z_FAR)
    back_side = send(out_side, owners, X)
    cross, _ = tie((cross, out_far_side))
    cross_side = send(cross, owners, X)
    (out_cross,) = work(cross)
    back_cross = send(out_cross, owners, Z_NEAR ^ Z_FAR)
    near_side, back_far, back_side, _ = tie((near_side, back_far, back_side, out_cross))
    out_near, out_near_side, out_own = work(near, near_side, rows)
    back_near_side = send(out_near_side, owners, X ^ Z_NEAR)
    back_near = send(out_near, owners, Z_NEAR)
    cross_side, _ = tie((cross_side, out_near_side))
    (out_cross_side,) = work(cross_side)
    back_cross_side = send(out_cross_side, owners, X ^ Z_NEAR ^ Z_FAR)
    far_parts = {
        0: out_own,
        Z_FAR: back_far,
        X ^ Z_FAR: back_far_side,
        Z_NEAR ^ Z_FAR: back_cross,
        X ^ Z_NEAR ^ Z_FAR: back_cross_side,
    }
    near_parts = {X: back_side, Z_NEAR: back_near, X ^ Z_NEAR: back_near_side}
    out = pick_routes(route_ids.T, near_parts, pick_routes(route_ids.T, far_parts))
    return out.reshape(1, tokens, top, weight_mat.shape[0])


def slotted_device(section_grad, route_ids, route_gates, weight_mat, capacity):
    tokens, top = route_ids.shape
    owners = lax.axis_size("expert")
    ids = jnp.arange(owners, dtype=jnp.int32)
    slots = jnp.arange(capacity, dtype=jnp.int32)
    matched = (route_ids[:, :, None] == ids[None, None, :]).astype(jnp.int32)
    hits = jnp.sum(matched, axis=1)
    rank = jnp.cumsum(hits, axis=0) - hits
    position = route_ids * capacity + jnp.sum(matched * rank[:, None, :], axis=2)
    gate_owner = jnp.einsum(
        "tk,tke->te", route_gates.astype(jnp.float32), matched.astype(jnp.float32)
    )
    slot_pick = (hits[:, :, None] == 1) & (rank[:, :, None] == slots[None, None, :])
    send_rows = jnp.einsum(
        "tem,td->emd",
        slot_pick.astype(jnp.bfloat16),
        section_grad,
        preferred_element_type=jnp.float32,
    ).astype(jnp.bfloat16)
    send_gates = jnp.einsum("tem,te->em", slot_pick.astype(jnp.float32), gate_owner).astype(
        jnp.bfloat16
    )
    got_rows = lax.all_to_all(send_rows, "expert", split_axis=0, concat_axis=0, tiled=True)
    got_gates = lax.all_to_all(send_gates, "expert", split_axis=0, concat_axis=0, tiled=True)
    product = lax.dot_general(
        got_rows.reshape(owners * capacity, got_rows.shape[2]),
        weight_mat,
        (((1,), (1,)), ((), ())),
        preferred_element_type=jnp.float32,
    ).reshape(owners, capacity, weight_mat.shape[0])
    returned = lax.all_to_all(
        (product * got_gates.astype(jnp.float32)[:, :, None]).astype(jnp.bfloat16),
        "expert",
        split_axis=0,
        concat_axis=0,
        tiled=True,
    )
    flat = returned.reshape(owners * capacity, returned.shape[2])
    out = jnp.take(flat, position.reshape(tokens * top), axis=0)
    return out.reshape(1, tokens, top, returned.shape[2])


def per_device(upstream, expert_ids, gate_weights, expert_weight):
    route_ids = expert_ids[0]
    route_gates = gate_weights[0]
    weight_mat = expert_weight[0, 0]
    tokens, top = route_ids.shape
    owners = lax.axis_size("expert")
    capacity = 2 * tokens * top // owners
    if capacity >= tokens and owners == CORES * 2 * Z_FAR:
        return dense_device(upstream[0], route_ids, route_gates, weight_mat)
    section_grad = shifted(upstream, "pipe", -1)[0]
    return slotted_device(section_grad, route_ids, route_gates, weight_mat, capacity)


def solution(mesh):
    in_specs = (
        P("pipe", "expert", None),
        P("pipe", "expert", None),
        P("pipe", "expert", None),
        P("pipe", "expert", None, None),
    )
    out_specs = P("pipe", "expert", None, None)
    return jax.shard_map(
        per_device, mesh=mesh, in_specs=in_specs, out_specs=out_specs, check_vma=False
    )
```

```python
import functools

import jax
import jax.numpy as jnp
from jax import lax
from jax.experimental import pallas as pl
from jax.experimental.pallas import tpu as pltpu
from jax.sharding import PartitionSpec as P

CORES = 2
X, Z_NEAR, Z_FAR = 1, 2, 4
LANES = 128


def shifted(block, axis, distance):
    devices = range(lax.axis_size(axis))
    route = [((i - distance) % len(devices), i) for i in devices]
    return lax.ppermute(block, axis, route)


def send(block, owners, flip, core=0):
    route = [(i, ((i // CORES) ^ flip) * CORES + ((i % CORES) ^ core)) for i in range(owners)]
    return lax.ppermute(block, "expert", route)


def send_across(block, owners, flip):
    sections = lax.axis_size("pipe")
    route = []
    for s in range(sections):
        for i in range(owners):
            target = ((i // CORES) ^ flip) * CORES + i % CORES
            route.append((s * owners + i, (s - 1) % sections * owners + target))
    return lax.ppermute(block, ("pipe", "expert"), route)


def gates_kernel(ids, gates, out):
    top, tokens = ids.shape
    expert = lax.broadcasted_iota(jnp.int32, (LANES, tokens), 0)
    total = jnp.zeros((LANES, tokens), jnp.float32)
    for k in range(top):
        gate = gates[k : k + 1, :].astype(jnp.float32)
        total += jnp.where(expert == ids[k : k + 1, :], gate, 0.0)
    out[...] = total.T.astype(jnp.bfloat16)


def gate_columns(ids, gates):
    return pl.pallas_call(
        gates_kernel,
        out_shape=jax.ShapeDtypeStruct((ids.shape[1], LANES), jnp.bfloat16),
        compiler_params=pltpu.CompilerParams(vmem_limit_bytes=16 << 20),
    )(ids, gates)


def widen_kernel(rows, columns, out):
    depth = rows.shape[1]
    out[:, :depth] = rows[...]
    out[:, depth:] = columns[...]


def widened(rows, columns):
    width = rows.shape[1] + columns.shape[1]
    return pl.pallas_call(
        widen_kernel,
        out_shape=jax.ShapeDtypeStruct((rows.shape[0], width), jnp.bfloat16),
        compiler_params=pltpu.CompilerParams(vmem_limit_bytes=16 << 20),
    )(rows, columns)


def turn_kernel(weight, other, out):
    hidden = weight.shape[0]
    out[:, :hidden] = weight[...].T
    out[:, hidden:] = other[...].T


def turned(weight, other):
    hidden, depth = weight.shape
    return pl.pallas_call(
        turn_kernel,
        out_shape=jax.ShapeDtypeStruct((depth, CORES * hidden), weight.dtype),
        compiler_params=pltpu.CompilerParams(vmem_limit_bytes=24 << 20),
        cost_estimate=pl.CostEstimate(
            flops=4 * CORES * 1024 * hidden * depth, bytes_accessed=0, transcendentals=0
        ),
    )(weight, other)


def products_kernel(count, weights, *refs):
    pieces, outs = refs[:count], refs[count:]
    depth, width = weights.shape
    hidden = width // CORES
    tokens = outs[0].shape[1]
    me = lax.axis_index("expert")
    core = lax.rem(me, CORES)
    stacked = jnp.concatenate([p[...] for p in pieces], axis=0)
    gates = stacked[:, depth:].astype(jnp.float32)
    column = lax.broadcasted_iota(jnp.int32, gates.shape, 1)
    product = jnp.dot(stacked[:, :depth], weights[...], preferred_element_type=jnp.float32)
    for half, to in enumerate((core, 1 - core)):
        scale = jnp.sum(jnp.where(column == me - core + to, gates, 0.0), axis=1, keepdims=True)
        scaled = (product[:, half * hidden : (half + 1) * hidden] * scale).astype(jnp.bfloat16)
        for j, out in enumerate(outs):
            out[to] = scaled[j * tokens : (j + 1) * tokens]


def products(pieces, tokens, weights):
    depth, width = weights.shape
    total = sum(p.shape[0] for p in pieces)
    one = jax.ShapeDtypeStruct((CORES, tokens, width // CORES), jnp.bfloat16)
    return pl.pallas_call(
        functools.partial(products_kernel, len(pieces)),
        out_shape=[one] * (total // tokens),
        compiler_params=pltpu.CompilerParams(vmem_limit_bytes=16 << 20),
        cost_estimate=pl.CostEstimate(
            flops=20 * total * width * depth,
            bytes_accessed=2 * (total * (width + depth) + width * depth),
            transcendentals=0,
        ),
    )(weights, *pieces)


def pick_kernel(ids, *refs):
    blocks, out = refs[:-1], refs[-1]
    experts, tokens, _ = blocks[0].shape
    top = ids.shape[0]
    span = 16
    chip = lax.div(lax.axis_index("expert"), CORES)
    label = (lax.div(ids[...], CORES) ^ chip) * CORES + lax.rem(ids[...], CORES)
    column = lax.broadcasted_iota(jnp.int32, (top, len(blocks) * experts * span), 1)
    for g in range(tokens // span):
        stacked = jnp.concatenate(
            [b[c, g * span : (g + 1) * span, :] for b in blocks for c in range(experts)], axis=0
        )
        picks = [
            jnp.where(column == label[:, g * span + t : g * span + t + 1] * span + t, 1.0, 0.0)
            for t in range(span)
        ]
        pick = jnp.concatenate(picks, axis=0).astype(jnp.bfloat16)
        rows = jnp.dot(pick, stacked, preferred_element_type=jnp.float32)
        out[g * span * top : (g + 1) * span * top, :] = rows.astype(jnp.bfloat16)


def pick_routes(ids, blocks):
    top, tokens = ids.shape
    return pl.pallas_call(
        pick_kernel,
        out_shape=jax.ShapeDtypeStruct((top * tokens, blocks[0].shape[2]), jnp.bfloat16),
        compiler_params=pltpu.CompilerParams(vmem_limit_bytes=16 << 20),
    )(ids, *blocks)


def dense_device(upstream, route_ids, route_gates, weight_mat):
    tokens, top = route_ids.shape
    owners = lax.axis_size("expert")
    tie = lax.optimization_barrier

    def work(*pieces):
        return products(list(pieces), tokens, weights)

    far = send_across(upstream, owners, Z_FAR)
    rows = send_across(upstream, owners, 0)
    other_mat = send(weight_mat, owners, 0, 1)
    columns = gate_columns(route_ids.T, route_gates.T)
    far_columns = send(columns, owners, Z_FAR)
    weights = turned(weight_mat, other_mat)
    rows, columns, weights = tie((rows, columns, weights))
    rows = widened(rows, columns)
    side = send(rows, owners, X)
    near = send(rows, owners, Z_NEAR)
    far, far_columns, rows = tie((far, far_columns, rows))
    far = widened(far, far_columns)
    cross = send(far, owners, Z_NEAR)
    far_side = send(far, owners, X)
    (out_far,) = work(far)
    back_far = send(out_far, owners, Z_FAR)
    side, _ = tie((side, out_far))
    near, side = tie((near, side))
    near_side = send(near, owners, X)
    cross, _ = tie((cross, near))
    cross_side = send(cross, owners, X)
    (out_cross,) = work(cross)
    back_cross = send(out_cross, owners, Z_NEAR ^ Z_FAR)
    far_side, back_far, _ = tie((far_side, back_far, out_cross))
    (out_far_side,) = work(far_side)
    back_far_side = send(out_far_side, owners, X ^ Z_FAR)
    cross_side, _ = tie((cross_side, out_far_side))
    (out_cross_side,) = work(cross_side)
    back_cross_side = send(out_cross_side, owners, X ^ Z_NEAR ^ Z_FAR)
    near_side, _ = tie((near_side, out_cross_side))
    out_side, out_near, out_near_side = work(side, near, near_side)
    back_near_side = send(out_near_side, owners, X ^ Z_NEAR)
    back_side = send(out_side, owners, X)
    out_near, back_cross = tie((out_near, back_cross))
    back_near = send(out_near, owners, Z_NEAR)
    rows, _ = tie((rows, out_near_side))
    (out_own,) = work(rows)
    received = {
        0: out_own,
        X: back_side,
        Z_NEAR: back_near,
        X ^ Z_NEAR: back_near_side,
        Z_FAR: back_far,
        X ^ Z_FAR: back_far_side,
        Z_NEAR ^ Z_FAR: back_cross,
        X ^ Z_NEAR ^ Z_FAR: back_cross_side,
    }
    out = pick_routes(route_ids.T, [received[flip] for flip in sorted(received)])
    return out.reshape(1, tokens, top, weight_mat.shape[0])


def slotted_device(section_grad, route_ids, route_gates, weight_mat, capacity):
    tokens, top = route_ids.shape
    owners = lax.axis_size("expert")
    ids = jnp.arange(owners, dtype=jnp.int32)
    slots = jnp.arange(capacity, dtype=jnp.int32)
    matched = (route_ids[:, :, None] == ids[None, None, :]).astype(jnp.int32)
    hits = jnp.sum(matched, axis=1)
    rank = jnp.cumsum(hits, axis=0) - hits
    position = route_ids * capacity + jnp.sum(matched * rank[:, None, :], axis=2)
    gate_owner = jnp.einsum(
        "tk,tke->te", route_gates.astype(jnp.float32), matched.astype(jnp.float32)
    )
    slot_pick = (hits[:, :, None] == 1) & (rank[:, :, None] == slots[None, None, :])
    send_rows = jnp.einsum(
        "tem,td->emd",
        slot_pick.astype(jnp.bfloat16),
        section_grad,
        preferred_element_type=jnp.float32,
    ).astype(jnp.bfloat16)
    send_gates = jnp.einsum("tem,te->em", slot_pick.astype(jnp.float32), gate_owner).astype(
        jnp.bfloat16
    )
    got_rows = lax.all_to_all(send_rows, "expert", split_axis=0, concat_axis=0, tiled=True)
    got_gates = lax.all_to_all(send_gates, "expert", split_axis=0, concat_axis=0, tiled=True)
    product = lax.dot_general(
        got_rows.reshape(owners * capacity, got_rows.shape[2]),
        weight_mat,
        (((1,), (1,)), ((), ())),
        preferred_element_type=jnp.float32,
    ).reshape(owners, capacity, weight_mat.shape[0])
    returned = lax.all_to_all(
        (product * got_gates.astype(jnp.float32)[:, :, None]).astype(jnp.bfloat16),
        "expert",
        split_axis=0,
        concat_axis=0,
        tiled=True,
    )
    flat = returned.reshape(owners * capacity, returned.shape[2])
    out = jnp.take(flat, position.reshape(tokens * top), axis=0)
    return out.reshape(1, tokens, top, returned.shape[2])


def per_device(upstream, expert_ids, gate_weights, expert_weight):
    route_ids = expert_ids[0]
    route_gates = gate_weights[0]
    weight_mat = expert_weight[0, 0]
    tokens, top = route_ids.shape
    owners = lax.axis_size("expert")
    capacity = 2 * tokens * top // owners
    if capacity >= tokens and owners == CORES * 2 * Z_FAR:
        return dense_device(upstream[0], route_ids, route_gates, weight_mat)
    section_grad = shifted(upstream, "pipe", -1)[0]
    return slotted_device(section_grad, route_ids, route_gates, weight_mat, capacity)


def solution(mesh):
    in_specs = (
        P("pipe", "expert", None),
        P("pipe", "expert", None),
        P("pipe", "expert", None),
        P("pipe", "expert", None, None),
    )
    out_specs = P("pipe", "expert", None, None)
    return jax.shard_map(
        per_device, mesh=mesh, in_specs=in_specs, out_specs=out_specs, check_vma=False
    )
```

```python
import functools

import jax
import jax.numpy as jnp
from jax import lax
from jax.experimental import pallas as pl
from jax.experimental.pallas import tpu as pltpu
from jax.sharding import PartitionSpec as P

CORES = 2
X, Z_NEAR, Z_FAR = 1, 2, 4
LANES = 128


def shifted(block, axis, distance):
    devices = range(lax.axis_size(axis))
    route = [((i - distance) % len(devices), i) for i in devices]
    return lax.ppermute(block, axis, route)


def send(block, owners, flip, core=0):
    route = [(i, ((i // CORES) ^ flip) * CORES + ((i % CORES) ^ core)) for i in range(owners)]
    return lax.ppermute(block, "expert", route)


def send_across(block, owners, flip):
    sections = lax.axis_size("pipe")
    route = []
    for s in range(sections):
        for i in range(owners):
            target = ((i // CORES) ^ flip) * CORES + i % CORES
            route.append((s * owners + i, (s - 1) % sections * owners + target))
    return lax.ppermute(block, ("pipe", "expert"), route)


def gates_kernel(ids, gates, out):
    top, tokens = ids.shape
    expert = lax.broadcasted_iota(jnp.int32, (LANES, tokens), 0)
    total = jnp.zeros((LANES, tokens), jnp.float32)
    for k in range(top):
        gate = gates[k : k + 1, :].astype(jnp.float32)
        total += jnp.where(expert == ids[k : k + 1, :], gate, 0.0)
    out[...] = total.T.astype(jnp.bfloat16)


def gate_columns(ids, gates):
    return pl.pallas_call(
        gates_kernel,
        out_shape=jax.ShapeDtypeStruct((ids.shape[1], LANES), jnp.bfloat16),
        compiler_params=pltpu.CompilerParams(vmem_limit_bytes=16 << 20),
    )(ids, gates)


def widen_kernel(rows, columns, out):
    depth = rows.shape[1]
    out[:, :depth] = rows[...]
    out[:, depth:] = columns[...]


def widened(rows, columns):
    width = rows.shape[1] + columns.shape[1]
    return pl.pallas_call(
        widen_kernel,
        out_shape=jax.ShapeDtypeStruct((rows.shape[0], width), jnp.bfloat16),
        compiler_params=pltpu.CompilerParams(vmem_limit_bytes=16 << 20),
    )(rows, columns)


def turn_kernel(weight, other, out):
    hidden = weight.shape[0]
    out[:, :hidden] = weight[...].T
    out[:, hidden:] = other[...].T


def turned(weight, other):
    hidden, depth = weight.shape
    return pl.pallas_call(
        turn_kernel,
        out_shape=jax.ShapeDtypeStruct((depth, CORES * hidden), weight.dtype),
        compiler_params=pltpu.CompilerParams(vmem_limit_bytes=24 << 20),
        cost_estimate=pl.CostEstimate(
            flops=4 * CORES * 1024 * hidden * depth, bytes_accessed=0, transcendentals=0
        ),
    )(weight, other)


def products_kernel(count, weights, *refs):
    pieces, outs = refs[:count], refs[count:]
    depth, width = weights.shape
    hidden = width // CORES
    tokens = outs[0].shape[1]
    me = lax.axis_index("expert")
    core = lax.rem(me, CORES)
    stacked = jnp.concatenate([p[...] for p in pieces], axis=0)
    gates = stacked[:, depth:].astype(jnp.float32)
    column = lax.broadcasted_iota(jnp.int32, gates.shape, 1)
    product = jnp.dot(stacked[:, :depth], weights[...], preferred_element_type=jnp.float32)
    for half, to in enumerate((core, 1 - core)):
        scale = jnp.sum(jnp.where(column == me - core + to, gates, 0.0), axis=1, keepdims=True)
        scaled = (product[:, half * hidden : (half + 1) * hidden] * scale).astype(jnp.bfloat16)
        for j, out in enumerate(outs):
            out[to] = scaled[j * tokens : (j + 1) * tokens]


def products(pieces, tokens, weights):
    depth, width = weights.shape
    total = sum(p.shape[0] for p in pieces)
    one = jax.ShapeDtypeStruct((CORES, tokens, width // CORES), jnp.bfloat16)
    return pl.pallas_call(
        functools.partial(products_kernel, len(pieces)),
        out_shape=[one] * (total // tokens),
        compiler_params=pltpu.CompilerParams(vmem_limit_bytes=16 << 20),
        cost_estimate=pl.CostEstimate(
            flops=20 * total * width * depth,
            bytes_accessed=2 * (total * (width + depth) + width * depth),
            transcendentals=0,
        ),
    )(weights, *pieces)


def pick_kernel(ids, *refs):
    blocks, out = refs[:-1], refs[-1]
    experts, tokens, _ = blocks[0].shape
    top = ids.shape[0]
    span = 16
    chip = lax.div(lax.axis_index("expert"), CORES)
    label = (lax.div(ids[...], CORES) ^ chip) * CORES + lax.rem(ids[...], CORES)
    column = lax.broadcasted_iota(jnp.int32, (top, len(blocks) * experts * span), 1)
    for g in range(tokens // span):
        stacked = jnp.concatenate(
            [b[c, g * span : (g + 1) * span, :] for b in blocks for c in range(experts)], axis=0
        )
        picks = [
            jnp.where(column == label[:, g * span + t : g * span + t + 1] * span + t, 1.0, 0.0)
            for t in range(span)
        ]
        pick = jnp.concatenate(picks, axis=0).astype(jnp.bfloat16)
        rows = jnp.dot(pick, stacked, preferred_element_type=jnp.float32)
        out[g * span * top : (g + 1) * span * top, :] = rows.astype(jnp.bfloat16)


def pick_routes(ids, blocks):
    top, tokens = ids.shape
    return pl.pallas_call(
        pick_kernel,
        out_shape=jax.ShapeDtypeStruct((top * tokens, blocks[0].shape[2]), jnp.bfloat16),
        compiler_params=pltpu.CompilerParams(vmem_limit_bytes=16 << 20),
    )(ids, *blocks)


def dense_device(upstream, route_ids, route_gates, weight_mat):
    tokens, top = route_ids.shape
    owners = lax.axis_size("expert")
    tie = lax.optimization_barrier

    def work(*pieces):
        return products(list(pieces), tokens, weights)

    far = send_across(upstream, owners, Z_FAR)
    rows = send_across(upstream, owners, 0)
    other_mat = send(weight_mat, owners, 0, 1)
    columns = gate_columns(route_ids.T, route_gates.T)
    far_columns = send(columns, owners, Z_FAR)
    weights = turned(weight_mat, other_mat)
    rows, columns, weights = tie((rows, columns, weights))
    rows = widened(rows, columns)
    side = send(rows, owners, X)
    near = send(rows, owners, Z_NEAR)
    far, far_columns, rows = tie((far, far_columns, rows))
    far = widened(far, far_columns)
    cross = send(far, owners, Z_NEAR)
    far_side = send(far, owners, X)
    (out_far,) = work(far)
    back_far = send(out_far, owners, Z_FAR)
    side, _ = tie((side, out_far))
    near, side = tie((near, side))
    near_side = send(near, owners, X)
    cross, _ = tie((cross, near))
    cross_side = send(cross, owners, X)
    (out_cross,) = work(cross)
    back_cross = send(out_cross, owners, Z_NEAR ^ Z_FAR)
    far_side, back_far, _ = tie((far_side, back_far, out_cross))
    out_far_side, out_side, out_own = work(far_side, side, rows)
    back_far_side = send(out_far_side, owners, X ^ Z_FAR)
    cross_side, _ = tie((cross_side, out_far_side))
    (out_cross_side,) = work(cross_side)
    back_cross_side = send(out_cross_side, owners, X ^ Z_NEAR ^ Z_FAR)
    out_side, _ = tie((out_side, out_cross_side))
    back_side = send(out_side, owners, X)
    near_side, _ = tie((near_side, out_cross_side))
    out_near, out_near_side = work(near, near_side)
    back_near_side = send(out_near_side, owners, X ^ Z_NEAR)
    out_near, back_side = tie((out_near, back_side))
    back_near = send(out_near, owners, Z_NEAR)
    received = {
        0: out_own,
        X: back_side,
        Z_NEAR: back_near,
        X ^ Z_NEAR: back_near_side,
        Z_FAR: back_far,
        X ^ Z_FAR: back_far_side,
        Z_NEAR ^ Z_FAR: back_cross,
        X ^ Z_NEAR ^ Z_FAR: back_cross_side,
    }
    out = pick_routes(route_ids.T, [received[flip] for flip in sorted(received)])
    return out.reshape(1, tokens, top, weight_mat.shape[0])


def slotted_device(section_grad, route_ids, route_gates, weight_mat, capacity):
    tokens, top = route_ids.shape
    owners = lax.axis_size("expert")
    ids = jnp.arange(owners, dtype=jnp.int32)
    slots = jnp.arange(capacity, dtype=jnp.int32)
    matched = (route_ids[:, :, None] == ids[None, None, :]).astype(jnp.int32)
    hits = jnp.sum(matched, axis=1)
    rank = jnp.cumsum(hits, axis=0) - hits
    position = route_ids * capacity + jnp.sum(matched * rank[:, None, :], axis=2)
    gate_owner = jnp.einsum(
        "tk,tke->te", route_gates.astype(jnp.float32), matched.astype(jnp.float32)
    )
    slot_pick = (hits[:, :, None] == 1) & (rank[:, :, None] == slots[None, None, :])
    send_rows = jnp.einsum(
        "tem,td->emd",
        slot_pick.astype(jnp.bfloat16),
        section_grad,
        preferred_element_type=jnp.float32,
    ).astype(jnp.bfloat16)
    send_gates = jnp.einsum("tem,te->em", slot_pick.astype(jnp.float32), gate_owner).astype(
        jnp.bfloat16
    )
    got_rows = lax.all_to_all(send_rows, "expert", split_axis=0, concat_axis=0, tiled=True)
    got_gates = lax.all_to_all(send_gates, "expert", split_axis=0, concat_axis=0, tiled=True)
    product = lax.dot_general(
        got_rows.reshape(owners * capacity, got_rows.shape[2]),
        weight_mat,
        (((1,), (1,)), ((), ())),
        preferred_element_type=jnp.float32,
    ).reshape(owners, capacity, weight_mat.shape[0])
    returned = lax.all_to_all(
        (product * got_gates.astype(jnp.float32)[:, :, None]).astype(jnp.bfloat16),
        "expert",
        split_axis=0,
        concat_axis=0,
        tiled=True,
    )
    flat = returned.reshape(owners * capacity, returned.shape[2])
    out = jnp.take(flat, position.reshape(tokens * top), axis=0)
    return out.reshape(1, tokens, top, returned.shape[2])


def per_device(upstream, expert_ids, gate_weights, expert_weight):
    route_ids = expert_ids[0]
    route_gates = gate_weights[0]
    weight_mat = expert_weight[0, 0]
    tokens, top = route_ids.shape
    owners = lax.axis_size("expert")
    capacity = 2 * tokens * top // owners
    if capacity >= tokens and owners == CORES * 2 * Z_FAR:
        return dense_device(upstream[0], route_ids, route_gates, weight_mat)
    section_grad = shifted(upstream, "pipe", -1)[0]
    return slotted_device(section_grad, route_ids, route_gates, weight_mat, capacity)


def solution(mesh):
    in_specs = (
        P("pipe", "expert", None),
        P("pipe", "expert", None),
        P("pipe", "expert", None),
        P("pipe", "expert", None, None),
    )
    out_specs = P("pipe", "expert", None, None)
    return jax.shard_map(
        per_device, mesh=mesh, in_specs=in_specs, out_specs=out_specs, check_vma=False
    )
```

```python
import functools

import jax
import jax.numpy as jnp
from jax import lax
from jax.experimental import pallas as pl
from jax.experimental.pallas import tpu as pltpu
from jax.sharding import PartitionSpec as P

CORES = 2
X, Z_NEAR, Z_FAR = 1, 2, 4
LANES = 128


def shifted(block, axis, distance):
    devices = range(lax.axis_size(axis))
    route = [((i - distance) % len(devices), i) for i in devices]
    return lax.ppermute(block, axis, route)


def send(block, owners, flip, core=0):
    route = [(i, ((i // CORES) ^ flip) * CORES + ((i % CORES) ^ core)) for i in range(owners)]
    return lax.ppermute(block, "expert", route)


def send_across(block, owners, flip):
    sections = lax.axis_size("pipe")
    route = []
    for s in range(sections):
        for i in range(owners):
            target = ((i // CORES) ^ flip) * CORES + i % CORES
            route.append((s * owners + i, (s - 1) % sections * owners + target))
    return lax.ppermute(block, ("pipe", "expert"), route)


def gates_kernel(ids, gates, out):
    top, tokens = ids.shape
    expert = lax.broadcasted_iota(jnp.int32, (LANES, tokens), 0)
    total = jnp.zeros((LANES, tokens), jnp.float32)
    for k in range(top):
        gate = gates[k : k + 1, :].astype(jnp.float32)
        total += jnp.where(expert == ids[k : k + 1, :], gate, 0.0)
    out[...] = total.T.astype(jnp.bfloat16)


def gate_columns(ids, gates):
    return pl.pallas_call(
        gates_kernel,
        out_shape=jax.ShapeDtypeStruct((ids.shape[1], LANES), jnp.bfloat16),
        compiler_params=pltpu.CompilerParams(vmem_limit_bytes=16 << 20),
    )(ids, gates)


def widen_kernel(rows, columns, out):
    depth = rows.shape[1]
    out[:, :depth] = rows[...]
    out[:, depth:] = columns[...]


def widened(rows, columns):
    width = rows.shape[1] + columns.shape[1]
    return pl.pallas_call(
        widen_kernel,
        out_shape=jax.ShapeDtypeStruct((rows.shape[0], width), jnp.bfloat16),
        compiler_params=pltpu.CompilerParams(vmem_limit_bytes=16 << 20),
    )(rows, columns)


def turn_kernel(weight, other, out):
    hidden = weight.shape[0]
    out[:, :hidden] = weight[...].T
    out[:, hidden:] = other[...].T


def turned(weight, other):
    hidden, depth = weight.shape
    return pl.pallas_call(
        turn_kernel,
        out_shape=jax.ShapeDtypeStruct((depth, CORES * hidden), weight.dtype),
        compiler_params=pltpu.CompilerParams(vmem_limit_bytes=24 << 20),
        cost_estimate=pl.CostEstimate(
            flops=4 * CORES * 1024 * hidden * depth, bytes_accessed=0, transcendentals=0
        ),
    )(weight, other)


def products_kernel(count, weights, *refs):
    pieces, outs = refs[:count], refs[count:]
    depth, width = weights.shape
    hidden = width // CORES
    tokens = outs[0].shape[1]
    me = lax.axis_index("expert")
    core = lax.rem(me, CORES)
    stacked = jnp.concatenate([p[...] for p in pieces], axis=0)
    gates = stacked[:, depth:].astype(jnp.float32)
    column = lax.broadcasted_iota(jnp.int32, gates.shape, 1)
    product = jnp.dot(stacked[:, :depth], weights[...], preferred_element_type=jnp.float32)
    for half, to in enumerate((core, 1 - core)):
        scale = jnp.sum(jnp.where(column == me - core + to, gates, 0.0), axis=1, keepdims=True)
        scaled = (product[:, half * hidden : (half + 1) * hidden] * scale).astype(jnp.bfloat16)
        for j, out in enumerate(outs):
            out[to] = scaled[j * tokens : (j + 1) * tokens]


def products(pieces, tokens, weights):
    depth, width = weights.shape
    total = sum(p.shape[0] for p in pieces)
    one = jax.ShapeDtypeStruct((CORES, tokens, width // CORES), jnp.bfloat16)
    return pl.pallas_call(
        functools.partial(products_kernel, len(pieces)),
        out_shape=[one] * (total // tokens),
        compiler_params=pltpu.CompilerParams(vmem_limit_bytes=16 << 20),
        cost_estimate=pl.CostEstimate(
            flops=20 * total * width * depth,
            bytes_accessed=2 * (total * (width + depth) + width * depth),
            transcendentals=0,
        ),
    )(weights, *pieces)


def group_kernel(flips, weights, *refs):
    pieces, out = refs[: len(flips)], refs[len(flips)]
    depth, width = weights.shape
    hidden = width // CORES
    tokens = out.shape[2]
    me = lax.axis_index("expert")
    core, chip = lax.rem(me, CORES), lax.div(me, CORES)
    stacked = jnp.concatenate([p[...] for p in pieces], axis=0)
    gates = stacked[:, depth:].astype(jnp.float32)
    column = lax.broadcasted_iota(jnp.int32, gates.shape, 1)
    product = jnp.dot(stacked[:, :depth], weights[...], preferred_element_type=jnp.float32)
    for half, to in enumerate((core, 1 - core)):
        scale = jnp.sum(jnp.where(column == me - core + to, gates, 0.0), axis=1, keepdims=True)
        scaled = (product[:, half * hidden : (half + 1) * hidden] * scale).astype(jnp.bfloat16)
        for j, flip in enumerate(flips):
            slot = lax.rem(chip, len(flips)) ^ flip
            out[slot, to] = scaled[j * tokens : (j + 1) * tokens]


def group_results(pieces, tokens, weights):
    flips = sorted(pieces)
    depth, width = weights.shape
    shape = (len(flips), CORES, tokens, width // CORES)
    return pl.pallas_call(
        functools.partial(group_kernel, flips),
        out_shape=jax.ShapeDtypeStruct(shape, jnp.bfloat16),
        compiler_params=pltpu.CompilerParams(vmem_limit_bytes=16 << 20),
        cost_estimate=pl.CostEstimate(
            flops=20 * len(flips) * tokens * width * depth,
            bytes_accessed=2 * (len(flips) * tokens * (width + depth) + width * depth),
            transcendentals=0,
        ),
    )(weights, *[pieces[flip] for flip in flips])


def pick_kernel(flips, ids, *refs):
    count = len(flips) or 1
    blocks, kept, out = refs[:count], refs[count:-1], refs[-1]
    top, tokens = ids.shape
    span = 16
    chip = lax.div(lax.axis_index("expert"), CORES)
    owner, core = lax.div(ids[...], CORES), lax.rem(ids[...], CORES)
    if flips:
        parts = [(b, (c,)) for b in blocks for c in range(CORES)]
        place = jnp.full(owner.shape, -1, jnp.int32)
        for j, flip in enumerate(flips):
            place = jnp.where((owner ^ chip) == flip, j * CORES + core, place)
    else:
        size = blocks[0].shape[0]
        parts = [(blocks[0], (j, c)) for j in range(size) for c in range(CORES)]
        mine = lax.div(owner, size) == lax.div(chip, size)
        place = jnp.where(mine, lax.rem(owner, size) * CORES + core, -1)
    column = lax.broadcasted_iota(jnp.int32, (top, len(parts) * span), 1)
    for g in range(tokens // span):
        rows = slice(g * span, (g + 1) * span)
        stacked = jnp.concatenate([b[(*at, rows)] for b, at in parts], axis=0)
        picks = [
            jnp.where(column == place[:, g * span + t : g * span + t + 1] * span + t, 1.0, 0.0)
            for t in range(span)
        ]
        pick = jnp.concatenate(picks, axis=0).astype(jnp.bfloat16)
        found = jnp.dot(pick, stacked, preferred_element_type=jnp.float32).astype(jnp.bfloat16)
        routes = slice(g * span * top, (g + 1) * span * top)
        out[routes, :] = found + kept[0][routes, :] if kept else found


def pick_routes(ids, blocks, *kept):
    top, tokens = ids.shape
    flips = sorted(blocks) if isinstance(blocks, dict) else []
    arrays = [blocks[flip] for flip in flips] if flips else [blocks]
    return pl.pallas_call(
        functools.partial(pick_kernel, flips),
        out_shape=jax.ShapeDtypeStruct((top * tokens, arrays[0].shape[-1]), jnp.bfloat16),
        compiler_params=pltpu.CompilerParams(vmem_limit_bytes=16 << 20),
    )(ids, *arrays, *kept)


def dense_device(upstream, route_ids, route_gates, weight_mat):
    tokens, top = route_ids.shape
    owners = lax.axis_size("expert")
    tie = lax.optimization_barrier

    def work(*pieces):
        return products(list(pieces), tokens, weights)

    far = send_across(upstream, owners, Z_FAR)
    rows = send_across(upstream, owners, 0)
    other_mat = send(weight_mat, owners, 0, 1)
    columns = gate_columns(route_ids.T, route_gates.T)
    far_columns = send(columns, owners, Z_FAR)
    weights = turned(weight_mat, other_mat)
    rows, columns, weights = tie((rows, columns, weights))
    rows = widened(rows, columns)
    side = send(rows, owners, X)
    near = send(rows, owners, Z_NEAR)
    far, far_columns, rows = tie((far, far_columns, rows))
    far = widened(far, far_columns)
    cross = send(far, owners, Z_NEAR)
    far_side = send(far, owners, X)
    (out_far,) = work(far)
    back_far = send(out_far, owners, Z_FAR)
    side, _ = tie((side, out_far))
    near, side = tie((near, side))
    near_side = send(near, owners, X)
    cross, _ = tie((cross, near))
    cross_side = send(cross, owners, X)
    (out_cross,) = work(cross)
    back_cross = send(out_cross, owners, Z_NEAR ^ Z_FAR)
    far_side, back_far, _ = tie((far_side, back_far, out_cross))
    (out_far_side,) = work(far_side)
    back_far_side = send(out_far_side, owners, X ^ Z_FAR)
    cross_side, _ = tie((cross_side, out_far_side))
    (out_cross_side,) = work(cross_side)
    back_cross_side = send(out_cross_side, owners, X ^ Z_NEAR ^ Z_FAR)
    near_side, rows, _ = tie((near_side, rows, out_cross_side))
    family = {0: rows, X: side, Z_NEAR: near, X ^ Z_NEAR: near_side}
    found = group_results(family, tokens, weights)
    span = Z_FAR * CORES
    groups = [
        [first + core + CORES * j for j in range(Z_FAR)]
        for first in range(0, owners, span)
        for core in range(CORES)
    ]
    back_near = lax.all_to_all(
        found.reshape(Z_FAR, CORES * tokens, found.shape[3]),
        "expert",
        split_axis=0,
        concat_axis=0,
        tiled=True,
        axis_index_groups=groups,
    ).reshape(found.shape)
    far_parts = {
        Z_FAR: back_far,
        X ^ Z_FAR: back_far_side,
        Z_NEAR ^ Z_FAR: back_cross,
        X ^ Z_NEAR ^ Z_FAR: back_cross_side,
    }
    out = pick_routes(route_ids.T, far_parts, pick_routes(route_ids.T, back_near))
    return out.reshape(1, tokens, top, weight_mat.shape[0])


def slotted_device(section_grad, route_ids, route_gates, weight_mat, capacity):
    tokens, top = route_ids.shape
    owners = lax.axis_size("expert")
    ids = jnp.arange(owners, dtype=jnp.int32)
    slots = jnp.arange(capacity, dtype=jnp.int32)
    matched = (route_ids[:, :, None] == ids[None, None, :]).astype(jnp.int32)
    hits = jnp.sum(matched, axis=1)
    rank = jnp.cumsum(hits, axis=0) - hits
    position = route_ids * capacity + jnp.sum(matched * rank[:, None, :], axis=2)
    gate_owner = jnp.einsum(
        "tk,tke->te", route_gates.astype(jnp.float32), matched.astype(jnp.float32)
    )
    slot_pick = (hits[:, :, None] == 1) & (rank[:, :, None] == slots[None, None, :])
    send_rows = jnp.einsum(
        "tem,td->emd",
        slot_pick.astype(jnp.bfloat16),
        section_grad,
        preferred_element_type=jnp.float32,
    ).astype(jnp.bfloat16)
    send_gates = jnp.einsum("tem,te->em", slot_pick.astype(jnp.float32), gate_owner).astype(
        jnp.bfloat16
    )
    got_rows = lax.all_to_all(send_rows, "expert", split_axis=0, concat_axis=0, tiled=True)
    got_gates = lax.all_to_all(send_gates, "expert", split_axis=0, concat_axis=0, tiled=True)
    product = lax.dot_general(
        got_rows.reshape(owners * capacity, got_rows.shape[2]),
        weight_mat,
        (((1,), (1,)), ((), ())),
        preferred_element_type=jnp.float32,
    ).reshape(owners, capacity, weight_mat.shape[0])
    returned = lax.all_to_all(
        (product * got_gates.astype(jnp.float32)[:, :, None]).astype(jnp.bfloat16),
        "expert",
        split_axis=0,
        concat_axis=0,
        tiled=True,
    )
    flat = returned.reshape(owners * capacity, returned.shape[2])
    out = jnp.take(flat, position.reshape(tokens * top), axis=0)
    return out.reshape(1, tokens, top, returned.shape[2])


def per_device(upstream, expert_ids, gate_weights, expert_weight):
    route_ids = expert_ids[0]
    route_gates = gate_weights[0]
    weight_mat = expert_weight[0, 0]
    tokens, top = route_ids.shape
    owners = lax.axis_size("expert")
    capacity = 2 * tokens * top // owners
    if capacity >= tokens and owners == CORES * 2 * Z_FAR:
        return dense_device(upstream[0], route_ids, route_gates, weight_mat)
    section_grad = shifted(upstream, "pipe", -1)[0]
    return slotted_device(section_grad, route_ids, route_gates, weight_mat, capacity)


def solution(mesh):
    in_specs = (
        P("pipe", "expert", None),
        P("pipe", "expert", None),
        P("pipe", "expert", None),
        P("pipe", "expert", None, None),
    )
    out_specs = P("pipe", "expert", None, None)
    return jax.shard_map(
        per_device, mesh=mesh, in_specs=in_specs, out_specs=out_specs, check_vma=False
    )
```

```python
import functools

import jax
import jax.numpy as jnp
from jax import lax
from jax.experimental import pallas as pl
from jax.experimental.pallas import tpu as pltpu
from jax.sharding import PartitionSpec as P

CORES = 2
X, Z_NEAR, Z_FAR = 1, 2, 4
LANES = 128


def shifted(block, axis, distance):
    devices = range(lax.axis_size(axis))
    route = [((i - distance) % len(devices), i) for i in devices]
    return lax.ppermute(block, axis, route)


def send(block, owners, flip, core=0):
    route = [(i, ((i // CORES) ^ flip) * CORES + ((i % CORES) ^ core)) for i in range(owners)]
    return lax.ppermute(block, "expert", route)


def send_across(block, owners, flip):
    sections = lax.axis_size("pipe")
    route = []
    for s in range(sections):
        for i in range(owners):
            target = ((i // CORES) ^ flip) * CORES + i % CORES
            route.append((s * owners + i, (s - 1) % sections * owners + target))
    return lax.ppermute(block, ("pipe", "expert"), route)


def gates_kernel(ids, gates, out):
    top, tokens = ids.shape
    expert = lax.broadcasted_iota(jnp.int32, (LANES, tokens), 0)
    total = jnp.zeros((LANES, tokens), jnp.float32)
    for k in range(top):
        gate = gates[k : k + 1, :].astype(jnp.float32)
        total += jnp.where(expert == ids[k : k + 1, :], gate, 0.0)
    out[...] = total.T.astype(jnp.bfloat16)


def gate_columns(ids, gates):
    return pl.pallas_call(
        gates_kernel,
        out_shape=jax.ShapeDtypeStruct((ids.shape[1], LANES), jnp.bfloat16),
        compiler_params=pltpu.CompilerParams(vmem_limit_bytes=16 << 20),
    )(ids, gates)


def widen_kernel(rows, columns, out):
    depth = rows.shape[1]
    out[:, :depth] = rows[...]
    out[:, depth:] = columns[...]


def widened(rows, columns):
    width = rows.shape[1] + columns.shape[1]
    return pl.pallas_call(
        widen_kernel,
        out_shape=jax.ShapeDtypeStruct((rows.shape[0], width), jnp.bfloat16),
        compiler_params=pltpu.CompilerParams(vmem_limit_bytes=16 << 20),
    )(rows, columns)


def turn_kernel(weight, other, out):
    hidden = weight.shape[0]
    out[:, :hidden] = weight[...].T
    out[:, hidden:] = other[...].T


def turned(weight, other):
    hidden, depth = weight.shape
    return pl.pallas_call(
        turn_kernel,
        out_shape=jax.ShapeDtypeStruct((depth, CORES * hidden), weight.dtype),
        compiler_params=pltpu.CompilerParams(vmem_limit_bytes=24 << 20),
        cost_estimate=pl.CostEstimate(
            flops=4 * CORES * 1024 * hidden * depth, bytes_accessed=0, transcendentals=0
        ),
    )(weight, other)


def products_kernel(count, weights, *refs):
    pieces, outs = refs[:count], refs[count:]
    depth, width = weights.shape
    hidden = width // CORES
    tokens = outs[0].shape[1]
    me = lax.axis_index("expert")
    core = lax.rem(me, CORES)
    stacked = jnp.concatenate([p[...] for p in pieces], axis=0)
    gates = stacked[:, depth:].astype(jnp.float32)
    column = lax.broadcasted_iota(jnp.int32, gates.shape, 1)
    product = jnp.dot(stacked[:, :depth], weights[...], preferred_element_type=jnp.float32)
    for half, to in enumerate((core, 1 - core)):
        scale = jnp.sum(jnp.where(column == me - core + to, gates, 0.0), axis=1, keepdims=True)
        scaled = (product[:, half * hidden : (half + 1) * hidden] * scale).astype(jnp.bfloat16)
        for j, out in enumerate(outs):
            out[to] = scaled[j * tokens : (j + 1) * tokens]


def products(pieces, tokens, weights):
    depth, width = weights.shape
    total = sum(p.shape[0] for p in pieces)
    one = jax.ShapeDtypeStruct((CORES, tokens, width // CORES), jnp.bfloat16)
    return pl.pallas_call(
        functools.partial(products_kernel, len(pieces)),
        out_shape=[one] * (total // tokens),
        compiler_params=pltpu.CompilerParams(vmem_limit_bytes=16 << 20),
        cost_estimate=pl.CostEstimate(
            flops=20 * total * width * depth,
            bytes_accessed=2 * (total * (width + depth) + width * depth),
            transcendentals=0,
        ),
    )(weights, *pieces)


def group_kernel(flips, weights, *refs):
    pieces, out = refs[: len(flips)], refs[len(flips)]
    depth, width = weights.shape
    hidden = width // CORES
    tokens = out.shape[2]
    me = lax.axis_index("expert")
    core, chip = lax.rem(me, CORES), lax.div(me, CORES)
    stacked = jnp.concatenate([p[...] for p in pieces], axis=0)
    gates = stacked[:, depth:].astype(jnp.float32)
    column = lax.broadcasted_iota(jnp.int32, gates.shape, 1)
    product = jnp.dot(stacked[:, :depth], weights[...], preferred_element_type=jnp.float32)
    for half, to in enumerate((core, 1 - core)):
        scale = jnp.sum(jnp.where(column == me - core + to, gates, 0.0), axis=1, keepdims=True)
        scaled = (product[:, half * hidden : (half + 1) * hidden] * scale).astype(jnp.bfloat16)
        for j, flip in enumerate(flips):
            slot = lax.rem(chip, len(flips)) ^ flip
            out[slot, to] = scaled[j * tokens : (j + 1) * tokens]


def group_results(pieces, tokens, weights):
    flips = sorted(pieces)
    depth, width = weights.shape
    shape = (len(flips), CORES, tokens, width // CORES)
    return pl.pallas_call(
        functools.partial(group_kernel, flips),
        out_shape=jax.ShapeDtypeStruct(shape, jnp.bfloat16),
        compiler_params=pltpu.CompilerParams(vmem_limit_bytes=16 << 20),
        cost_estimate=pl.CostEstimate(
            flops=20 * len(flips) * tokens * width * depth,
            bytes_accessed=2 * (len(flips) * tokens * (width + depth) + width * depth),
            transcendentals=0,
        ),
    )(weights, *[pieces[flip] for flip in flips])


def pick_kernel(flips, ids, *refs):
    count = len(flips) or 1
    blocks, kept, out = refs[:count], refs[count:-1], refs[-1]
    top, tokens = ids.shape
    span = 16
    chip = lax.div(lax.axis_index("expert"), CORES)
    owner, core = lax.div(ids[...], CORES), lax.rem(ids[...], CORES)
    if flips:
        parts = [(b, (c,)) for b in blocks for c in range(CORES)]
        place = jnp.full(owner.shape, -1, jnp.int32)
        for j, flip in enumerate(flips):
            place = jnp.where((owner ^ chip) == flip, j * CORES + core, place)
    else:
        size = blocks[0].shape[0]
        parts = [(blocks[0], (j, c)) for j in range(size) for c in range(CORES)]
        mine = lax.div(owner, size) == lax.div(chip, size)
        place = jnp.where(mine, lax.rem(owner, size) * CORES + core, -1)
    column = lax.broadcasted_iota(jnp.int32, (top, len(parts) * span), 1)
    for g in range(tokens // span):
        rows = slice(g * span, (g + 1) * span)
        stacked = jnp.concatenate([b[(*at, rows)] for b, at in parts], axis=0)
        picks = [
            jnp.where(column == place[:, g * span + t : g * span + t + 1] * span + t, 1.0, 0.0)
            for t in range(span)
        ]
        pick = jnp.concatenate(picks, axis=0).astype(jnp.bfloat16)
        found = jnp.dot(pick, stacked, preferred_element_type=jnp.float32).astype(jnp.bfloat16)
        routes = slice(g * span * top, (g + 1) * span * top)
        out[routes, :] = found + kept[0][routes, :] if kept else found


def pick_routes(ids, blocks, *kept):
    top, tokens = ids.shape
    flips = sorted(blocks) if isinstance(blocks, dict) else []
    arrays = [blocks[flip] for flip in flips] if flips else [blocks]
    return pl.pallas_call(
        functools.partial(pick_kernel, flips),
        out_shape=jax.ShapeDtypeStruct((top * tokens, arrays[0].shape[-1]), jnp.bfloat16),
        compiler_params=pltpu.CompilerParams(vmem_limit_bytes=16 << 20),
    )(ids, *arrays, *kept)


def dense_device(upstream, route_ids, route_gates, weight_mat):
    tokens, top = route_ids.shape
    owners = lax.axis_size("expert")
    tie = lax.optimization_barrier

    def work(*pieces):
        return products(list(pieces), tokens, weights)

    far = send_across(upstream, owners, Z_FAR)
    rows = send_across(upstream, owners, 0)
    other_mat = send(weight_mat, owners, 0, 1)
    columns = gate_columns(route_ids.T, route_gates.T)
    far_columns = send(columns, owners, Z_FAR)
    weights = turned(weight_mat, other_mat)
    rows, columns, weights = tie((rows, columns, weights))
    rows = widened(rows, columns)
    side = send(rows, owners, X)
    near = send(rows, owners, Z_NEAR)
    far, far_columns, rows = tie((far, far_columns, rows))
    far = widened(far, far_columns)
    cross = send(far, owners, Z_NEAR)
    far_side = send(far, owners, X)
    (out_far,) = work(far)
    back_far = send(out_far, owners, Z_FAR)
    side, _ = tie((side, out_far))
    near, side = tie((near, side))
    near_side = send(near, owners, X)
    cross, _ = tie((cross, near))
    cross_side = send(cross, owners, X)
    (out_cross,) = work(cross)
    back_cross = send(out_cross, owners, Z_NEAR ^ Z_FAR)
    far_side, back_far, _ = tie((far_side, back_far, out_cross))
    (out_far_side,) = work(far_side)
    back_far_side = send(out_far_side, owners, X ^ Z_FAR)
    cross_side, _ = tie((cross_side, out_far_side))
    (out_cross_side,) = work(cross_side)
    back_cross_side = send(out_cross_side, owners, X ^ Z_NEAR ^ Z_FAR)
    near_side, rows, _ = tie((near_side, rows, out_cross_side))
    family = {0: rows, X: side, Z_NEAR: near, X ^ Z_NEAR: near_side}
    found = group_results(family, tokens, weights)
    span = Z_FAR * CORES
    groups = [
        [first + core + CORES * j for j in range(Z_FAR)]
        for first in range(0, owners, span)
        for core in range(CORES)
    ]
    back_near = lax.all_to_all(
        found.reshape(Z_FAR, CORES * tokens, found.shape[3]),
        "expert",
        split_axis=0,
        concat_axis=0,
        tiled=True,
        axis_index_groups=groups,
    ).reshape(found.shape)
    far_parts = {
        Z_FAR: back_far,
        X ^ Z_FAR: back_far_side,
        Z_NEAR ^ Z_FAR: back_cross,
        X ^ Z_NEAR ^ Z_FAR: back_cross_side,
    }
    out = pick_routes(route_ids.T, back_near, pick_routes(route_ids.T, far_parts))
    return out.reshape(1, tokens, top, weight_mat.shape[0])


def slotted_device(section_grad, route_ids, route_gates, weight_mat, capacity):
    tokens, top = route_ids.shape
    owners = lax.axis_size("expert")
    ids = jnp.arange(owners, dtype=jnp.int32)
    slots = jnp.arange(capacity, dtype=jnp.int32)
    matched = (route_ids[:, :, None] == ids[None, None, :]).astype(jnp.int32)
    hits = jnp.sum(matched, axis=1)
    rank = jnp.cumsum(hits, axis=0) - hits
    position = route_ids * capacity + jnp.sum(matched * rank[:, None, :], axis=2)
    gate_owner = jnp.einsum(
        "tk,tke->te", route_gates.astype(jnp.float32), matched.astype(jnp.float32)
    )
    slot_pick = (hits[:, :, None] == 1) & (rank[:, :, None] == slots[None, None, :])
    send_rows = jnp.einsum(
        "tem,td->emd",
        slot_pick.astype(jnp.bfloat16),
        section_grad,
        preferred_element_type=jnp.float32,
    ).astype(jnp.bfloat16)
    send_gates = jnp.einsum("tem,te->em", slot_pick.astype(jnp.float32), gate_owner).astype(
        jnp.bfloat16
    )
    got_rows = lax.all_to_all(send_rows, "expert", split_axis=0, concat_axis=0, tiled=True)
    got_gates = lax.all_to_all(send_gates, "expert", split_axis=0, concat_axis=0, tiled=True)
    product = lax.dot_general(
        got_rows.reshape(owners * capacity, got_rows.shape[2]),
        weight_mat,
        (((1,), (1,)), ((), ())),
        preferred_element_type=jnp.float32,
    ).reshape(owners, capacity, weight_mat.shape[0])
    returned = lax.all_to_all(
        (product * got_gates.astype(jnp.float32)[:, :, None]).astype(jnp.bfloat16),
        "expert",
        split_axis=0,
        concat_axis=0,
        tiled=True,
    )
    flat = returned.reshape(owners * capacity, returned.shape[2])
    out = jnp.take(flat, position.reshape(tokens * top), axis=0)
    return out.reshape(1, tokens, top, returned.shape[2])


def per_device(upstream, expert_ids, gate_weights, expert_weight):
    route_ids = expert_ids[0]
    route_gates = gate_weights[0]
    weight_mat = expert_weight[0, 0]
    tokens, top = route_ids.shape
    owners = lax.axis_size("expert")
    capacity = 2 * tokens * top // owners
    if capacity >= tokens and owners == CORES * 2 * Z_FAR:
        return dense_device(upstream[0], route_ids, route_gates, weight_mat)
    section_grad = shifted(upstream, "pipe", -1)[0]
    return slotted_device(section_grad, route_ids, route_gates, weight_mat, capacity)


def solution(mesh):
    in_specs = (
        P("pipe", "expert", None),
        P("pipe", "expert", None),
        P("pipe", "expert", None),
        P("pipe", "expert", None, None),
    )
    out_specs = P("pipe", "expert", None, None)
    return jax.shard_map(
        per_device, mesh=mesh, in_specs=in_specs, out_specs=out_specs, check_vma=False
    )
```

```python
import functools

import jax
import jax.numpy as jnp
from jax import lax
from jax.experimental import pallas as pl
from jax.experimental.pallas import tpu as pltpu
from jax.sharding import PartitionSpec as P

CORES = 2
X, Z_NEAR, Z_FAR = 1, 2, 4
LANES = 128


def shifted(block, axis, distance):
    devices = range(lax.axis_size(axis))
    route = [((i - distance) % len(devices), i) for i in devices]
    return lax.ppermute(block, axis, route)


def send(block, owners, flip, core=0):
    route = [(i, ((i // CORES) ^ flip) * CORES + ((i % CORES) ^ core)) for i in range(owners)]
    return lax.ppermute(block, "expert", route)


def send_across(block, owners, flip):
    sections = lax.axis_size("pipe")
    route = []
    for s in range(sections):
        for i in range(owners):
            target = ((i // CORES) ^ flip) * CORES + i % CORES
            route.append((s * owners + i, (s - 1) % sections * owners + target))
    return lax.ppermute(block, ("pipe", "expert"), route)


def gates_kernel(ids, gates, out):
    top, tokens = ids.shape
    expert = lax.broadcasted_iota(jnp.int32, (LANES, tokens), 0)
    total = jnp.zeros((LANES, tokens), jnp.float32)
    for k in range(top):
        gate = gates[k : k + 1, :].astype(jnp.float32)
        total += jnp.where(expert == ids[k : k + 1, :], gate, 0.0)
    out[...] = total.T.astype(jnp.bfloat16)


def gate_columns(ids, gates):
    return pl.pallas_call(
        gates_kernel,
        out_shape=jax.ShapeDtypeStruct((ids.shape[1], LANES), jnp.bfloat16),
        compiler_params=pltpu.CompilerParams(vmem_limit_bytes=16 << 20),
    )(ids, gates)


def widen_kernel(rows, columns, out):
    depth = rows.shape[1]
    out[:, :depth] = rows[...]
    out[:, depth:] = columns[...]


def widened(rows, columns):
    width = rows.shape[1] + columns.shape[1]
    return pl.pallas_call(
        widen_kernel,
        out_shape=jax.ShapeDtypeStruct((rows.shape[0], width), jnp.bfloat16),
        compiler_params=pltpu.CompilerParams(vmem_limit_bytes=16 << 20),
    )(rows, columns)


def turn_kernel(weight, other, out):
    hidden = weight.shape[0]
    out[:, :hidden] = weight[...].T
    out[:, hidden:] = other[...].T


def turned(weight, other):
    hidden, depth = weight.shape
    return pl.pallas_call(
        turn_kernel,
        out_shape=jax.ShapeDtypeStruct((depth, CORES * hidden), weight.dtype),
        compiler_params=pltpu.CompilerParams(vmem_limit_bytes=24 << 20),
        cost_estimate=pl.CostEstimate(
            flops=4 * CORES * 1024 * hidden * depth, bytes_accessed=0, transcendentals=0
        ),
    )(weight, other)


def products_kernel(count, weights, *refs):
    pieces, outs = refs[:count], refs[count:]
    depth, width = weights.shape
    hidden = width // CORES
    tokens = outs[0].shape[1]
    me = lax.axis_index("expert")
    core = lax.rem(me, CORES)
    stacked = jnp.concatenate([p[...] for p in pieces], axis=0)
    gates = stacked[:, depth:].astype(jnp.float32)
    column = lax.broadcasted_iota(jnp.int32, gates.shape, 1)
    product = jnp.dot(stacked[:, :depth], weights[...], preferred_element_type=jnp.float32)
    for half, to in enumerate((core, 1 - core)):
        scale = jnp.sum(jnp.where(column == me - core + to, gates, 0.0), axis=1, keepdims=True)
        scaled = (product[:, half * hidden : (half + 1) * hidden] * scale).astype(jnp.bfloat16)
        for j, out in enumerate(outs):
            out[to] = scaled[j * tokens : (j + 1) * tokens]


def products(pieces, tokens, weights):
    depth, width = weights.shape
    total = sum(p.shape[0] for p in pieces)
    one = jax.ShapeDtypeStruct((CORES, tokens, width // CORES), jnp.bfloat16)
    return pl.pallas_call(
        functools.partial(products_kernel, len(pieces)),
        out_shape=[one] * (total // tokens),
        compiler_params=pltpu.CompilerParams(vmem_limit_bytes=16 << 20),
        cost_estimate=pl.CostEstimate(
            flops=20 * total * width * depth,
            bytes_accessed=2 * (total * (width + depth) + width * depth),
            transcendentals=0,
        ),
    )(weights, *pieces)


def pick_kernel(flips, ids, *refs):
    blocks, kept, out = refs[: len(flips)], refs[len(flips) : -1], refs[-1]
    experts, tokens, _ = blocks[0].shape
    top = ids.shape[0]
    span = 16
    chip = lax.div(lax.axis_index("expert"), CORES)
    flip = lax.div(ids[...], CORES) ^ chip
    place = jnp.full(flip.shape, -1, jnp.int32)
    for j, known in enumerate(flips):
        place = jnp.where(flip == known, j * CORES + lax.rem(ids[...], CORES), place)
    column = lax.broadcasted_iota(jnp.int32, (top, len(blocks) * experts * span), 1)
    for g in range(tokens // span):
        stacked = jnp.concatenate(
            [b[c, g * span : (g + 1) * span, :] for b in blocks for c in range(experts)], axis=0
        )
        picks = [
            jnp.where(column == place[:, g * span + t : g * span + t + 1] * span + t, 1.0, 0.0)
            for t in range(span)
        ]
        pick = jnp.concatenate(picks, axis=0).astype(jnp.bfloat16)
        rows = jnp.dot(pick, stacked, preferred_element_type=jnp.float32).astype(jnp.bfloat16)
        part = slice(g * span * top, (g + 1) * span * top)
        out[part, :] = rows + kept[0][part, :] if kept else rows


def pick_routes(ids, received, *kept):
    top, tokens = ids.shape
    flips = sorted(received)
    blocks = [received[flip] for flip in flips]
    return pl.pallas_call(
        functools.partial(pick_kernel, flips),
        out_shape=jax.ShapeDtypeStruct((top * tokens, blocks[0].shape[2]), jnp.bfloat16),
        compiler_params=pltpu.CompilerParams(vmem_limit_bytes=16 << 20),
    )(ids, *blocks, *kept)


def dense_device(upstream, route_ids, route_gates, weight_mat):
    tokens, top = route_ids.shape
    owners = lax.axis_size("expert")
    tie = lax.optimization_barrier

    def work(*pieces):
        return products(list(pieces), tokens, weights)

    far = send_across(upstream, owners, Z_FAR)
    rows = send_across(upstream, owners, 0)
    other_mat = send(weight_mat, owners, 0, 1)
    columns = gate_columns(route_ids.T, route_gates.T)
    far_columns = send(columns, owners, Z_FAR)
    upstream, columns = tie((upstream, columns))
    near = send_across(upstream, owners, Z_NEAR)
    near_columns = send(columns, owners, Z_NEAR)
    weights = turned(weight_mat, other_mat)
    rows, columns, weights, near_columns = tie((rows, columns, weights, near_columns))
    rows = widened(rows, columns)
    side = send(rows, owners, X)
    far, far_columns, rows = tie((far, far_columns, rows))
    far = widened(far, far_columns)
    cross = send(far, owners, Z_NEAR)
    far_side = send(far, owners, X)
    (out_far,) = work(far)
    back_far = send(out_far, owners, Z_FAR)
    side, _ = tie((side, out_far))
    near, side = tie((near, side))
    near = widened(near, near_columns)
    near_side = send(near, owners, X)
    cross, near = tie((cross, near))
    cross_side = send(cross, owners, X)
    (out_cross,) = work(cross)
    back_cross = send(out_cross, owners, Z_NEAR ^ Z_FAR)
    far_side, side, back_far, _ = tie((far_side, side, back_far, out_cross))
    out_far_side, out_side, out_own = work(far_side, side, rows)
    back_far_side = send(out_far_side, owners, X ^ Z_FAR)
    cross_side, _ = tie((cross_side, out_far_side))
    (out_cross_side,) = work(cross_side)
    back_cross_side = send(out_cross_side, owners, X ^ Z_NEAR ^ Z_FAR)
    back_side = send(out_side, owners, X)
    near_side, back_side, _ = tie((near_side, back_side, out_cross_side))
    out_near, out_near_side = work(near, near_side)
    back_near_side = send(out_near_side, owners, X ^ Z_NEAR)
    back_near = send(out_near, owners, Z_NEAR)
    far_parts = {
        0: out_own,
        Z_FAR: back_far,
        X ^ Z_FAR: back_far_side,
        Z_NEAR ^ Z_FAR: back_cross,
        X ^ Z_NEAR ^ Z_FAR: back_cross_side,
    }
    near_parts = {X: back_side, Z_NEAR: back_near, X ^ Z_NEAR: back_near_side}
    out = pick_routes(route_ids.T, near_parts, pick_routes(route_ids.T, far_parts))
    return out.reshape(1, tokens, top, weight_mat.shape[0])


def slotted_device(section_grad, route_ids, route_gates, weight_mat, capacity):
    tokens, top = route_ids.shape
    owners = lax.axis_size("expert")
    ids = jnp.arange(owners, dtype=jnp.int32)
    slots = jnp.arange(capacity, dtype=jnp.int32)
    matched = (route_ids[:, :, None] == ids[None, None, :]).astype(jnp.int32)
    hits = jnp.sum(matched, axis=1)
    rank = jnp.cumsum(hits, axis=0) - hits
    position = route_ids * capacity + jnp.sum(matched * rank[:, None, :], axis=2)
    gate_owner = jnp.einsum(
        "tk,tke->te", route_gates.astype(jnp.float32), matched.astype(jnp.float32)
    )
    slot_pick = (hits[:, :, None] == 1) & (rank[:, :, None] == slots[None, None, :])
    send_rows = jnp.einsum(
        "tem,td->emd",
        slot_pick.astype(jnp.bfloat16),
        section_grad,
        preferred_element_type=jnp.float32,
    ).astype(jnp.bfloat16)
    send_gates = jnp.einsum("tem,te->em", slot_pick.astype(jnp.float32), gate_owner).astype(
        jnp.bfloat16
    )
    got_rows = lax.all_to_all(send_rows, "expert", split_axis=0, concat_axis=0, tiled=True)
    got_gates = lax.all_to_all(send_gates, "expert", split_axis=0, concat_axis=0, tiled=True)
    product = lax.dot_general(
        got_rows.reshape(owners * capacity, got_rows.shape[2]),
        weight_mat,
        (((1,), (1,)), ((), ())),
        preferred_element_type=jnp.float32,
    ).reshape(owners, capacity, weight_mat.shape[0])
    returned = lax.all_to_all(
        (product * got_gates.astype(jnp.float32)[:, :, None]).astype(jnp.bfloat16),
        "expert",
        split_axis=0,
        concat_axis=0,
        tiled=True,
    )
    flat = returned.reshape(owners * capacity, returned.shape[2])
    out = jnp.take(flat, position.reshape(tokens * top), axis=0)
    return out.reshape(1, tokens, top, returned.shape[2])


def per_device(upstream, expert_ids, gate_weights, expert_weight):
    route_ids = expert_ids[0]
    route_gates = gate_weights[0]
    weight_mat = expert_weight[0, 0]
    tokens, top = route_ids.shape
    owners = lax.axis_size("expert")
    capacity = 2 * tokens * top // owners
    if capacity >= tokens and owners == CORES * 2 * Z_FAR:
        return dense_device(upstream[0], route_ids, route_gates, weight_mat)
    section_grad = shifted(upstream, "pipe", -1)[0]
    return slotted_device(section_grad, route_ids, route_gates, weight_mat, capacity)


def solution(mesh):
    in_specs = (
        P("pipe", "expert", None),
        P("pipe", "expert", None),
        P("pipe", "expert", None),
        P("pipe", "expert", None, None),
    )
    out_specs = P("pipe", "expert", None, None)
    return jax.shard_map(
        per_device, mesh=mesh, in_specs=in_specs, out_specs=out_specs, check_vma=False
    )
```

```python
import functools

import jax
import jax.numpy as jnp
from jax import lax
from jax.experimental import pallas as pl
from jax.experimental.pallas import tpu as pltpu
from jax.sharding import PartitionSpec as P

CORES = 2
X, Z_NEAR, Z_FAR = 1, 2, 4
LANES = 128


def shifted(block, axis, distance):
    devices = range(lax.axis_size(axis))
    route = [((i - distance) % len(devices), i) for i in devices]
    return lax.ppermute(block, axis, route)


def send(block, owners, flip, core=0):
    route = [(i, ((i // CORES) ^ flip) * CORES + ((i % CORES) ^ core)) for i in range(owners)]
    return lax.ppermute(block, "expert", route)


def send_across(block, owners, flip):
    sections = lax.axis_size("pipe")
    route = []
    for s in range(sections):
        for i in range(owners):
            target = ((i // CORES) ^ flip) * CORES + i % CORES
            route.append((s * owners + i, (s - 1) % sections * owners + target))
    return lax.ppermute(block, ("pipe", "expert"), route)


def gates_kernel(ids, gates, out):
    top, tokens = ids.shape
    expert = lax.broadcasted_iota(jnp.int32, (LANES, tokens), 0)
    total = jnp.zeros((LANES, tokens), jnp.float32)
    for k in range(top):
        gate = gates[k : k + 1, :].astype(jnp.float32)
        total += jnp.where(expert == ids[k : k + 1, :], gate, 0.0)
    out[...] = total.T.astype(jnp.bfloat16)


def gate_columns(ids, gates):
    return pl.pallas_call(
        gates_kernel,
        out_shape=jax.ShapeDtypeStruct((ids.shape[1], LANES), jnp.bfloat16),
        compiler_params=pltpu.CompilerParams(vmem_limit_bytes=16 << 20),
    )(ids, gates)


def widen_kernel(rows, columns, out):
    depth = rows.shape[1]
    out[:, :depth] = rows[...]
    out[:, depth:] = columns[...]


def widened(rows, columns):
    width = rows.shape[1] + columns.shape[1]
    return pl.pallas_call(
        widen_kernel,
        out_shape=jax.ShapeDtypeStruct((rows.shape[0], width), jnp.bfloat16),
        compiler_params=pltpu.CompilerParams(vmem_limit_bytes=16 << 20),
    )(rows, columns)


def turn_kernel(weight, other, out):
    hidden = weight.shape[0]
    out[:, :hidden] = weight[...].T
    out[:, hidden:] = other[...].T


def turned(weight, other):
    hidden, depth = weight.shape
    return pl.pallas_call(
        turn_kernel,
        out_shape=jax.ShapeDtypeStruct((depth, CORES * hidden), weight.dtype),
        compiler_params=pltpu.CompilerParams(vmem_limit_bytes=24 << 20),
        cost_estimate=pl.CostEstimate(
            flops=4 * CORES * 1024 * hidden * depth, bytes_accessed=0, transcendentals=0
        ),
    )(weight, other)


def products_kernel(count, weights, *refs):
    pieces, outs = refs[:count], refs[count:]
    depth, width = weights.shape
    hidden = width // CORES
    tokens = outs[0].shape[1]
    me = lax.axis_index("expert")
    core = lax.rem(me, CORES)
    stacked = jnp.concatenate([p[...] for p in pieces], axis=0)
    gates = stacked[:, depth:].astype(jnp.float32)
    column = lax.broadcasted_iota(jnp.int32, gates.shape, 1)
    product = jnp.dot(stacked[:, :depth], weights[...], preferred_element_type=jnp.float32)
    for half, to in enumerate((core, 1 - core)):
        scale = jnp.sum(jnp.where(column == me - core + to, gates, 0.0), axis=1, keepdims=True)
        scaled = (product[:, half * hidden : (half + 1) * hidden] * scale).astype(jnp.bfloat16)
        for j, out in enumerate(outs):
            out[to] = scaled[j * tokens : (j + 1) * tokens]


def products(pieces, tokens, weights):
    depth, width = weights.shape
    total = sum(p.shape[0] for p in pieces)
    one = jax.ShapeDtypeStruct((CORES, tokens, width // CORES), jnp.bfloat16)
    return pl.pallas_call(
        functools.partial(products_kernel, len(pieces)),
        out_shape=[one] * (total // tokens),
        compiler_params=pltpu.CompilerParams(vmem_limit_bytes=16 << 20),
        cost_estimate=pl.CostEstimate(
            flops=20 * total * width * depth,
            bytes_accessed=2 * (total * (width + depth) + width * depth),
            transcendentals=0,
        ),
    )(weights, *pieces)


def pick_kernel(flips, ids, *refs):
    blocks, kept, out = refs[: len(flips)], refs[len(flips) : -1], refs[-1]
    experts, tokens, _ = blocks[0].shape
    top = ids.shape[0]
    span = 16
    chip = lax.div(lax.axis_index("expert"), CORES)
    flip = lax.div(ids[...], CORES) ^ chip
    place = jnp.full(flip.shape, -1, jnp.int32)
    for j, known in enumerate(flips):
        place = jnp.where(flip == known, j * CORES + lax.rem(ids[...], CORES), place)
    column = lax.broadcasted_iota(jnp.int32, (top, len(blocks) * experts * span), 1)
    for g in range(tokens // span):
        stacked = jnp.concatenate(
            [b[c, g * span : (g + 1) * span, :] for b in blocks for c in range(experts)], axis=0
        )
        picks = [
            jnp.where(column == place[:, g * span + t : g * span + t + 1] * span + t, 1.0, 0.0)
            for t in range(span)
        ]
        pick = jnp.concatenate(picks, axis=0).astype(jnp.bfloat16)
        rows = jnp.dot(pick, stacked, preferred_element_type=jnp.float32).astype(jnp.bfloat16)
        part = slice(g * span * top, (g + 1) * span * top)
        out[part, :] = rows + kept[0][part, :] if kept else rows


def pick_routes(ids, received, *kept):
    top, tokens = ids.shape
    flips = sorted(received)
    blocks = [received[flip] for flip in flips]
    return pl.pallas_call(
        functools.partial(pick_kernel, flips),
        out_shape=jax.ShapeDtypeStruct((top * tokens, blocks[0].shape[2]), jnp.bfloat16),
        compiler_params=pltpu.CompilerParams(vmem_limit_bytes=16 << 20),
    )(ids, *blocks, *kept)


def dense_device(upstream, route_ids, route_gates, weight_mat):
    tokens, top = route_ids.shape
    owners = lax.axis_size("expert")
    tie = lax.optimization_barrier

    def work(*pieces):
        return products(list(pieces), tokens, weights)

    far = send_across(upstream, owners, Z_FAR)
    rows = send_across(upstream, owners, 0)
    other_mat = send(weight_mat, owners, 0, 1)
    columns = gate_columns(route_ids.T, route_gates.T)
    far_columns = send(columns, owners, Z_FAR)
    upstream, columns = tie((upstream, columns))
    near = send_across(upstream, owners, Z_NEAR)
    near_columns = send(columns, owners, Z_NEAR)
    weights = turned(weight_mat, other_mat)
    weights, near_columns = tie((weights, near_columns))
    far, far_columns, weights = tie((far, far_columns, weights))
    far = widened(far, far_columns)
    cross = send(far, owners, Z_NEAR)
    far_side = send(far, owners, X)
    (out_far,) = work(far)
    back_far = send(out_far, owners, Z_FAR)
    near, _ = tie((near, out_far))
    near = widened(near, near_columns)
    near_side = send(near, owners, X)
    rows, near = tie((rows, near))
    rows = widened(rows, columns)
    side = send(rows, owners, X)
    cross, near, rows = tie((cross, near, rows))
    cross_side = send(cross, owners, X)
    (out_cross,) = work(cross)
    back_cross = send(out_cross, owners, Z_NEAR ^ Z_FAR)
    far_side, back_far, _ = tie((far_side, back_far, out_cross))
    (out_far_side,) = work(far_side)
    back_far_side = send(out_far_side, owners, X ^ Z_FAR)
    cross_side, _ = tie((cross_side, out_far_side))
    (out_cross_side,) = work(cross_side)
    back_cross_side = send(out_cross_side, owners, X ^ Z_NEAR ^ Z_FAR)
    near_side, side, _ = tie((near_side, side, out_cross_side))
    out_own, out_side, out_near, out_near_side = work(rows, side, near, near_side)
    back_near_side = send(out_near_side, owners, X ^ Z_NEAR)
    out_side, back_far_side = tie((out_side, back_far_side))
    back_side = send(out_side, owners, X)
    back_near = send(out_near, owners, Z_NEAR)
    far_parts = {
        0: out_own,
        Z_FAR: back_far,
        X ^ Z_FAR: back_far_side,
        Z_NEAR ^ Z_FAR: back_cross,
        X ^ Z_NEAR ^ Z_FAR: back_cross_side,
    }
    near_parts = {X: back_side, Z_NEAR: back_near, X ^ Z_NEAR: back_near_side}
    out = pick_routes(route_ids.T, near_parts, pick_routes(route_ids.T, far_parts))
    return out.reshape(1, tokens, top, weight_mat.shape[0])


def slotted_device(section_grad, route_ids, route_gates, weight_mat, capacity):
    tokens, top = route_ids.shape
    owners = lax.axis_size("expert")
    ids = jnp.arange(owners, dtype=jnp.int32)
    slots = jnp.arange(capacity, dtype=jnp.int32)
    matched = (route_ids[:, :, None] == ids[None, None, :]).astype(jnp.int32)
    hits = jnp.sum(matched, axis=1)
    rank = jnp.cumsum(hits, axis=0) - hits
    position = route_ids * capacity + jnp.sum(matched * rank[:, None, :], axis=2)
    gate_owner = jnp.einsum(
        "tk,tke->te", route_gates.astype(jnp.float32), matched.astype(jnp.float32)
    )
    slot_pick = (hits[:, :, None] == 1) & (rank[:, :, None] == slots[None, None, :])
    send_rows = jnp.einsum(
        "tem,td->emd",
        slot_pick.astype(jnp.bfloat16),
        section_grad,
        preferred_element_type=jnp.float32,
    ).astype(jnp.bfloat16)
    send_gates = jnp.einsum("tem,te->em", slot_pick.astype(jnp.float32), gate_owner).astype(
        jnp.bfloat16
    )
    got_rows = lax.all_to_all(send_rows, "expert", split_axis=0, concat_axis=0, tiled=True)
    got_gates = lax.all_to_all(send_gates, "expert", split_axis=0, concat_axis=0, tiled=True)
    product = lax.dot_general(
        got_rows.reshape(owners * capacity, got_rows.shape[2]),
        weight_mat,
        (((1,), (1,)), ((), ())),
        preferred_element_type=jnp.float32,
    ).reshape(owners, capacity, weight_mat.shape[0])
    returned = lax.all_to_all(
        (product * got_gates.astype(jnp.float32)[:, :, None]).astype(jnp.bfloat16),
        "expert",
        split_axis=0,
        concat_axis=0,
        tiled=True,
    )
    flat = returned.reshape(owners * capacity, returned.shape[2])
    out = jnp.take(flat, position.reshape(tokens * top), axis=0)
    return out.reshape(1, tokens, top, returned.shape[2])


def per_device(upstream, expert_ids, gate_weights, expert_weight):
    route_ids = expert_ids[0]
    route_gates = gate_weights[0]
    weight_mat = expert_weight[0, 0]
    tokens, top = route_ids.shape
    owners = lax.axis_size("expert")
    capacity = 2 * tokens * top // owners
    if capacity >= tokens and owners == CORES * 2 * Z_FAR:
        return dense_device(upstream[0], route_ids, route_gates, weight_mat)
    section_grad = shifted(upstream, "pipe", -1)[0]
    return slotted_device(section_grad, route_ids, route_gates, weight_mat, capacity)


def solution(mesh):
    in_specs = (
        P("pipe", "expert", None),
        P("pipe", "expert", None),
        P("pipe", "expert", None),
        P("pipe", "expert", None, None),
    )
    out_specs = P("pipe", "expert", None, None)
    return jax.shard_map(
        per_device, mesh=mesh, in_specs=in_specs, out_specs=out_specs, check_vma=False
    )
```

```python
import functools

import jax
import jax.numpy as jnp
from jax import lax
from jax.experimental import pallas as pl
from jax.experimental.pallas import tpu as pltpu
from jax.sharding import PartitionSpec as P

CORES = 2
X, Z_NEAR, Z_FAR = 1, 2, 4
LANES = 128


def shifted(block, axis, distance):
    devices = range(lax.axis_size(axis))
    route = [((i - distance) % len(devices), i) for i in devices]
    return lax.ppermute(block, axis, route)


def send(block, owners, flip, core=0):
    route = [(i, ((i // CORES) ^ flip) * CORES + ((i % CORES) ^ core)) for i in range(owners)]
    return lax.ppermute(block, "expert", route)


def send_across(block, owners, flip):
    sections = lax.axis_size("pipe")
    route = []
    for s in range(sections):
        for i in range(owners):
            target = ((i // CORES) ^ flip) * CORES + i % CORES
            route.append((s * owners + i, (s - 1) % sections * owners + target))
    return lax.ppermute(block, ("pipe", "expert"), route)


def gates_kernel(ids, gates, out):
    top, tokens = ids.shape
    expert = lax.broadcasted_iota(jnp.int32, (LANES, tokens), 0)
    total = jnp.zeros((LANES, tokens), jnp.float32)
    for k in range(top):
        gate = gates[k : k + 1, :].astype(jnp.float32)
        total += jnp.where(expert == ids[k : k + 1, :], gate, 0.0)
    out[...] = total.T.astype(jnp.bfloat16)


def gate_columns(ids, gates):
    return pl.pallas_call(
        gates_kernel,
        out_shape=jax.ShapeDtypeStruct((ids.shape[1], LANES), jnp.bfloat16),
        compiler_params=pltpu.CompilerParams(vmem_limit_bytes=16 << 20),
    )(ids, gates)


def widen_kernel(*refs):
    third = len(refs) // 3
    for rows, columns, out in zip(refs[:third], refs[third : 2 * third], refs[2 * third :]):
        depth = rows.shape[1]
        out[:, :depth] = rows[...]
        out[:, depth:] = columns[...]


def widened(rows, columns):
    shapes = [
        jax.ShapeDtypeStruct((r.shape[0], r.shape[1] + c.shape[1]), jnp.bfloat16)
        for r, c in zip(rows, columns)
    ]
    return pl.pallas_call(
        widen_kernel,
        out_shape=shapes,
        compiler_params=pltpu.CompilerParams(vmem_limit_bytes=16 << 20),
    )(*rows, *columns)


def turn_kernel(weight, other, out):
    hidden = weight.shape[0]
    out[:, :hidden] = weight[...].T
    out[:, hidden:] = other[...].T


def turned(weight, other):
    hidden, depth = weight.shape
    return pl.pallas_call(
        turn_kernel,
        out_shape=jax.ShapeDtypeStruct((depth, CORES * hidden), weight.dtype),
        compiler_params=pltpu.CompilerParams(vmem_limit_bytes=24 << 20),
        cost_estimate=pl.CostEstimate(
            flops=4 * CORES * 1024 * hidden * depth, bytes_accessed=0, transcendentals=0
        ),
    )(weight, other)


def products_kernel(count, weights, *refs):
    pieces, outs = refs[:count], refs[count:]
    depth, width = weights.shape
    hidden = width // CORES
    tokens = outs[0].shape[1]
    me = lax.axis_index("expert")
    core = lax.rem(me, CORES)
    stacked = jnp.concatenate([p[...] for p in pieces], axis=0)
    gates = stacked[:, depth:].astype(jnp.float32)
    column = lax.broadcasted_iota(jnp.int32, gates.shape, 1)
    product = jnp.dot(stacked[:, :depth], weights[...], preferred_element_type=jnp.float32)
    for half, to in enumerate((core, 1 - core)):
        scale = jnp.sum(jnp.where(column == me - core + to, gates, 0.0), axis=1, keepdims=True)
        scaled = (product[:, half * hidden : (half + 1) * hidden] * scale).astype(jnp.bfloat16)
        for j, out in enumerate(outs):
            out[to] = scaled[j * tokens : (j + 1) * tokens]


def products(pieces, tokens, weights):
    depth, width = weights.shape
    total = sum(p.shape[0] for p in pieces)
    one = jax.ShapeDtypeStruct((CORES, tokens, width // CORES), jnp.bfloat16)
    return pl.pallas_call(
        functools.partial(products_kernel, len(pieces)),
        out_shape=[one] * (total // tokens),
        compiler_params=pltpu.CompilerParams(vmem_limit_bytes=16 << 20),
        cost_estimate=pl.CostEstimate(
            flops=20 * total * width * depth,
            bytes_accessed=2 * (total * (width + depth) + width * depth),
            transcendentals=0,
        ),
    )(weights, *pieces)


def pick_kernel(flips, ids, *refs):
    blocks, kept, out = refs[: len(flips)], refs[len(flips) : -1], refs[-1]
    experts, tokens, _ = blocks[0].shape
    top = ids.shape[0]
    span = 16
    chip = lax.div(lax.axis_index("expert"), CORES)
    flip = lax.div(ids[...], CORES) ^ chip
    place = jnp.full(flip.shape, -1, jnp.int32)
    for j, known in enumerate(flips):
        place = jnp.where(flip == known, j * CORES + lax.rem(ids[...], CORES), place)
    column = lax.broadcasted_iota(jnp.int32, (top, len(blocks) * experts * span), 1)
    for g in range(tokens // span):
        stacked = jnp.concatenate(
            [b[c, g * span : (g + 1) * span, :] for b in blocks for c in range(experts)], axis=0
        )
        picks = [
            jnp.where(column == place[:, g * span + t : g * span + t + 1] * span + t, 1.0, 0.0)
            for t in range(span)
        ]
        pick = jnp.concatenate(picks, axis=0).astype(jnp.bfloat16)
        rows = jnp.dot(pick, stacked, preferred_element_type=jnp.float32).astype(jnp.bfloat16)
        part = slice(g * span * top, (g + 1) * span * top)
        out[part, :] = rows + kept[0][part, :] if kept else rows


def pick_routes(ids, received, *kept):
    top, tokens = ids.shape
    flips = sorted(received)
    blocks = [received[flip] for flip in flips]
    return pl.pallas_call(
        functools.partial(pick_kernel, flips),
        out_shape=jax.ShapeDtypeStruct((top * tokens, blocks[0].shape[2]), jnp.bfloat16),
        compiler_params=pltpu.CompilerParams(vmem_limit_bytes=16 << 20),
    )(ids, *blocks, *kept)


def dense_device(upstream, route_ids, route_gates, weight_mat):
    tokens, top = route_ids.shape
    owners = lax.axis_size("expert")
    tie = lax.optimization_barrier

    def work(*pieces):
        return products(list(pieces), tokens, weights)

    far = send_across(upstream, owners, Z_FAR)
    side = send_across(upstream, owners, X)
    other_mat = send(weight_mat, owners, 0, 1)
    route_gates, other_mat = tie((route_gates, other_mat))
    columns = gate_columns(route_ids.T, route_gates.T)
    far_columns = send(columns, owners, Z_FAR)
    side_columns = send(columns, owners, X)
    rows = send_across(upstream, owners, 0)
    weights = turned(weight_mat, other_mat)
    far, far_columns, side, side_columns, weights = tie(
        (far, far_columns, side, side_columns, weights)
    )
    far, side = widened([far, side], [far_columns, side_columns])
    cross = send(far, owners, Z_NEAR)
    far_side = send(far, owners, X)
    out_far, out_side = work(far, side)
    back_far = send(out_far, owners, Z_FAR)
    rows, columns, _ = tie((rows, columns, out_far))
    (rows,) = widened([rows], [columns])
    near = send(rows, owners, Z_NEAR)
    back_side = send(tie((out_side, rows))[0], owners, X)
    cross, rows = tie((cross, rows))
    cross_side = send(cross, owners, X)
    (out_cross,) = work(cross)
    back_cross = send(out_cross, owners, Z_NEAR ^ Z_FAR)
    far_side, back_far, near, back_side, _ = tie((far_side, back_far, near, back_side, out_cross))
    near_side = send(near, owners, X)
    (out_far_side,) = work(far_side)
    back_far_side = send(out_far_side, owners, X ^ Z_FAR)
    cross_side, _ = tie((cross_side, out_far_side))
    (out_cross_side,) = work(cross_side)
    back_cross_side = send(out_cross_side, owners, X ^ Z_NEAR ^ Z_FAR)
    near_side, _ = tie((near_side, out_cross_side))
    out_near, out_near_side, out_own = work(near, near_side, rows)
    back_near_side = send(out_near_side, owners, X ^ Z_NEAR)
    back_near = send(out_near, owners, Z_NEAR)
    far_parts = {
        0: out_own,
        Z_FAR: back_far,
        X ^ Z_FAR: back_far_side,
        Z_NEAR ^ Z_FAR: back_cross,
        X ^ Z_NEAR ^ Z_FAR: back_cross_side,
    }
    near_parts = {X: back_side, Z_NEAR: back_near, X ^ Z_NEAR: back_near_side}
    out = pick_routes(route_ids.T, near_parts, pick_routes(route_ids.T, far_parts))
    return out.reshape(1, tokens, top, weight_mat.shape[0])


def slotted_device(section_grad, route_ids, route_gates, weight_mat, capacity):
    tokens, top = route_ids.shape
    owners = lax.axis_size("expert")
    ids = jnp.arange(owners, dtype=jnp.int32)
    slots = jnp.arange(capacity, dtype=jnp.int32)
    matched = (route_ids[:, :, None] == ids[None, None, :]).astype(jnp.int32)
    hits = jnp.sum(matched, axis=1)
    rank = jnp.cumsum(hits, axis=0) - hits
    position = route_ids * capacity + jnp.sum(matched * rank[:, None, :], axis=2)
    gate_owner = jnp.einsum(
        "tk,tke->te", route_gates.astype(jnp.float32), matched.astype(jnp.float32)
    )
    slot_pick = (hits[:, :, None] == 1) & (rank[:, :, None] == slots[None, None, :])
    send_rows = jnp.einsum(
        "tem,td->emd",
        slot_pick.astype(jnp.bfloat16),
        section_grad,
        preferred_element_type=jnp.float32,
    ).astype(jnp.bfloat16)
    send_gates = jnp.einsum("tem,te->em", slot_pick.astype(jnp.float32), gate_owner).astype(
        jnp.bfloat16
    )
    got_rows = lax.all_to_all(send_rows, "expert", split_axis=0, concat_axis=0, tiled=True)
    got_gates = lax.all_to_all(send_gates, "expert", split_axis=0, concat_axis=0, tiled=True)
    product = lax.dot_general(
        got_rows.reshape(owners * capacity, got_rows.shape[2]),
        weight_mat,
        (((1,), (1,)), ((), ())),
        preferred_element_type=jnp.float32,
    ).reshape(owners, capacity, weight_mat.shape[0])
    returned = lax.all_to_all(
        (product * got_gates.astype(jnp.float32)[:, :, None]).astype(jnp.bfloat16),
        "expert",
        split_axis=0,
        concat_axis=0,
        tiled=True,
    )
    flat = returned.reshape(owners * capacity, returned.shape[2])
    out = jnp.take(flat, position.reshape(tokens * top), axis=0)
    return out.reshape(1, tokens, top, returned.shape[2])


def per_device(upstream, expert_ids, gate_weights, expert_weight):
    route_ids = expert_ids[0]
    route_gates = gate_weights[0]
    weight_mat = expert_weight[0, 0]
    tokens, top = route_ids.shape
    owners = lax.axis_size("expert")
    capacity = 2 * tokens * top // owners
    if capacity >= tokens and owners == CORES * 2 * Z_FAR:
        return dense_device(upstream[0], route_ids, route_gates, weight_mat)
    section_grad = shifted(upstream, "pipe", -1)[0]
    return slotted_device(section_grad, route_ids, route_gates, weight_mat, capacity)


def solution(mesh):
    in_specs = (
        P("pipe", "expert", None),
        P("pipe", "expert", None),
        P("pipe", "expert", None),
        P("pipe", "expert", None, None),
    )
    out_specs = P("pipe", "expert", None, None)
    return jax.shard_map(
        per_device, mesh=mesh, in_specs=in_specs, out_specs=out_specs, check_vma=False
    )
```

```python
import functools

import jax
import jax.numpy as jnp
from jax import lax
from jax.experimental import pallas as pl
from jax.experimental.pallas import tpu as pltpu
from jax.sharding import PartitionSpec as P

CORES = 2
X, Z_NEAR, Z_FAR = 1, 2, 4
LANES = 128


def shifted(block, axis, distance):
    devices = range(lax.axis_size(axis))
    route = [((i - distance) % len(devices), i) for i in devices]
    return lax.ppermute(block, axis, route)


def send(block, owners, flip, core=0):
    route = [(i, ((i // CORES) ^ flip) * CORES + ((i % CORES) ^ core)) for i in range(owners)]
    return lax.ppermute(block, "expert", route)


def send_across(block, owners, flip):
    sections = lax.axis_size("pipe")
    route = []
    for s in range(sections):
        for i in range(owners):
            target = ((i // CORES) ^ flip) * CORES + i % CORES
            route.append((s * owners + i, (s - 1) % sections * owners + target))
    return lax.ppermute(block, ("pipe", "expert"), route)


def gates_kernel(ids, gates, out):
    top, tokens = ids.shape
    expert = lax.broadcasted_iota(jnp.int32, (LANES, tokens), 0)
    total = jnp.zeros((LANES, tokens), jnp.float32)
    for k in range(top):
        gate = gates[k : k + 1, :].astype(jnp.float32)
        total += jnp.where(expert == ids[k : k + 1, :], gate, 0.0)
    out[...] = total.T.astype(jnp.bfloat16)


def gate_columns(ids, gates):
    return pl.pallas_call(
        gates_kernel,
        out_shape=jax.ShapeDtypeStruct((ids.shape[1], LANES), jnp.bfloat16),
        compiler_params=pltpu.CompilerParams(vmem_limit_bytes=16 << 20),
    )(ids, gates)


def widen_kernel(*refs):
    third = len(refs) // 3
    for rows, columns, out in zip(refs[:third], refs[third : 2 * third], refs[2 * third :]):
        depth = rows.shape[1]
        out[:, :depth] = rows[...]
        out[:, depth:] = columns[...]


def widened(rows, columns):
    shapes = [
        jax.ShapeDtypeStruct((r.shape[0], r.shape[1] + c.shape[1]), jnp.bfloat16)
        for r, c in zip(rows, columns)
    ]
    return pl.pallas_call(
        widen_kernel,
        out_shape=shapes,
        compiler_params=pltpu.CompilerParams(vmem_limit_bytes=16 << 20),
    )(*rows, *columns)


def turn_kernel(weight, other, out):
    hidden = weight.shape[0]
    out[:, :hidden] = weight[...].T
    out[:, hidden:] = other[...].T


def turned(weight, other):
    hidden, depth = weight.shape
    return pl.pallas_call(
        turn_kernel,
        out_shape=jax.ShapeDtypeStruct((depth, CORES * hidden), weight.dtype),
        compiler_params=pltpu.CompilerParams(vmem_limit_bytes=24 << 20),
        cost_estimate=pl.CostEstimate(
            flops=4 * CORES * 1024 * hidden * depth, bytes_accessed=0, transcendentals=0
        ),
    )(weight, other)


def products_kernel(count, weights, *refs):
    pieces, outs = refs[:count], refs[count:]
    depth, width = weights.shape
    hidden = width // CORES
    tokens = outs[0].shape[1]
    me = lax.axis_index("expert")
    core = lax.rem(me, CORES)
    stacked = jnp.concatenate([p[...] for p in pieces], axis=0)
    gates = stacked[:, depth:].astype(jnp.float32)
    column = lax.broadcasted_iota(jnp.int32, gates.shape, 1)
    product = jnp.dot(stacked[:, :depth], weights[...], preferred_element_type=jnp.float32)
    for half, to in enumerate((core, 1 - core)):
        scale = jnp.sum(jnp.where(column == me - core + to, gates, 0.0), axis=1, keepdims=True)
        scaled = (product[:, half * hidden : (half + 1) * hidden] * scale).astype(jnp.bfloat16)
        for j, out in enumerate(outs):
            out[to] = scaled[j * tokens : (j + 1) * tokens]


def products(pieces, tokens, weights):
    depth, width = weights.shape
    total = sum(p.shape[0] for p in pieces)
    one = jax.ShapeDtypeStruct((CORES, tokens, width // CORES), jnp.bfloat16)
    return pl.pallas_call(
        functools.partial(products_kernel, len(pieces)),
        out_shape=[one] * (total // tokens),
        compiler_params=pltpu.CompilerParams(vmem_limit_bytes=16 << 20),
        cost_estimate=pl.CostEstimate(
            flops=20 * total * width * depth,
            bytes_accessed=2 * (total * (width + depth) + width * depth),
            transcendentals=0,
        ),
    )(weights, *pieces)


def pick_kernel(flips, ids, *refs):
    blocks, kept, out = refs[: len(flips)], refs[len(flips) : -1], refs[-1]
    experts, tokens, _ = blocks[0].shape
    top = ids.shape[0]
    span = 16
    chip = lax.div(lax.axis_index("expert"), CORES)
    flip = lax.div(ids[...], CORES) ^ chip
    place = jnp.full(flip.shape, -1, jnp.int32)
    for j, known in enumerate(flips):
        place = jnp.where(flip == known, j * CORES + lax.rem(ids[...], CORES), place)
    column = lax.broadcasted_iota(jnp.int32, (top, len(blocks) * experts * span), 1)
    for g in range(tokens // span):
        stacked = jnp.concatenate(
            [b[c, g * span : (g + 1) * span, :] for b in blocks for c in range(experts)], axis=0
        )
        picks = [
            jnp.where(column == place[:, g * span + t : g * span + t + 1] * span + t, 1.0, 0.0)
            for t in range(span)
        ]
        pick = jnp.concatenate(picks, axis=0).astype(jnp.bfloat16)
        rows = jnp.dot(pick, stacked, preferred_element_type=jnp.float32).astype(jnp.bfloat16)
        part = slice(g * span * top, (g + 1) * span * top)
        out[part, :] = rows + kept[0][part, :] if kept else rows


def pick_routes(ids, received, *kept):
    top, tokens = ids.shape
    flips = sorted(received)
    blocks = [received[flip] for flip in flips]
    return pl.pallas_call(
        functools.partial(pick_kernel, flips),
        out_shape=jax.ShapeDtypeStruct((top * tokens, blocks[0].shape[2]), jnp.bfloat16),
        compiler_params=pltpu.CompilerParams(vmem_limit_bytes=16 << 20),
    )(ids, *blocks, *kept)


def dense_device(upstream, route_ids, route_gates, weight_mat):
    tokens, top = route_ids.shape
    owners = lax.axis_size("expert")
    tie = lax.optimization_barrier

    def work(*pieces):
        return products(list(pieces), tokens, weights)

    far = send_across(upstream, owners, Z_FAR)
    side = send_across(upstream, owners, X)
    near = send_across(upstream, owners, Z_NEAR)
    other_mat = send(weight_mat, owners, 0, 1)
    route_gates, other_mat = tie((route_gates, other_mat))
    columns = gate_columns(route_ids.T, route_gates.T)
    far_columns = send(columns, owners, Z_FAR)
    side_columns = send(columns, owners, X)
    near_columns = send(columns, owners, Z_NEAR)
    weights = turned(weight_mat, other_mat)
    far, far_columns, side, side_columns, weights = tie(
        (far, far_columns, side, side_columns, weights)
    )
    far, side = widened([far, side], [far_columns, side_columns])
    cross = send(far, owners, Z_NEAR)
    far_side = send(far, owners, X)
    out_far, out_side = work(far, side)
    back_far = send(out_far, owners, Z_FAR)
    near, near_columns, _ = tie((near, near_columns, out_far))
    (near,) = widened([near], [near_columns])
    near_side = send(near, owners, X)
    back_side = send(tie((out_side, near))[0], owners, X)
    cross, near = tie((cross, near))
    cross_side = send(cross, owners, X)
    (out_cross,) = work(cross)
    back_cross = send(out_cross, owners, Z_NEAR ^ Z_FAR)
    far_side, back_far, back_side, upstream, _ = tie(
        (far_side, back_far, back_side, upstream, out_cross)
    )
    rows = send_across(upstream, owners, 0)
    (out_far_side,) = work(far_side)
    back_far_side = send(out_far_side, owners, X ^ Z_FAR)
    cross_side, _ = tie((cross_side, out_far_side))
    (out_cross_side,) = work(cross_side)
    back_cross_side = send(out_cross_side, owners, X ^ Z_NEAR ^ Z_FAR)
    rows, near_side, _ = tie((rows, near_side, out_cross_side))
    (rows,) = widened([rows], [columns])
    out_near, out_near_side, out_own = work(near, near_side, rows)
    back_near_side = send(out_near_side, owners, X ^ Z_NEAR)
    back_near = send(out_near, owners, Z_NEAR)
    far_parts = {
        0: out_own,
        Z_FAR: back_far,
        X ^ Z_FAR: back_far_side,
        Z_NEAR ^ Z_FAR: back_cross,
        X ^ Z_NEAR ^ Z_FAR: back_cross_side,
    }
    near_parts = {X: back_side, Z_NEAR: back_near, X ^ Z_NEAR: back_near_side}
    out = pick_routes(route_ids.T, near_parts, pick_routes(route_ids.T, far_parts))
    return out.reshape(1, tokens, top, weight_mat.shape[0])


def slotted_device(section_grad, route_ids, route_gates, weight_mat, capacity):
    tokens, top = route_ids.shape
    owners = lax.axis_size("expert")
    ids = jnp.arange(owners, dtype=jnp.int32)
    slots = jnp.arange(capacity, dtype=jnp.int32)
    matched = (route_ids[:, :, None] == ids[None, None, :]).astype(jnp.int32)
    hits = jnp.sum(matched, axis=1)
    rank = jnp.cumsum(hits, axis=0) - hits
    position = route_ids * capacity + jnp.sum(matched * rank[:, None, :], axis=2)
    gate_owner = jnp.einsum(
        "tk,tke->te", route_gates.astype(jnp.float32), matched.astype(jnp.float32)
    )
    slot_pick = (hits[:, :, None] == 1) & (rank[:, :, None] == slots[None, None, :])
    send_rows = jnp.einsum(
        "tem,td->emd",
        slot_pick.astype(jnp.bfloat16),
        section_grad,
        preferred_element_type=jnp.float32,
    ).astype(jnp.bfloat16)
    send_gates = jnp.einsum("tem,te->em", slot_pick.astype(jnp.float32), gate_owner).astype(
        jnp.bfloat16
    )
    got_rows = lax.all_to_all(send_rows, "expert", split_axis=0, concat_axis=0, tiled=True)
    got_gates = lax.all_to_all(send_gates, "expert", split_axis=0, concat_axis=0, tiled=True)
    product = lax.dot_general(
        got_rows.reshape(owners * capacity, got_rows.shape[2]),
        weight_mat,
        (((1,), (1,)), ((), ())),
        preferred_element_type=jnp.float32,
    ).reshape(owners, capacity, weight_mat.shape[0])
    returned = lax.all_to_all(
        (product * got_gates.astype(jnp.float32)[:, :, None]).astype(jnp.bfloat16),
        "expert",
        split_axis=0,
        concat_axis=0,
        tiled=True,
    )
    flat = returned.reshape(owners * capacity, returned.shape[2])
    out = jnp.take(flat, position.reshape(tokens * top), axis=0)
    return out.reshape(1, tokens, top, returned.shape[2])


def per_device(upstream, expert_ids, gate_weights, expert_weight):
    route_ids = expert_ids[0]
    route_gates = gate_weights[0]
    weight_mat = expert_weight[0, 0]
    tokens, top = route_ids.shape
    owners = lax.axis_size("expert")
    capacity = 2 * tokens * top // owners
    if capacity >= tokens and owners == CORES * 2 * Z_FAR:
        return dense_device(upstream[0], route_ids, route_gates, weight_mat)
    section_grad = shifted(upstream, "pipe", -1)[0]
    return slotted_device(section_grad, route_ids, route_gates, weight_mat, capacity)


def solution(mesh):
    in_specs = (
        P("pipe", "expert", None),
        P("pipe", "expert", None),
        P("pipe", "expert", None),
        P("pipe", "expert", None, None),
    )
    out_specs = P("pipe", "expert", None, None)
    return jax.shard_map(
        per_device, mesh=mesh, in_specs=in_specs, out_specs=out_specs, check_vma=False
    )
```

```python
import functools

import jax
import jax.numpy as jnp
from jax import lax
from jax.experimental import pallas as pl
from jax.experimental.pallas import tpu as pltpu
from jax.sharding import PartitionSpec as P

CORES = 2
X, Z_NEAR, Z_FAR = 1, 2, 4
LANES = 128


def shifted(block, axis, distance):
    devices = range(lax.axis_size(axis))
    route = [((i - distance) % len(devices), i) for i in devices]
    return lax.ppermute(block, axis, route)


def send(block, owners, flip, core=0):
    route = [(i, ((i // CORES) ^ flip) * CORES + ((i % CORES) ^ core)) for i in range(owners)]
    return lax.ppermute(block, "expert", route)


def send_across(block, owners, flip):
    sections = lax.axis_size("pipe")
    route = []
    for s in range(sections):
        for i in range(owners):
            target = ((i // CORES) ^ flip) * CORES + i % CORES
            route.append((s * owners + i, (s - 1) % sections * owners + target))
    return lax.ppermute(block, ("pipe", "expert"), route)


def gates_kernel(ids, gates, out):
    top, tokens = ids.shape
    expert = lax.broadcasted_iota(jnp.int32, (LANES, tokens), 0)
    total = jnp.zeros((LANES, tokens), jnp.float32)
    for k in range(top):
        gate = gates[k : k + 1, :].astype(jnp.float32)
        total += jnp.where(expert == ids[k : k + 1, :], gate, 0.0)
    out[...] = total.T.astype(jnp.bfloat16)


def gate_columns(ids, gates):
    return pl.pallas_call(
        gates_kernel,
        out_shape=jax.ShapeDtypeStruct((ids.shape[1], LANES), jnp.bfloat16),
        compiler_params=pltpu.CompilerParams(vmem_limit_bytes=16 << 20),
    )(ids, gates)


def widen_kernel(*refs):
    third = len(refs) // 3
    for rows, columns, out in zip(refs[:third], refs[third : 2 * third], refs[2 * third :]):
        depth = rows.shape[1]
        out[:, :depth] = rows[...]
        out[:, depth:] = columns[...]


def widened(rows, columns):
    shapes = [
        jax.ShapeDtypeStruct((r.shape[0], r.shape[1] + c.shape[1]), jnp.bfloat16)
        for r, c in zip(rows, columns)
    ]
    return pl.pallas_call(
        widen_kernel,
        out_shape=shapes,
        compiler_params=pltpu.CompilerParams(vmem_limit_bytes=16 << 20),
    )(*rows, *columns)


def turn_kernel(weight, other, out):
    hidden = weight.shape[0]
    out[:, :hidden] = weight[...].T
    out[:, hidden:] = other[...].T


def turned(weight, other):
    hidden, depth = weight.shape
    return pl.pallas_call(
        turn_kernel,
        out_shape=jax.ShapeDtypeStruct((depth, CORES * hidden), weight.dtype),
        compiler_params=pltpu.CompilerParams(vmem_limit_bytes=24 << 20),
        cost_estimate=pl.CostEstimate(
            flops=4 * CORES * 1024 * hidden * depth, bytes_accessed=0, transcendentals=0
        ),
    )(weight, other)


def products_kernel(count, weights, *refs):
    pieces, outs = refs[:count], refs[count:]
    depth, width = weights.shape
    hidden = width // CORES
    tokens = outs[0].shape[1]
    me = lax.axis_index("expert")
    core = lax.rem(me, CORES)
    stacked = jnp.concatenate([p[...] for p in pieces], axis=0)
    gates = stacked[:, depth:].astype(jnp.float32)
    column = lax.broadcasted_iota(jnp.int32, gates.shape, 1)
    product = jnp.dot(stacked[:, :depth], weights[...], preferred_element_type=jnp.float32)
    for half, to in enumerate((core, 1 - core)):
        scale = jnp.sum(jnp.where(column == me - core + to, gates, 0.0), axis=1, keepdims=True)
        scaled = (product[:, half * hidden : (half + 1) * hidden] * scale).astype(jnp.bfloat16)
        for j, out in enumerate(outs):
            out[to] = scaled[j * tokens : (j + 1) * tokens]


def products(pieces, tokens, weights):
    depth, width = weights.shape
    total = sum(p.shape[0] for p in pieces)
    one = jax.ShapeDtypeStruct((CORES, tokens, width // CORES), jnp.bfloat16)
    return pl.pallas_call(
        functools.partial(products_kernel, len(pieces)),
        out_shape=[one] * (total // tokens),
        compiler_params=pltpu.CompilerParams(vmem_limit_bytes=16 << 20),
        cost_estimate=pl.CostEstimate(
            flops=20 * total * width * depth,
            bytes_accessed=2 * (total * (width + depth) + width * depth),
            transcendentals=0,
        ),
    )(weights, *pieces)


def pick_kernel(flips, ids, *refs):
    blocks, kept, out = refs[: len(flips)], refs[len(flips) : -1], refs[-1]
    experts, tokens, _ = blocks[0].shape
    top = ids.shape[0]
    span = 16
    chip = lax.div(lax.axis_index("expert"), CORES)
    flip = lax.div(ids[...], CORES) ^ chip
    place = jnp.full(flip.shape, -1, jnp.int32)
    for j, known in enumerate(flips):
        place = jnp.where(flip == known, j * CORES + lax.rem(ids[...], CORES), place)
    column = lax.broadcasted_iota(jnp.int32, (top, len(blocks) * experts * span), 1)
    for g in range(tokens // span):
        stacked = jnp.concatenate(
            [b[c, g * span : (g + 1) * span, :] for b in blocks for c in range(experts)], axis=0
        )
        picks = [
            jnp.where(column == place[:, g * span + t : g * span + t + 1] * span + t, 1.0, 0.0)
            for t in range(span)
        ]
        pick = jnp.concatenate(picks, axis=0).astype(jnp.bfloat16)
        rows = jnp.dot(pick, stacked, preferred_element_type=jnp.float32).astype(jnp.bfloat16)
        part = slice(g * span * top, (g + 1) * span * top)
        out[part, :] = rows + kept[0][part, :] if kept else rows


def pick_routes(ids, received, *kept):
    top, tokens = ids.shape
    flips = sorted(received)
    blocks = [received[flip] for flip in flips]
    return pl.pallas_call(
        functools.partial(pick_kernel, flips),
        out_shape=jax.ShapeDtypeStruct((top * tokens, blocks[0].shape[2]), jnp.bfloat16),
        compiler_params=pltpu.CompilerParams(vmem_limit_bytes=16 << 20),
    )(ids, *blocks, *kept)


def dense_device(upstream, route_ids, route_gates, weight_mat):
    tokens, top = route_ids.shape
    owners = lax.axis_size("expert")
    tie = lax.optimization_barrier

    def work(*pieces):
        return products(list(pieces), tokens, weights)

    far = send_across(upstream, owners, Z_FAR)
    side = send_across(upstream, owners, X)
    near = send_across(upstream, owners, Z_NEAR)
    other_mat = send(weight_mat, owners, 0, 1)
    route_gates, other_mat = tie((route_gates, other_mat))
    columns = gate_columns(route_ids.T, route_gates.T)
    far_columns = send(columns, owners, Z_FAR)
    side_columns = send(columns, owners, X)
    near_columns = send(columns, owners, Z_NEAR)
    weights = turned(weight_mat, other_mat)
    far, far_columns, side, side_columns, weights = tie(
        (far, far_columns, side, side_columns, weights)
    )
    far, side = widened([far, side], [far_columns, side_columns])
    cross = send(far, owners, Z_NEAR)
    far_side = send(far, owners, X)
    out_far, out_side = work(far, side)
    back_far = send(out_far, owners, Z_FAR)
    near, near_columns, _ = tie((near, near_columns, out_far))
    (near,) = widened([near], [near_columns])
    near_side = send(near, owners, X)
    upstream, near = tie((upstream, near))
    rows = send_across(upstream, owners, 0)
    cross, near = tie((cross, near))
    cross_side = send(cross, owners, X)
    (out_cross,) = work(cross)
    back_cross = send(out_cross, owners, Z_NEAR ^ Z_FAR)
    far_side, back_far, rows, _ = tie((far_side, back_far, rows, out_cross))
    (rows,) = widened([rows], [columns])
    out_far_side, out_own = work(far_side, rows)
    back_far_side = send(out_far_side, owners, X ^ Z_FAR)
    cross_side, _ = tie((cross_side, out_far_side))
    (out_cross_side,) = work(cross_side)
    back_cross_side = send(out_cross_side, owners, X ^ Z_NEAR ^ Z_FAR)
    near_side, out_side, _ = tie((near_side, out_side, out_cross_side))
    out_near, out_near_side = work(near, near_side)
    back_side = send(out_side, owners, X)
    back_near_side = send(out_near_side, owners, X ^ Z_NEAR)
    back_near = send(out_near, owners, Z_NEAR)
    far_parts = {
        0: out_own,
        Z_FAR: back_far,
        X ^ Z_FAR: back_far_side,
        Z_NEAR ^ Z_FAR: back_cross,
        X ^ Z_NEAR ^ Z_FAR: back_cross_side,
    }
    near_parts = {X: back_side, Z_NEAR: back_near, X ^ Z_NEAR: back_near_side}
    out = pick_routes(route_ids.T, near_parts, pick_routes(route_ids.T, far_parts))
    return out.reshape(1, tokens, top, weight_mat.shape[0])


def slotted_device(section_grad, route_ids, route_gates, weight_mat, capacity):
    tokens, top = route_ids.shape
    owners = lax.axis_size("expert")
    ids = jnp.arange(owners, dtype=jnp.int32)
    slots = jnp.arange(capacity, dtype=jnp.int32)
    matched = (route_ids[:, :, None] == ids[None, None, :]).astype(jnp.int32)
    hits = jnp.sum(matched, axis=1)
    rank = jnp.cumsum(hits, axis=0) - hits
    position = route_ids * capacity + jnp.sum(matched * rank[:, None, :], axis=2)
    gate_owner = jnp.einsum(
        "tk,tke->te", route_gates.astype(jnp.float32), matched.astype(jnp.float32)
    )
    slot_pick = (hits[:, :, None] == 1) & (rank[:, :, None] == slots[None, None, :])
    send_rows = jnp.einsum(
        "tem,td->emd",
        slot_pick.astype(jnp.bfloat16),
        section_grad,
        preferred_element_type=jnp.float32,
    ).astype(jnp.bfloat16)
    send_gates = jnp.einsum("tem,te->em", slot_pick.astype(jnp.float32), gate_owner).astype(
        jnp.bfloat16
    )
    got_rows = lax.all_to_all(send_rows, "expert", split_axis=0, concat_axis=0, tiled=True)
    got_gates = lax.all_to_all(send_gates, "expert", split_axis=0, concat_axis=0, tiled=True)
    product = lax.dot_general(
        got_rows.reshape(owners * capacity, got_rows.shape[2]),
        weight_mat,
        (((1,), (1,)), ((), ())),
        preferred_element_type=jnp.float32,
    ).reshape(owners, capacity, weight_mat.shape[0])
    returned = lax.all_to_all(
        (product * got_gates.astype(jnp.float32)[:, :, None]).astype(jnp.bfloat16),
        "expert",
        split_axis=0,
        concat_axis=0,
        tiled=True,
    )
    flat = returned.reshape(owners * capacity, returned.shape[2])
    out = jnp.take(flat, position.reshape(tokens * top), axis=0)
    return out.reshape(1, tokens, top, returned.shape[2])


def per_device(upstream, expert_ids, gate_weights, expert_weight):
    route_ids = expert_ids[0]
    route_gates = gate_weights[0]
    weight_mat = expert_weight[0, 0]
    tokens, top = route_ids.shape
    owners = lax.axis_size("expert")
    capacity = 2 * tokens * top // owners
    if capacity >= tokens and owners == CORES * 2 * Z_FAR:
        return dense_device(upstream[0], route_ids, route_gates, weight_mat)
    section_grad = shifted(upstream, "pipe", -1)[0]
    return slotted_device(section_grad, route_ids, route_gates, weight_mat, capacity)


def solution(mesh):
    in_specs = (
        P("pipe", "expert", None),
        P("pipe", "expert", None),
        P("pipe", "expert", None),
        P("pipe", "expert", None, None),
    )
    out_specs = P("pipe", "expert", None, None)
    return jax.shard_map(
        per_device, mesh=mesh, in_specs=in_specs, out_specs=out_specs, check_vma=False
    )
```

```python
import functools

import jax
import jax.numpy as jnp
from jax import lax
from jax.experimental import pallas as pl
from jax.experimental.pallas import tpu as pltpu
from jax.sharding import PartitionSpec as P

CORES = 2
X, Z_NEAR, Z_FAR = 1, 2, 4
LANES = 128


def shifted(block, axis, distance):
    devices = range(lax.axis_size(axis))
    route = [((i - distance) % len(devices), i) for i in devices]
    return lax.ppermute(block, axis, route)


def send(block, owners, flip, core=0):
    route = [(i, ((i // CORES) ^ flip) * CORES + ((i % CORES) ^ core)) for i in range(owners)]
    return lax.ppermute(block, "expert", route)


def send_across(block, owners, flip):
    sections = lax.axis_size("pipe")
    route = []
    for s in range(sections):
        for i in range(owners):
            target = ((i // CORES) ^ flip) * CORES + i % CORES
            route.append((s * owners + i, (s - 1) % sections * owners + target))
    return lax.ppermute(block, ("pipe", "expert"), route)


def gates_kernel(ids, gates, out):
    top, tokens = ids.shape
    expert = lax.broadcasted_iota(jnp.int32, (LANES, tokens), 0)
    total = jnp.zeros((LANES, tokens), jnp.float32)
    for k in range(top):
        gate = gates[k : k + 1, :].astype(jnp.float32)
        total += jnp.where(expert == ids[k : k + 1, :], gate, 0.0)
    out[...] = total.T.astype(jnp.bfloat16)


def gate_columns(ids, gates):
    return pl.pallas_call(
        gates_kernel,
        out_shape=jax.ShapeDtypeStruct((ids.shape[1], LANES), jnp.bfloat16),
        compiler_params=pltpu.CompilerParams(vmem_limit_bytes=16 << 20),
    )(ids, gates)


def widen_kernel(rows, columns, out):
    depth = rows.shape[1]
    out[:, :depth] = rows[...]
    out[:, depth:] = columns[...]


def widened(rows, columns):
    width = rows.shape[1] + columns.shape[1]
    return pl.pallas_call(
        widen_kernel,
        out_shape=jax.ShapeDtypeStruct((rows.shape[0], width), jnp.bfloat16),
        compiler_params=pltpu.CompilerParams(vmem_limit_bytes=16 << 20),
    )(rows, columns)


def turn_kernel(weight, other, out):
    hidden = weight.shape[0]
    out[:, :hidden] = weight[...].T
    out[:, hidden:] = other[...].T


def turned(weight, other):
    hidden, depth = weight.shape
    return pl.pallas_call(
        turn_kernel,
        out_shape=jax.ShapeDtypeStruct((depth, CORES * hidden), weight.dtype),
        compiler_params=pltpu.CompilerParams(vmem_limit_bytes=24 << 20),
        cost_estimate=pl.CostEstimate(
            flops=4 * CORES * 1024 * hidden * depth, bytes_accessed=0, transcendentals=0
        ),
    )(weight, other)


def products_kernel(count, weights, *refs):
    pieces, outs = refs[:count], refs[count:]
    depth, width = weights.shape
    hidden = width // CORES
    tokens = outs[0].shape[1]
    me = lax.axis_index("expert")
    core = lax.rem(me, CORES)
    stacked = jnp.concatenate([p[...] for p in pieces], axis=0)
    gates = stacked[:, depth:].astype(jnp.float32)
    column = lax.broadcasted_iota(jnp.int32, gates.shape, 1)
    product = jnp.dot(stacked[:, :depth], weights[...], preferred_element_type=jnp.float32)
    for half, to in enumerate((core, 1 - core)):
        scale = jnp.sum(jnp.where(column == me - core + to, gates, 0.0), axis=1, keepdims=True)
        scaled = (product[:, half * hidden : (half + 1) * hidden] * scale).astype(jnp.bfloat16)
        for j, out in enumerate(outs):
            out[to] = scaled[j * tokens : (j + 1) * tokens]


def products(pieces, tokens, weights):
    depth, width = weights.shape
    total = sum(p.shape[0] for p in pieces)
    one = jax.ShapeDtypeStruct((CORES, tokens, width // CORES), jnp.bfloat16)
    return pl.pallas_call(
        functools.partial(products_kernel, len(pieces)),
        out_shape=[one] * (total // tokens),
        compiler_params=pltpu.CompilerParams(vmem_limit_bytes=16 << 20),
        cost_estimate=pl.CostEstimate(
            flops=20 * total * width * depth,
            bytes_accessed=2 * (total * (width + depth) + width * depth),
            transcendentals=0,
        ),
    )(weights, *pieces)


def pick_kernel(flips, ids, *refs):
    blocks, kept, out = refs[: len(flips)], refs[len(flips) : -1], refs[-1]
    experts, tokens, _ = blocks[0].shape
    top = ids.shape[0]
    span = 16
    chip = lax.div(lax.axis_index("expert"), CORES)
    flip = lax.div(ids[...], CORES) ^ chip
    place = jnp.full(flip.shape, -1, jnp.int32)
    for j, known in enumerate(flips):
        place = jnp.where(flip == known, j * CORES + lax.rem(ids[...], CORES), place)
    column = lax.broadcasted_iota(jnp.int32, (top, len(blocks) * experts * span), 1)
    for g in range(tokens // span):
        stacked = jnp.concatenate(
            [b[c, g * span : (g + 1) * span, :] for b in blocks for c in range(experts)], axis=0
        )
        picks = [
            jnp.where(column == place[:, g * span + t : g * span + t + 1] * span + t, 1.0, 0.0)
            for t in range(span)
        ]
        pick = jnp.concatenate(picks, axis=0).astype(jnp.bfloat16)
        rows = jnp.dot(pick, stacked, preferred_element_type=jnp.float32).astype(jnp.bfloat16)
        part = slice(g * span * top, (g + 1) * span * top)
        out[part, :] = rows + kept[0][part, :] if kept else rows


def pick_routes(ids, received, *kept):
    top, tokens = ids.shape
    flips = sorted(received)
    blocks = [received[flip] for flip in flips]
    return pl.pallas_call(
        functools.partial(pick_kernel, flips),
        out_shape=jax.ShapeDtypeStruct((top * tokens, blocks[0].shape[2]), jnp.bfloat16),
        compiler_params=pltpu.CompilerParams(vmem_limit_bytes=16 << 20),
    )(ids, *blocks, *kept)


def dense_device(upstream, route_ids, route_gates, weight_mat):
    tokens, top = route_ids.shape
    owners = lax.axis_size("expert")
    tie = lax.optimization_barrier

    def work(*pieces):
        return products(list(pieces), tokens, weights)

    far = send_across(upstream, owners, Z_FAR)
    rows = send_across(upstream, owners, 0)
    other_mat = send(weight_mat, owners, 0, 1)
    columns = gate_columns(route_ids.T, route_gates.T)
    far_columns = send(columns, owners, Z_FAR)
    upstream, columns = tie((upstream, columns))
    near = send_across(upstream, owners, Z_NEAR)
    near_columns = send(columns, owners, Z_NEAR)
    weights = turned(weight_mat, other_mat)
    weights, near_columns = tie((weights, near_columns))
    far, far_columns, weights = tie((far, far_columns, weights))
    far = widened(far, far_columns)
    cross = send(far, owners, Z_NEAR)
    far_side = send(far, owners, X)
    (out_far,) = work(far)
    back_far = send(out_far, owners, Z_FAR)
    near, _ = tie((near, out_far))
    near = widened(near, near_columns)
    near_side = send(near, owners, X)
    cross, near = tie((cross, near))
    cross_side = send(cross, owners, X)
    (out_cross,) = work(cross)
    back_cross = send(out_cross, owners, Z_NEAR ^ Z_FAR)
    far_side, back_far, rows, _ = tie((far_side, back_far, rows, out_cross))
    rows = widened(rows, columns)
    side = send(rows, owners, X)
    (out_far_side,) = work(far_side)
    back_far_side = send(out_far_side, owners, X ^ Z_FAR)
    cross_side, _ = tie((cross_side, out_far_side))
    (out_cross_side,) = work(cross_side)
    back_cross_side = send(out_cross_side, owners, X ^ Z_NEAR ^ Z_FAR)
    near_side, _ = tie((near_side, out_cross_side))
    out_near, out_near_side = work(near, near_side)
    back_near_side = send(out_near_side, owners, X ^ Z_NEAR)
    back_near = send(out_near, owners, Z_NEAR)
    side, rows, _ = tie((side, rows, out_near_side))
    out_side, out_own = work(side, rows)
    back_side = send(out_side, owners, X)
    far_parts = {
        0: out_own,
        Z_FAR: back_far,
        X ^ Z_FAR: back_far_side,
        Z_NEAR ^ Z_FAR: back_cross,
        X ^ Z_NEAR ^ Z_FAR: back_cross_side,
    }
    near_parts = {X: back_side, Z_NEAR: back_near, X ^ Z_NEAR: back_near_side}
    out = pick_routes(route_ids.T, near_parts, pick_routes(route_ids.T, far_parts))
    return out.reshape(1, tokens, top, weight_mat.shape[0])


def slotted_device(section_grad, route_ids, route_gates, weight_mat, capacity):
    tokens, top = route_ids.shape
    owners = lax.axis_size("expert")
    ids = jnp.arange(owners, dtype=jnp.int32)
    slots = jnp.arange(capacity, dtype=jnp.int32)
    matched = (route_ids[:, :, None] == ids[None, None, :]).astype(jnp.int32)
    hits = jnp.sum(matched, axis=1)
    rank = jnp.cumsum(hits, axis=0) - hits
    position = route_ids * capacity + jnp.sum(matched * rank[:, None, :], axis=2)
    gate_owner = jnp.einsum(
        "tk,tke->te", route_gates.astype(jnp.float32), matched.astype(jnp.float32)
    )
    slot_pick = (hits[:, :, None] == 1) & (rank[:, :, None] == slots[None, None, :])
    send_rows = jnp.einsum(
        "tem,td->emd",
        slot_pick.astype(jnp.bfloat16),
        section_grad,
        preferred_element_type=jnp.float32,
    ).astype(jnp.bfloat16)
    send_gates = jnp.einsum("tem,te->em", slot_pick.astype(jnp.float32), gate_owner).astype(
        jnp.bfloat16
    )
    got_rows = lax.all_to_all(send_rows, "expert", split_axis=0, concat_axis=0, tiled=True)
    got_gates = lax.all_to_all(send_gates, "expert", split_axis=0, concat_axis=0, tiled=True)
    product = lax.dot_general(
        got_rows.reshape(owners * capacity, got_rows.shape[2]),
        weight_mat,
        (((1,), (1,)), ((), ())),
        preferred_element_type=jnp.float32,
    ).reshape(owners, capacity, weight_mat.shape[0])
    returned = lax.all_to_all(
        (product * got_gates.astype(jnp.float32)[:, :, None]).astype(jnp.bfloat16),
        "expert",
        split_axis=0,
        concat_axis=0,
        tiled=True,
    )
    flat = returned.reshape(owners * capacity, returned.shape[2])
    out = jnp.take(flat, position.reshape(tokens * top), axis=0)
    return out.reshape(1, tokens, top, returned.shape[2])


def per_device(upstream, expert_ids, gate_weights, expert_weight):
    route_ids = expert_ids[0]
    route_gates = gate_weights[0]
    weight_mat = expert_weight[0, 0]
    tokens, top = route_ids.shape
    owners = lax.axis_size("expert")
    capacity = 2 * tokens * top // owners
    if capacity >= tokens and owners == CORES * 2 * Z_FAR:
        return dense_device(upstream[0], route_ids, route_gates, weight_mat)
    section_grad = shifted(upstream, "pipe", -1)[0]
    return slotted_device(section_grad, route_ids, route_gates, weight_mat, capacity)


def solution(mesh):
    in_specs = (
        P("pipe", "expert", None),
        P("pipe", "expert", None),
        P("pipe", "expert", None),
        P("pipe", "expert", None, None),
    )
    out_specs = P("pipe", "expert", None, None)
    return jax.shard_map(
        per_device, mesh=mesh, in_specs=in_specs, out_specs=out_specs, check_vma=False
    )
```

```python
import functools

import jax
import jax.numpy as jnp
from jax import lax
from jax.experimental import pallas as pl
from jax.experimental.pallas import tpu as pltpu
from jax.sharding import PartitionSpec as P

CORES = 2
X, Z_NEAR, Z_FAR = 1, 2, 4
LANES = 128


def shifted(block, axis, distance):
    devices = range(lax.axis_size(axis))
    route = [((i - distance) % len(devices), i) for i in devices]
    return lax.ppermute(block, axis, route)


def send(block, owners, flip, core=0):
    route = [(i, ((i // CORES) ^ flip) * CORES + ((i % CORES) ^ core)) for i in range(owners)]
    return lax.ppermute(block, "expert", route)


def send_across(block, owners, flip):
    sections = lax.axis_size("pipe")
    route = []
    for s in range(sections):
        for i in range(owners):
            target = ((i // CORES) ^ flip) * CORES + i % CORES
            route.append((s * owners + i, (s - 1) % sections * owners + target))
    return lax.ppermute(block, ("pipe", "expert"), route)


def gates_kernel(ids, gates, out):
    top, tokens = ids.shape
    expert = lax.broadcasted_iota(jnp.int32, (LANES, tokens), 0)
    total = jnp.zeros((LANES, tokens), jnp.float32)
    for k in range(top):
        gate = gates[k : k + 1, :].astype(jnp.float32)
        total += jnp.where(expert == ids[k : k + 1, :], gate, 0.0)
    out[...] = total.T.astype(jnp.bfloat16)


def gate_columns(ids, gates):
    return pl.pallas_call(
        gates_kernel,
        out_shape=jax.ShapeDtypeStruct((ids.shape[1], LANES), jnp.bfloat16),
        compiler_params=pltpu.CompilerParams(vmem_limit_bytes=16 << 20),
    )(ids, gates)


def widen_kernel(rows, columns, out):
    depth = rows.shape[1]
    out[:, :depth] = rows[...]
    out[:, depth:] = columns[...]


def widened(rows, columns):
    width = rows.shape[1] + columns.shape[1]
    return pl.pallas_call(
        widen_kernel,
        out_shape=jax.ShapeDtypeStruct((rows.shape[0], width), jnp.bfloat16),
        compiler_params=pltpu.CompilerParams(vmem_limit_bytes=16 << 20),
    )(rows, columns)


def turn_kernel(weight, other, out):
    hidden = weight.shape[0]
    out[:, :hidden] = weight[...].T
    out[:, hidden:] = other[...].T


def turned(weight, other):
    hidden, depth = weight.shape
    return pl.pallas_call(
        turn_kernel,
        out_shape=jax.ShapeDtypeStruct((depth, CORES * hidden), weight.dtype),
        compiler_params=pltpu.CompilerParams(vmem_limit_bytes=24 << 20),
        cost_estimate=pl.CostEstimate(
            flops=4 * CORES * 1024 * hidden * depth, bytes_accessed=0, transcendentals=0
        ),
    )(weight, other)


def products_kernel(count, weights, *refs):
    pieces, outs = refs[:count], refs[count:]
    depth, width = weights.shape
    hidden = width // CORES
    tokens = outs[0].shape[1]
    me = lax.axis_index("expert")
    core = lax.rem(me, CORES)
    stacked = jnp.concatenate([p[...] for p in pieces], axis=0)
    gates = stacked[:, depth:].astype(jnp.float32)
    column = lax.broadcasted_iota(jnp.int32, gates.shape, 1)
    product = jnp.dot(stacked[:, :depth], weights[...], preferred_element_type=jnp.float32)
    for half, to in enumerate((core, 1 - core)):
        scale = jnp.sum(jnp.where(column == me - core + to, gates, 0.0), axis=1, keepdims=True)
        scaled = (product[:, half * hidden : (half + 1) * hidden] * scale).astype(jnp.bfloat16)
        for j, out in enumerate(outs):
            out[to] = scaled[j * tokens : (j + 1) * tokens]


def products(pieces, tokens, weights):
    depth, width = weights.shape
    total = sum(p.shape[0] for p in pieces)
    one = jax.ShapeDtypeStruct((CORES, tokens, width // CORES), jnp.bfloat16)
    return pl.pallas_call(
        functools.partial(products_kernel, len(pieces)),
        out_shape=[one] * (total // tokens),
        compiler_params=pltpu.CompilerParams(vmem_limit_bytes=16 << 20),
        cost_estimate=pl.CostEstimate(
            flops=20 * total * width * depth,
            bytes_accessed=2 * (total * (width + depth) + width * depth),
            transcendentals=0,
        ),
    )(weights, *pieces)


def pick_kernel(flips, ids, *refs):
    blocks, kept, out = refs[: len(flips)], refs[len(flips) : -1], refs[-1]
    experts, tokens, _ = blocks[0].shape
    top = ids.shape[0]
    span = 16
    chip = lax.div(lax.axis_index("expert"), CORES)
    flip = lax.div(ids[...], CORES) ^ chip
    place = jnp.full(flip.shape, -1, jnp.int32)
    for j, known in enumerate(flips):
        place = jnp.where(flip == known, j * CORES + lax.rem(ids[...], CORES), place)
    column = lax.broadcasted_iota(jnp.int32, (top, len(blocks) * experts * span), 1)
    for g in range(tokens // span):
        stacked = jnp.concatenate(
            [b[c, g * span : (g + 1) * span, :] for b in blocks for c in range(experts)], axis=0
        )
        picks = [
            jnp.where(column == place[:, g * span + t : g * span + t + 1] * span + t, 1.0, 0.0)
            for t in range(span)
        ]
        pick = jnp.concatenate(picks, axis=0).astype(jnp.bfloat16)
        rows = jnp.dot(pick, stacked, preferred_element_type=jnp.float32).astype(jnp.bfloat16)
        part = slice(g * span * top, (g + 1) * span * top)
        out[part, :] = rows + kept[0][part, :] if kept else rows


def pick_routes(ids, received, *kept):
    top, tokens = ids.shape
    flips = sorted(received)
    blocks = [received[flip] for flip in flips]
    return pl.pallas_call(
        functools.partial(pick_kernel, flips),
        out_shape=jax.ShapeDtypeStruct((top * tokens, blocks[0].shape[2]), jnp.bfloat16),
        compiler_params=pltpu.CompilerParams(vmem_limit_bytes=16 << 20),
    )(ids, *blocks, *kept)


def dense_device(upstream, route_ids, route_gates, weight_mat):
    tokens, top = route_ids.shape
    owners = lax.axis_size("expert")
    tie = lax.optimization_barrier

    def work(*pieces):
        return products(list(pieces), tokens, weights)

    far = send_across(upstream, owners, Z_FAR)
    rows = send_across(upstream, owners, 0)
    other_mat = send(weight_mat, owners, 0, 1)
    columns = gate_columns(route_ids.T, route_gates.T)
    far_columns = send(columns, owners, Z_FAR)
    upstream, columns = tie((upstream, columns))
    near = send_across(upstream, owners, Z_NEAR)
    near_columns = send(columns, owners, Z_NEAR)
    weights = turned(weight_mat, other_mat)
    weights, near_columns = tie((weights, near_columns))
    far, far_columns, weights = tie((far, far_columns, weights))
    far = widened(far, far_columns)
    cross = send(far, owners, Z_NEAR)
    far_side = send(far, owners, X)
    (out_far,) = work(far)
    back_far = send(out_far, owners, Z_FAR)
    near, _ = tie((near, out_far))
    near = widened(near, near_columns)
    near_side = send(near, owners, X)
    cross, near = tie((cross, near))
    cross_side = send(cross, owners, X)
    (out_cross,) = work(cross)
    back_cross = send(out_cross, owners, Z_NEAR ^ Z_FAR)
    far_side, back_far, rows, _ = tie((far_side, back_far, rows, out_cross))
    rows = widened(rows, columns)
    side = send(rows, owners, X)
    (out_far_side,) = work(far_side)
    back_far_side = send(out_far_side, owners, X ^ Z_FAR)
    cross_side, _ = tie((cross_side, out_far_side))
    (out_cross_side,) = work(cross_side)
    back_cross_side = send(out_cross_side, owners, X ^ Z_NEAR ^ Z_FAR)
    near_side, _ = tie((near_side, out_cross_side))
    out_near, out_near_side = work(near, near_side)
    back_near_side = send(out_near_side, owners, X ^ Z_NEAR)
    back_near = send(out_near, owners, Z_NEAR)
    side, rows, _ = tie((side, rows, out_near_side))
    out_side, out_own = work(side, rows)
    back_side = send(out_side, owners, X)
    first_parts = {
        Z_NEAR: back_near,
        X ^ Z_NEAR: back_near_side,
        Z_FAR: back_far,
        X ^ Z_FAR: back_far_side,
        Z_NEAR ^ Z_FAR: back_cross,
        X ^ Z_NEAR ^ Z_FAR: back_cross_side,
    }
    last_parts = {0: out_own, X: back_side}
    out = pick_routes(route_ids.T, last_parts, pick_routes(route_ids.T, first_parts))
    return out.reshape(1, tokens, top, weight_mat.shape[0])


def slotted_device(section_grad, route_ids, route_gates, weight_mat, capacity):
    tokens, top = route_ids.shape
    owners = lax.axis_size("expert")
    ids = jnp.arange(owners, dtype=jnp.int32)
    slots = jnp.arange(capacity, dtype=jnp.int32)
    matched = (route_ids[:, :, None] == ids[None, None, :]).astype(jnp.int32)
    hits = jnp.sum(matched, axis=1)
    rank = jnp.cumsum(hits, axis=0) - hits
    position = route_ids * capacity + jnp.sum(matched * rank[:, None, :], axis=2)
    gate_owner = jnp.einsum(
        "tk,tke->te", route_gates.astype(jnp.float32), matched.astype(jnp.float32)
    )
    slot_pick = (hits[:, :, None] == 1) & (rank[:, :, None] == slots[None, None, :])
    send_rows = jnp.einsum(
        "tem,td->emd",
        slot_pick.astype(jnp.bfloat16),
        section_grad,
        preferred_element_type=jnp.float32,
    ).astype(jnp.bfloat16)
    send_gates = jnp.einsum("tem,te->em", slot_pick.astype(jnp.float32), gate_owner).astype(
        jnp.bfloat16
    )
    got_rows = lax.all_to_all(send_rows, "expert", split_axis=0, concat_axis=0, tiled=True)
    got_gates = lax.all_to_all(send_gates, "expert", split_axis=0, concat_axis=0, tiled=True)
    product = lax.dot_general(
        got_rows.reshape(owners * capacity, got_rows.shape[2]),
        weight_mat,
        (((1,), (1,)), ((), ())),
        preferred_element_type=jnp.float32,
    ).reshape(owners, capacity, weight_mat.shape[0])
    returned = lax.all_to_all(
        (product * got_gates.astype(jnp.float32)[:, :, None]).astype(jnp.bfloat16),
        "expert",
        split_axis=0,
        concat_axis=0,
        tiled=True,
    )
    flat = returned.reshape(owners * capacity, returned.shape[2])
    out = jnp.take(flat, position.reshape(tokens * top), axis=0)
    return out.reshape(1, tokens, top, returned.shape[2])


def per_device(upstream, expert_ids, gate_weights, expert_weight):
    route_ids = expert_ids[0]
    route_gates = gate_weights[0]
    weight_mat = expert_weight[0, 0]
    tokens, top = route_ids.shape
    owners = lax.axis_size("expert")
    capacity = 2 * tokens * top // owners
    if capacity >= tokens and owners == CORES * 2 * Z_FAR:
        return dense_device(upstream[0], route_ids, route_gates, weight_mat)
    section_grad = shifted(upstream, "pipe", -1)[0]
    return slotted_device(section_grad, route_ids, route_gates, weight_mat, capacity)


def solution(mesh):
    in_specs = (
        P("pipe", "expert", None),
        P("pipe", "expert", None),
        P("pipe", "expert", None),
        P("pipe", "expert", None, None),
    )
    out_specs = P("pipe", "expert", None, None)
    return jax.shard_map(
        per_device, mesh=mesh, in_specs=in_specs, out_specs=out_specs, check_vma=False
    )
```

```python
import functools

import jax
import jax.numpy as jnp
from jax import lax
from jax.experimental import pallas as pl
from jax.experimental.pallas import tpu as pltpu
from jax.sharding import PartitionSpec as P

CORES = 2
X, Z_NEAR, Z_FAR = 1, 2, 4
LANES = 128


def shifted(block, axis, distance):
    devices = range(lax.axis_size(axis))
    route = [((i - distance) % len(devices), i) for i in devices]
    return lax.ppermute(block, axis, route)


def send(block, owners, flip, core=0):
    route = [(i, ((i // CORES) ^ flip) * CORES + ((i % CORES) ^ core)) for i in range(owners)]
    return lax.ppermute(block, "expert", route)


def send_across(block, owners, flip):
    sections = lax.axis_size("pipe")
    route = []
    for s in range(sections):
        for i in range(owners):
            target = ((i // CORES) ^ flip) * CORES + i % CORES
            route.append((s * owners + i, (s - 1) % sections * owners + target))
    return lax.ppermute(block, ("pipe", "expert"), route)


def gates_kernel(ids, gates, out):
    top, tokens = ids.shape
    expert = lax.broadcasted_iota(jnp.int32, (LANES, tokens), 0)
    total = jnp.zeros((LANES, tokens), jnp.float32)
    wide = gates[...].astype(jnp.float32)
    for k in range(top):
        total += jnp.where(expert == ids[k : k + 1, :], wide[k : k + 1, :], 0.0)
    out[...] = total.T.astype(jnp.bfloat16)


def gate_columns(ids, gates):
    return pl.pallas_call(
        gates_kernel,
        out_shape=jax.ShapeDtypeStruct((ids.shape[1], LANES), jnp.bfloat16),
        compiler_params=pltpu.CompilerParams(vmem_limit_bytes=16 << 20),
    )(ids, gates)


def widen_kernel(rows, columns, out):
    depth = rows.shape[1]
    out[:, :depth] = rows[...]
    out[:, depth:] = columns[...]


def widened(rows, columns):
    width = rows.shape[1] + columns.shape[1]
    return pl.pallas_call(
        widen_kernel,
        out_shape=jax.ShapeDtypeStruct((rows.shape[0], width), jnp.bfloat16),
        compiler_params=pltpu.CompilerParams(vmem_limit_bytes=16 << 20),
    )(rows, columns)


def turn_kernel(weight, other, out):
    hidden = weight.shape[0]
    out[:, :hidden] = weight[...].T
    out[:, hidden:] = other[...].T


def turned(weight, other):
    hidden, depth = weight.shape
    return pl.pallas_call(
        turn_kernel,
        out_shape=jax.ShapeDtypeStruct((depth, CORES * hidden), weight.dtype),
        compiler_params=pltpu.CompilerParams(vmem_limit_bytes=24 << 20),
        cost_estimate=pl.CostEstimate(
            flops=4 * CORES * 1024 * hidden * depth, bytes_accessed=0, transcendentals=0
        ),
    )(weight, other)


def products_kernel(count, weights, *refs):
    pieces, outs = refs[:count], refs[count:]
    depth, width = weights.shape
    hidden = width // CORES
    tokens = outs[0].shape[1]
    me = lax.axis_index("expert")
    core = lax.rem(me, CORES)
    stacked = jnp.concatenate([p[...] for p in pieces], axis=0)
    gates = stacked[:, depth:].astype(jnp.float32)
    column = lax.broadcasted_iota(jnp.int32, gates.shape, 1)
    product = jnp.dot(stacked[:, :depth], weights[...], preferred_element_type=jnp.float32)
    for half, to in enumerate((core, 1 - core)):
        scale = jnp.sum(jnp.where(column == me - core + to, gates, 0.0), axis=1, keepdims=True)
        scaled = (product[:, half * hidden : (half + 1) * hidden] * scale).astype(jnp.bfloat16)
        for j, out in enumerate(outs):
            out[to] = scaled[j * tokens : (j + 1) * tokens]


def products(pieces, tokens, weights):
    depth, width = weights.shape
    total = sum(p.shape[0] for p in pieces)
    one = jax.ShapeDtypeStruct((CORES, tokens, width // CORES), jnp.bfloat16)
    return pl.pallas_call(
        functools.partial(products_kernel, len(pieces)),
        out_shape=[one] * (total // tokens),
        compiler_params=pltpu.CompilerParams(vmem_limit_bytes=16 << 20),
        cost_estimate=pl.CostEstimate(
            flops=20 * total * width * depth,
            bytes_accessed=2 * (total * (width + depth) + width * depth),
            transcendentals=0,
        ),
    )(weights, *pieces)


def pick_kernel(flips, ids, *refs):
    blocks, kept, out = refs[: len(flips)], refs[len(flips) : -1], refs[-1]
    experts, tokens, _ = blocks[0].shape
    top = ids.shape[0]
    span = 16
    chip = lax.div(lax.axis_index("expert"), CORES)
    flip = lax.div(ids[...], CORES) ^ chip
    place = jnp.full(flip.shape, -1, jnp.int32)
    for j, known in enumerate(flips):
        place = jnp.where(flip == known, j * CORES + lax.rem(ids[...], CORES), place)
    column = lax.broadcasted_iota(jnp.int32, (top, len(blocks) * experts * span), 1)
    for g in range(tokens // span):
        stacked = jnp.concatenate(
            [b[c, g * span : (g + 1) * span, :] for b in blocks for c in range(experts)], axis=0
        )
        picks = [
            jnp.where(column == place[:, g * span + t : g * span + t + 1] * span + t, 1.0, 0.0)
            for t in range(span)
        ]
        pick = jnp.concatenate(picks, axis=0).astype(jnp.bfloat16)
        rows = jnp.dot(pick, stacked, preferred_element_type=jnp.float32).astype(jnp.bfloat16)
        part = slice(g * span * top, (g + 1) * span * top)
        out[part, :] = rows + kept[0][part, :] if kept else rows


def pick_routes(ids, received, *kept):
    top, tokens = ids.shape
    flips = sorted(received)
    blocks = [received[flip] for flip in flips]
    return pl.pallas_call(
        functools.partial(pick_kernel, flips),
        out_shape=jax.ShapeDtypeStruct((top * tokens, blocks[0].shape[2]), jnp.bfloat16),
        compiler_params=pltpu.CompilerParams(vmem_limit_bytes=16 << 20),
    )(ids, *blocks, *kept)


def dense_device(upstream, route_ids, route_gates, weight_mat):
    tokens, top = route_ids.shape
    owners = lax.axis_size("expert")
    tie = lax.optimization_barrier

    def work(*pieces):
        return products(list(pieces), tokens, weights)

    far = send_across(upstream, owners, Z_FAR)
    rows = send_across(upstream, owners, 0)
    other_mat = send(weight_mat, owners, 0, 1)
    columns = gate_columns(route_ids.T, route_gates.T)
    far_columns = send(columns, owners, Z_FAR)
    upstream, columns = tie((upstream, columns))
    near = send_across(upstream, owners, Z_NEAR)
    near_columns = send(columns, owners, Z_NEAR)
    weights = turned(weight_mat, other_mat)
    weights, near_columns = tie((weights, near_columns))
    far, far_columns, weights = tie((far, far_columns, weights))
    far = widened(far, far_columns)
    cross = send(far, owners, Z_NEAR)
    far_side = send(far, owners, X)
    (out_far,) = work(far)
    back_far = send(out_far, owners, Z_FAR)
    near, _ = tie((near, out_far))
    near = widened(near, near_columns)
    near_side = send(near, owners, X)
    cross, near = tie((cross, near))
    cross_side = send(cross, owners, X)
    (out_cross,) = work(cross)
    back_cross = send(out_cross, owners, Z_NEAR ^ Z_FAR)
    far_side, back_far, rows, _ = tie((far_side, back_far, rows, out_cross))
    rows = widened(rows, columns)
    side = send(rows, owners, X)
    (out_far_side,) = work(far_side)
    back_far_side = send(out_far_side, owners, X ^ Z_FAR)
    cross_side, _ = tie((cross_side, out_far_side))
    (out_cross_side,) = work(cross_side)
    back_cross_side = send(out_cross_side, owners, X ^ Z_NEAR ^ Z_FAR)
    near_side, _ = tie((near_side, out_cross_side))
    out_near, out_near_side = work(near, near_side)
    back_near_side = send(out_near_side, owners, X ^ Z_NEAR)
    back_near = send(out_near, owners, Z_NEAR)
    side, rows, _ = tie((side, rows, out_near_side))
    out_side, out_own = work(side, rows)
    back_side = send(out_side, owners, X)
    far_parts = {
        0: out_own,
        Z_FAR: back_far,
        X ^ Z_FAR: back_far_side,
        Z_NEAR ^ Z_FAR: back_cross,
        X ^ Z_NEAR ^ Z_FAR: back_cross_side,
    }
    near_parts = {X: back_side, Z_NEAR: back_near, X ^ Z_NEAR: back_near_side}
    out = pick_routes(route_ids.T, near_parts, pick_routes(route_ids.T, far_parts))
    return out.reshape(1, tokens, top, weight_mat.shape[0])


def slotted_device(section_grad, route_ids, route_gates, weight_mat, capacity):
    tokens, top = route_ids.shape
    owners = lax.axis_size("expert")
    ids = jnp.arange(owners, dtype=jnp.int32)
    slots = jnp.arange(capacity, dtype=jnp.int32)
    matched = (route_ids[:, :, None] == ids[None, None, :]).astype(jnp.int32)
    hits = jnp.sum(matched, axis=1)
    rank = jnp.cumsum(hits, axis=0) - hits
    position = route_ids * capacity + jnp.sum(matched * rank[:, None, :], axis=2)
    gate_owner = jnp.einsum(
        "tk,tke->te", route_gates.astype(jnp.float32), matched.astype(jnp.float32)
    )
    slot_pick = (hits[:, :, None] == 1) & (rank[:, :, None] == slots[None, None, :])
    send_rows = jnp.einsum(
        "tem,td->emd",
        slot_pick.astype(jnp.bfloat16),
        section_grad,
        preferred_element_type=jnp.float32,
    ).astype(jnp.bfloat16)
    send_gates = jnp.einsum("tem,te->em", slot_pick.astype(jnp.float32), gate_owner).astype(
        jnp.bfloat16
    )
    got_rows = lax.all_to_all(send_rows, "expert", split_axis=0, concat_axis=0, tiled=True)
    got_gates = lax.all_to_all(send_gates, "expert", split_axis=0, concat_axis=0, tiled=True)
    product = lax.dot_general(
        got_rows.reshape(owners * capacity, got_rows.shape[2]),
        weight_mat,
        (((1,), (1,)), ((), ())),
        preferred_element_type=jnp.float32,
    ).reshape(owners, capacity, weight_mat.shape[0])
    returned = lax.all_to_all(
        (product * got_gates.astype(jnp.float32)[:, :, None]).astype(jnp.bfloat16),
        "expert",
        split_axis=0,
        concat_axis=0,
        tiled=True,
    )
    flat = returned.reshape(owners * capacity, returned.shape[2])
    out = jnp.take(flat, position.reshape(tokens * top), axis=0)
    return out.reshape(1, tokens, top, returned.shape[2])


def per_device(upstream, expert_ids, gate_weights, expert_weight):
    route_ids = expert_ids[0]
    route_gates = gate_weights[0]
    weight_mat = expert_weight[0, 0]
    tokens, top = route_ids.shape
    owners = lax.axis_size("expert")
    capacity = 2 * tokens * top // owners
    if capacity >= tokens and owners == CORES * 2 * Z_FAR:
        return dense_device(upstream[0], route_ids, route_gates, weight_mat)
    section_grad = shifted(upstream, "pipe", -1)[0]
    return slotted_device(section_grad, route_ids, route_gates, weight_mat, capacity)


def solution(mesh):
    in_specs = (
        P("pipe", "expert", None),
        P("pipe", "expert", None),
        P("pipe", "expert", None),
        P("pipe", "expert", None, None),
    )
    out_specs = P("pipe", "expert", None, None)
    return jax.shard_map(
        per_device, mesh=mesh, in_specs=in_specs, out_specs=out_specs, check_vma=False
    )
```

```python
import functools

import jax
import jax.numpy as jnp
from jax import lax
from jax.experimental import pallas as pl
from jax.experimental.pallas import tpu as pltpu
from jax.sharding import PartitionSpec as P

CORES = 2
X, Z_NEAR, Z_FAR = 1, 2, 4
LANES = 128


def shifted(block, axis, distance):
    devices = range(lax.axis_size(axis))
    route = [((i - distance) % len(devices), i) for i in devices]
    return lax.ppermute(block, axis, route)


def send(block, owners, flip, core=0):
    route = [(i, ((i // CORES) ^ flip) * CORES + ((i % CORES) ^ core)) for i in range(owners)]
    return lax.ppermute(block, "expert", route)


def send_across(block, owners, flip):
    sections = lax.axis_size("pipe")
    route = []
    for s in range(sections):
        for i in range(owners):
            target = ((i // CORES) ^ flip) * CORES + i % CORES
            route.append((s * owners + i, (s - 1) % sections * owners + target))
    return lax.ppermute(block, ("pipe", "expert"), route)


def gates_kernel(ids, gates, out):
    top, tokens = ids.shape
    expert = lax.broadcasted_iota(jnp.int32, (LANES, tokens), 0)
    total = jnp.zeros((LANES, tokens), jnp.float32)
    wide = gates[...].astype(jnp.float32)
    for k in range(top):
        total += jnp.where(expert == ids[k : k + 1, :], wide[k : k + 1, :], 0.0)
    out[...] = total.T.astype(jnp.bfloat16)


def gate_columns(ids, gates):
    return pl.pallas_call(
        gates_kernel,
        out_shape=jax.ShapeDtypeStruct((ids.shape[1], LANES), jnp.bfloat16),
        compiler_params=pltpu.CompilerParams(vmem_limit_bytes=16 << 20),
    )(ids, gates)


def widen_kernel(rows, columns, out):
    depth = rows.shape[1]
    out[:, :depth] = rows[...]
    out[:, depth:] = columns[...]


def widened(rows, columns):
    width = rows.shape[1] + columns.shape[1]
    return pl.pallas_call(
        widen_kernel,
        out_shape=jax.ShapeDtypeStruct((rows.shape[0], width), jnp.bfloat16),
        compiler_params=pltpu.CompilerParams(vmem_limit_bytes=16 << 20),
    )(rows, columns)


def turn_kernel(weight, other, out):
    hidden = weight.shape[0]
    out[:, :hidden] = weight[...].T
    out[:, hidden:] = other[...].T


def turned(weight, other):
    hidden, depth = weight.shape
    return pl.pallas_call(
        turn_kernel,
        out_shape=jax.ShapeDtypeStruct((depth, CORES * hidden), weight.dtype),
        compiler_params=pltpu.CompilerParams(vmem_limit_bytes=24 << 20),
        cost_estimate=pl.CostEstimate(
            flops=4 * CORES * 1024 * hidden * depth, bytes_accessed=0, transcendentals=0
        ),
    )(weight, other)


def products_kernel(count, weights, *refs):
    pieces, outs = refs[:count], refs[count:]
    depth, width = weights.shape
    hidden = width // CORES
    tokens = outs[0].shape[1]
    me = lax.axis_index("expert")
    core = lax.rem(me, CORES)
    stacked = jnp.concatenate([p[...] for p in pieces], axis=0)
    gates = stacked[:, depth:].astype(jnp.float32)
    column = lax.broadcasted_iota(jnp.int32, gates.shape, 1)
    product = jnp.dot(stacked[:, :depth], weights[...], preferred_element_type=jnp.float32)
    for half, to in enumerate((core, 1 - core)):
        scale = jnp.sum(jnp.where(column == me - core + to, gates, 0.0), axis=1, keepdims=True)
        scaled = (product[:, half * hidden : (half + 1) * hidden] * scale).astype(jnp.bfloat16)
        for j, out in enumerate(outs):
            out[to] = scaled[j * tokens : (j + 1) * tokens]


def products(pieces, tokens, weights):
    depth, width = weights.shape
    total = sum(p.shape[0] for p in pieces)
    one = jax.ShapeDtypeStruct((CORES, tokens, width // CORES), jnp.bfloat16)
    return pl.pallas_call(
        functools.partial(products_kernel, len(pieces)),
        out_shape=[one] * (total // tokens),
        compiler_params=pltpu.CompilerParams(vmem_limit_bytes=16 << 20),
        cost_estimate=pl.CostEstimate(
            flops=20 * total * width * depth,
            bytes_accessed=2 * (total * (width + depth) + width * depth),
            transcendentals=0,
        ),
    )(weights, *pieces)


def pick_kernel(flips, ids, *refs):
    blocks, kept, out = refs[: len(flips)], refs[len(flips) : -1], refs[-1]
    experts, tokens, _ = blocks[0].shape
    top = ids.shape[0]
    span = 16
    chip = lax.div(lax.axis_index("expert"), CORES)
    flip = lax.div(ids[...], CORES) ^ chip
    place = jnp.full(flip.shape, -1, jnp.int32)
    for j, known in enumerate(flips):
        place = jnp.where(flip == known, j * CORES + lax.rem(ids[...], CORES), place)
    column = lax.broadcasted_iota(jnp.int32, (top, len(blocks) * experts * span), 1)
    for g in range(tokens // span):
        stacked = jnp.concatenate(
            [b[c, g * span : (g + 1) * span, :] for b in blocks for c in range(experts)], axis=0
        )
        picks = [
            jnp.where(column == place[:, g * span + t : g * span + t + 1] * span + t, 1.0, 0.0)
            for t in range(span)
        ]
        pick = jnp.concatenate(picks, axis=0).astype(jnp.bfloat16)
        rows = jnp.dot(pick, stacked, preferred_element_type=jnp.float32).astype(jnp.bfloat16)
        part = slice(g * span * top, (g + 1) * span * top)
        out[part, :] = rows + kept[0][part, :] if kept else rows


def pick_routes(ids, received, *kept):
    top, tokens = ids.shape
    flips = sorted(received)
    blocks = [received[flip] for flip in flips]
    return pl.pallas_call(
        functools.partial(pick_kernel, flips),
        out_shape=jax.ShapeDtypeStruct((top * tokens, blocks[0].shape[2]), jnp.bfloat16),
        compiler_params=pltpu.CompilerParams(vmem_limit_bytes=16 << 20),
    )(ids, *blocks, *kept)


def dense_device(upstream, route_ids, route_gates, weight_mat):
    tokens, top = route_ids.shape
    owners = lax.axis_size("expert")
    tie = lax.optimization_barrier

    def work(*pieces):
        return products(list(pieces), tokens, weights)

    far = send_across(upstream, owners, Z_FAR)
    rows = send_across(upstream, owners, 0)
    other_mat = send(weight_mat, owners, 0, 1)
    columns = gate_columns(route_ids.T, route_gates.T)
    far_columns = send(columns, owners, Z_FAR)
    upstream, columns = tie((upstream, columns))
    near = send_across(upstream, owners, Z_NEAR)
    near_columns = send(columns, owners, Z_NEAR)
    weights = turned(weight_mat, other_mat)
    weights, near_columns = tie((weights, near_columns))
    far, far_columns, weights = tie((far, far_columns, weights))
    far = widened(far, far_columns)
    cross = send(far, owners, Z_NEAR)
    far_side = send(far, owners, X)
    (out_far,) = work(far)
    back_far = send(out_far, owners, Z_FAR)
    near, _ = tie((near, out_far))
    near = widened(near, near_columns)
    near_side = send(near, owners, X)
    cross, near = tie((cross, near))
    cross_side = send(cross, owners, X)
    (out_cross,) = work(cross)
    back_cross = send(out_cross, owners, Z_NEAR ^ Z_FAR)
    far_side, back_far, rows, _ = tie((far_side, back_far, rows, out_cross))
    rows = widened(rows, columns)
    side = send(rows, owners, X)
    (out_far_side,) = work(far_side)
    back_far_side = send(out_far_side, owners, X ^ Z_FAR)
    cross_side, _ = tie((cross_side, out_far_side))
    (out_cross_side,) = work(cross_side)
    back_cross_side = send(out_cross_side, owners, X ^ Z_NEAR ^ Z_FAR)
    near_side, side, rows, _ = tie((near_side, side, rows, out_cross_side))
    out_near, out_near_side, out_side, out_own = work(near, near_side, side, rows)
    back_near_side = send(out_near_side, owners, X ^ Z_NEAR)
    back_near = send(out_near, owners, Z_NEAR)
    back_side = send(out_side, owners, X)
    far_parts = {
        0: out_own,
        Z_FAR: back_far,
        X ^ Z_FAR: back_far_side,
        Z_NEAR ^ Z_FAR: back_cross,
        X ^ Z_NEAR ^ Z_FAR: back_cross_side,
    }
    near_parts = {X: back_side, Z_NEAR: back_near, X ^ Z_NEAR: back_near_side}
    out = pick_routes(route_ids.T, near_parts, pick_routes(route_ids.T, far_parts))
    return out.reshape(1, tokens, top, weight_mat.shape[0])


def slotted_device(section_grad, route_ids, route_gates, weight_mat, capacity):
    tokens, top = route_ids.shape
    owners = lax.axis_size("expert")
    ids = jnp.arange(owners, dtype=jnp.int32)
    slots = jnp.arange(capacity, dtype=jnp.int32)
    matched = (route_ids[:, :, None] == ids[None, None, :]).astype(jnp.int32)
    hits = jnp.sum(matched, axis=1)
    rank = jnp.cumsum(hits, axis=0) - hits
    position = route_ids * capacity + jnp.sum(matched * rank[:, None, :], axis=2)
    gate_owner = jnp.einsum(
        "tk,tke->te", route_gates.astype(jnp.float32), matched.astype(jnp.float32)
    )
    slot_pick = (hits[:, :, None] == 1) & (rank[:, :, None] == slots[None, None, :])
    send_rows = jnp.einsum(
        "tem,td->emd",
        slot_pick.astype(jnp.bfloat16),
        section_grad,
        preferred_element_type=jnp.float32,
    ).astype(jnp.bfloat16)
    send_gates = jnp.einsum("tem,te->em", slot_pick.astype(jnp.float32), gate_owner).astype(
        jnp.bfloat16
    )
    got_rows = lax.all_to_all(send_rows, "expert", split_axis=0, concat_axis=0, tiled=True)
    got_gates = lax.all_to_all(send_gates, "expert", split_axis=0, concat_axis=0, tiled=True)
    product = lax.dot_general(
        got_rows.reshape(owners * capacity, got_rows.shape[2]),
        weight_mat,
        (((1,), (1,)), ((), ())),
        preferred_element_type=jnp.float32,
    ).reshape(owners, capacity, weight_mat.shape[0])
    returned = lax.all_to_all(
        (product * got_gates.astype(jnp.float32)[:, :, None]).astype(jnp.bfloat16),
        "expert",
        split_axis=0,
        concat_axis=0,
        tiled=True,
    )
    flat = returned.reshape(owners * capacity, returned.shape[2])
    out = jnp.take(flat, position.reshape(tokens * top), axis=0)
    return out.reshape(1, tokens, top, returned.shape[2])


def per_device(upstream, expert_ids, gate_weights, expert_weight):
    route_ids = expert_ids[0]
    route_gates = gate_weights[0]
    weight_mat = expert_weight[0, 0]
    tokens, top = route_ids.shape
    owners = lax.axis_size("expert")
    capacity = 2 * tokens * top // owners
    if capacity >= tokens and owners == CORES * 2 * Z_FAR:
        return dense_device(upstream[0], route_ids, route_gates, weight_mat)
    section_grad = shifted(upstream, "pipe", -1)[0]
    return slotted_device(section_grad, route_ids, route_gates, weight_mat, capacity)


def solution(mesh):
    in_specs = (
        P("pipe", "expert", None),
        P("pipe", "expert", None),
        P("pipe", "expert", None),
        P("pipe", "expert", None, None),
    )
    out_specs = P("pipe", "expert", None, None)
    return jax.shard_map(
        per_device, mesh=mesh, in_specs=in_specs, out_specs=out_specs, check_vma=False
    )
```

```python
import functools

import jax
import jax.numpy as jnp
from jax import lax
from jax.experimental import pallas as pl
from jax.experimental.pallas import tpu as pltpu
from jax.sharding import PartitionSpec as P

CORES = 2
X, Z_NEAR, Z_FAR = 1, 2, 4
LANES = 128


def shifted(block, axis, distance):
    devices = range(lax.axis_size(axis))
    route = [((i - distance) % len(devices), i) for i in devices]
    return lax.ppermute(block, axis, route)


def send(block, owners, flip, core=0):
    route = [(i, ((i // CORES) ^ flip) * CORES + ((i % CORES) ^ core)) for i in range(owners)]
    return lax.ppermute(block, "expert", route)


def send_across(block, owners, flip):
    sections = lax.axis_size("pipe")
    route = []
    for s in range(sections):
        for i in range(owners):
            target = ((i // CORES) ^ flip) * CORES + i % CORES
            route.append((s * owners + i, (s - 1) % sections * owners + target))
    return lax.ppermute(block, ("pipe", "expert"), route)


def gates_kernel(ids, gates, out):
    top, tokens = ids.shape
    expert = lax.broadcasted_iota(jnp.int32, (LANES, tokens), 0)
    total = jnp.zeros((LANES, tokens), jnp.float32)
    wide = gates[...].astype(jnp.float32)
    for k in range(top):
        total += jnp.where(expert == ids[k : k + 1, :], wide[k : k + 1, :], 0.0)
    out[...] = total.T.astype(jnp.bfloat16)


def gate_columns(ids, gates):
    return pl.pallas_call(
        gates_kernel,
        out_shape=jax.ShapeDtypeStruct((ids.shape[1], LANES), jnp.bfloat16),
        compiler_params=pltpu.CompilerParams(vmem_limit_bytes=16 << 20),
    )(ids, gates)


def widen_kernel(rows, columns, out):
    depth = rows.shape[1]
    out[:, :depth] = rows[...]
    out[:, depth:] = columns[...]


def widened(rows, columns):
    width = rows.shape[1] + columns.shape[1]
    return pl.pallas_call(
        widen_kernel,
        out_shape=jax.ShapeDtypeStruct((rows.shape[0], width), jnp.bfloat16),
        compiler_params=pltpu.CompilerParams(vmem_limit_bytes=16 << 20),
    )(rows, columns)


def turn_kernel(weight, other, out):
    hidden = weight.shape[0]
    out[:, :hidden] = weight[...].T
    out[:, hidden:] = other[...].T


def turned(weight, other):
    hidden, depth = weight.shape
    return pl.pallas_call(
        turn_kernel,
        out_shape=jax.ShapeDtypeStruct((depth, CORES * hidden), weight.dtype),
        compiler_params=pltpu.CompilerParams(vmem_limit_bytes=24 << 20),
        cost_estimate=pl.CostEstimate(
            flops=4 * CORES * 1024 * hidden * depth, bytes_accessed=0, transcendentals=0
        ),
    )(weight, other)


def products_kernel(count, weights, *refs):
    pieces, outs = refs[:count], refs[count:]
    depth, width = weights.shape
    hidden = width // CORES
    tokens = outs[0].shape[1]
    me = lax.axis_index("expert")
    core = lax.rem(me, CORES)
    stacked = jnp.concatenate([p[...] for p in pieces], axis=0)
    gates = stacked[:, depth:].astype(jnp.float32)
    column = lax.broadcasted_iota(jnp.int32, gates.shape, 1)
    product = jnp.dot(stacked[:, :depth], weights[...], preferred_element_type=jnp.float32)
    for half, to in enumerate((core, 1 - core)):
        scale = jnp.sum(jnp.where(column == me - core + to, gates, 0.0), axis=1, keepdims=True)
        scaled = (product[:, half * hidden : (half + 1) * hidden] * scale).astype(jnp.bfloat16)
        for j, out in enumerate(outs):
            out[to] = scaled[j * tokens : (j + 1) * tokens]


def products(pieces, tokens, weights):
    depth, width = weights.shape
    total = sum(p.shape[0] for p in pieces)
    one = jax.ShapeDtypeStruct((CORES, tokens, width // CORES), jnp.bfloat16)
    return pl.pallas_call(
        functools.partial(products_kernel, len(pieces)),
        out_shape=[one] * (total // tokens),
        compiler_params=pltpu.CompilerParams(vmem_limit_bytes=16 << 20),
        cost_estimate=pl.CostEstimate(
            flops=20 * total * width * depth,
            bytes_accessed=2 * (total * (width + depth) + width * depth),
            transcendentals=0,
        ),
    )(weights, *pieces)


def pick_kernel(flips, ids, *refs):
    blocks, kept, out = refs[: len(flips)], refs[len(flips) : -1], refs[-1]
    experts, tokens, _ = blocks[0].shape
    top = ids.shape[0]
    span = 16
    chip = lax.div(lax.axis_index("expert"), CORES)
    flip = lax.div(ids[...], CORES) ^ chip
    place = jnp.full(flip.shape, -1, jnp.int32)
    for j, known in enumerate(flips):
        place = jnp.where(flip == known, j * CORES + lax.rem(ids[...], CORES), place)
    column = lax.broadcasted_iota(jnp.int32, (top, len(blocks) * experts * span), 1)
    for g in range(tokens // span):
        stacked = jnp.concatenate(
            [b[c, g * span : (g + 1) * span, :] for b in blocks for c in range(experts)], axis=0
        )
        picks = [
            jnp.where(column == place[:, g * span + t : g * span + t + 1] * span + t, 1.0, 0.0)
            for t in range(span)
        ]
        pick = jnp.concatenate(picks, axis=0).astype(jnp.bfloat16)
        rows = jnp.dot(pick, stacked, preferred_element_type=jnp.float32).astype(jnp.bfloat16)
        part = slice(g * span * top, (g + 1) * span * top)
        out[part, :] = rows + kept[0][part, :] if kept else rows


def pick_routes(ids, received, *kept):
    top, tokens = ids.shape
    flips = sorted(received)
    blocks = [received[flip] for flip in flips]
    return pl.pallas_call(
        functools.partial(pick_kernel, flips),
        out_shape=jax.ShapeDtypeStruct((top * tokens, blocks[0].shape[2]), jnp.bfloat16),
        compiler_params=pltpu.CompilerParams(vmem_limit_bytes=16 << 20),
    )(ids, *blocks, *kept)


def dense_device(upstream, route_ids, route_gates, weight_mat):
    tokens, top = route_ids.shape
    owners = lax.axis_size("expert")
    tie = lax.optimization_barrier

    def work(*pieces):
        return products(list(pieces), tokens, weights)

    far = send_across(upstream, owners, Z_FAR)
    rows = send_across(upstream, owners, 0)
    other_mat = send(weight_mat, owners, 0, 1)
    columns = gate_columns(route_ids.T, route_gates.T)
    far_columns = send(columns, owners, Z_FAR)
    upstream, columns = tie((upstream, columns))
    near = send_across(upstream, owners, Z_NEAR)
    near_columns = send(columns, owners, Z_NEAR)
    weights = turned(weight_mat, other_mat)
    weights, near_columns = tie((weights, near_columns))
    far, far_columns, weights = tie((far, far_columns, weights))
    far = widened(far, far_columns)
    cross = send(far, owners, Z_NEAR)
    far_side = send(far, owners, X)
    (out_far,) = work(far)
    back_far = send(out_far, owners, Z_FAR)
    near, _ = tie((near, out_far))
    near = widened(near, near_columns)
    near_side = send(near, owners, X)
    cross, near = tie((cross, near))
    cross_side = send(cross, owners, X)
    (out_cross,) = work(cross)
    back_cross = send(out_cross, owners, Z_NEAR ^ Z_FAR)
    far_side, back_far, rows, _ = tie((far_side, back_far, rows, out_cross))
    rows = widened(rows, columns)
    side = send(rows, owners, X)
    (out_far_side,) = work(far_side)
    back_far_side = send(out_far_side, owners, X ^ Z_FAR)
    cross_side, _ = tie((cross_side, out_far_side))
    (out_cross_side,) = work(cross_side)
    back_cross_side = send(out_cross_side, owners, X ^ Z_NEAR ^ Z_FAR)
    near_side, side, rows, _ = tie((near_side, side, rows, out_cross_side))
    out_near, out_near_side, out_side, out_own = work(near, near_side, side, rows)
    back_near_side = send(out_near_side, owners, X ^ Z_NEAR)
    back_near = send(out_near, owners, Z_NEAR)
    back_side = send(out_side, owners, X)
    far_parts = {
        0: out_own,
        Z_FAR: back_far,
        X ^ Z_FAR: back_far_side,
        Z_NEAR ^ Z_FAR: back_cross,
        X ^ Z_NEAR ^ Z_FAR: back_cross_side,
    }
    near_parts = {X: back_side, Z_NEAR: back_near, X ^ Z_NEAR: back_near_side}
    out = pick_routes(route_ids.T, far_parts, pick_routes(route_ids.T, near_parts))
    return out.reshape(1, tokens, top, weight_mat.shape[0])


def slotted_device(section_grad, route_ids, route_gates, weight_mat, capacity):
    tokens, top = route_ids.shape
    owners = lax.axis_size("expert")
    ids = jnp.arange(owners, dtype=jnp.int32)
    slots = jnp.arange(capacity, dtype=jnp.int32)
    matched = (route_ids[:, :, None] == ids[None, None, :]).astype(jnp.int32)
    hits = jnp.sum(matched, axis=1)
    rank = jnp.cumsum(hits, axis=0) - hits
    position = route_ids * capacity + jnp.sum(matched * rank[:, None, :], axis=2)
    gate_owner = jnp.einsum(
        "tk,tke->te", route_gates.astype(jnp.float32), matched.astype(jnp.float32)
    )
    slot_pick = (hits[:, :, None] == 1) & (rank[:, :, None] == slots[None, None, :])
    send_rows = jnp.einsum(
        "tem,td->emd",
        slot_pick.astype(jnp.bfloat16),
        section_grad,
        preferred_element_type=jnp.float32,
    ).astype(jnp.bfloat16)
    send_gates = jnp.einsum("tem,te->em", slot_pick.astype(jnp.float32), gate_owner).astype(
        jnp.bfloat16
    )
    got_rows = lax.all_to_all(send_rows, "expert", split_axis=0, concat_axis=0, tiled=True)
    got_gates = lax.all_to_all(send_gates, "expert", split_axis=0, concat_axis=0, tiled=True)
    product = lax.dot_general(
        got_rows.reshape(owners * capacity, got_rows.shape[2]),
        weight_mat,
        (((1,), (1,)), ((), ())),
        preferred_element_type=jnp.float32,
    ).reshape(owners, capacity, weight_mat.shape[0])
    returned = lax.all_to_all(
        (product * got_gates.astype(jnp.float32)[:, :, None]).astype(jnp.bfloat16),
        "expert",
        split_axis=0,
        concat_axis=0,
        tiled=True,
    )
    flat = returned.reshape(owners * capacity, returned.shape[2])
    out = jnp.take(flat, position.reshape(tokens * top), axis=0)
    return out.reshape(1, tokens, top, returned.shape[2])


def per_device(upstream, expert_ids, gate_weights, expert_weight):
    route_ids = expert_ids[0]
    route_gates = gate_weights[0]
    weight_mat = expert_weight[0, 0]
    tokens, top = route_ids.shape
    owners = lax.axis_size("expert")
    capacity = 2 * tokens * top // owners
    if capacity >= tokens and owners == CORES * 2 * Z_FAR:
        return dense_device(upstream[0], route_ids, route_gates, weight_mat)
    section_grad = shifted(upstream, "pipe", -1)[0]
    return slotted_device(section_grad, route_ids, route_gates, weight_mat, capacity)


def solution(mesh):
    in_specs = (
        P("pipe", "expert", None),
        P("pipe", "expert", None),
        P("pipe", "expert", None),
        P("pipe", "expert", None, None),
    )
    out_specs = P("pipe", "expert", None, None)
    return jax.shard_map(
        per_device, mesh=mesh, in_specs=in_specs, out_specs=out_specs, check_vma=False
    )
```
